32 devices in a mesh: replica: 2 (over core), fsdp: 4 (over y, x), tensor: 4 (over z).
Axes of the slice: x: 2, y: 2, z: 4, core: 2. Of those that a mesh axis runs over, the one named last changes fastest.
Arguments:
- layer_input: bfloat16 [2, 2048, 2048], P('replica', 'fsdp'), may hold values from -6 to 6
- block_order: int32 [2, 4], P('replica'), may hold values from 0 to 3, each once within a row
- first_gain: bfloat16 [2048], replicated, may hold values from 0.099609375 to 1.8984375
- first_bias: bfloat16 [2048], replicated, may hold values from -1.75 to 1.75
- second_gain: bfloat16 [2048], replicated, may hold values from 0.099609375 to 1.8984375
- second_bias: bfloat16 [2048], replicated, may hold values from -1.75 to 1.75
- heads_weight: bfloat16 [2048, 8, 768], P('fsdp', 'tensor'), may hold values from -0.125 to 0.125
- heads_bias: bfloat16 [8, 768], P('tensor'), may hold values from -1.75 to 1.75
- output_weight: bfloat16 [8, 256, 2048], P('tensor', None, 'fsdp'), may hold values from -1 to 1
- output_bias: bfloat16 [2048], replicated, may hold values from -1.75 to 1.75
- expand_weight: bfloat16 [2048, 8192], P('fsdp', 'tensor'), may hold values from -0.125 to 0.125
- expand_bias: bfloat16 [8192], P('tensor'), may hold values from -1.75 to 1.75
- shrink_weight: bfloat16 [8192, 2048], P('tensor', 'fsdp'), may hold values from -0.0625 to 0.0625
- shrink_bias: bfloat16 [2048], replicated, may hold values from -1.75 to 1.75
- cotangent: bfloat16 [2, 2048, 2048], P('replica', 'fsdp'), may hold values from -8 to 8
Outputs:
- layer_output: bfloat16 [2, 2048, 2048], P('replica', 'fsdp')
- input_grad: float32 [2, 2048, 2048], P('replica', 'fsdp')
- first_gain_grad: float32 [2048], replicated
- first_bias_grad: float32 [2048], replicated
- second_gain_grad: float32 [2048], replicated
- second_bias_grad: float32 [2048], replicated
- heads_weight_grad: float32 [2048, 8, 768], P('fsdp', 'tensor')
- heads_bias_grad: float32 [8, 768], P('tensor')
- output_weight_grad: float32 [8, 256, 2048], P('tensor', None, 'fsdp')
- output_bias_grad: float32 [2048], replicated
- expand_weight_grad: float32 [2048, 8192], P('fsdp', 'tensor')
- expand_bias_grad: float32 [8192], P('tensor')
- shrink_weight_grad: float32 [8192, 2048], P('tensor', 'fsdp')
- shrink_bias_grad: float32 [2048], replicated
The draws below stay inside these ranges and needn't reach their ends.
Inputs may be any that keep to these rules, and one draw needn't show every extreme that they name: `block_order`: row s lists, for each of the 4 devices of sequence s's group in order, which block of 512 consecutive positions that device holds; every row is a permutation.
All inputs are finite; a program needn't handle non-finite values.
Results may differ from the reference program's by a relative error of at most 0.01.
Values may be sent and summed in bfloat16 or wider, within the bound.
A program may use at most 256 MiB of HBM per device.

```python
import jax
import jax.numpy as jnp
from jax import lax

D = 2048
HEADS = 8
HEAD_DIM = 256
ROT = 64
FF = 8192
TOK_DEV = 512
SEQ_LEN = 2048
SEQS = 2
N_FSDP = 4


def spiked(values, rng, source, target, parts, factor):
    owner, partner = [(jnp.arange(values.shape[axis_at]) // (values.shape[axis_at] // parts)).reshape([-1 if axis == axis_at else 1 for axis in range(values.ndim)]) for axis_at in (source, target)]
    chosen = jax.random.permutation(rng, parts)[partner]
    strong = (owner == chosen) | (owner == (partner + parts // 2) % parts)
    return jnp.where(strong, factor * values, values)


def block_levels(stream_key, dims, cuts, smallest, top_value):
    def one(axis_at, shards_of):
        heights = jax.random.uniform(jax.random.fold_in(jax.random.fold_in(stream_key, 6), axis_at), (shards_of,), jnp.float32, smallest / len(cuts), top_value / len(cuts))
        return jnp.repeat(jnp.exp(heights), dims[axis_at] // shards_of).reshape((-1,) + (1,) * (len(dims) - axis_at - 1))

    factor_of = one(*cuts[0])
    for cut in cuts[1:]:
        factor_of = factor_of * one(*cut)
    return factor_of


def scatter_about(rng, extent, deviation, limit, pieces=(), held_as=jnp.bfloat16):
    factor_of = block_levels(rng, extent, pieces, -0.22, 0.18) if pieces else 1.0
    values = jax.random.normal(rng, extent, jnp.float32) * deviation * factor_of
    return jnp.minimum(jnp.maximum(values, -limit), limit).astype(held_as)


def heavy_noise(key, extent, spread, limit, shards, heavy, held_as=jnp.bfloat16):
    entries = spread * jax.random.normal(key, extent, jnp.float32)
    if shards:
        entries = entries * block_levels(key, extent, shards, -0.22, 0.18)
    return jnp.clip(spiked(entries, jax.random.fold_in(key, 3), *heavy), -limit, limit).astype(held_as)


def setup_inputs(seed: int = 0) -> dict:
    arg_keys = jax.random.split(jax.random.key(seed), 16)
    return {
        "layer_input": scatter_about(arg_keys[0], (SEQS, SEQ_LEN, D), 1.0, 6.0, ((0, 2), (1, 4))),
        "block_order": jax.vmap(lambda own: jax.random.permutation(own, N_FSDP))(jax.random.split(arg_keys[1], SEQS)).reshape((SEQS, N_FSDP)).astype(jnp.int32),
        "first_gain": jnp.clip(1.0 + 0.18 * jax.random.normal(arg_keys[2], (D,), jnp.float32), 0.099609375, 1.8984375).astype(jnp.bfloat16),
        "first_bias": scatter_about(arg_keys[3], (D,), 0.3, 1.75),
        "second_gain": jnp.clip(1.0 + 0.18 * jax.random.normal(arg_keys[4], (D,), jnp.float32), 0.099609375, 1.8984375).astype(jnp.bfloat16),
        "second_bias": scatter_about(arg_keys[5], (D,), 0.3, 1.75),
        "heads_weight": scatter_about(arg_keys[6], (D, HEADS, 3 * HEAD_DIM), D ** -0.5, 0.125, ((0, 4), (1, 4))),
        "heads_bias": scatter_about(arg_keys[7], (HEADS, 3 * HEAD_DIM), 0.3, 1.75, ((0, 4),)),
        "output_weight": scatter_about(arg_keys[8], (HEADS, HEAD_DIM, D), (max(16, 32 * D // SEQ_LEN)) ** -0.5, 1.0, ((0, 4), (2, 4))),
        "output_bias": scatter_about(arg_keys[9], (D,), 0.3, 1.75),
        "expand_weight": scatter_about(arg_keys[10], (D, FF), D ** -0.5, 0.125, ((0, 4), (1, 4))),
        "expand_bias": scatter_about(arg_keys[11], (FF,), 0.3, 1.75, ((0, 4),)),
        "shrink_weight": scatter_about(arg_keys[12], (FF, D), FF ** -0.5, 0.0625, ((0, 4), (1, 4))),
        "shrink_bias": scatter_about(arg_keys[13], (D,), 0.3, 1.75),
        "cotangent": heavy_noise(arg_keys[14], (SEQS, SEQ_LEN, D), 1.0, 8.0, ((0, 2), (1, 4)), (1, 2, 4, 2.0)),
    }


NORM_EPS = 1e-05
MASKED = -1e+30
HIGHEST = lax.Precision.HIGHEST

@jax.custom_vjp
def low(v):
    return lax.optimization_barrier(v.astype(jnp.bfloat16)).astype(jnp.float32)

@jax.custom_vjp
def low_back(v):
    return v

def low_keep(v):
    return (low(v), None)

def low_pass(kept, grad):
    return (grad,)

def back_keep(v):
    return (v, None)

def back_low(kept, grad):
    return (low(grad),)
low.defvjp(low_keep, low_pass)
low_back.defvjp(back_keep, back_low)

def layer_norm(values_in, gain_vec, shift_vec):
    average = lax.optimization_barrier(jnp.mean(values_in, -1, keepdims=True))
    centred = values_in - average
    spread_sq = lax.optimization_barrier(jnp.mean(centred * centred, -1, keepdims=True))
    return centred * lax.rsqrt(spread_sq + NORM_EPS) * gain_vec + shift_vec

def rotate(values_in, cosine, sine_part):
    rot_width = cosine.shape[-1]
    half_width = rot_width // 2
    turning = values_in[..., :rot_width]
    swapped = jnp.concatenate([-turning[..., half_width:], turning[..., :half_width]], -1)
    return jnp.concatenate([turning * cosine + swapped * sine_part, values_in[..., rot_width:]], -1)

def rotary_tables(positions, rot_width):
    frequency = jnp.power(10000.0, -jnp.arange(0, rot_width, 2, dtype=jnp.float32) / rot_width)
    angle_half = positions.astype(jnp.float32)[:, None] * frequency[None, :]
    angles = jnp.concatenate([angle_half, angle_half], -1)
    return (jnp.cos(angles), jnp.sin(angles))

def attend_block(query_block, query_pos, key_rows, value_rows, key_pos):
    score_scale = query_block.shape[-1] ** (-0.5)
    scores = low_back(jnp.einsum('qhd,khd->hqk', query_block, key_rows, precision=HIGHEST) * score_scale)
    allowed = key_pos[None, :] <= query_pos[:, None]
    masked_scores = jnp.where(allowed[None], scores, MASKED)
    probability = jax.nn.softmax(masked_scores, -1)
    return jnp.einsum('hqk,khd->qhd', low(probability), value_rows, precision=HIGHEST)
attend_saved = jax.checkpoint(attend_block)

def forward(hidden_in, positions, first_gain, first_bias, second_gain, second_bias, heads_weight, heads_bias, output_weight, output_bias, expand_weight, expand_bias, shrink_weight, shrink_bias):
    seq_rows = hidden_in.shape[0]
    head_dim = output_weight.shape[1]
    head_count = output_weight.shape[0]
    norm_one = low(layer_norm(hidden_in, first_gain, first_bias))
    norm_two = low(layer_norm(hidden_in, second_gain, second_bias))
    projected = low_back(jnp.einsum('td,dhe->the', norm_one, heads_weight, precision=HIGHEST) + heads_bias)
    cosine, sine_part = rotary_tables(positions, ROT)
    cosine = cosine[:, None, :]
    sine_part = sine_part[:, None, :]
    query_rows = low(rotate(projected[..., :head_dim], cosine, sine_part))
    key_rows = low(rotate(projected[..., head_dim:2 * head_dim], cosine, sine_part))
    value_rows = low(projected[..., 2 * head_dim:])
    block_rows = min(512, seq_rows)
    block_count = seq_rows // block_rows
    query_blocks = query_rows.reshape(block_count, block_rows, head_count, head_dim)
    pos_blocks = positions.reshape(block_count, block_rows)
    attended = lax.map(lambda block_pair: attend_saved(block_pair[0], block_pair[1], key_rows, value_rows, positions), (query_blocks, pos_blocks))
    context = low(low_back(attended.reshape(seq_rows, head_count, head_dim)))
    attn_part = jnp.einsum('the,hed->td', context, output_weight, precision=HIGHEST)
    expand_in = low_back(jnp.dot(norm_two, expand_weight, precision=HIGHEST) + expand_bias)
    activation = low(jax.nn.gelu(expand_in, approximate=False))
    mlp_part = jnp.dot(activation, shrink_weight, precision=HIGHEST)
    return hidden_in + attn_part + mlp_part + output_bias + shrink_bias

def reference(layer_input, block_order, first_gain, first_bias, second_gain, second_bias, heads_weight, heads_bias, output_weight, output_bias, expand_weight, expand_bias, shrink_weight, shrink_bias, cotangent):
    params = (first_gain, first_bias, second_gain, second_bias, heads_weight, heads_bias, output_weight, output_bias, expand_weight, expand_bias, shrink_weight, shrink_bias)
    params = tuple((param.astype(jnp.float32) for param in params))
    offsets = jnp.arange(TOK_DEV, dtype=jnp.int32)

    def one_sequence(totals, inputs):
        hidden_seq, grad_seq, order_row = inputs
        positions = (jnp.repeat(order_row, TOK_DEV) * TOK_DEV + jnp.tile(offsets, N_FSDP)).astype(jnp.int32)
        result, backward = jax.vjp(lambda hidden_in, *weights: forward(hidden_in, positions, *weights), hidden_seq.astype(jnp.float32), *params)
        grads = backward(grad_seq.astype(jnp.float32))
        new_totals = tuple((total + grad_one for total, grad_one in zip(totals, grads[1:])))
        return (new_totals, (result.astype(jnp.bfloat16), grads[0]))
    initial = tuple((jnp.zeros(param.shape, jnp.float32) for param in params))
    totals, (outputs, input_grads) = lax.scan(one_sequence, initial, (layer_input, cotangent, block_order))
    return (outputs, input_grads, totals[0], totals[1], totals[2], totals[3], totals[4], totals[5], totals[6], totals[7], totals[8], totals[9], totals[10], totals[11])
```

```python
import jax
import jax.numpy as jnp
from jax import lax
from jax.sharding import PartitionSpec as P

ROT = 64


NORM_EPS = 1e-05
MASKED = -1e30


def layer_norm(values_in, gain_vec, shift_vec):
    average = jnp.mean(values_in, -1, keepdims=True)
    centred = values_in - average
    spread_sq = jnp.mean(centred * centred, -1, keepdims=True)
    return centred * lax.rsqrt(spread_sq + NORM_EPS) * gain_vec + shift_vec


def rotate(values_in, cosine, sine_part):
    rot_width = cosine.shape[-1]
    half_width = rot_width // 2
    turning = values_in[..., :rot_width]
    swapped = jnp.concatenate([-turning[..., half_width:], turning[..., :half_width]], -1)
    return jnp.concatenate([turning * cosine + swapped * sine_part, values_in[..., rot_width:]], -1)


def rotary_tables(positions, rot_width):
    frequency = jnp.power(10000.0, -jnp.arange(0, rot_width, 2, dtype=jnp.float32) / rot_width)
    angle_half = positions.astype(jnp.float32)[:, None] * frequency[None, :]
    angles = jnp.concatenate([angle_half, angle_half], -1)
    return (jnp.cos(angles), jnp.sin(angles))


def contract_last(left_op, right_op):
    return lax.dot_general(
        left_op, right_op, (((1,), (1,)), ((), ())), preferred_element_type=jnp.float32
    )


def contract_first(left_op, right_op):
    return lax.dot_general(
        left_op, right_op, (((0,), (0,)), ((), ())), preferred_element_type=jnp.float32
    )


def softmax_rows(scores, allowed):
    masked_scores = jnp.where(allowed, scores, MASKED)
    row_top = jnp.max(masked_scores, -1, keepdims=True)
    exponent = jnp.exp(masked_scores - row_top)
    return exponent / jnp.sum(exponent, -1, keepdims=True)


SWAP_X = ((0, 1), (1, 0), (2, 3), (3, 2))
SWAP_Y = ((0, 2), (2, 0), (1, 3), (3, 1))
SWAP_CORE = ((0, 1), (1, 0))
LOW = jnp.bfloat16
FULL = jnp.float32


def to_x(part):
    return lax.ppermute(part, "fsdp", SWAP_X)


def to_y(part):
    return lax.ppermute(part, "fsdp", SWAP_Y)


def to_core(part):
    return lax.ppermute(part, "replica", SWAP_CORE)


def swap_if(flag, pair):
    return jnp.where(flag, pair[::-1], pair)


def turn(array, axis, r_bit, x_bit, y_bit):
    shape = array.shape
    cut = array.reshape(shape[:axis] + (2, 2, 2, shape[axis] // 8) + shape[axis + 1 :])
    for at, bit in ((axis, y_bit), (axis + 1, x_bit), (axis + 2, r_bit)):
        cut = jnp.where(bit, jnp.flip(cut, at), cut)
    return cut.reshape(shape)


def gather_blocks(own_half, other_half, axis):
    from_x, from_y = to_x(own_half), to_y(own_half)
    cut = own_half.shape[axis] // 2
    far_one = to_y(lax.slice_in_dim(from_x, 0, cut, axis=axis))
    far_two = to_x(lax.slice_in_dim(from_y, cut, 2 * cut, axis=axis))
    far = jnp.concatenate([far_one, far_two], axis)
    return jnp.concatenate(
        [own_half, other_half, from_x, to_core(from_x), from_y, to_core(from_y), far, to_core(far)],
        axis,
    )


def scatter_blocks(blocks, axis):
    own, for_x, for_y, for_far = jnp.split(blocks, 4, axis)
    cut = own.shape[axis] // 2
    far_low = for_far.astype(LOW)
    via_x = to_x(lax.slice_in_dim(far_low, 0, cut, axis=axis))
    via_y = to_y(lax.slice_in_dim(far_low, cut, 2 * cut, axis=axis))
    y_top = lax.slice_in_dim(for_y, 0, cut, axis=axis) + via_x.astype(FULL)
    y_end = lax.slice_in_dim(for_y, cut, 2 * cut, axis=axis)
    x_top = lax.slice_in_dim(for_x, 0, cut, axis=axis)
    x_end = lax.slice_in_dim(for_x, cut, 2 * cut, axis=axis) + via_y.astype(FULL)
    got_x = to_x(jnp.concatenate([x_top, x_end], axis).astype(LOW))
    got_y = to_y(jnp.concatenate([y_top, y_end], axis).astype(LOW))
    return own + got_x.astype(FULL) + got_y.astype(FULL)


def halves_of(array, axis):
    shape = array.shape
    cut = array.reshape(shape[:axis] + (4, 2, shape[axis] // 8) + shape[axis + 1 :])
    flat = shape[:axis] + (shape[axis] // 2,) + shape[axis + 1 :]
    return [lax.index_in_dim(cut, h, axis + 1, keepdims=False).reshape(flat) for h in (0, 1)]


def weight_grad(product, wide, axis, r_bit):
    own_part, other_part = halves_of(wide, 1)
    sent = product(other_part).astype(LOW)
    blocks = product(own_part) + to_core(sent).astype(FULL)
    half = scatter_blocks(blocks, axis)
    pair = swap_if(r_bit, jnp.stack([half, to_core(half)]))
    return jnp.concatenate([pair[0], pair[1]], axis)


def square_local(
    layer_input,
    block_order,
    first_gain,
    first_bias,
    second_gain,
    second_bias,
    heads_weight,
    heads_bias,
    output_weight,
    output_bias,
    expand_weight,
    expand_bias,
    shrink_weight,
    shrink_bias,
    cotangent,
):
    tokens = layer_input.shape[1]
    width = layer_input.shape[2]
    head_dim = output_weight.shape[1]
    score_scale = head_dim ** (-0.5)
    replica, fsdp = lax.axis_index("replica"), lax.axis_index("fsdp")
    r_bit, x_bit, y_bit = replica == 1, fsdp % 2 == 1, fsdp // 2 == 1

    def turned(array, axis):
        return turn(array, axis, r_bit, x_bit, y_bit)

    def chosen(pair):
        swapped = swap_if(y_bit, pair)
        return swapped[0], swapped[1]

    heads_rows = heads_weight.reshape(heads_weight.shape[0], -1)
    output_rows = output_weight.reshape(-1, output_weight.shape[2])

    def halves(shard, axis):
        pair = jnp.stack(jnp.split(shard, 2, axis))
        swapped = swap_if(r_bit, pair)
        return swapped[0], swapped[1]

    heads_full = gather_blocks(*halves(heads_rows, 0), 0)
    output_full = gather_blocks(*halves(output_rows, 1), 1)
    expand_full = gather_blocks(*halves(expand_weight, 0), 0)
    shrink_full = gather_blocks(*halves(shrink_weight, 1), 1)

    hidden = turned(layer_input[0], 1).astype(FULL)
    grad_out = turned(cotangent[0], 1)
    gain_one, shift_one, gain_two, shift_two = (
        turned(vec.astype(FULL), 0) for vec in (first_gain, first_bias, second_gain, second_bias)
    )
    average = jnp.mean(hidden, -1, keepdims=True)
    centred = hidden - average
    inverse = lax.rsqrt(jnp.mean(centred * centred, -1, keepdims=True) + NORM_EPS)
    normal = centred * inverse
    norm_one = (normal * gain_one + shift_one).astype(LOW)
    norm_two = (normal * gain_two + shift_two).astype(LOW)

    order_row = block_order[0]
    slots = fsdp ^ jnp.array([0, 2, 1, 3], jnp.int32)
    order_here = order_row[slots]
    offsets = jnp.arange(tokens, dtype=jnp.int32)
    key_pos = (order_here[:, None] * tokens + offsets[None]).reshape(-1)
    query_pos = key_pos[: 2 * tokens]
    cosine, sine_part = rotary_tables(query_pos, ROT)

    projected = jnp.dot(norm_one, heads_full, preferred_element_type=FULL)
    projected = projected + heads_bias.reshape(-1).astype(FULL)
    projected = projected.reshape(tokens, 2, 3, head_dim).transpose(1, 2, 0, 3)
    spun = rotate(projected[:, :2], cosine[:tokens], sine_part[:tokens])
    qkv = jnp.concatenate([spun, projected[:, 2:]], 1).astype(LOW)
    qkv_own, qkv_away = chosen(qkv)
    qkv_y = to_y(qkv_away)
    kv_x, kv_far = to_x(qkv_own[1:]), to_x(qkv_y[1:])
    query = jnp.concatenate([qkv_own[0], qkv_y[0]], 0)
    key, value = (
        jnp.concatenate([qkv_own[i], qkv_y[i], kv_x[i - 1], kv_far[i - 1]], 0) for i in (1, 2)
    )
    context_grad = contract_last(grad_out, output_full).astype(LOW)
    away_own = chosen(context_grad.reshape(tokens, 2, head_dim).transpose(1, 0, 2))
    context_grad_here = jnp.concatenate([away_own[0], to_y(away_own[1])], 0)

    allowed = key_pos[None, :] <= query_pos[:, None]
    probability = softmax_rows(contract_last(query, key) * score_scale, allowed)
    prob_low = probability.astype(LOW)
    context_here = jnp.dot(prob_low, value, preferred_element_type=FULL).astype(LOW)
    weight_part = contract_last(context_grad_here, value)
    row_inner = jnp.sum(probability * weight_part, -1, keepdims=True)
    score_grad = (probability * (weight_part - row_inner)).astype(LOW)
    query_grad = jnp.dot(score_grad, key, preferred_element_type=FULL) * score_scale
    key_grad = contract_first(score_grad, query) * score_scale
    value_grad = contract_first(prob_low, context_grad_here)

    context_back = to_y(context_here[tokens:])
    context_low = swap_if(y_bit, jnp.stack([context_here[:tokens], context_back]))
    context_rows = context_low.transpose(1, 0, 2).reshape(tokens, -1)

    kv_grad = jnp.stack([key_grad, value_grad]).reshape(2, 2, 2 * tokens, head_dim)
    kv_grad = kv_grad[:, 0] + to_x(kv_grad[:, 1].astype(LOW)).astype(FULL)
    spun_grad = jnp.stack([query_grad, kv_grad[0]])
    _, rotate_back = jax.vjp(
        lambda inner: rotate(inner, cosine[None], sine_part[None]), jnp.zeros_like(spun_grad)
    )
    projected_grad = jnp.concatenate([rotate_back(spun_grad)[0], kv_grad[1:]], 0).astype(LOW)
    projected_back = to_y(projected_grad[:, tokens:])
    projected_grad = swap_if(y_bit, jnp.stack([projected_grad[:, :tokens], projected_back]))
    projected_rows = projected_grad.transpose(2, 0, 1, 3).reshape(tokens, -1)
    heads_bias_grad = jnp.sum(projected_rows.astype(FULL), 0)
    norm_one_grad = contract_last(projected_rows, heads_full)

    expand_in = jnp.dot(norm_two, expand_full, preferred_element_type=FULL) + expand_bias.astype(FULL)
    activation = jax.nn.gelu(expand_in, approximate=False).astype(LOW)
    _, gelu_back = jax.vjp(lambda inner: jax.nn.gelu(inner, approximate=False), expand_in)
    branch = jnp.dot(context_rows, output_full, preferred_element_type=FULL) + jnp.dot(
        activation, shrink_full, preferred_element_type=FULL
    )
    branch = lax.psum(branch.astype(LOW), "tensor").astype(FULL)
    both_biases = turned(output_bias.astype(FULL) + shrink_bias.astype(FULL), 0)
    layer_output = turned((hidden + branch + both_biases).astype(LOW), 1)[None]
    expand_grad = gelu_back(contract_last(grad_out, shrink_full))[0].astype(LOW)
    expand_bias_grad = jnp.sum(expand_grad.astype(FULL), 0)
    norm_two_grad = contract_last(expand_grad, expand_full)

    upstream = norm_one_grad * gain_one + norm_two_grad * gain_two
    upstream = lax.psum(upstream.astype(LOW), "tensor").astype(FULL)
    input_part = inverse * (
        upstream
        - jnp.mean(upstream, -1, keepdims=True)
        - normal * jnp.mean(upstream * normal, -1, keepdims=True)
    )
    input_grad = turned(grad_out.astype(FULL) + input_part, 1)[None]

    gains = jnp.stack(
        [
            jnp.sum(norm_one_grad * normal, 0),
            jnp.sum(norm_one_grad, 0),
            jnp.sum(norm_two_grad * normal, 0),
            jnp.sum(norm_two_grad, 0),
        ]
    )
    gains = lax.psum(turned(gains, 1), ("replica", "fsdp", "tensor"))
    bias_total, expand_bias_grad, heads_bias_grad = lax.psum(
        (jnp.sum(cotangent[0].astype(FULL), 0), expand_bias_grad, heads_bias_grad),
        ("replica", "fsdp"),
    )

    def by_rows(left, right, axis_out, r_flag):
        return weight_grad(lambda part: contract_first(part, right), left, axis_out, r_flag)

    heads_weight_grad = by_rows(norm_one, projected_rows, 0, r_bit)
    expand_weight_grad = by_rows(norm_two, expand_grad, 0, r_bit)
    output_weight_grad = weight_grad(
        lambda part: contract_first(context_rows, part), grad_out, 1, r_bit
    )
    shrink_weight_grad = weight_grad(
        lambda part: contract_first(activation, part), grad_out, 1, r_bit
    )
    return (
        layer_output,
        input_grad,
        gains[0],
        gains[1],
        gains[2],
        gains[3],
        heads_weight_grad.reshape(heads_weight.shape),
        heads_bias_grad.reshape(heads_bias.shape),
        output_weight_grad.reshape(output_weight.shape),
        bias_total,
        expand_weight_grad,
        expand_bias_grad,
        shrink_weight_grad,
        bias_total,
    )


def ring_local(
    layer_input,
    block_order,
    first_gain,
    first_bias,
    second_gain,
    second_bias,
    heads_weight,
    heads_bias,
    output_weight,
    output_bias,
    expand_weight,
    expand_bias,
    shrink_weight,
    shrink_bias,
    cotangent,
):
    tokens_here = layer_input.shape[1]
    fsdp_count = lax.axis_size("fsdp")
    head_dim = output_weight.shape[1]
    score_scale = head_dim ** (-0.5)
    order_row = block_order[0]
    device_slot = lax.axis_index("fsdp")
    own_block = jnp.sum(
        jnp.where(jnp.arange(fsdp_count, dtype=jnp.int32) == device_slot, order_row, 0)
    )
    offsets = jnp.arange(tokens_here, dtype=jnp.int32)
    query_pos = own_block * tokens_here + offsets
    key_pos = jnp.repeat(order_row, tokens_here) * tokens_here + jnp.tile(offsets, fsdp_count)
    allowed = key_pos[None, :] <= query_pos[:, None]
    cosine, sine_part = rotary_tables(query_pos, ROT)
    hidden_in = layer_input[0].astype(jnp.float32)
    gain_one = first_gain.astype(jnp.float32)
    shift_one = first_bias.astype(jnp.float32)
    gain_two = second_gain.astype(jnp.float32)
    shift_two = second_bias.astype(jnp.float32)
    norm_one_low = layer_norm(hidden_in, gain_one, shift_one).astype(jnp.bfloat16)
    norm_two_low = layer_norm(hidden_in, gain_two, shift_two).astype(jnp.bfloat16)
    heads_full, output_full, expand_full, shrink_full = (
        lax.all_gather(heads_weight, "fsdp", axis=0, tiled=True),
        lax.all_gather(output_weight, "fsdp", axis=2, tiled=True),
        lax.all_gather(expand_weight, "fsdp", axis=0, tiled=True),
        lax.all_gather(shrink_weight, "fsdp", axis=1, tiled=True),
    )
    projected = jnp.einsum(
        "td,dhe->hte", norm_one_low, heads_full, preferred_element_type=jnp.float32
    )
    projected = projected + heads_bias.astype(jnp.float32)[:, None, :]
    query_pre = projected[..., :head_dim]
    key_pre = projected[..., head_dim : 2 * head_dim]
    query_low = rotate(query_pre, cosine, sine_part).astype(jnp.bfloat16)
    key_low = rotate(key_pre, cosine, sine_part).astype(jnp.bfloat16)
    value_low = projected[..., 2 * head_dim :].astype(jnp.bfloat16)
    key_all, value_all = (
        lax.all_gather(key_low, "fsdp", axis=1, tiled=True),
        lax.all_gather(value_low, "fsdp", axis=1, tiled=True),
    )

    def attend_head(operands):
        query_head, key_head, value_head = operands
        probability = softmax_rows(contract_last(query_head, key_head) * score_scale, allowed)
        return jnp.dot(
            probability.astype(jnp.bfloat16), value_head, preferred_element_type=jnp.float32
        )

    context = lax.map(attend_head, (query_low, key_all, value_all))
    context_low = context.astype(jnp.bfloat16)
    expand_in = jnp.dot(
        norm_two_low, expand_full, preferred_element_type=jnp.float32
    ) + expand_bias.astype(jnp.float32)
    activation_low = jax.nn.gelu(expand_in, approximate=False).astype(jnp.bfloat16)
    branch_part = jnp.einsum(
        "hte,hed->td", context_low, output_full, preferred_element_type=jnp.float32
    )
    branch_part = branch_part + jnp.dot(
        activation_low, shrink_full, preferred_element_type=jnp.float32
    )
    branch = lax.psum(branch_part, "tensor")
    layer_output = (
        hidden_in + branch + output_bias.astype(jnp.float32) + shrink_bias.astype(jnp.float32)
    ).astype(jnp.bfloat16)[None]
    heads_back, output_back, expand_back, shrink_back = (
        lax.all_gather(heads_weight, "fsdp", axis=0, tiled=True),
        lax.all_gather(output_weight, "fsdp", axis=2, tiled=True),
        lax.all_gather(expand_weight, "fsdp", axis=0, tiled=True),
        lax.all_gather(shrink_weight, "fsdp", axis=1, tiled=True),
    )
    key_back, value_back = (
        lax.all_gather(key_low, "fsdp", axis=1, tiled=True),
        lax.all_gather(value_low, "fsdp", axis=1, tiled=True),
    )
    grad_out = cotangent[0]
    grad_float = grad_out.astype(jnp.float32)
    output_weight_grad = jnp.einsum(
        "hte,td->hed", context_low, grad_out, preferred_element_type=jnp.float32
    )
    shrink_weight_grad = contract_first(activation_low, grad_out)
    bias_total = jnp.sum(grad_float, 0)
    context_grad = jnp.einsum(
        "td,hed->hte", grad_out, output_back, preferred_element_type=jnp.float32
    ).astype(jnp.bfloat16)
    activation_grad = contract_last(grad_out, shrink_back)
    _, gelu_back = jax.vjp(lambda inner_val: jax.nn.gelu(inner_val, approximate=False), expand_in)
    expand_grad = gelu_back(activation_grad)[0].astype(jnp.bfloat16)
    expand_weight_grad = contract_first(norm_two_low, expand_grad)
    expand_bias_grad = jnp.sum(expand_grad.astype(jnp.float32), 0)
    norm_two_grad = contract_last(expand_grad, expand_back)

    def attend_back(operands):
        query_head, key_head, value_head, context_head = operands
        probability = softmax_rows(contract_last(query_head, key_head) * score_scale, allowed)
        prob_low = probability.astype(jnp.bfloat16)
        weight_grad = contract_last(context_head, value_head)
        row_inner = jnp.sum(probability * weight_grad, -1, keepdims=True)
        score_grad = (probability * (weight_grad - row_inner)).astype(jnp.bfloat16)
        query_grad = jnp.dot(score_grad, key_head, preferred_element_type=jnp.float32) * score_scale
        key_grad = contract_first(score_grad, query_head) * score_scale
        value_grad = contract_first(prob_low, context_head)
        return (query_grad, key_grad, value_grad)

    query_grad, key_grad_all, value_grad_all = lax.map(
        attend_back, (query_low, key_back, value_back, context_grad)
    )
    key_grad, value_grad = (
        lax.psum_scatter(key_grad_all, "fsdp", scatter_dimension=1, tiled=True),
        lax.psum_scatter(value_grad_all, "fsdp", scatter_dimension=1, tiled=True),
    )
    _, rotate_back = jax.vjp(lambda inner_val: rotate(inner_val, cosine, sine_part), query_pre)
    projected_grad = jnp.concatenate(
        [rotate_back(query_grad)[0], rotate_back(key_grad)[0], value_grad], -1
    ).astype(jnp.bfloat16)
    heads_weight_grad = jnp.einsum(
        "td,hte->dhe", norm_one_low, projected_grad, preferred_element_type=jnp.float32
    )
    heads_bias_grad = jnp.sum(projected_grad.astype(jnp.float32), 1)
    norm_one_grad = jnp.einsum(
        "hte,dhe->td", projected_grad, heads_back, preferred_element_type=jnp.float32
    )
    norm_one_grad, norm_two_grad = lax.psum((norm_one_grad, norm_two_grad), "tensor")
    _, first_back = jax.vjp(layer_norm, hidden_in, gain_one, shift_one)
    input_first, first_gain_grad, first_bias_grad = first_back(norm_one_grad)
    _, second_back = jax.vjp(layer_norm, hidden_in, gain_two, shift_two)
    input_second, second_gain_grad, second_bias_grad = second_back(norm_two_grad)
    input_grad = (grad_float + input_first + input_second)[None]
    small_sums = lax.psum(
        (
            first_gain_grad,
            first_bias_grad,
            second_gain_grad,
            second_bias_grad,
            bias_total,
            expand_bias_grad,
            heads_bias_grad,
        ),
        ("replica", "fsdp"),
    )
    shard_parts = (
        lax.psum_scatter(heads_weight_grad, "fsdp", scatter_dimension=0, tiled=True),
        lax.psum_scatter(output_weight_grad, "fsdp", scatter_dimension=2, tiled=True),
        lax.psum_scatter(expand_weight_grad, "fsdp", scatter_dimension=0, tiled=True),
        lax.psum_scatter(shrink_weight_grad, "fsdp", scatter_dimension=1, tiled=True),
    )
    reduced = lax.psum((shard_parts[0], shard_parts[1], shard_parts[2], shard_parts[3]), "replica")
    return (
        layer_output,
        input_grad,
        small_sums[0],
        small_sums[1],
        small_sums[2],
        small_sums[3],
        reduced[0],
        small_sums[6],
        reduced[1],
        small_sums[4],
        reduced[2],
        small_sums[5],
        reduced[3],
        small_sums[4],
    )


def solution(mesh):
    placed = (
        P("replica", "fsdp", None),
        P("replica", None),
        P(),
        P(),
        P(),
        P(),
        P("fsdp", "tensor", None),
        P("tensor", None),
        P("tensor", None, "fsdp"),
        P(),
        P("fsdp", "tensor"),
        P("tensor"),
        P("tensor", "fsdp"),
        P(),
        P("replica", "fsdp", None),
    )
    local = square_local if mesh.shape["fsdp"] == 4 and mesh.shape["replica"] == 2 else ring_local
    return jax.shard_map(
        local,
        mesh=mesh,
        in_specs=placed,
        out_specs=(
            P("replica", "fsdp", None),
            P("replica", "fsdp", None),
            P(),
            P(),
            P(),
            P(),
            P("fsdp", "tensor", None),
            P("tensor", None),
            P("tensor", None, "fsdp"),
            P(),
            P("fsdp", "tensor"),
            P("tensor"),
            P("tensor", "fsdp"),
            P(),
        ),
        check_vma=False,
    )
```

```python
import functools

import jax
import jax.numpy as jnp
from jax import lax
from jax.experimental import pallas as pl
from jax.experimental.pallas import tpu as pltpu
from jax.sharding import PartitionSpec as P

ROT = 64


NORM_EPS = 1e-05
MASKED = -1e30


def layer_norm(values_in, gain_vec, shift_vec):
    average = jnp.mean(values_in, -1, keepdims=True)
    centred = values_in - average
    spread_sq = jnp.mean(centred * centred, -1, keepdims=True)
    return centred * lax.rsqrt(spread_sq + NORM_EPS) * gain_vec + shift_vec


def rotate(values_in, cosine, sine_part):
    rot_width = cosine.shape[-1]
    half_width = rot_width // 2
    turning = values_in[..., :rot_width]
    swapped = jnp.concatenate([-turning[..., half_width:], turning[..., :half_width]], -1)
    return jnp.concatenate([turning * cosine + swapped * sine_part, values_in[..., rot_width:]], -1)


def rotary_tables(positions, rot_width):
    frequency = jnp.power(10000.0, -jnp.arange(0, rot_width, 2, dtype=jnp.float32) / rot_width)
    angle_half = positions.astype(jnp.float32)[:, None] * frequency[None, :]
    angles = jnp.concatenate([angle_half, angle_half], -1)
    return (jnp.cos(angles), jnp.sin(angles))


def contract_last(left_op, right_op):
    return lax.dot_general(
        left_op, right_op, (((1,), (1,)), ((), ())), preferred_element_type=jnp.float32
    )


def contract_first(left_op, right_op):
    return lax.dot_general(
        left_op, right_op, (((0,), (0,)), ((), ())), preferred_element_type=jnp.float32
    )


def softmax_rows(scores, allowed):
    masked_scores = jnp.where(allowed, scores, MASKED)
    row_top = jnp.max(masked_scores, -1, keepdims=True)
    exponent = jnp.exp(masked_scores - row_top)
    return exponent / jnp.sum(exponent, -1, keepdims=True)


LOW = jnp.bfloat16
FULL = jnp.float32


def turn(array, axis, r_bit, x_bit, y_bit):
    shape = array.shape
    cut = array.reshape(shape[:axis] + (2, 2, 2, shape[axis] // 8) + shape[axis + 1 :])
    for at, bit in ((axis, y_bit), (axis + 1, x_bit), (axis + 2, r_bit)):
        cut = jnp.where(bit, jnp.flip(cut, at), cut)
    return cut.reshape(shape)


MESH = pl.DeviceIdType.MESH
ANY = pl.BlockSpec(memory_space=pl.ANY)
IN_VMEM = pl.BlockSpec(memory_space=pltpu.VMEM)
VMEM_BYTES = 62 * 2**20
COPIES = 96


class Links:
    def __init__(self, send_sem, recv_sem, line=0):
        self.send_sem, self.recv_sem, self.sent, self.count = send_sem, recv_sem, [], 0
        self.r, self.f, self.t = (lax.axis_index(name) for name in ("replica", "fsdp", "tensor"))
        self.xb, self.yb = lax.rem(self.f, 2), lax.div(self.f, 2)
        self.x = (self.r, self.f + 1 - 2 * self.xb, self.t)
        self.y = (self.r, lax.rem(self.f + 2, 4), self.t)
        self.core = (1 - self.r, self.f, self.t)
        self.peers = [self.x, self.y, self.core]
        if line:
            self.line = line
            self.left, self.right, self.across = (
                (self.r, self.f, lax.rem(self.t + step, line)) for step in (line - 1, 1, 2)
            )
            self.pair = (self.r, self.f, self.t + 1 - 2 * lax.rem(self.t, 2))
            self.peers += [self.left, self.right, self.across]

    def meet(self):
        barrier = pltpu.get_barrier_semaphore()
        for peer in self.peers:
            pl.semaphore_signal(barrier, inc=1, device_id=peer, device_id_type=MESH)
        pl.semaphore_wait(barrier, len(self.peers))

    def prepare(self, source, target, peer):
        k = self.count
        self.count += 1
        return pltpu.make_async_remote_copy(
            src_ref=source,
            dst_ref=target,
            send_sem=self.send_sem.at[k],
            recv_sem=self.recv_sem.at[k],
            device_id=peer,
            device_id_type=MESH,
        )

    def send(self, source, target, peer):
        copy = self.prepare(source, target, peer)
        copy.start()
        self.sent.append(copy)
        return copy

    def end(self):
        for copy in self.sent:
            copy.wait_send()

    def block(self, i):
        bits = [(1 - bit) if i >> at & 1 else bit for at, bit in ((2, self.yb), (1, self.xb), (0, self.r))]
        return (bits[0] * 2 + bits[1]) * 2 + bits[2]


class Local:
    def __init__(self, sem):
        self.sem, self.count, self.open = sem, 0, []

    def start(self, source, target):
        copy = pltpu.make_async_copy(source, target, self.sem.at[self.count])
        self.count += 1
        copy.start()
        self.open.append(copy)
        return copy

    def wait(self, *copies):
        for copy in copies:
            copy.wait()
            self.open = [other for other in self.open if other is not copy]

    def end(self):
        self.wait(*list(self.open))


def at_rows(ref, start, size):
    return ref.at[pl.ds(start, size), :]


def at_columns(ref, start, size):
    return ref.at[:, pl.ds(start, size)]


class Gathered:
    def __init__(self, links, local, shard, full, cut, unit):
        self.links, self.local, self.full, self.cut, self.unit = links, local, full, cut, unit
        mine = cut(shard, pl.multiple_of(links.r * unit, unit), unit)
        self.copies = [
            local.start(mine, self.at(0)),
            local.start(cut(shard, pl.multiple_of((1 - links.r) * unit, unit), unit), self.at(1)),
        ]
        self.mine = mine

    def at(self, block, start=0, size=None):
        return self.cut(self.full, block * self.unit + start, self.unit if size is None else size)

    def first(self):
        self.from_x = self.links.send(self.mine, self.at(2), self.links.x)
        self.from_y = self.links.send(self.mine, self.at(4), self.links.y)

    def relay_x(self):
        half = self.unit // 2
        self.from_x.wait_recv()
        self.far_top = self.links.send(self.at(2, 0, half), self.at(6, 0, half), self.links.y)
        self.core_x = self.links.send(self.at(2), self.at(3), self.links.core)

    def relay_y(self):
        half = self.unit // 2
        self.from_y.wait_recv()
        self.far_end = self.links.send(self.at(4, half, half), self.at(6, half, half), self.links.x)
        self.core_y = self.links.send(self.at(4), self.at(5), self.links.core)

    def relay_far(self):
        self.far_top.wait_recv()
        self.far_end.wait_recv()
        self.core_far = self.links.send(self.at(6), self.at(7), self.links.core)

    def whole(self):
        self.local.wait(*self.copies)
        for copy in (self.core_x, self.core_y, self.core_far):
            copy.wait_recv()


def tile_of(j, size):
    return pl.ds(pl.multiple_of(j * size, size), size)


def dot(left, right):
    return jnp.dot(left, right, preferred_element_type=FULL)


def spin(values_in, cosine, sine_one, sine_two):
    head = values_in[:, :128]
    turned_head = (
        head * cosine + pltpu.roll(head, 96, 1) * sine_one + pltpu.roll(head, 32, 1) * sine_two
    )
    return jnp.concatenate([turned_head, values_in[:, 128:]], -1)


def gather_kernel(
    score_scale,
    x_hbm, g_hbm, wh_hbm, wo_hbm, we_hbm, ws_hbm, vecs, key_pos, query_pos, cosine, sine_one, sine_two,
    we, ws, wo_out, act_out, slope_out, n2t_out, up_out, ctx_out, red_heads, red_out, red_shrink, sums,
    wh, wo, xr, g, n1, n2, n1t, n2t, stat, qkv_away, qkv, dctx_away, dctx, ctxt, ctxt_away,
    pg, pg_away, kvg, kvg_away, kvg_got, got_heads, got_out, got_shrink, local_sem, tile_sem, send_sem, recv_sem,
):
    links, local = Links(send_sem, recv_sem), Local(local_sem)
    tokens, width = xr.shape
    hd = dctx.shape[1]
    unit = width // 8
    blocks = range(8)
    x_in, g_in = [], []
    for i in blocks:
        cols = pl.ds(pl.multiple_of(links.block(i) * unit, unit), unit)
        x_in.append(local.start(x_hbm.at[:, cols], xr.at[:, pl.ds(i * unit, unit)]))
        g_in.append(local.start(g_hbm.at[:, cols], g.at[:, pl.ds(i * unit, unit)]))
    links.meet()
    heads = Gathered(links, local, wh_hbm, wh, at_rows, unit)
    output = Gathered(links, local, wo_hbm, wo, at_columns, unit)
    expand = Gathered(links, local, we_hbm, we, at_rows, unit)
    shrink = Gathered(links, local, ws_hbm, ws, at_columns, unit)
    heads.first()
    output.first()

    local.wait(*x_in)

    def norm_rows(c, carry):
        rows = tile_of(c, 64)
        value = xr[rows, :].astype(FULL)
        average = jnp.mean(value, -1, keepdims=True)
        centred = value - average
        inverse = lax.rsqrt(jnp.mean(centred * centred, -1, keepdims=True) + NORM_EPS)
        normal = centred * inverse
        stat[rows, :] = jnp.concatenate(
            [jnp.broadcast_to(average, (64, 128)), jnp.broadcast_to(inverse, (64, 128))], -1
        )
        n1[rows, :] = (normal * vecs[0:1, :] + vecs[1:2, :]).astype(LOW)
        n2[rows, :] = (normal * vecs[2:3, :] + vecs[3:4, :]).astype(LOW)
        return carry

    lax.fori_loop(0, tokens // 64, norm_rows, 0)

    def turn_tiles(j, carry):
        cols = tile_of(j, unit)
        n1t[cols, :] = n1[:, cols].T
        n2t[cols, :] = n2[:, cols].T
        return carry

    lax.fori_loop(0, 8, turn_tiles, 0)
    local.start(n2t, n2t_out)
    sums[...] = jnp.zeros_like(sums)
    local.wait(*g_in)
    for i in blocks:
        cols = pl.ds(pl.multiple_of(links.block(i) * unit, unit), unit)
        sums[4:5, cols] = jnp.sum(g[:, i * unit : (i + 1) * unit].astype(FULL), 0, keepdims=True)

    heads.relay_x()
    heads.relay_y()
    output.relay_x()
    output.relay_y()
    heads.relay_far()
    expand.first()
    output.relay_far()
    heads.whole()

    own, away = links.yb * 3 * hd, (1 - links.yb) * 3 * hd

    def project(start, target):
        def one(c, carry):
            cols = pl.ds(pl.multiple_of(start + c * hd, hd), hd)
            value = dot(n1[...], wh[:, cols]) + vecs[5:6, cols]
            spun = spin(value, cosine[:tokens, :], sine_one[:tokens, :], sine_two[:tokens, :])
            target[c, :tokens, :] = jnp.where(c < 2, spun, value).astype(LOW)
            return carry

        lax.fori_loop(0, 3, one, 0)

    project(away, qkv_away)
    qkv_from_y = links.send(qkv_away, qkv.at[:, pl.ds(tokens, tokens), :], links.y)
    project(own, qkv)
    kv_from_x = links.send(
        qkv.at[pl.ds(1, 2), pl.ds(0, tokens), :], qkv.at[pl.ds(1, 2), pl.ds(2 * tokens, tokens), :], links.x
    )
    output.whole()
    local.start(wo, wo_out)
    rows_own = pl.ds(pl.multiple_of(links.yb * hd, hd), hd)
    rows_away = pl.ds(pl.multiple_of((1 - links.yb) * hd, hd), hd)
    dctx_away[...] = contract_last(g[...], wo[rows_away, :]).astype(LOW)
    dctx_from_y = links.send(dctx_away, dctx.at[pl.ds(tokens, tokens), :], links.y)
    dctx[:tokens, :] = contract_last(g[...], wo[rows_own, :]).astype(LOW)

    qkv_from_y.wait_recv()
    kv_from_far = links.send(
        qkv.at[pl.ds(1, 2), pl.ds(tokens, tokens), :],
        qkv.at[pl.ds(1, 2), pl.ds(3 * tokens, tokens), :],
        links.x,
    )
    expand.relay_x()
    expand.relay_y()
    shrink.first()
    dctx_from_y.wait_recv()
    kv_from_x.wait_recv()
    kv_from_far.wait_recv()

    def attention(kt, vt, dk, dv, prob, wgt, prob_low, grad_low):
        keys = qkv.shape[1]
        step = 512
        parts = [pl.ds(i * step, step) for i in range(keys // step)]
        for part in parts:
            kt[:, part] = qkv[1, part, :].T
            vt[:, part] = qkv[2, part, :].T
        dk[...] = jnp.zeros_like(dk)
        dv[...] = jnp.zeros_like(dv)

        def one(b, carry):
            rows = tile_of(b, hd)
            query, grad = qkv[0, rows, :], dctx[rows, :]
            spot = query_pos[:, rows]
            top = jnp.full((1, hd), MASKED, FULL)
            for part in parts:
                scores = contract_last(qkv[1, part, :], query) * score_scale
                scores = jnp.where(key_pos[part, :] <= spot, scores, MASKED)
                prob[part, :] = scores
                top = jnp.maximum(top, jnp.max(scores, 0, keepdims=True))
            total = jnp.zeros((1, hd), FULL)
            for part in parts:
                exponent = jnp.exp(prob[part, :] - top)
                prob[part, :] = exponent
                total = total + jnp.sum(exponent, 0, keepdims=True)
            share = 1.0 / total
            inner = jnp.zeros((1, hd), FULL)
            for part in parts:
                weight = contract_last(qkv[2, part, :], grad)
                chance = prob[part, :] * share
                prob[part, :] = chance
                prob_low[part, :] = chance.astype(LOW)
                wgt[part, :] = weight
                inner = inner + jnp.sum(chance * weight, 0, keepdims=True)
            for part in parts:
                grad_low[part, :] = (prob[part, :] * (wgt[part, :] - inner)).astype(LOW)
            context = dot(vt[...], prob_low[...]).astype(LOW)
            query_grad = dot(kt[...], grad_low[...]) * score_scale
            for part in parts:
                dv[part, :] += dot(prob_low[part, :], grad)
                dk[part, :] += dot(grad_low[part, :], query)
            turned_grad = spin(query_grad.T, cosine[rows, :], -sine_one[rows, :], -sine_two[rows, :]).astype(LOW)
            return context, turned_grad

        def here(b, carry):
            context, turned_grad = one(b, carry)
            rows = tile_of(b, hd)
            ctxt[rows_own, rows] = context
            pg[rows, pl.ds(pl.multiple_of(own, hd), hd)] = turned_grad
            return carry

        def there(b, carry):
            context, turned_grad = one(b + tokens // hd, carry)
            rows = tile_of(b, hd)
            ctxt_away[:, rows] = context
            pg_away[rows, :hd] = turned_grad
            return carry

        lax.fori_loop(0, tokens // hd, there, 0)
        lax.fori_loop(0, tokens // hd, here, 0)
        for i, total in enumerate((dk, dv)):
            kvg_away[i, :, :] = total[2 * tokens :, :].astype(LOW)
            kvg[i, :, :] = total[: 2 * tokens, :]

    keys = qkv.shape[1]
    pl.run_scoped(
        attention,
        pltpu.VMEM((hd, keys), LOW),
        pltpu.VMEM((hd, keys), LOW),
        pltpu.VMEM((keys, hd), FULL),
        pltpu.VMEM((keys, hd), FULL),
        pltpu.VMEM((keys, hd), FULL),
        pltpu.VMEM((keys, hd), FULL),
        pltpu.VMEM((keys, hd), LOW),
        pltpu.VMEM((keys, hd), LOW),
    )
    ctx_from_y = links.send(ctxt_away, ctxt.at[rows_own, :], links.y)
    kvg_from_x = links.send(kvg_away, kvg_got, links.x)
    expand.relay_far()
    expand.whole()

    def rest(tiles, slope, actt, send_heads, send_out, send_shrink):
        act = n1

        def load(j):
            return pltpu.make_async_copy(
                we.at[:, tile_of(j, unit)], tiles.at[lax.rem(j, 2)], tile_sem.at[lax.rem(j, 2)]
            )

        load(0).start()

        def forward(j, carry):
            @pl.when(j < 7)
            def _():
                load(j + 1).start()

            load(j).wait()
            cols = tile_of(j, unit)
            value = dot(n2[...], tiles[lax.rem(j, 2)]) + vecs[4:5, cols]
            normal_share = 0.5 * (1.0 + lax.erf(value * (0.5**0.5)))
            low_act = (value * normal_share).astype(LOW)
            act[:, cols] = low_act
            actt[cols, :] = low_act.T
            density = jnp.exp(value * value * -0.5) * 0.3989422804014327
            slope[:, cols] = (normal_share + value * density).astype(LOW)
            return carry

        lax.fori_loop(0, 4, forward, 0)
        shrink.relay_x()
        shrink.relay_y()
        lax.fori_loop(4, 8, forward, 0)
        local.start(act, act_out)
        local.start(slope, slope_out)

        kvg_from_x.wait_recv()
        for i in range(2):
            for away_rows, target in ((False, pg), (True, pg_away)):
                rows = pl.ds(tokens if away_rows else 0, tokens)
                total = kvg[i, rows, :] + kvg_got[i, rows, :].astype(FULL)
                if i == 0:
                    total = spin(total * score_scale, cosine[rows, :], -sine_one[rows, :], -sine_two[rows, :])
                start = (0 if away_rows else own) + (1 + i) * hd
                target[:, pl.ds(pl.multiple_of(start, hd), hd)] = total.astype(LOW)
        pg_from_y = links.send(pg_away, pg.at[:, pl.ds(pl.multiple_of(own, 3 * hd), 3 * hd)], links.y)

        def shrink_block(i, target, extra):
            def one(c, carry):
                rows = tile_of(c, 512)
                part = dot(actt[rows, :], g[:, i * unit : (i + 1) * unit])
                if extra is not None:
                    part = part + extra[rows, :].astype(FULL)
                target[rows, :] = part.astype(LOW)
                return carry

            lax.fori_loop(0, actt.shape[0] // 512, one, 0)

        shrink_got, out_got, heads_got = [], [], []
        for k in range(4):
            shrink_block(2 * k + 1, send_shrink.at[k], None)
            shrink_got.append(links.send(send_shrink.at[k], got_shrink.at[k], links.core))
        ctx_from_y.wait_recv()
        local.start(ctxt, ctx_out)
        for k in range(4):
            i = 2 * k + 1
            send_out[k, :, :] = dot(ctxt[...], g[:, i * unit : (i + 1) * unit]).astype(LOW)
            out_got.append(links.send(send_out.at[k], got_out.at[k], links.core))
        for k in range(4):
            shrink_got[k].wait_recv()
            shrink_block(2 * k, got_shrink.at[k], got_shrink.at[k])
            local.start(got_shrink.at[k], red_shrink.at[k])
        for k in range(4):
            out_got[k].wait_recv()
            total = dot(ctxt[...], g[:, 2 * k * unit : (2 * k + 1) * unit])
            got_out[k, :, :] = (total + got_out[k, :, :].astype(FULL)).astype(LOW)
            local.start(got_out.at[k], red_out.at[k])
        shrink.relay_far()
        pg_from_y.wait_recv()
        for k in range(4):
            rows = pl.ds((2 * k + 1) * unit, unit)
            send_heads[k, :, :] = dot(n1t[rows, :], pg[...]).astype(LOW)
            heads_got.append(links.send(send_heads.at[k], got_heads.at[k], links.core))

        up = n2
        for i in blocks:
            cols = slice(i * unit, (i + 1) * unit)
            grad = contract_last(pg[...], wh[cols, :])
            normal = (xr[:, cols].astype(FULL) - stat[:, 0:1]) * stat[:, 128:129]
            place = pl.ds(pl.multiple_of(links.block(i) * unit, unit), unit)
            sums[0:1, place] = jnp.sum(grad * normal, 0, keepdims=True)
            sums[1:2, place] = jnp.sum(grad, 0, keepdims=True)
            up[:, cols] = (grad * vecs[0:1, cols]).astype(LOW)
        local.start(up, up_out)
        sums[6:7, : pg.shape[1]] = jnp.sum(pg[...].astype(FULL), 0, keepdims=True)
        for k in range(4):
            heads_got[k].wait_recv()
            total = dot(n1t[2 * k * unit : (2 * k + 1) * unit, :], pg[...])
            got_heads[k, :, :] = (total + got_heads[k, :, :].astype(FULL)).astype(LOW)
            local.start(got_heads.at[k], red_heads.at[k])
        shrink.whole()
        links.end()
        local.end()

    pl.run_scoped(
        rest,
        pltpu.VMEM((2, width, unit), LOW),
        pltpu.VMEM(n2.shape, LOW),
        pltpu.VMEM((we.shape[1], tokens), LOW),
        pltpu.VMEM(got_heads.shape, LOW),
        pltpu.VMEM(got_out.shape, LOW),
        pltpu.VMEM(got_shrink.shape, LOW),
    )


def gather_call(x, g, heads_rows, output_rows, expand_weight, shrink_weight, vecs, key_pos, query_pos, tables):
    tokens, width = x.shape
    heads_wide, out_wide, units = heads_rows.shape[1], output_rows.shape[0], expand_weight.shape[1]
    hd = heads_wide // 6
    keys = key_pos.shape[0]
    unit = width // 8
    low = lambda *shape: jax.ShapeDtypeStruct(shape, LOW)
    outs = [
        low(width, units),
        low(units, width),
        low(out_wide, width),
        low(tokens, units),
        low(tokens, units),
        low(width, tokens),
        low(tokens, width),
        low(out_wide, tokens),
        low(4, unit, heads_wide),
        low(4, out_wide, unit),
        low(4, units, unit),
        jax.ShapeDtypeStruct((8, width), FULL),
    ]
    vm = lambda *shape: pltpu.VMEM(shape, LOW)
    scratch = [
        vm(width, heads_wide),
        vm(out_wide, width),
        vm(tokens, width),
        vm(tokens, width),
        vm(tokens, width),
        vm(tokens, width),
        vm(width, tokens),
        vm(width, tokens),
        pltpu.VMEM((tokens, 256), FULL),
        vm(3, tokens, hd),
        vm(3, keys, hd),
        vm(tokens, hd),
        vm(2 * tokens, hd),
        vm(out_wide, tokens),
        vm(hd, tokens),
        vm(tokens, heads_wide),
        vm(tokens, 3 * hd),
        pltpu.VMEM((2, 2 * tokens, hd), FULL),
        vm(2, 2 * tokens, hd),
        vm(2, 2 * tokens, hd),
        vm(4, unit, heads_wide),
        vm(4, out_wide, unit),
        vm(4, units, unit),
        pltpu.SemaphoreType.DMA((64,)),
        pltpu.SemaphoreType.DMA((2,)),
        pltpu.SemaphoreType.DMA((COPIES,)),
        pltpu.SemaphoreType.DMA((COPIES,)),
    ]
    return pl.pallas_call(
        functools.partial(gather_kernel, hd**-0.5),
        out_shape=outs,
        in_specs=[ANY] * 6 + [IN_VMEM] * 6,
        out_specs=[ANY] * 11 + [IN_VMEM],
        scratch_shapes=scratch,
        compiler_params=pltpu.CompilerParams(
            collective_id=0, has_side_effects=True, vmem_limit_bytes=VMEM_BYTES
        ),
    )(x, g, heads_rows, output_rows, expand_weight, shrink_weight, vecs, key_pos, query_pos, *tables)


class Scattered:
    def __init__(self, links, local, block, cut, unit, via, got, stage, own, loaded):
        self.links, self.local, self.block, self.cut, self.unit = links, local, block, cut, unit
        self.via, self.got, self.stage, self.own = via, got, stage, own
        self.half = unit // 2
        if loaded:
            self.loads = [
                local.start(cut(block(1), self.half, self.half), stage.at[0]),
                local.start(cut(block(2), 0, self.half), stage.at[1]),
                local.start(block(0), own),
            ]

    def first(self):
        half, cut, far = self.half, self.cut, self.block(3)
        self.via_x = self.links.send(cut(far, 0, half), self.via.at[0], self.links.x)
        self.via_y = self.links.send(cut(far, half, half), self.via.at[1], self.links.y)

    def direct(self):
        half, cut = self.half, self.cut
        self.x_top = self.links.send(cut(self.block(1), 0, half), cut(self.got.at[0], 0, half), self.links.x)
        self.y_end = self.links.send(cut(self.block(2), half, half), cut(self.got.at[1], half, half), self.links.y)

    def second(self):
        half, cut = self.half, self.cut
        self.local.wait(*self.loads[:2])
        self.via_x.wait_recv()
        add_rows(self.stage.at[1], self.stage.at[1], self.via.at[0])
        self.y_top = self.links.send(self.stage.at[1], cut(self.got.at[1], 0, half), self.links.y)
        self.via_y.wait_recv()
        add_rows(self.stage.at[0], self.stage.at[0], self.via.at[1])
        self.x_end = self.links.send(self.stage.at[0], cut(self.got.at[0], half, half), self.links.x)

    def third(self, total, place):
        for copy in (self.x_top, self.x_end, self.y_top, self.y_end):
            copy.wait_recv()
        self.local.wait(self.loads[2])
        add_rows(total, self.own, self.got.at[0], self.got.at[1])
        self.kept = self.local.start(total, place)
        self.other = self.links.send(total, place, self.links.core)


def add_rows(target, *parts):
    rows, wide = target.shape
    step = min(rows, 32 if wide > 512 else 256)

    def one(c, carry):
        at = pl.ds(pl.multiple_of(c * step, step), step)
        total = parts[0][at, :].astype(FULL)
        for part in parts[1:]:
            total = total + part[at, :].astype(FULL)
        target[at, :] = total.astype(target.dtype)
        return carry

    lax.fori_loop(0, rows // step, one, 0)


class Line:
    def __init__(self, links, part, low_got, high_got, final, finish):
        self.links, self.part, self.final, self.finish = links, part, final, finish
        self.low_got, self.high_got = low_got, high_got
        self.half = part.shape[0] // 2
        self.step = self.half // CHUNKS
        self.first, self.last = links.t == 0, links.t == links.line - 1
        self.up = {}
        self.down = {}

    def rows(self, c, low):
        return pl.ds((0 if low else self.half) + c * self.step, self.step)

    def make(self, c, low, back):
        rows = self.rows(c, low)
        got = self.low_got if low else self.high_got
        source = (self.final if back else self.part).at[rows, :]
        target = self.final.at[rows, :] if back else got.at[pl.ds(c * self.step, self.step), :]
        return self.links.prepare(source, target, self.links.left if low != back else self.links.right)

    def toward(self, c, ends):
        for low in (True, False):
            key = (c, low)
            if ends:
                self.up[key] = self.make(c, low, False)
            source_end, target_end = (self.last, self.first) if low else (self.first, self.last)
            copy = self.up[key]
            if ends:
                pl.when(source_end)(copy.start)
                continue
            rows = self.rows(c, low)
            got = (self.low_got if low else self.high_got).at[pl.ds(c * self.step, self.step), :]

            def take(copy=copy, rows=rows, got=got):
                copy.wait_recv()
                add_rows(self.part.at[rows, :], self.part.at[rows, :], got)

            pl.when(jnp.logical_not(source_end))(take)
            between = jnp.logical_and(jnp.logical_not(source_end), jnp.logical_not(target_end))
            pl.when(between)(copy.start)

    def back(self, c):
        for low in (True, False):
            copy = self.make(c, low, True)
            self.down[(c, low)] = copy
            source_end, target_end = (self.first, self.last) if low else (self.last, self.first)
            rows = self.rows(c, low)

            def end(copy=copy, rows=rows):
                self.finish(rows)
                copy.start()

            def between(copy=copy):
                copy.wait_recv()

            pl.when(source_end)(end)
            pl.when(jnp.logical_not(source_end))(between)
            pl.when(jnp.logical_and(jnp.logical_not(source_end), jnp.logical_not(target_end)))(copy.start)

    def end(self):
        for (c, low), copy in self.up.items():
            pl.when(jnp.logical_not(self.first if low else self.last))(copy.wait_send)
        for (c, low), copy in self.down.items():
            pl.when(jnp.logical_not(self.last if low else self.first))(copy.wait_send)


CHUNKS = 4


def scatter_kernel(
    line_size,
    we_hbm, ws_hbm, wo_hbm, act_hbm, slope_hbm, n2t_hbm, up_hbm, ctxt_hbm, red_heads, red_out, red_shrink, x_hbm, g_hbm,
    vecs, sums_in,
    layer_out, input_grad, heads_grad, output_grad, expand_grad, shrink_grad, got_expand, sums_out,
    ws, we, wo, act, slope, n2t, up, ctxt, g, part_branch, final_branch, final_up, low_branch, high_branch, low_up, high_up,
    via_h, got_h, stage_h, own_h, via_o, got_o, stage_o, own_o, via_s, got_s, stage_s, own_s, via_e, got_e,
    total_rows, total_columns, total_out, grad_rows, sums, sums_got, local_sem, send_sem, recv_sem,
):
    links, local = Links(send_sem, recv_sem, line_size), Local(local_sem)
    tokens, width = g.shape
    unit = width // 8
    blocks = range(8)
    place = [pl.ds(pl.multiple_of(links.block(i) * unit, unit), unit) for i in blocks]

    def here(i):
        return pl.ds(i * unit, unit)

    first_loads = [local.start(ws_hbm, ws), local.start(act_hbm, act), local.start(ctxt_hbm, ctxt), local.start(wo_hbm, wo)]
    g_loads = [local.start(g_hbm.at[:, place[i]], g.at[:, here(i)]) for i in blocks]
    slope_load = local.start(slope_hbm, slope)
    we_load, up_load, n2t_load = local.start(we_hbm, we), local.start(up_hbm, up), local.start(n2t_hbm, n2t)
    links.meet()

    shrink = Scattered(links, local, lambda k: red_shrink.at[k], at_columns, unit, via_s, got_s, stage_s, own_s, True)
    heads = Scattered(links, local, lambda k: red_heads.at[k], at_rows, unit, via_h, got_h, stage_h, own_h, True)
    output = Scattered(links, local, lambda k: red_out.at[k], at_columns, unit, via_o, got_o, stage_o, own_o, True)
    shrink.first()
    heads.first()
    output.first()

    local.wait(*first_loads)
    context = ctxt[...].T

    def branch_tile(j, carry):
        cols = tile_of(j, unit)
        part_branch[:, cols] = (dot(context, wo[:, cols]) + dot(act[...], ws[:, cols])).astype(LOW)
        return carry

    lax.fori_loop(0, 8, branch_tile, 0)
    x = act
    x_loads = [local.start(x_hbm.at[:, place[i]], x.at[:, here(i)]) for i in blocks]

    def finish_branch(rows):
        def one(c, carry):
            at = pl.ds(pl.multiple_of(rows.start + c * 16, 16), 16)
            total = x[at, :].astype(FULL) + part_branch[at, :].astype(FULL) + vecs[1:2, :]
            final_branch[at, :] = total.astype(LOW)
            return carry

        lax.fori_loop(0, rows.size // 16, one, 0)

    def finish_up(rows):
        final_up[rows, :] = up[rows, :]

    line_branch = Line(links, part_branch, low_branch, high_branch, final_branch, finish_branch)
    line_up = Line(links, up, low_up, high_up, final_up, finish_up)
    for c in range(CHUNKS):
        line_branch.toward(c, True)

    local.wait(*g_loads, slope_load)
    sums[0, :, :] = sums_in[...]

    def hidden_tile(j, carry):
        cols = tile_of(j, unit)
        grad = (contract_last(g[...], ws[cols, :]) * slope[:, cols].astype(FULL)).astype(LOW)
        slope[:, cols] = grad
        sums[0, 5:6, cols] = jnp.sum(grad.astype(FULL), 0, keepdims=True)
        return carry

    lax.fori_loop(0, 8, hidden_tile, 0)
    local.wait(*x_loads, we_load, up_load, n2t_load)
    shrink.direct()
    heads.direct()
    output.direct()

    def up_block(i):
        cols = here(i)
        grad = contract_last(slope[...], we[i * unit : (i + 1) * unit, :])
        value = x[:, cols].astype(FULL)
        normal = (value - average) * inverse
        sums[0, 2:3, place[i]] = jnp.sum(grad * normal, 0, keepdims=True)
        sums[0, 3:4, place[i]] = jnp.sum(grad, 0, keepdims=True)
        up[:, cols] = (up[:, cols].astype(FULL) + grad * vecs[0:1, cols]).astype(LOW)

    total = jnp.zeros((tokens, 1), FULL)
    for i in blocks:
        total = total + jnp.sum(x[:, here(i)].astype(FULL), -1, keepdims=True)
    average = total * (1.0 / width)
    total = jnp.zeros((tokens, 1), FULL)
    for i in blocks:
        centred = x[:, here(i)].astype(FULL) - average
        total = total + jnp.sum(centred * centred, -1, keepdims=True)
    inverse = lax.rsqrt(total * (1.0 / width) + NORM_EPS)

    line_branch.toward(0, False)
    for i in range(4):
        up_block(i)
    line_branch.toward(1, False)
    for i in range(4, 8):
        up_block(i)
    for c in range(CHUNKS):
        line_up.toward(c, True)
    line_branch.toward(2, False)
    shrink.second()

    expand_got = []

    def expand_block(i, target):
        def one(c, carry):
            cols = tile_of(c, 512)
            part = dot(n2t[i * unit : (i + 1) * unit, :], slope[:, cols])
            if target is we:
                part = part + target[(i // 2) * unit : (i // 2 + 1) * unit, cols].astype(FULL)
            target[(i // 2) * unit : (i // 2 + 1) * unit, cols] = part.astype(LOW)
            return carry

        lax.fori_loop(0, slope.shape[1] // 512, one, 0)

    for k in (3, 1, 2, 0):
        expand_block(2 * k + 1, ws)
        rows = pl.ds(k * unit, unit)
        expand_got.append((k, links.send(ws.at[rows, :], got_expand.at[k], links.core)))
    line_branch.toward(3, False)
    heads.second()
    output.second()
    loads = []
    for k, copy in expand_got:
        copy.wait_recv()
        loads.append(local.start(got_expand.at[k], we.at[pl.ds(k * unit, unit), :]))
    line_branch.back(0)
    for (k, copy), load in zip(expand_got, loads):
        local.wait(load)
        expand_block(2 * k, we)
    expand = Scattered(
        links, local, lambda k: we.at[pl.ds(k * unit, unit), :], at_rows, unit, via_e, got_e, None, None, False
    )
    expand.first()
    expand.direct()

    hops = []

    def hop(s, peer):
        hops.append(links.send(sums.at[s], sums_got.at[s], peer))

    def hop_end(s):
        hops[s].wait_recv()
        sums[s + 1, :, :] = sums[s, :, :] + sums_got[s, :, :]

    hop(0, links.core)
    line_up.toward(0, False)
    line_branch.back(1)
    hop_end(0)
    hop(1, links.x)
    line_up.toward(1, False)
    line_branch.back(2)
    hop_end(1)
    hop(2, links.y)
    shrink.third(total_columns, shrink_grad.at[:, pl.ds(pl.multiple_of(links.r * unit, unit), unit)])
    line_up.toward(2, False)
    line_branch.back(3)
    hop_end(2)
    hop(3, links.pair)
    for i in blocks:
        local.start(final_branch.at[:, here(i)], layer_out.at[:, place[i]])
    line_up.toward(3, False)
    line_up.back(0)
    output.third(total_out, output_grad.at[:, pl.ds(pl.multiple_of(links.r * unit, unit), unit)])
    hop_end(3)
    hop(4, links.across)
    heads.third(total_rows.at[:, pl.ds(0, own_h.shape[1])], heads_grad.at[pl.ds(pl.multiple_of(links.r * unit, unit), unit), :])
    line_up.back(1)
    expand.via_x.wait_recv()
    top, end = pl.ds(2 * unit, unit // 2), pl.ds(unit + unit // 2, unit // 2)
    add_rows(we.at[top, :], we.at[top, :], via_e.at[0])
    expand.y_top = links.send(we.at[top, :], got_e.at[1, pl.ds(0, unit // 2), :], links.y)
    expand.via_y.wait_recv()
    add_rows(we.at[end, :], we.at[end, :], via_e.at[1])
    expand.x_end = links.send(we.at[end, :], got_e.at[0, pl.ds(unit // 2, unit // 2), :], links.x)
    hop_end(4)
    sums_out[0:4, :] = sums[5, 0:4, :]
    sums_out[4:8, :] = sums[3, 4:8, :]
    line_up.back(2)
    line_up.back(3)

    out_copies = {}
    step = grad_rows.shape[1]
    for c in range(tokens // step):
        slot = c % 2
        if c >= 2:
            local.wait(*out_copies[c - 2])
        rows = pl.ds(c * step, step)
        value = x[rows, :].astype(FULL)
        centred = value - jnp.mean(value, -1, keepdims=True)
        scale = lax.rsqrt(jnp.mean(centred * centred, -1, keepdims=True) + NORM_EPS)
        normal = centred * scale
        upstream = final_up[rows, :].astype(FULL)
        inner = upstream - jnp.mean(upstream, -1, keepdims=True)
        inner = inner - normal * jnp.mean(upstream * normal, -1, keepdims=True)
        grad_rows[slot, :, :] = g[rows, :].astype(FULL) + inner * scale
        out_copies[c] = [
            local.start(grad_rows.at[slot, :, here(i)], input_grad.at[rows, place[i]]) for i in blocks
        ]

    for copy in (expand.x_top, expand.x_end, expand.y_top, expand.y_end):
        copy.wait_recv()
    heads.other.wait_send()
    local.wait(heads.kept)
    add_rows(total_rows, we.at[pl.ds(0, unit), :], got_e.at[0], got_e.at[1])
    spot = expand_grad.at[pl.ds(pl.multiple_of(links.r * unit, unit), unit), :]
    local.start(total_rows, spot)
    last = links.send(total_rows, spot, links.core)
    for copy in (shrink.other, output.other, heads.other, last):
        copy.wait_recv()
    links.sent = [copy for copy in links.sent if copy is not heads.other]
    links.end()
    line_branch.end()
    line_up.end()
    local.end()


def scatter_call(line_size, arrays, x, g, vecs, sums):
    tokens, width = x.shape
    expand_full, shrink_full, output_full, act, slope, n2t, up, ctxt, red_heads, red_out, red_shrink = arrays
    unit = width // 8
    units, heads_wide, out_wide = act.shape[1], red_heads.shape[2], ctxt.shape[0]
    low = lambda *shape: pltpu.VMEM(shape, LOW)
    full = lambda *shape: pltpu.VMEM(shape, FULL)
    half = unit // 2
    outs = [
        jax.ShapeDtypeStruct((tokens, width), LOW),
        jax.ShapeDtypeStruct((tokens, width), FULL),
        jax.ShapeDtypeStruct((2 * unit, heads_wide), FULL),
        jax.ShapeDtypeStruct((out_wide, 2 * unit), FULL),
        jax.ShapeDtypeStruct((2 * unit, units), FULL),
        jax.ShapeDtypeStruct((units, 2 * unit), FULL),
        jax.ShapeDtypeStruct((4, unit, units), LOW),
        jax.ShapeDtypeStruct((8, width), FULL),
    ]
    scratch = [
        low(units, width),
        low(width, units),
        low(out_wide, width),
        low(tokens, units),
        low(tokens, units),
        low(width, tokens),
        low(tokens, width),
        low(out_wide, tokens),
        low(tokens, width),
        low(tokens, width),
        low(tokens, width),
        low(tokens, width),
        *[low(tokens // 2, width)] * 4,
        low(2, half, heads_wide), low(2, unit, heads_wide), low(2, half, heads_wide), low(unit, heads_wide),
        low(2, out_wide, half), low(2, out_wide, unit), low(2, out_wide, half), low(out_wide, unit),
        low(2, units, half), low(2, units, unit), low(2, units, half), low(units, unit),
        low(2, half, units), low(2, unit, units),
        full(unit, units),
        full(units, unit),
        full(out_wide, unit),
        full(2, 32, width),
        full(6, 8, width),
        full(5, 8, width),
        pltpu.SemaphoreType.DMA((224,)),
        pltpu.SemaphoreType.DMA((COPIES,)),
        pltpu.SemaphoreType.DMA((COPIES,)),
    ]
    return pl.pallas_call(
        functools.partial(scatter_kernel, line_size),
        out_shape=outs,
        in_specs=[ANY] * 13 + [IN_VMEM] * 2,
        out_specs=[ANY] * 7 + [IN_VMEM],
        scratch_shapes=scratch,
        compiler_params=pltpu.CompilerParams(
            collective_id=1, has_side_effects=True, vmem_limit_bytes=VMEM_BYTES
        ),
    )(expand_full, shrink_full, output_full, act, slope, n2t, up, ctxt, red_heads, red_out, red_shrink, x, g, vecs, sums)


def square_local(
    layer_input,
    block_order,
    first_gain,
    first_bias,
    second_gain,
    second_bias,
    heads_weight,
    heads_bias,
    output_weight,
    output_bias,
    expand_weight,
    expand_bias,
    shrink_weight,
    shrink_bias,
    cotangent,
):
    tokens = layer_input.shape[1]
    width = layer_input.shape[2]
    replica, fsdp = lax.axis_index("replica"), lax.axis_index("fsdp")
    r_bit, x_bit, y_bit = replica == 1, fsdp % 2 == 1, fsdp // 2 == 1

    def turned(array, axis):
        return turn(array, axis, r_bit, x_bit, y_bit)

    heads_rows = heads_weight.reshape(heads_weight.shape[0], -1)
    output_rows = output_weight.reshape(-1, output_weight.shape[2])
    wide = heads_rows.shape[1]
    gain_one, shift_one, gain_two, shift_two = (
        turned(vec.astype(FULL), 0) for vec in (first_gain, first_bias, second_gain, second_bias)
    )
    vecs = jnp.stack(
        [
            gain_one,
            shift_one,
            gain_two,
            shift_two,
            expand_bias.astype(FULL),
            jnp.pad(heads_bias.reshape(-1).astype(FULL), (0, width - wide)),
            jnp.zeros((width,), FULL),
            jnp.zeros((width,), FULL),
        ]
    )
    order_row = block_order[0]
    slots = fsdp ^ jnp.array([0, 2, 1, 3], jnp.int32)
    order_here = order_row[slots]
    offsets = jnp.arange(tokens, dtype=jnp.int32)
    key_pos = (order_here[:, None] * tokens + offsets[None]).reshape(-1)
    query_pos = key_pos[: 2 * tokens]
    cosine, sine_part = rotary_tables(query_pos, ROT)
    still = jnp.zeros((2 * tokens, 128 - ROT), FULL)
    left, right = jnp.split(sine_part, 2, 1)
    tables = (
        jnp.concatenate([cosine, still + 1.0], 1),
        jnp.concatenate([-left, jnp.zeros_like(right), still], 1),
        jnp.concatenate([jnp.zeros_like(left), right, still], 1),
    )
    *gathered, sums = gather_call(
        layer_input[0], cotangent[0], heads_rows, output_rows, expand_weight, shrink_weight,
        vecs, key_pos[:, None], query_pos[None, :], tables,
    )

    second = jnp.stack([gain_two, turned(output_bias.astype(FULL) + shrink_bias.astype(FULL), 0)])
    layer_output, input_grad, heads_grad, output_grad, expand_weight_grad, shrink_weight_grad, _, sums = scatter_call(
        lax.axis_size("tensor"),
        gathered,
        layer_input[0],
        cotangent[0],
        jnp.pad(second, ((0, 6), (0, 0))),
        sums,
    )
    return (
        layer_output[None],
        input_grad[None],
        sums[0],
        sums[1],
        sums[2],
        sums[3],
        heads_grad.reshape(heads_weight.shape),
        sums[6, :wide].reshape(heads_bias.shape),
        output_grad.reshape(output_weight.shape),
        sums[4],
        expand_weight_grad,
        sums[5],
        shrink_weight_grad,
        sums[4],
    )


def ring_local(
    layer_input,
    block_order,
    first_gain,
    first_bias,
    second_gain,
    second_bias,
    heads_weight,
    heads_bias,
    output_weight,
    output_bias,
    expand_weight,
    expand_bias,
    shrink_weight,
    shrink_bias,
    cotangent,
):
    tokens_here = layer_input.shape[1]
    fsdp_count = lax.axis_size("fsdp")
    head_dim = output_weight.shape[1]
    score_scale = head_dim ** (-0.5)
    order_row = block_order[0]
    device_slot = lax.axis_index("fsdp")
    own_block = jnp.sum(
        jnp.where(jnp.arange(fsdp_count, dtype=jnp.int32) == device_slot, order_row, 0)
    )
    offsets = jnp.arange(tokens_here, dtype=jnp.int32)
    query_pos = own_block * tokens_here + offsets
    key_pos = jnp.repeat(order_row, tokens_here) * tokens_here + jnp.tile(offsets, fsdp_count)
    allowed = key_pos[None, :] <= query_pos[:, None]
    cosine, sine_part = rotary_tables(query_pos, ROT)
    hidden_in = layer_input[0].astype(jnp.float32)
    gain_one = first_gain.astype(jnp.float32)
    shift_one = first_bias.astype(jnp.float32)
    gain_two = second_gain.astype(jnp.float32)
    shift_two = second_bias.astype(jnp.float32)
    norm_one_low = layer_norm(hidden_in, gain_one, shift_one).astype(jnp.bfloat16)
    norm_two_low = layer_norm(hidden_in, gain_two, shift_two).astype(jnp.bfloat16)
    heads_full, output_full, expand_full, shrink_full = (
        lax.all_gather(heads_weight, "fsdp", axis=0, tiled=True),
        lax.all_gather(output_weight, "fsdp", axis=2, tiled=True),
        lax.all_gather(expand_weight, "fsdp", axis=0, tiled=True),
        lax.all_gather(shrink_weight, "fsdp", axis=1, tiled=True),
    )
    projected = jnp.einsum(
        "td,dhe->hte", norm_one_low, heads_full, preferred_element_type=jnp.float32
    )
    projected = projected + heads_bias.astype(jnp.float32)[:, None, :]
    query_pre = projected[..., :head_dim]
    key_pre = projected[..., head_dim : 2 * head_dim]
    query_low = rotate(query_pre, cosine, sine_part).astype(jnp.bfloat16)
    key_low = rotate(key_pre, cosine, sine_part).astype(jnp.bfloat16)
    value_low = projected[..., 2 * head_dim :].astype(jnp.bfloat16)
    key_all, value_all = (
        lax.all_gather(key_low, "fsdp", axis=1, tiled=True),
        lax.all_gather(value_low, "fsdp", axis=1, tiled=True),
    )

    def attend_head(operands):
        query_head, key_head, value_head = operands
        probability = softmax_rows(contract_last(query_head, key_head) * score_scale, allowed)
        return jnp.dot(
            probability.astype(jnp.bfloat16), value_head, preferred_element_type=jnp.float32
        )

    context = lax.map(attend_head, (query_low, key_all, value_all))
    context_low = context.astype(jnp.bfloat16)
    expand_in = jnp.dot(
        norm_two_low, expand_full, preferred_element_type=jnp.float32
    ) + expand_bias.astype(jnp.float32)
    activation_low = jax.nn.gelu(expand_in, approximate=False).astype(jnp.bfloat16)
    branch_part = jnp.einsum(
        "hte,hed->td", context_low, output_full, preferred_element_type=jnp.float32
    )
    branch_part = branch_part + jnp.dot(
        activation_low, shrink_full, preferred_element_type=jnp.float32
    )
    branch = lax.psum(branch_part, "tensor")
    layer_output = (
        hidden_in + branch + output_bias.astype(jnp.float32) + shrink_bias.astype(jnp.float32)
    ).astype(jnp.bfloat16)[None]
    heads_back, output_back, expand_back, shrink_back = (
        lax.all_gather(heads_weight, "fsdp", axis=0, tiled=True),
        lax.all_gather(output_weight, "fsdp", axis=2, tiled=True),
        lax.all_gather(expand_weight, "fsdp", axis=0, tiled=True),
        lax.all_gather(shrink_weight, "fsdp", axis=1, tiled=True),
    )
    key_back, value_back = (
        lax.all_gather(key_low, "fsdp", axis=1, tiled=True),
        lax.all_gather(value_low, "fsdp", axis=1, tiled=True),
    )
    grad_out = cotangent[0]
    grad_float = grad_out.astype(jnp.float32)
    output_weight_grad = jnp.einsum(
        "hte,td->hed", context_low, grad_out, preferred_element_type=jnp.float32
    )
    shrink_weight_grad = contract_first(activation_low, grad_out)
    bias_total = jnp.sum(grad_float, 0)
    context_grad = jnp.einsum(
        "td,hed->hte", grad_out, output_back, preferred_element_type=jnp.float32
    ).astype(jnp.bfloat16)
    activation_grad = contract_last(grad_out, shrink_back)
    _, gelu_back = jax.vjp(lambda inner_val: jax.nn.gelu(inner_val, approximate=False), expand_in)
    expand_grad = gelu_back(activation_grad)[0].astype(jnp.bfloat16)
    expand_weight_grad = contract_first(norm_two_low, expand_grad)
    expand_bias_grad = jnp.sum(expand_grad.astype(jnp.float32), 0)
    norm_two_grad = contract_last(expand_grad, expand_back)

    def attend_back(operands):
        query_head, key_head, value_head, context_head = operands
        probability = softmax_rows(contract_last(query_head, key_head) * score_scale, allowed)
        prob_low = probability.astype(jnp.bfloat16)
        weight_grad = contract_last(context_head, value_head)
        row_inner = jnp.sum(probability * weight_grad, -1, keepdims=True)
        score_grad = (probability * (weight_grad - row_inner)).astype(jnp.bfloat16)
        query_grad = jnp.dot(score_grad, key_head, preferred_element_type=jnp.float32) * score_scale
        key_grad = contract_first(score_grad, query_head) * score_scale
        value_grad = contract_first(prob_low, context_head)
        return (query_grad, key_grad, value_grad)

    query_grad, key_grad_all, value_grad_all = lax.map(
        attend_back, (query_low, key_back, value_back, context_grad)
    )
    key_grad, value_grad = (
        lax.psum_scatter(key_grad_all, "fsdp", scatter_dimension=1, tiled=True),
        lax.psum_scatter(value_grad_all, "fsdp", scatter_dimension=1, tiled=True),
    )
    _, rotate_back = jax.vjp(lambda inner_val: rotate(inner_val, cosine, sine_part), query_pre)
    projected_grad = jnp.concatenate(
        [rotate_back(query_grad)[0], rotate_back(key_grad)[0], value_grad], -1
    ).astype(jnp.bfloat16)
    heads_weight_grad = jnp.einsum(
        "td,hte->dhe", norm_one_low, projected_grad, preferred_element_type=jnp.float32
    )
    heads_bias_grad = jnp.sum(projected_grad.astype(jnp.float32), 1)
    norm_one_grad = jnp.einsum(
        "hte,dhe->td", projected_grad, heads_back, preferred_element_type=jnp.float32
    )
    norm_one_grad, norm_two_grad = lax.psum((norm_one_grad, norm_two_grad), "tensor")
    _, first_back = jax.vjp(layer_norm, hidden_in, gain_one, shift_one)
    input_first, first_gain_grad, first_bias_grad = first_back(norm_one_grad)
    _, second_back = jax.vjp(layer_norm, hidden_in, gain_two, shift_two)
    input_second, second_gain_grad, second_bias_grad = second_back(norm_two_grad)
    input_grad = (grad_float + input_first + input_second)[None]
    small_sums = lax.psum(
        (
            first_gain_grad,
            first_bias_grad,
            second_gain_grad,
            second_bias_grad,
            bias_total,
            expand_bias_grad,
            heads_bias_grad,
        ),
        ("replica", "fsdp"),
    )
    shard_parts = (
        lax.psum_scatter(heads_weight_grad, "fsdp", scatter_dimension=0, tiled=True),
        lax.psum_scatter(output_weight_grad, "fsdp", scatter_dimension=2, tiled=True),
        lax.psum_scatter(expand_weight_grad, "fsdp", scatter_dimension=0, tiled=True),
        lax.psum_scatter(shrink_weight_grad, "fsdp", scatter_dimension=1, tiled=True),
    )
    reduced = lax.psum((shard_parts[0], shard_parts[1], shard_parts[2], shard_parts[3]), "replica")
    return (
        layer_output,
        input_grad,
        small_sums[0],
        small_sums[1],
        small_sums[2],
        small_sums[3],
        reduced[0],
        small_sums[6],
        reduced[1],
        small_sums[4],
        reduced[2],
        small_sums[5],
        reduced[3],
        small_sums[4],
    )


def solution(mesh):
    placed = (
        P("replica", "fsdp", None),
        P("replica", None),
        P(),
        P(),
        P(),
        P(),
        P("fsdp", "tensor", None),
        P("tensor", None),
        P("tensor", None, "fsdp"),
        P(),
        P("fsdp", "tensor"),
        P("tensor"),
        P("tensor", "fsdp"),
        P(),
        P("replica", "fsdp", None),
    )
    local = square_local if mesh.shape["fsdp"] == 4 and mesh.shape["replica"] == 2 and mesh.shape["tensor"] == 4 else ring_local
    return jax.shard_map(
        local,
        mesh=mesh,
        in_specs=placed,
        out_specs=(
            P("replica", "fsdp", None),
            P("replica", "fsdp", None),
            P(),
            P(),
            P(),
            P(),
            P("fsdp", "tensor", None),
            P("tensor", None),
            P("tensor", None, "fsdp"),
            P(),
            P("fsdp", "tensor"),
            P("tensor"),
            P("tensor", "fsdp"),
            P(),
        ),
        check_vma=False,
    )
```

```python
import functools

import jax
import jax.numpy as jnp
from jax import lax
from jax.experimental import pallas as pl
from jax.experimental.pallas import tpu as pltpu
from jax.sharding import PartitionSpec as P

ROT = 64


NORM_EPS = 1e-05
MASKED = -1e30


def layer_norm(values_in, gain_vec, shift_vec):
    average = jnp.mean(values_in, -1, keepdims=True)
    centred = values_in - average
    spread_sq = jnp.mean(centred * centred, -1, keepdims=True)
    return centred * lax.rsqrt(spread_sq + NORM_EPS) * gain_vec + shift_vec


def rotate(values_in, cosine, sine_part):
    rot_width = cosine.shape[-1]
    half_width = rot_width // 2
    turning = values_in[..., :rot_width]
    swapped = jnp.concatenate([-turning[..., half_width:], turning[..., :half_width]], -1)
    return jnp.concatenate([turning * cosine + swapped * sine_part, values_in[..., rot_width:]], -1)


def rotary_tables(positions, rot_width):
    frequency = jnp.power(10000.0, -jnp.arange(0, rot_width, 2, dtype=jnp.float32) / rot_width)
    angle_half = positions.astype(jnp.float32)[:, None] * frequency[None, :]
    angles = jnp.concatenate([angle_half, angle_half], -1)
    return (jnp.cos(angles), jnp.sin(angles))


def contract_last(left_op, right_op):
    return lax.dot_general(
        left_op, right_op, (((1,), (1,)), ((), ())), preferred_element_type=jnp.float32
    )


def contract_first(left_op, right_op):
    return lax.dot_general(
        left_op, right_op, (((0,), (0,)), ((), ())), preferred_element_type=jnp.float32
    )


def softmax_rows(scores, allowed):
    masked_scores = jnp.where(allowed, scores, MASKED)
    row_top = jnp.max(masked_scores, -1, keepdims=True)
    exponent = jnp.exp(masked_scores - row_top)
    return exponent / jnp.sum(exponent, -1, keepdims=True)


LOW = jnp.bfloat16
FULL = jnp.float32


def turn(array, axis, r_bit, x_bit, y_bit):
    shape = array.shape
    cut = array.reshape(shape[:axis] + (2, 2, 2, shape[axis] // 8) + shape[axis + 1 :])
    for at, bit in ((axis, y_bit), (axis + 1, x_bit), (axis + 2, r_bit)):
        cut = jnp.where(bit, jnp.flip(cut, at), cut)
    return cut.reshape(shape)


MESH = pl.DeviceIdType.MESH
ANY = pl.BlockSpec(memory_space=pl.ANY)
IN_VMEM = pl.BlockSpec(memory_space=pltpu.VMEM)
VMEM_BYTES = 62 * 2**20
COPIES = 96


class Links:
    def __init__(self, send_sem, recv_sem, line=0):
        self.send_sem, self.recv_sem, self.sent, self.count = send_sem, recv_sem, [], 0
        self.r, self.f, self.t = (lax.axis_index(name) for name in ("replica", "fsdp", "tensor"))
        self.xb, self.yb = lax.rem(self.f, 2), lax.div(self.f, 2)
        self.x = (self.r, self.f + 1 - 2 * self.xb, self.t)
        self.y = (self.r, lax.rem(self.f + 2, 4), self.t)
        self.core = (1 - self.r, self.f, self.t)
        self.peers = [self.x, self.y, self.core]
        if line:
            self.line = line
            self.left, self.right, self.across = (
                (self.r, self.f, lax.rem(self.t + step, line)) for step in (line - 1, 1, 2)
            )
            self.pair = (self.r, self.f, self.t + 1 - 2 * lax.rem(self.t, 2))
            self.mirror = (self.r, self.f, line - 1 - self.t)
            self.peers += [self.left, self.right, self.across]

    def meet(self):
        barrier = pltpu.get_barrier_semaphore()
        for peer in self.peers:
            pl.semaphore_signal(barrier, inc=1, device_id=peer, device_id_type=MESH)
        pl.semaphore_wait(barrier, len(self.peers))

    def prepare(self, source, target, peer):
        k = self.count
        self.count += 1
        return pltpu.make_async_remote_copy(
            src_ref=source,
            dst_ref=target,
            send_sem=self.send_sem.at[k],
            recv_sem=self.recv_sem.at[k],
            device_id=peer,
            device_id_type=MESH,
        )

    def send(self, source, target, peer):
        copy = self.prepare(source, target, peer)
        copy.start()
        self.sent.append(copy)
        return copy

    def end(self):
        for copy in self.sent:
            copy.wait_send()

    def block(self, i):
        bits = [(1 - bit) if i >> at & 1 else bit for at, bit in ((2, self.yb), (1, self.xb), (0, self.r))]
        return (bits[0] * 2 + bits[1]) * 2 + bits[2]


class Local:
    def __init__(self, sem):
        self.sem, self.count, self.open = sem, 0, []

    def start(self, source, target):
        copy = pltpu.make_async_copy(source, target, self.sem.at[self.count])
        self.count += 1
        copy.start()
        self.open.append(copy)
        return copy

    def wait(self, *copies):
        for copy in copies:
            copy.wait()
            self.open = [other for other in self.open if other is not copy]

    def end(self):
        self.wait(*list(self.open))


def at_rows(ref, start, size):
    return ref.at[pl.ds(start, size), :]


def at_columns(ref, start, size):
    return ref.at[:, pl.ds(start, size)]


class Gathered:
    def __init__(self, links, local, shard, full, cut, unit):
        self.links, self.local, self.full, self.cut, self.unit = links, local, full, cut, unit
        mine = cut(shard, pl.multiple_of(links.r * unit, unit), unit)
        self.copies = [
            local.start(mine, self.at(0)),
            local.start(cut(shard, pl.multiple_of((1 - links.r) * unit, unit), unit), self.at(1)),
        ]
        self.mine = mine

    def at(self, block, start=0, size=None):
        return self.cut(self.full, block * self.unit + start, self.unit if size is None else size)

    def first(self):
        self.from_x = self.links.send(self.mine, self.at(2), self.links.x)
        self.from_y = self.links.send(self.mine, self.at(4), self.links.y)

    def relay_x(self):
        half = self.unit // 2
        self.from_x.wait_recv()
        self.far_top = self.links.send(self.at(2, 0, half), self.at(6, 0, half), self.links.y)
        self.core_x = self.links.send(self.at(2), self.at(3), self.links.core)

    def relay_y(self):
        half = self.unit // 2
        self.from_y.wait_recv()
        self.far_end = self.links.send(self.at(4, half, half), self.at(6, half, half), self.links.x)
        self.core_y = self.links.send(self.at(4), self.at(5), self.links.core)

    def relay_far(self):
        self.far_top.wait_recv()
        self.far_end.wait_recv()
        self.core_far = self.links.send(self.at(6), self.at(7), self.links.core)

    def whole(self):
        self.local.wait(*self.copies)
        for copy in (self.core_x, self.core_y, self.core_far):
            copy.wait_recv()


def tile_of(j, size):
    return pl.ds(pl.multiple_of(j * size, size), size)


def dot(left, right):
    return jnp.dot(left, right, preferred_element_type=FULL)


def spin(values_in, cosine, sine_one, sine_two):
    head = values_in[:, :128]
    turned_head = (
        head * cosine + pltpu.roll(head, 96, 1) * sine_one + pltpu.roll(head, 32, 1) * sine_two
    )
    return jnp.concatenate([turned_head, values_in[:, 128:]], -1)


def gather_kernel(
    score_scale,
    x_hbm, g_hbm, wh_hbm, wo_hbm, we_hbm, ws_hbm, vecs, key_pos, query_pos, cosine, sine_one, sine_two,
    we, ws, wo_out, act_out, slope_out, n2t_out, up_out, ctx_out, red_heads, red_out, red_shrink, sums,
    wh, wo, xr, g, n1, n2, n1t, n2t, stat, qkv_away, qkv, dctx_away, dctx, ctxt, ctxt_away,
    pg, pg_away, kvg, kvg_away, kvg_got, got_heads, got_out, got_shrink, local_sem, tile_sem, send_sem, recv_sem,
):
    links, local = Links(send_sem, recv_sem), Local(local_sem)
    tokens, width = xr.shape
    hd = dctx.shape[1]
    unit = width // 8
    blocks = range(8)
    x_in, g_in = [], []
    for i in blocks:
        cols = pl.ds(pl.multiple_of(links.block(i) * unit, unit), unit)
        x_in.append(local.start(x_hbm.at[:, cols], xr.at[:, pl.ds(i * unit, unit)]))
        g_in.append(local.start(g_hbm.at[:, cols], g.at[:, pl.ds(i * unit, unit)]))
    links.meet()
    heads = Gathered(links, local, wh_hbm, wh, at_rows, unit)
    output = Gathered(links, local, wo_hbm, wo, at_columns, unit)
    expand = Gathered(links, local, we_hbm, we, at_rows, unit)
    shrink = Gathered(links, local, ws_hbm, ws, at_columns, unit)
    heads.first()
    output.first()

    local.wait(*x_in)

    def norm_rows(c, carry):
        rows = tile_of(c, 64)
        value = xr[rows, :].astype(FULL)
        average = jnp.mean(value, -1, keepdims=True)
        centred = value - average
        inverse = lax.rsqrt(jnp.mean(centred * centred, -1, keepdims=True) + NORM_EPS)
        normal = centred * inverse
        stat[rows, :] = jnp.concatenate(
            [jnp.broadcast_to(average, (64, 128)), jnp.broadcast_to(inverse, (64, 128))], -1
        )
        n1[rows, :] = (normal * vecs[0:1, :] + vecs[1:2, :]).astype(LOW)
        n2[rows, :] = (normal * vecs[2:3, :] + vecs[3:4, :]).astype(LOW)
        return carry

    lax.fori_loop(0, tokens // 64, norm_rows, 0)

    def turn_tiles(j, carry):
        cols = tile_of(j, unit)
        n1t[cols, :] = n1[:, cols].T
        n2t[cols, :] = n2[:, cols].T
        return carry

    lax.fori_loop(0, 8, turn_tiles, 0)
    local.start(n2t, n2t_out)
    sums[...] = jnp.zeros_like(sums)
    local.wait(*g_in)
    for i in blocks:
        cols = pl.ds(pl.multiple_of(links.block(i) * unit, unit), unit)
        sums[4:5, cols] = jnp.sum(g[:, i * unit : (i + 1) * unit].astype(FULL), 0, keepdims=True)

    heads.relay_x()
    heads.relay_y()
    output.relay_x()
    output.relay_y()
    heads.relay_far()
    expand.first()
    output.relay_far()
    heads.whole()

    own, away = links.yb * 3 * hd, (1 - links.yb) * 3 * hd

    def project(start, target):
        def one(c, carry):
            cols = pl.ds(pl.multiple_of(start + c * hd, hd), hd)
            value = dot(n1[...], wh[:, cols]) + vecs[5:6, cols]
            spun = spin(value, cosine[:tokens, :], sine_one[:tokens, :], sine_two[:tokens, :])
            target[c, :tokens, :] = jnp.where(c < 2, spun, value).astype(LOW)
            return carry

        lax.fori_loop(0, 3, one, 0)

    project(away, qkv_away)
    qkv_from_y = links.send(qkv_away, qkv.at[:, pl.ds(tokens, tokens), :], links.y)
    project(own, qkv)
    kv_from_x = links.send(
        qkv.at[pl.ds(1, 2), pl.ds(0, tokens), :], qkv.at[pl.ds(1, 2), pl.ds(2 * tokens, tokens), :], links.x
    )
    output.whole()
    local.start(wo, wo_out)
    rows_own = pl.ds(pl.multiple_of(links.yb * hd, hd), hd)
    rows_away = pl.ds(pl.multiple_of((1 - links.yb) * hd, hd), hd)
    dctx_away[...] = contract_last(g[...], wo[rows_away, :]).astype(LOW)
    dctx_from_y = links.send(dctx_away, dctx.at[pl.ds(tokens, tokens), :], links.y)
    dctx[:tokens, :] = contract_last(g[...], wo[rows_own, :]).astype(LOW)

    qkv_from_y.wait_recv()
    kv_from_far = links.send(
        qkv.at[pl.ds(1, 2), pl.ds(tokens, tokens), :],
        qkv.at[pl.ds(1, 2), pl.ds(3 * tokens, tokens), :],
        links.x,
    )
    expand.relay_x()
    expand.relay_y()
    shrink.first()
    dctx_from_y.wait_recv()
    kv_from_x.wait_recv()
    kv_from_far.wait_recv()

    def attention(kt, vt, dk, dv, prob, wgt, prob_low, grad_low):
        keys = qkv.shape[1]
        step = 512
        parts = [pl.ds(i * step, step) for i in range(keys // step)]
        for part in parts:
            kt[:, part] = qkv[1, part, :].T
            vt[:, part] = qkv[2, part, :].T
        dk[...] = jnp.zeros_like(dk)
        dv[...] = jnp.zeros_like(dv)

        def one(b, carry):
            rows = tile_of(b, hd)
            query, grad = qkv[0, rows, :], dctx[rows, :]
            spot = query_pos[:, rows]
            top = jnp.full((1, hd), MASKED, FULL)
            for part in parts:
                scores = contract_last(qkv[1, part, :], query) * score_scale
                scores = jnp.where(key_pos[part, :] <= spot, scores, MASKED)
                prob[part, :] = scores
                top = jnp.maximum(top, jnp.max(scores, 0, keepdims=True))
            total = jnp.zeros((1, hd), FULL)
            for part in parts:
                exponent = jnp.exp(prob[part, :] - top)
                prob[part, :] = exponent
                total = total + jnp.sum(exponent, 0, keepdims=True)
            share = 1.0 / total
            inner = jnp.zeros((1, hd), FULL)
            for part in parts:
                weight = contract_last(qkv[2, part, :], grad)
                chance = prob[part, :] * share
                prob[part, :] = chance
                prob_low[part, :] = chance.astype(LOW)
                wgt[part, :] = weight
                inner = inner + jnp.sum(chance * weight, 0, keepdims=True)
            for part in parts:
                grad_low[part, :] = (prob[part, :] * (wgt[part, :] - inner)).astype(LOW)
            context = dot(vt[...], prob_low[...]).astype(LOW)
            query_grad = dot(kt[...], grad_low[...]) * score_scale
            for part in parts:
                dv[part, :] += dot(prob_low[part, :], grad)
                dk[part, :] += dot(grad_low[part, :], query)
            turned_grad = spin(query_grad.T, cosine[rows, :], -sine_one[rows, :], -sine_two[rows, :]).astype(LOW)
            return context, turned_grad

        def here(b, carry):
            context, turned_grad = one(b, carry)
            rows = tile_of(b, hd)
            ctxt[rows_own, rows] = context
            pg[rows, pl.ds(pl.multiple_of(own, hd), hd)] = turned_grad
            return carry

        def there(b, carry):
            context, turned_grad = one(b + tokens // hd, carry)
            rows = tile_of(b, hd)
            ctxt_away[:, rows] = context
            pg_away[rows, :hd] = turned_grad
            return carry

        lax.fori_loop(0, tokens // hd, there, 0)
        lax.fori_loop(0, tokens // hd, here, 0)
        for i, total in enumerate((dk, dv)):
            kvg_away[i, :, :] = total[2 * tokens :, :].astype(LOW)
            kvg[i, :, :] = total[: 2 * tokens, :]

    keys = qkv.shape[1]
    pl.run_scoped(
        attention,
        pltpu.VMEM((hd, keys), LOW),
        pltpu.VMEM((hd, keys), LOW),
        pltpu.VMEM((keys, hd), FULL),
        pltpu.VMEM((keys, hd), FULL),
        pltpu.VMEM((keys, hd), FULL),
        pltpu.VMEM((keys, hd), FULL),
        pltpu.VMEM((keys, hd), LOW),
        pltpu.VMEM((keys, hd), LOW),
    )
    ctx_from_y = links.send(ctxt_away, ctxt.at[rows_own, :], links.y)
    kvg_from_x = links.send(kvg_away, kvg_got, links.x)
    expand.relay_far()
    expand.whole()

    def rest(tiles, slope, actt, send_heads, send_out, send_shrink):
        act = n1

        def load(j):
            return pltpu.make_async_copy(
                we.at[:, tile_of(j, unit)], tiles.at[lax.rem(j, 2)], tile_sem.at[lax.rem(j, 2)]
            )

        load(0).start()

        def forward(j, carry):
            @pl.when(j < 7)
            def _():
                load(j + 1).start()

            load(j).wait()
            cols = tile_of(j, unit)
            value = dot(n2[...], tiles[lax.rem(j, 2)]) + vecs[4:5, cols]
            normal_share = 0.5 * (1.0 + lax.erf(value * (0.5**0.5)))
            low_act = (value * normal_share).astype(LOW)
            act[:, cols] = low_act
            actt[cols, :] = low_act.T
            density = jnp.exp(value * value * -0.5) * 0.3989422804014327
            slope[:, cols] = (normal_share + value * density).astype(LOW)
            return carry

        lax.fori_loop(0, 4, forward, 0)
        shrink.relay_x()
        shrink.relay_y()
        lax.fori_loop(4, 8, forward, 0)
        local.start(act, act_out)
        local.start(slope, slope_out)

        kvg_from_x.wait_recv()
        for i in range(2):
            for away_rows, target in ((False, pg), (True, pg_away)):
                rows = pl.ds(tokens if away_rows else 0, tokens)
                total = kvg[i, rows, :] + kvg_got[i, rows, :].astype(FULL)
                if i == 0:
                    total = spin(total * score_scale, cosine[rows, :], -sine_one[rows, :], -sine_two[rows, :])
                start = (0 if away_rows else own) + (1 + i) * hd
                target[:, pl.ds(pl.multiple_of(start, hd), hd)] = total.astype(LOW)
        pg_from_y = links.send(pg_away, pg.at[:, pl.ds(pl.multiple_of(own, 3 * hd), 3 * hd)], links.y)

        def shrink_block(i, target, extra):
            def one(c, carry):
                rows = tile_of(c, 512)
                part = dot(actt[rows, :], g[:, i * unit : (i + 1) * unit])
                if extra is not None:
                    part = part + extra[rows, :].astype(FULL)
                target[rows, :] = part.astype(LOW)
                return carry

            lax.fori_loop(0, actt.shape[0] // 512, one, 0)

        shrink_got, out_got, heads_got = [], [], []
        for k in range(4):
            shrink_block(2 * k + 1, send_shrink.at[k], None)
            shrink_got.append(links.send(send_shrink.at[k], got_shrink.at[k], links.core))
        ctx_from_y.wait_recv()
        local.start(ctxt, ctx_out)
        for k in range(4):
            i = 2 * k + 1
            send_out[k, :, :] = dot(ctxt[...], g[:, i * unit : (i + 1) * unit]).astype(LOW)
            out_got.append(links.send(send_out.at[k], got_out.at[k], links.core))
        for k in range(4):
            shrink_got[k].wait_recv()
            shrink_block(2 * k, got_shrink.at[k], got_shrink.at[k])
            local.start(got_shrink.at[k], red_shrink.at[k])
        for k in range(4):
            out_got[k].wait_recv()
            total = dot(ctxt[...], g[:, 2 * k * unit : (2 * k + 1) * unit])
            got_out[k, :, :] = (total + got_out[k, :, :].astype(FULL)).astype(LOW)
            local.start(got_out.at[k], red_out.at[k])
        shrink.relay_far()
        pg_from_y.wait_recv()
        for k in range(4):
            rows = pl.ds((2 * k + 1) * unit, unit)
            send_heads[k, :, :] = dot(n1t[rows, :], pg[...]).astype(LOW)
            heads_got.append(links.send(send_heads.at[k], got_heads.at[k], links.core))

        up = n2
        for i in blocks:
            cols = slice(i * unit, (i + 1) * unit)
            grad = contract_last(pg[...], wh[cols, :])
            normal = (xr[:, cols].astype(FULL) - stat[:, 0:1]) * stat[:, 128:129]
            place = pl.ds(pl.multiple_of(links.block(i) * unit, unit), unit)
            sums[0:1, place] = jnp.sum(grad * normal, 0, keepdims=True)
            sums[1:2, place] = jnp.sum(grad, 0, keepdims=True)
            up[:, cols] = (grad * vecs[0:1, cols]).astype(LOW)
        local.start(up, up_out)
        sums[6:7, : pg.shape[1]] = jnp.sum(pg[...].astype(FULL), 0, keepdims=True)
        for k in range(4):
            heads_got[k].wait_recv()
            total = dot(n1t[2 * k * unit : (2 * k + 1) * unit, :], pg[...])
            got_heads[k, :, :] = (total + got_heads[k, :, :].astype(FULL)).astype(LOW)
            local.start(got_heads.at[k], red_heads.at[k])
        shrink.whole()
        links.end()
        local.end()

    pl.run_scoped(
        rest,
        pltpu.VMEM((2, width, unit), LOW),
        pltpu.VMEM(n2.shape, LOW),
        pltpu.VMEM((we.shape[1], tokens), LOW),
        pltpu.VMEM(got_heads.shape, LOW),
        pltpu.VMEM(got_out.shape, LOW),
        pltpu.VMEM(got_shrink.shape, LOW),
    )


def gather_call(x, g, heads_rows, output_rows, expand_weight, shrink_weight, vecs, key_pos, query_pos, tables):
    tokens, width = x.shape
    heads_wide, out_wide, units = heads_rows.shape[1], output_rows.shape[0], expand_weight.shape[1]
    hd = heads_wide // 6
    keys = key_pos.shape[0]
    unit = width // 8
    low = lambda *shape: jax.ShapeDtypeStruct(shape, LOW)
    outs = [
        low(width, units),
        low(units, width),
        low(out_wide, width),
        low(tokens, units),
        low(tokens, units),
        low(width, tokens),
        low(tokens, width),
        low(out_wide, tokens),
        low(4, unit, heads_wide),
        low(4, out_wide, unit),
        low(4, units, unit),
        jax.ShapeDtypeStruct((8, width), FULL),
    ]
    vm = lambda *shape: pltpu.VMEM(shape, LOW)
    scratch = [
        vm(width, heads_wide),
        vm(out_wide, width),
        vm(tokens, width),
        vm(tokens, width),
        vm(tokens, width),
        vm(tokens, width),
        vm(width, tokens),
        vm(width, tokens),
        pltpu.VMEM((tokens, 256), FULL),
        vm(3, tokens, hd),
        vm(3, keys, hd),
        vm(tokens, hd),
        vm(2 * tokens, hd),
        vm(out_wide, tokens),
        vm(hd, tokens),
        vm(tokens, heads_wide),
        vm(tokens, 3 * hd),
        pltpu.VMEM((2, 2 * tokens, hd), FULL),
        vm(2, 2 * tokens, hd),
        vm(2, 2 * tokens, hd),
        vm(4, unit, heads_wide),
        vm(4, out_wide, unit),
        vm(4, units, unit),
        pltpu.SemaphoreType.DMA((64,)),
        pltpu.SemaphoreType.DMA((2,)),
        pltpu.SemaphoreType.DMA((COPIES,)),
        pltpu.SemaphoreType.DMA((COPIES,)),
    ]
    return pl.pallas_call(
        functools.partial(gather_kernel, hd**-0.5),
        out_shape=outs,
        in_specs=[ANY] * 6 + [IN_VMEM] * 6,
        out_specs=[ANY] * 11 + [IN_VMEM],
        scratch_shapes=scratch,
        compiler_params=pltpu.CompilerParams(
            collective_id=0, has_side_effects=True, vmem_limit_bytes=VMEM_BYTES
        ),
    )(x, g, heads_rows, output_rows, expand_weight, shrink_weight, vecs, key_pos, query_pos, *tables)


class Scattered:
    def __init__(self, links, local, block, cut, unit, via, got, stage, own, loaded):
        self.links, self.local, self.block, self.cut, self.unit = links, local, block, cut, unit
        self.via, self.got, self.stage, self.own = via, got, stage, own
        self.half = unit // 2
        if loaded:
            self.loads = [
                local.start(cut(block(1), self.half, self.half), stage.at[0]),
                local.start(cut(block(2), 0, self.half), stage.at[1]),
                local.start(block(0), own),
            ]

    def first(self):
        half, cut, far = self.half, self.cut, self.block(3)
        self.via_x = self.links.send(cut(far, 0, half), self.via.at[0], self.links.x)
        self.via_y = self.links.send(cut(far, half, half), self.via.at[1], self.links.y)

    def direct(self):
        half, cut = self.half, self.cut
        self.x_top = self.links.send(cut(self.block(1), 0, half), cut(self.got.at[0], 0, half), self.links.x)
        self.y_end = self.links.send(cut(self.block(2), half, half), cut(self.got.at[1], half, half), self.links.y)

    def second(self):
        half, cut = self.half, self.cut
        self.local.wait(*self.loads[:2])
        self.via_x.wait_recv()
        add_rows(self.stage.at[1], self.stage.at[1], self.via.at[0])
        self.y_top = self.links.send(self.stage.at[1], cut(self.got.at[1], 0, half), self.links.y)
        self.via_y.wait_recv()
        add_rows(self.stage.at[0], self.stage.at[0], self.via.at[1])
        self.x_end = self.links.send(self.stage.at[0], cut(self.got.at[0], half, half), self.links.x)

    def third(self, total, place):
        for copy in (self.x_top, self.x_end, self.y_top, self.y_end):
            copy.wait_recv()
        self.local.wait(self.loads[2])
        add_rows(total, self.own, self.got.at[0], self.got.at[1])
        self.kept = self.local.start(total, place)
        self.other = self.links.send(total, place, self.links.core)


def add_rows(target, *parts):
    rows, wide = target.shape
    step = min(rows, 32 if wide > 512 else 256)

    def one(c, carry):
        at = pl.ds(pl.multiple_of(c * step, step), step)
        total = parts[0][at, :].astype(FULL)
        for part in parts[1:]:
            total = total + part[at, :].astype(FULL)
        target[at, :] = total.astype(target.dtype)
        return carry

    lax.fori_loop(0, rows // step, one, 0)


class Line:
    def __init__(self, links, part, got, final, finish):
        self.links, self.part, self.got, self.final, self.finish = links, part, got, final, finish
        self.step = part.shape[0] // CHUNKS
        self.outer = jnp.logical_or(links.t == 0, links.t == links.line - 1)
        self.middle = jnp.logical_not(self.outer)
        self.inward = [self.make(c, part, final, links.pair) for c in range(CHUNKS)]
        self.across = [self.make(c, part, got, links.mirror) for c in range(CHUNKS)]
        self.outward = [self.make(c, final, final, links.pair) for c in range(CHUNKS)]

    def rows(self, c):
        return pl.ds(c * self.step, self.step)

    def make(self, c, source, target, peer):
        return self.links.prepare(source.at[self.rows(c), :], target.at[self.rows(c), :], peer)

    def start(self):
        @pl.when(self.outer)
        def _():
            for copy in self.inward:
                copy.start()

    def first(self, c):
        @pl.when(self.middle)
        def _():
            self.inward[c].wait_recv()
            rows = self.rows(c)
            add_rows(self.part.at[rows, :], self.part.at[rows, :], self.final.at[rows, :])
            self.across[c].start()

    def second(self, c):
        @pl.when(self.middle)
        def _():
            self.across[c].wait_recv()
            self.finish(self.rows(c))
            self.outward[c].start()

    def third(self, c):
        @pl.when(self.outer)
        def _():
            self.outward[c].wait_recv()

    def end(self):
        @pl.when(self.outer)
        def _():
            for copy in self.inward:
                copy.wait_send()

        @pl.when(self.middle)
        def _():
            for copy in self.across + self.outward:
                copy.wait_send()


CHUNKS = 8


def scatter_kernel(
    line_size,
    we_hbm, ws_hbm, wo_hbm, act_hbm, slope_hbm, n2t_hbm, up_hbm, ctxt_hbm, red_heads, red_out, red_shrink, x_hbm, g_hbm,
    vecs, sums_in,
    layer_out, input_grad, heads_grad, output_grad, expand_grad, shrink_grad, got_expand, sums_out,
    ws, we, wo, act, slope, n2t, up, ctxt, g, part_branch, final_branch, final_up, got_branch, got_up,
    via_h, got_h, stage_h, own_h, via_o, got_o, stage_o, own_o, via_s, got_s, stage_s, own_s, via_e, got_e,
    total_rows, total_columns, total_out, grad_rows, sums, sums_got, local_sem, send_sem, recv_sem,
):
    links, local = Links(send_sem, recv_sem, line_size), Local(local_sem)
    tokens, width = g.shape
    unit = width // 8
    blocks = range(8)
    place = [pl.ds(pl.multiple_of(links.block(i) * unit, unit), unit) for i in blocks]

    def here(i):
        return pl.ds(i * unit, unit)

    first_loads = [local.start(ws_hbm, ws), local.start(act_hbm, act), local.start(ctxt_hbm, ctxt), local.start(wo_hbm, wo)]
    g_loads = [local.start(g_hbm.at[:, place[i]], g.at[:, here(i)]) for i in blocks]
    slope_load = local.start(slope_hbm, slope)
    we_load, up_load, n2t_load = local.start(we_hbm, we), local.start(up_hbm, up), local.start(n2t_hbm, n2t)
    links.meet()

    shrink = Scattered(links, local, lambda k: red_shrink.at[k], at_columns, unit, via_s, got_s, stage_s, own_s, True)
    heads = Scattered(links, local, lambda k: red_heads.at[k], at_rows, unit, via_h, got_h, stage_h, own_h, True)
    output = Scattered(links, local, lambda k: red_out.at[k], at_columns, unit, via_o, got_o, stage_o, own_o, True)
    shrink.first()
    heads.first()
    output.first()

    local.wait(*first_loads)
    context = ctxt[...].T

    def branch_tile(j, carry):
        cols = tile_of(j, unit)
        part_branch[:, cols] = (dot(context, wo[:, cols]) + dot(act[...], ws[:, cols])).astype(LOW)
        return carry

    lax.fori_loop(0, 8, branch_tile, 0)
    x = act
    x_loads = [local.start(x_hbm.at[:, place[i]], x.at[:, here(i)]) for i in blocks]

    def finish_branch(rows):
        def one(c, carry):
            at = pl.ds(pl.multiple_of(rows.start + c * 16, 16), 16)
            total = part_branch[at, :].astype(FULL) + got_branch[at, :].astype(FULL)
            final_branch[at, :] = (x[at, :].astype(FULL) + total + vecs[1:2, :]).astype(LOW)
            return carry

        lax.fori_loop(0, rows.size // 16, one, 0)

    def finish_up(rows):
        add_rows(final_up.at[rows, :], up.at[rows, :], got_up.at[rows, :])

    line_branch = Line(links, part_branch, got_branch, final_branch, finish_branch)
    line_up = Line(links, up, got_up, final_up, finish_up)
    line_branch.start()

    local.wait(*g_loads, slope_load)
    sums[0, :, :] = sums_in[...]

    def hidden_tile(j, carry):
        cols = tile_of(j, unit)
        grad = (contract_last(g[...], ws[cols, :]) * slope[:, cols].astype(FULL)).astype(LOW)
        slope[:, cols] = grad
        sums[0, 5:6, cols] = jnp.sum(grad.astype(FULL), 0, keepdims=True)
        return carry

    lax.fori_loop(0, 8, hidden_tile, 0)
    local.wait(*x_loads, we_load, up_load, n2t_load)
    shrink.direct()
    heads.direct()
    output.direct()

    def up_block(i):
        cols = here(i)
        grad = contract_last(slope[...], we[i * unit : (i + 1) * unit, :])
        value = x[:, cols].astype(FULL)
        normal = (value - average) * inverse
        sums[0, 2:3, place[i]] = jnp.sum(grad * normal, 0, keepdims=True)
        sums[0, 3:4, place[i]] = jnp.sum(grad, 0, keepdims=True)
        up[:, cols] = (up[:, cols].astype(FULL) + grad * vecs[0:1, cols]).astype(LOW)

    total = jnp.zeros((tokens, 1), FULL)
    for i in blocks:
        total = total + jnp.sum(x[:, here(i)].astype(FULL), -1, keepdims=True)
    average = total * (1.0 / width)
    total = jnp.zeros((tokens, 1), FULL)
    for i in blocks:
        centred = x[:, here(i)].astype(FULL) - average
        total = total + jnp.sum(centred * centred, -1, keepdims=True)
    inverse = lax.rsqrt(total * (1.0 / width) + NORM_EPS)

    steps = [(line, c) for line in (line_branch, line_up) for c in range(CHUNKS)]

    def serve(count):
        for _ in range(count):
            at = serve.done
            if at < len(steps):
                steps[at][0].first(steps[at][1])
            if at >= 2:
                steps[at - 2][0].second(steps[at - 2][1])
            serve.done += 1

    serve.done = 0
    for i in range(4):
        up_block(i)
    serve(1)
    for i in range(4, 8):
        up_block(i)
    line_up.start()
    serve(1)
    shrink.second()
    heads.second()
    output.second()
    serve(1)

    expand_got = []

    def expand_block(i, target):
        def one(c, carry):
            cols = tile_of(c, 512)
            part = dot(n2t[i * unit : (i + 1) * unit, :], slope[:, cols])
            if target is we:
                part = part + target[(i // 2) * unit : (i // 2 + 1) * unit, cols].astype(FULL)
            target[(i // 2) * unit : (i // 2 + 1) * unit, cols] = part.astype(LOW)
            return carry

        lax.fori_loop(0, slope.shape[1] // 512, one, 0)

    for k in (3, 1, 2, 0):
        expand_block(2 * k + 1, ws)
        rows = pl.ds(k * unit, unit)
        expand_got.append((k, links.send(ws.at[rows, :], got_expand.at[k], links.core)))
        if k in (1, 0):
            serve(1)
    expand = Scattered(
        links, local, lambda k: we.at[pl.ds(k * unit, unit), :], at_rows, unit, via_e, got_e, None, None, False
    )
    loads = []
    for k, copy in expand_got:
        copy.wait_recv()
        loads.append(local.start(got_expand.at[k], we.at[pl.ds(k * unit, unit), :]))
    for (k, copy), load in zip(expand_got, loads):
        local.wait(load)
        expand_block(2 * k, we)
        if k == 3:
            expand.first()
        if k in (1, 0):
            serve(1)
    expand.direct()

    hops = []

    def hop(s, peer):
        hops.append(links.send(sums.at[s], sums_got.at[s], peer))

    def hop_end(s):
        hops[s].wait_recv()
        sums[s + 1, :, :] = sums[s, :, :] + sums_got[s, :, :]

    for s, peer in enumerate((links.core, links.x, links.y, links.pair, links.across)):
        hop(s, peer)
        serve(1)
        hop_end(s)
        if s == 2:
            output.third(total_out, output_grad.at[:, pl.ds(pl.multiple_of(links.r * unit, unit), unit)])
            heads.third(
                total_rows.at[:, pl.ds(0, own_h.shape[1])],
                heads_grad.at[pl.ds(pl.multiple_of(links.r * unit, unit), unit), :],
            )
        if s == 3:
            shrink.third(total_columns, shrink_grad.at[:, pl.ds(pl.multiple_of(links.r * unit, unit), unit)])
    sums_out[0:4, :] = sums[5, 0:4, :]
    sums_out[4:8, :] = sums[3, 4:8, :]

    expand.via_x.wait_recv()
    top, end = pl.ds(2 * unit, unit // 2), pl.ds(unit + unit // 2, unit // 2)
    add_rows(we.at[top, :], we.at[top, :], via_e.at[0])
    expand.y_top = links.send(we.at[top, :], got_e.at[1, pl.ds(0, unit // 2), :], links.y)
    expand.via_y.wait_recv()
    add_rows(we.at[end, :], we.at[end, :], via_e.at[1])
    expand.x_end = links.send(we.at[end, :], got_e.at[0, pl.ds(unit // 2, unit // 2), :], links.x)
    serve(len(steps) + 2 - serve.done)
    for c in range(CHUNKS):
        line_branch.third(c)
    for i in blocks:
        local.start(final_branch.at[:, here(i)], layer_out.at[:, place[i]])
    for c in range(CHUNKS):
        line_up.third(c)

    out_copies = {}
    step = grad_rows.shape[1]
    for c in range(tokens // step):
        slot = c % 2
        if c >= 2:
            local.wait(*out_copies[c - 2])
        rows = pl.ds(c * step, step)
        value = x[rows, :].astype(FULL)
        centred = value - jnp.mean(value, -1, keepdims=True)
        scale = lax.rsqrt(jnp.mean(centred * centred, -1, keepdims=True) + NORM_EPS)
        normal = centred * scale
        upstream = final_up[rows, :].astype(FULL)
        inner = upstream - jnp.mean(upstream, -1, keepdims=True)
        inner = inner - normal * jnp.mean(upstream * normal, -1, keepdims=True)
        grad_rows[slot, :, :] = g[rows, :].astype(FULL) + inner * scale
        out_copies[c] = [
            local.start(grad_rows.at[slot, :, here(i)], input_grad.at[rows, place[i]]) for i in blocks
        ]

    for copy in (expand.x_top, expand.x_end, expand.y_top, expand.y_end):
        copy.wait_recv()
    heads.other.wait_send()
    local.wait(heads.kept)
    add_rows(total_rows, we.at[pl.ds(0, unit), :], got_e.at[0], got_e.at[1])
    spot = expand_grad.at[pl.ds(pl.multiple_of(links.r * unit, unit), unit), :]
    local.start(total_rows, spot)
    last = links.send(total_rows, spot, links.core)
    for copy in (shrink.other, output.other, heads.other, last):
        copy.wait_recv()
    links.sent = [copy for copy in links.sent if copy is not heads.other]
    links.end()
    line_branch.end()
    line_up.end()
    local.end()


def scatter_call(line_size, arrays, x, g, vecs, sums):
    tokens, width = x.shape
    expand_full, shrink_full, output_full, act, slope, n2t, up, ctxt, red_heads, red_out, red_shrink = arrays
    unit = width // 8
    units, heads_wide, out_wide = act.shape[1], red_heads.shape[2], ctxt.shape[0]
    low = lambda *shape: pltpu.VMEM(shape, LOW)
    full = lambda *shape: pltpu.VMEM(shape, FULL)
    half = unit // 2
    outs = [
        jax.ShapeDtypeStruct((tokens, width), LOW),
        jax.ShapeDtypeStruct((tokens, width), FULL),
        jax.ShapeDtypeStruct((2 * unit, heads_wide), FULL),
        jax.ShapeDtypeStruct((out_wide, 2 * unit), FULL),
        jax.ShapeDtypeStruct((2 * unit, units), FULL),
        jax.ShapeDtypeStruct((units, 2 * unit), FULL),
        jax.ShapeDtypeStruct((4, unit, units), LOW),
        jax.ShapeDtypeStruct((8, width), FULL),
    ]
    scratch = [
        low(units, width),
        low(width, units),
        low(out_wide, width),
        low(tokens, units),
        low(tokens, units),
        low(width, tokens),
        low(tokens, width),
        low(out_wide, tokens),
        low(tokens, width),
        low(tokens, width),
        low(tokens, width),
        low(tokens, width),
        low(tokens, width),
        low(tokens, width),
        low(2, half, heads_wide), low(2, unit, heads_wide), low(2, half, heads_wide), low(unit, heads_wide),
        low(2, out_wide, half), low(2, out_wide, unit), low(2, out_wide, half), low(out_wide, unit),
        low(2, units, half), low(2, units, unit), low(2, units, half), low(units, unit),
        low(2, half, units), low(2, unit, units),
        full(unit, units),
        full(units, unit),
        full(out_wide, unit),
        full(2, 32, width),
        full(6, 8, width),
        full(5, 8, width),
        pltpu.SemaphoreType.DMA((224,)),
        pltpu.SemaphoreType.DMA((COPIES,)),
        pltpu.SemaphoreType.DMA((COPIES,)),
    ]
    return pl.pallas_call(
        functools.partial(scatter_kernel, line_size),
        out_shape=outs,
        in_specs=[ANY] * 13 + [IN_VMEM] * 2,
        out_specs=[ANY] * 7 + [IN_VMEM],
        scratch_shapes=scratch,
        compiler_params=pltpu.CompilerParams(
            collective_id=1, has_side_effects=True, vmem_limit_bytes=VMEM_BYTES
        ),
    )(expand_full, shrink_full, output_full, act, slope, n2t, up, ctxt, red_heads, red_out, red_shrink, x, g, vecs, sums)


def square_local(
    layer_input,
    block_order,
    first_gain,
    first_bias,
    second_gain,
    second_bias,
    heads_weight,
    heads_bias,
    output_weight,
    output_bias,
    expand_weight,
    expand_bias,
    shrink_weight,
    shrink_bias,
    cotangent,
):
    tokens = layer_input.shape[1]
    width = layer_input.shape[2]
    replica, fsdp = lax.axis_index("replica"), lax.axis_index("fsdp")
    r_bit, x_bit, y_bit = replica == 1, fsdp % 2 == 1, fsdp // 2 == 1

    def turned(array, axis):
        return turn(array, axis, r_bit, x_bit, y_bit)

    heads_rows = heads_weight.reshape(heads_weight.shape[0], -1)
    output_rows = output_weight.reshape(-1, output_weight.shape[2])
    wide = heads_rows.shape[1]
    gain_one, shift_one, gain_two, shift_two = (
        turned(vec.astype(FULL), 0) for vec in (first_gain, first_bias, second_gain, second_bias)
    )
    vecs = jnp.stack(
        [
            gain_one,
            shift_one,
            gain_two,
            shift_two,
            expand_bias.astype(FULL),
            jnp.pad(heads_bias.reshape(-1).astype(FULL), (0, width - wide)),
            jnp.zeros((width,), FULL),
            jnp.zeros((width,), FULL),
        ]
    )
    order_row = block_order[0]
    slots = fsdp ^ jnp.array([0, 2, 1, 3], jnp.int32)
    order_here = order_row[slots]
    offsets = jnp.arange(tokens, dtype=jnp.int32)
    key_pos = (order_here[:, None] * tokens + offsets[None]).reshape(-1)
    query_pos = key_pos[: 2 * tokens]
    cosine, sine_part = rotary_tables(query_pos, ROT)
    still = jnp.zeros((2 * tokens, 128 - ROT), FULL)
    left, right = jnp.split(sine_part, 2, 1)
    tables = (
        jnp.concatenate([cosine, still + 1.0], 1),
        jnp.concatenate([-left, jnp.zeros_like(right), still], 1),
        jnp.concatenate([jnp.zeros_like(left), right, still], 1),
    )
    *gathered, sums = gather_call(
        layer_input[0], cotangent[0], heads_rows, output_rows, expand_weight, shrink_weight,
        vecs, key_pos[:, None], query_pos[None, :], tables,
    )

    second = jnp.stack([gain_two, turned(output_bias.astype(FULL) + shrink_bias.astype(FULL), 0)])
    layer_output, input_grad, heads_grad, output_grad, expand_weight_grad, shrink_weight_grad, _, sums = scatter_call(
        lax.axis_size("tensor"),
        gathered,
        layer_input[0],
        cotangent[0],
        jnp.pad(second, ((0, 6), (0, 0))),
        sums,
    )
    return (
        layer_output[None],
        input_grad[None],
        sums[0],
        sums[1],
        sums[2],
        sums[3],
        heads_grad.reshape(heads_weight.shape),
        sums[6, :wide].reshape(heads_bias.shape),
        output_grad.reshape(output_weight.shape),
        sums[4],
        expand_weight_grad,
        sums[5],
        shrink_weight_grad,
        sums[4],
    )


def ring_local(
    layer_input,
    block_order,
    first_gain,
    first_bias,
    second_gain,
    second_bias,
    heads_weight,
    heads_bias,
    output_weight,
    output_bias,
    expand_weight,
    expand_bias,
    shrink_weight,
    shrink_bias,
    cotangent,
):
    tokens_here = layer_input.shape[1]
    fsdp_count = lax.axis_size("fsdp")
    head_dim = output_weight.shape[1]
    score_scale = head_dim ** (-0.5)
    order_row = block_order[0]
    device_slot = lax.axis_index("fsdp")
    own_block = jnp.sum(
        jnp.where(jnp.arange(fsdp_count, dtype=jnp.int32) == device_slot, order_row, 0)
    )
    offsets = jnp.arange(tokens_here, dtype=jnp.int32)
    query_pos = own_block * tokens_here + offsets
    key_pos = jnp.repeat(order_row, tokens_here) * tokens_here + jnp.tile(offsets, fsdp_count)
    allowed = key_pos[None, :] <= query_pos[:, None]
    cosine, sine_part = rotary_tables(query_pos, ROT)
    hidden_in = layer_input[0].astype(jnp.float32)
    gain_one = first_gain.astype(jnp.float32)
    shift_one = first_bias.astype(jnp.float32)
    gain_two = second_gain.astype(jnp.float32)
    shift_two = second_bias.astype(jnp.float32)
    norm_one_low = layer_norm(hidden_in, gain_one, shift_one).astype(jnp.bfloat16)
    norm_two_low = layer_norm(hidden_in, gain_two, shift_two).astype(jnp.bfloat16)
    heads_full, output_full, expand_full, shrink_full = (
        lax.all_gather(heads_weight, "fsdp", axis=0, tiled=True),
        lax.all_gather(output_weight, "fsdp", axis=2, tiled=True),
        lax.all_gather(expand_weight, "fsdp", axis=0, tiled=True),
        lax.all_gather(shrink_weight, "fsdp", axis=1, tiled=True),
    )
    projected = jnp.einsum(
        "td,dhe->hte", norm_one_low, heads_full, preferred_element_type=jnp.float32
    )
    projected = projected + heads_bias.astype(jnp.float32)[:, None, :]
    query_pre = projected[..., :head_dim]
    key_pre = projected[..., head_dim : 2 * head_dim]
    query_low = rotate(query_pre, cosine, sine_part).astype(jnp.bfloat16)
    key_low = rotate(key_pre, cosine, sine_part).astype(jnp.bfloat16)
    value_low = projected[..., 2 * head_dim :].astype(jnp.bfloat16)
    key_all, value_all = (
        lax.all_gather(key_low, "fsdp", axis=1, tiled=True),
        lax.all_gather(value_low, "fsdp", axis=1, tiled=True),
    )

    def attend_head(operands):
        query_head, key_head, value_head = operands
        probability = softmax_rows(contract_last(query_head, key_head) * score_scale, allowed)
        return jnp.dot(
            probability.astype(jnp.bfloat16), value_head, preferred_element_type=jnp.float32
        )

    context = lax.map(attend_head, (query_low, key_all, value_all))
    context_low = context.astype(jnp.bfloat16)
    expand_in = jnp.dot(
        norm_two_low, expand_full, preferred_element_type=jnp.float32
    ) + expand_bias.astype(jnp.float32)
    activation_low = jax.nn.gelu(expand_in, approximate=False).astype(jnp.bfloat16)
    branch_part = jnp.einsum(
        "hte,hed->td", context_low, output_full, preferred_element_type=jnp.float32
    )
    branch_part = branch_part + jnp.dot(
        activation_low, shrink_full, preferred_element_type=jnp.float32
    )
    branch = lax.psum(branch_part, "tensor")
    layer_output = (
        hidden_in + branch + output_bias.astype(jnp.float32) + shrink_bias.astype(jnp.float32)
    ).astype(jnp.bfloat16)[None]
    heads_back, output_back, expand_back, shrink_back = (
        lax.all_gather(heads_weight, "fsdp", axis=0, tiled=True),
        lax.all_gather(output_weight, "fsdp", axis=2, tiled=True),
        lax.all_gather(expand_weight, "fsdp", axis=0, tiled=True),
        lax.all_gather(shrink_weight, "fsdp", axis=1, tiled=True),
    )
    key_back, value_back = (
        lax.all_gather(key_low, "fsdp", axis=1, tiled=True),
        lax.all_gather(value_low, "fsdp", axis=1, tiled=True),
    )
    grad_out = cotangent[0]
    grad_float = grad_out.astype(jnp.float32)
    output_weight_grad = jnp.einsum(
        "hte,td->hed", context_low, grad_out, preferred_element_type=jnp.float32
    )
    shrink_weight_grad = contract_first(activation_low, grad_out)
    bias_total = jnp.sum(grad_float, 0)
    context_grad = jnp.einsum(
        "td,hed->hte", grad_out, output_back, preferred_element_type=jnp.float32
    ).astype(jnp.bfloat16)
    activation_grad = contract_last(grad_out, shrink_back)
    _, gelu_back = jax.vjp(lambda inner_val: jax.nn.gelu(inner_val, approximate=False), expand_in)
    expand_grad = gelu_back(activation_grad)[0].astype(jnp.bfloat16)
    expand_weight_grad = contract_first(norm_two_low, expand_grad)
    expand_bias_grad = jnp.sum(expand_grad.astype(jnp.float32), 0)
    norm_two_grad = contract_last(expand_grad, expand_back)

    def attend_back(operands):
        query_head, key_head, value_head, context_head = operands
        probability = softmax_rows(contract_last(query_head, key_head) * score_scale, allowed)
        prob_low = probability.astype(jnp.bfloat16)
        weight_grad = contract_last(context_head, value_head)
        row_inner = jnp.sum(probability * weight_grad, -1, keepdims=True)
        score_grad = (probability * (weight_grad - row_inner)).astype(jnp.bfloat16)
        query_grad = jnp.dot(score_grad, key_head, preferred_element_type=jnp.float32) * score_scale
        key_grad = contract_first(score_grad, query_head) * score_scale
        value_grad = contract_first(prob_low, context_head)
        return (query_grad, key_grad, value_grad)

    query_grad, key_grad_all, value_grad_all = lax.map(
        attend_back, (query_low, key_back, value_back, context_grad)
    )
    key_grad, value_grad = (
        lax.psum_scatter(key_grad_all, "fsdp", scatter_dimension=1, tiled=True),
        lax.psum_scatter(value_grad_all, "fsdp", scatter_dimension=1, tiled=True),
    )
    _, rotate_back = jax.vjp(lambda inner_val: rotate(inner_val, cosine, sine_part), query_pre)
    projected_grad = jnp.concatenate(
        [rotate_back(query_grad)[0], rotate_back(key_grad)[0], value_grad], -1
    ).astype(jnp.bfloat16)
    heads_weight_grad = jnp.einsum(
        "td,hte->dhe", norm_one_low, projected_grad, preferred_element_type=jnp.float32
    )
    heads_bias_grad = jnp.sum(projected_grad.astype(jnp.float32), 1)
    norm_one_grad = jnp.einsum(
        "hte,dhe->td", projected_grad, heads_back, preferred_element_type=jnp.float32
    )
    norm_one_grad, norm_two_grad = lax.psum((norm_one_grad, norm_two_grad), "tensor")
    _, first_back = jax.vjp(layer_norm, hidden_in, gain_one, shift_one)
    input_first, first_gain_grad, first_bias_grad = first_back(norm_one_grad)
    _, second_back = jax.vjp(layer_norm, hidden_in, gain_two, shift_two)
    input_second, second_gain_grad, second_bias_grad = second_back(norm_two_grad)
    input_grad = (grad_float + input_first + input_second)[None]
    small_sums = lax.psum(
        (
            first_gain_grad,
            first_bias_grad,
            second_gain_grad,
            second_bias_grad,
            bias_total,
            expand_bias_grad,
            heads_bias_grad,
        ),
        ("replica", "fsdp"),
    )
    shard_parts = (
        lax.psum_scatter(heads_weight_grad, "fsdp", scatter_dimension=0, tiled=True),
        lax.psum_scatter(output_weight_grad, "fsdp", scatter_dimension=2, tiled=True),
        lax.psum_scatter(expand_weight_grad, "fsdp", scatter_dimension=0, tiled=True),
        lax.psum_scatter(shrink_weight_grad, "fsdp", scatter_dimension=1, tiled=True),
    )
    reduced = lax.psum((shard_parts[0], shard_parts[1], shard_parts[2], shard_parts[3]), "replica")
    return (
        layer_output,
        input_grad,
        small_sums[0],
        small_sums[1],
        small_sums[2],
        small_sums[3],
        reduced[0],
        small_sums[6],
        reduced[1],
        small_sums[4],
        reduced[2],
        small_sums[5],
        reduced[3],
        small_sums[4],
    )


def solution(mesh):
    placed = (
        P("replica", "fsdp", None),
        P("replica", None),
        P(),
        P(),
        P(),
        P(),
        P("fsdp", "tensor", None),
        P("tensor", None),
        P("tensor", None, "fsdp"),
        P(),
        P("fsdp", "tensor"),
        P("tensor"),
        P("tensor", "fsdp"),
        P(),
        P("replica", "fsdp", None),
    )
    local = square_local if mesh.shape["fsdp"] == 4 and mesh.shape["replica"] == 2 and mesh.shape["tensor"] == 4 else ring_local
    return jax.shard_map(
        local,
        mesh=mesh,
        in_specs=placed,
        out_specs=(
            P("replica", "fsdp", None),
            P("replica", "fsdp", None),
            P(),
            P(),
            P(),
            P(),
            P("fsdp", "tensor", None),
            P("tensor", None),
            P("tensor", None, "fsdp"),
            P(),
            P("fsdp", "tensor"),
            P("tensor"),
            P("tensor", "fsdp"),
            P(),
        ),
        check_vma=False,
    )
```

```python
import functools
import math

import jax
import jax.numpy as jnp
from jax import lax
from jax.experimental import pallas as pl
from jax.experimental.pallas import tpu as pltpu
from jax.sharding import PartitionSpec as P

ROT = 64


NORM_EPS = 1e-05
MASKED = -1e30


def layer_norm(values_in, gain_vec, shift_vec):
    average = jnp.mean(values_in, -1, keepdims=True)
    centred = values_in - average
    spread_sq = jnp.mean(centred * centred, -1, keepdims=True)
    return centred * lax.rsqrt(spread_sq + NORM_EPS) * gain_vec + shift_vec


def rotate(values_in, cosine, sine_part):
    rot_width = cosine.shape[-1]
    half_width = rot_width // 2
    turning = values_in[..., :rot_width]
    swapped = jnp.concatenate([-turning[..., half_width:], turning[..., :half_width]], -1)
    return jnp.concatenate([turning * cosine + swapped * sine_part, values_in[..., rot_width:]], -1)


def rotary_tables(positions, rot_width):
    frequency = jnp.power(10000.0, -jnp.arange(0, rot_width, 2, dtype=jnp.float32) / rot_width)
    angle_half = positions.astype(jnp.float32)[:, None] * frequency[None, :]
    angles = jnp.concatenate([angle_half, angle_half], -1)
    return (jnp.cos(angles), jnp.sin(angles))


def contract_last(left_op, right_op):
    return lax.dot_general(
        left_op, right_op, (((1,), (1,)), ((), ())), preferred_element_type=jnp.float32
    )


def contract_first(left_op, right_op):
    return lax.dot_general(
        left_op, right_op, (((0,), (0,)), ((), ())), preferred_element_type=jnp.float32
    )


def softmax_rows(scores, allowed):
    masked_scores = jnp.where(allowed, scores, MASKED)
    row_top = jnp.max(masked_scores, -1, keepdims=True)
    exponent = jnp.exp(masked_scores - row_top)
    return exponent / jnp.sum(exponent, -1, keepdims=True)


LOW = jnp.bfloat16
FULL = jnp.float32


MESH = pl.DeviceIdType.MESH
ANY = pl.BlockSpec(memory_space=pl.ANY)
IN_VMEM = pl.BlockSpec(memory_space=pltpu.VMEM)
VMEM_BYTES = 63 * 2**20
COPIES = 96


class Links:
    def __init__(self, send_sem, recv_sem, line=0):
        self.send_sem, self.recv_sem, self.sent, self.count = send_sem, recv_sem, [], 0
        self.r, self.f, self.t = (lax.axis_index(name) for name in ("replica", "fsdp", "tensor"))
        self.xb, self.yb = lax.rem(self.f, 2), lax.div(self.f, 2)
        self.x = (self.r, self.f + 1 - 2 * self.xb, self.t)
        self.y = (self.r, lax.rem(self.f + 2, 4), self.t)
        self.core = (1 - self.r, self.f, self.t)
        self.peers = [self.x, self.y, self.core]
        if line:
            self.line = line
            self.left, self.right, self.across = (
                (self.r, self.f, lax.rem(self.t + step, line)) for step in (line - 1, 1, 2)
            )
            self.pair = (self.r, self.f, self.t + 1 - 2 * lax.rem(self.t, 2))
            self.far = (self.r, 3 - self.f, self.t)
            self.mirror = (self.r, self.f, line - 1 - self.t)
            self.peers += [self.far, self.left, self.right, self.across]

    def meet(self):
        barrier = pltpu.get_barrier_semaphore()
        for peer in self.peers:
            pl.semaphore_signal(barrier, inc=1, device_id=peer, device_id_type=MESH)
        pl.semaphore_wait(barrier, len(self.peers))

    def prepare(self, source, target, peer):
        k = self.count
        self.count += 1
        return pltpu.make_async_remote_copy(
            src_ref=source,
            dst_ref=target,
            send_sem=self.send_sem.at[k],
            recv_sem=self.recv_sem.at[k],
            device_id=peer,
            device_id_type=MESH,
        )

    def send(self, source, target, peer):
        copy = self.prepare(source, target, peer)
        copy.start()
        self.sent.append(copy)
        return copy

    def end(self):
        for copy in self.sent:
            copy.wait_send()

    def block(self, i):
        bits = [(1 - bit) if i >> at & 1 else bit for at, bit in ((2, self.yb), (1, self.xb), (0, self.r))]
        return (bits[0] * 2 + bits[1]) * 2 + bits[2]


class Local:
    def __init__(self, sem):
        self.sem, self.count, self.open = sem, 0, []

    def start(self, source, target):
        copy = pltpu.make_async_copy(source, target, self.sem.at[self.count])
        self.count += 1
        copy.start()
        self.open.append(copy)
        return copy

    def wait(self, *copies):
        for copy in copies:
            copy.wait()
            self.open = [other for other in self.open if other is not copy]

    def end(self):
        self.wait(*list(self.open))


def at_rows(ref, start, size):
    return ref.at[pl.ds(start, size), :]


def at_columns(ref, start, size):
    return ref.at[:, pl.ds(start, size)]


class Gathered:
    def __init__(self, links, local, shard, full, cut, unit):
        self.links, self.local, self.full, self.cut = links, local, full, cut
        self.shard, self.unit, self.half = shard, unit, unit // 2
        self.copies = [
            local.start(self.mine(0, unit), self.at(0)),
            local.start(cut(shard, pl.multiple_of((1 - links.r) * unit, unit), unit), self.at(1)),
        ]
        self.from_x, self.from_y = {}, {}

    def mine(self, start, size):
        return self.cut(self.shard, pl.multiple_of(self.links.r * self.unit + start, self.half), size)

    def at(self, block, start=0, size=None):
        return self.cut(self.full, block * self.unit + start, self.unit if size is None else size)

    def to_x(self, lower):
        start = self.half if lower else 0
        source, target = self.mine(start, self.half), self.at(2, start, self.half)
        self.from_x[lower] = self.links.send(source, target, self.links.x)

    def to_y(self, lower):
        start = self.half if lower else 0
        source, target = self.mine(start, self.half), self.at(4, start, self.half)
        self.from_y[lower] = self.links.send(source, target, self.links.y)

    def first(self):
        self.to_x(False)
        self.to_y(True)

    def rest(self):
        self.to_x(True)
        self.to_y(False)

    def relay(self):
        half = self.half
        self.from_x[False].wait_recv()
        self.far_top = self.links.send(self.at(2, 0, half), self.at(6, 0, half), self.links.y)
        self.from_y[True].wait_recv()
        self.far_end = self.links.send(self.at(4, half, half), self.at(6, half, half), self.links.x)

    def share(self):
        self.from_y[False].wait_recv()
        self.core_y = self.links.send(self.at(4), self.at(5), self.links.core)
        self.from_x[True].wait_recv()
        self.core_x = self.links.send(self.at(2), self.at(3), self.links.core)

    def share_far(self):
        self.far_top.wait_recv()
        self.far_end.wait_recv()
        self.core_far = self.links.send(self.at(6), self.at(7), self.links.core)

    def whole(self):
        self.local.wait(*self.copies)
        for copy in (self.core_x, self.core_y, self.core_far):
            copy.wait_recv()


def tile_of(j, size):
    return pl.ds(pl.multiple_of(j * size, size), size)


def dot(left, right):
    return jnp.dot(left, right, preferred_element_type=FULL)


def spin(values_in, cosine, sine_one, sine_two):
    head = values_in[:, :128]
    turned_head = (
        head * cosine + pltpu.roll(head, 96, 1) * sine_one + pltpu.roll(head, 32, 1) * sine_two
    )
    return jnp.concatenate([turned_head, values_in[:, 128:]], -1)


def gather_kernel(
    score_scale,
    x_hbm, g_hbm, wh_hbm, wo_hbm, we_hbm, ws_hbm, raw, order,
    we, ws, wo_out, act_out, slope_out, n2t_out, up_out, ctx_out, red_heads, red_out, red_shrink, sums,
    vecs, cosine, sine_one, sine_two, wh, wo, xr, g, n1, n2, n1t, n2t, stat, qkv_away, qkv, dctx_away, dctx, ctxt, ctxt_away,
    pg, pg_away, kvg, kvg_away, kvg_got, got_heads, got_out, got_shrink, local_sem, tile_sem, send_sem, recv_sem,
):
    links, local = Links(send_sem, recv_sem), Local(local_sem)
    tokens, width = xr.shape
    hd = dctx.shape[1]
    unit = width // 8
    blocks = range(8)
    x_in, g_in = [], []
    for i in blocks:
        cols = pl.ds(pl.multiple_of(links.block(i) * unit, unit), unit)
        x_in.append(local.start(x_hbm.at[:, cols], xr.at[:, pl.ds(i * unit, unit)]))
        g_in.append(local.start(g_hbm.at[:, cols], g.at[:, pl.ds(i * unit, unit)]))
    links.meet()
    heads = Gathered(links, local, wh_hbm, wh, at_rows, unit)
    output = Gathered(links, local, wo_hbm, wo, at_columns, unit)
    expand = Gathered(links, local, we_hbm, we, at_rows, unit)
    shrink = Gathered(links, local, ws_hbm, ws, at_columns, unit)
    heads.first()
    heads.rest()

    for i in blocks:
        cols = pl.ds(pl.multiple_of(links.block(i) * unit, unit), unit)
        vecs[0:4, i * unit : (i + 1) * unit] = raw[0:4, cols]
    local.wait(*x_in)

    def norm_rows(c, carry):
        rows = tile_of(c, 64)
        value = xr[rows, :].astype(FULL)
        average = jnp.mean(value, -1, keepdims=True)
        centred = value - average
        inverse = lax.rsqrt(jnp.mean(centred * centred, -1, keepdims=True) + NORM_EPS)
        normal = centred * inverse
        stat[rows, :] = jnp.concatenate(
            [jnp.broadcast_to(average, (64, 128)), jnp.broadcast_to(inverse, (64, 128))], -1
        )
        n1[rows, :] = (normal * vecs[0:1, :] + vecs[1:2, :]).astype(LOW)
        n2[rows, :] = (normal * vecs[2:3, :] + vecs[3:4, :]).astype(LOW)
        return carry

    lax.fori_loop(0, tokens // 64, norm_rows, 0)
    bases = [
        order[0, (links.yb if step < 2 else 1 - links.yb) * 2 + (links.xb if step % 2 == 0 else 1 - links.xb)]
        * tokens
        for step in (0, 2, 1, 3)
    ]

    def table_rows(c, carry):
        rows = tile_of(c, 64)
        lane = lax.broadcasted_iota(jnp.int32, (64, 128), 1)
        row = lax.broadcasted_iota(jnp.int32, (64, 128), 0) + c * 64
        spot = row + jnp.where(row < tokens, bases[0], bases[1] - tokens)
        pace = jnp.exp(lax.rem(lane, ROT // 2).astype(FULL) * (-2.0 / ROT * math.log(10000.0)))
        angle = spot.astype(FULL) * pace
        sine = jnp.sin(angle)
        cosine[rows, :] = jnp.where(lane < ROT, jnp.cos(angle), 1.0)
        sine_one[rows, :] = jnp.where(lane < ROT // 2, -sine, 0.0)
        sine_two[rows, :] = jnp.where(jnp.logical_and(lane >= ROT // 2, lane < ROT), sine, 0.0)
        return carry

    lax.fori_loop(0, 2 * tokens // 64, table_rows, 0)
    heads.relay()
    output.first()
    output.rest()

    def turn_tiles(j, carry):
        cols = tile_of(j, unit)
        n1t[cols, :] = n1[:, cols].T
        n2t[cols, :] = n2[:, cols].T
        return carry

    lax.fori_loop(0, 8, turn_tiles, 0)
    local.start(n2t, n2t_out)
    sums[...] = jnp.zeros_like(sums)
    local.wait(*g_in)
    for i in blocks:
        cols = pl.ds(pl.multiple_of(links.block(i) * unit, unit), unit)
        sums[4:5, cols] = jnp.sum(g[:, i * unit : (i + 1) * unit].astype(FULL), 0, keepdims=True)
    heads.share()
    heads.share_far()
    heads.whole()
    output.relay()

    own, away = links.yb * 3 * hd, (1 - links.yb) * 3 * hd

    def project(start, target):
        def one(c, carry):
            cols = pl.ds(pl.multiple_of(start + c * hd, hd), hd)
            value = dot(n1[...], wh[:, cols]) + raw[5:6, cols]
            spun = spin(value, cosine[:tokens, :], sine_one[:tokens, :], sine_two[:tokens, :])
            target[c, :tokens, :] = jnp.where(c < 2, spun, value).astype(LOW)
            return carry

        lax.fori_loop(0, 3, one, 0)

    project(away, qkv_away)
    qkv_from_y = links.send(qkv_away, qkv.at[:, pl.ds(tokens, tokens), :], links.y)
    project(own, qkv)
    kv_from_x = links.send(
        qkv.at[pl.ds(1, 2), pl.ds(0, tokens), :], qkv.at[pl.ds(1, 2), pl.ds(2 * tokens, tokens), :], links.x
    )
    expand.first()
    output.share()
    output.share_far()
    output.whole()
    local.start(wo, wo_out)
    rows_own = pl.ds(pl.multiple_of(links.yb * hd, hd), hd)
    rows_away = pl.ds(pl.multiple_of((1 - links.yb) * hd, hd), hd)
    dctx_away[...] = contract_last(g[...], wo[rows_away, :]).astype(LOW)
    dctx_from_y = links.send(dctx_away, dctx.at[pl.ds(tokens, tokens), :], links.y)
    dctx[:tokens, :] = contract_last(g[...], wo[rows_own, :]).astype(LOW)

    qkv_from_y.wait_recv()
    kv_from_far = links.send(
        qkv.at[pl.ds(1, 2), pl.ds(tokens, tokens), :],
        qkv.at[pl.ds(1, 2), pl.ds(3 * tokens, tokens), :],
        links.x,
    )
    expand.relay()
    expand.to_y(False)
    dctx_from_y.wait_recv()
    kv_from_x.wait_recv()
    kv_from_far.wait_recv()

    def attention(kt, vt, dk, dv, prob, wgt, prob_low, grad_low):
        keys = qkv.shape[1]
        step = tokens
        lag = lax.broadcasted_iota(jnp.int32, (step, hd), 0) - lax.broadcasted_iota(jnp.int32, (step, hd), 1)
        parts = [pl.ds(i * step, step) for i in range(keys // step)]
        for part in parts:
            kt[:, part] = qkv[1, part, :].T
            vt[:, part] = qkv[2, part, :].T
        dk[...] = jnp.zeros_like(dk)
        dv[...] = jnp.zeros_like(dv)

        def one(b, carry):
            rows = tile_of(b, hd)
            query, grad = qkv[0, rows, :], dctx[rows, :]
            ahead = jnp.where(b < tokens // hd, bases[0], bases[1] - tokens) + b * hd
            top = jnp.full((1, hd), MASKED, FULL)
            for i, part in enumerate(parts):
                scores = contract_last(qkv[1, part, :], query) * score_scale
                scores = jnp.where(lag <= ahead - bases[i], scores, MASKED)
                prob[part, :] = scores
                top = jnp.maximum(top, jnp.max(scores, 0, keepdims=True))
            total = jnp.zeros((1, hd), FULL)
            for part in parts:
                exponent = jnp.exp(prob[part, :] - top)
                prob[part, :] = exponent
                total = total + jnp.sum(exponent, 0, keepdims=True)
            share = 1.0 / total
            inner = jnp.zeros((1, hd), FULL)
            for part in parts:
                weight = contract_last(qkv[2, part, :], grad)
                chance = prob[part, :] * share
                prob[part, :] = chance
                prob_low[part, :] = chance.astype(LOW)
                wgt[part, :] = weight
                inner = inner + jnp.sum(chance * weight, 0, keepdims=True)
            for part in parts:
                grad_low[part, :] = (prob[part, :] * (wgt[part, :] - inner)).astype(LOW)
            context = dot(vt[...], prob_low[...]).astype(LOW)
            query_grad = dot(kt[...], grad_low[...]) * score_scale
            for part in parts:
                dv[part, :] += dot(prob_low[part, :], grad)
                dk[part, :] += dot(grad_low[part, :], query)
            turned_grad = spin(query_grad.T, cosine[rows, :], -sine_one[rows, :], -sine_two[rows, :]).astype(LOW)
            return context, turned_grad

        def here(b, carry):
            context, turned_grad = one(b, carry)
            rows = tile_of(b, hd)
            ctxt[rows_own, rows] = context
            pg[rows, pl.ds(pl.multiple_of(own, hd), hd)] = turned_grad
            return carry

        def there(b, carry):
            context, turned_grad = one(b + tokens // hd, carry)
            rows = tile_of(b, hd)
            ctxt_away[:, rows] = context
            pg_away[rows, :hd] = turned_grad
            return carry

        lax.fori_loop(0, tokens // hd, there, 0)
        lax.fori_loop(0, tokens // hd, here, 0)
        for i, total in enumerate((dk, dv)):
            kvg_away[i, :, :] = total[2 * tokens :, :].astype(LOW)
            kvg[i, :, :] = total[: 2 * tokens, :]

    keys = qkv.shape[1]
    pl.run_scoped(
        attention,
        pltpu.VMEM((hd, keys), LOW),
        pltpu.VMEM((hd, keys), LOW),
        pltpu.VMEM((keys, hd), FULL),
        pltpu.VMEM((keys, hd), FULL),
        pltpu.VMEM((keys, hd), FULL),
        pltpu.VMEM((keys, hd), FULL),
        pltpu.VMEM((keys, hd), LOW),
        pltpu.VMEM((keys, hd), LOW),
    )
    ctx_from_y = links.send(ctxt_away, ctxt.at[rows_own, :], links.y)
    kvg_from_x = links.send(kvg_away, kvg_got, links.x)
    expand.to_x(True)
    shrink.first()

    def rest(tiles, slope, actt, send_heads, send_out, send_shrink):
        act = n1

        def load(j):
            return pltpu.make_async_copy(
                we.at[:, tile_of(j, unit)], tiles.at[lax.rem(j, 2)], tile_sem.at[lax.rem(j, 2)]
            )

        def forward(j, carry):
            @pl.when(j < 7)
            def _():
                load(j + 1).start()

            load(j).wait()
            cols = tile_of(j, unit)
            value = dot(n2[...], tiles[lax.rem(j, 2)]) + raw[4:5, cols]
            normal_share = 0.5 * (1.0 + lax.erf(value * (0.5**0.5)))
            low_act = (value * normal_share).astype(LOW)
            act[:, cols] = low_act
            actt[cols, :] = low_act.T
            density = jnp.exp(value * value * -0.5) * 0.3989422804014327
            slope[:, cols] = (normal_share + value * density).astype(LOW)
            return carry

        def shrink_block(i, target, extra):
            def one(c, carry):
                rows = tile_of(c, 512)
                part = dot(actt[rows, :], g[:, i * unit : (i + 1) * unit])
                if extra is not None:
                    part = part + extra[rows, :].astype(FULL)
                target[rows, :] = part.astype(LOW)
                return carry

            lax.fori_loop(0, actt.shape[0] // 512, one, 0)

        shrink_got, out_got, heads_got = [], [], []
        ctx_from_y.wait_recv()
        local.start(ctxt, ctx_out)
        for k in range(4):
            i = 2 * k + 1
            send_out[k, :, :] = dot(ctxt[...], g[:, i * unit : (i + 1) * unit]).astype(LOW)
            out_got.append(links.send(send_out.at[k], got_out.at[k], links.core))

        kvg_from_x.wait_recv()
        for i in range(2):
            for away_rows, target in ((True, pg_away), (False, pg)):
                rows = pl.ds(tokens if away_rows else 0, tokens)
                total = kvg[i, rows, :] + kvg_got[i, rows, :].astype(FULL)
                if i == 0:
                    total = spin(total * score_scale, cosine[rows, :], -sine_one[rows, :], -sine_two[rows, :])
                start = (0 if away_rows else own) + (1 + i) * hd
                target[:, pl.ds(pl.multiple_of(start, hd), hd)] = total.astype(LOW)
        pg_from_y = links.send(pg_away, pg.at[:, pl.ds(pl.multiple_of(own, 3 * hd), 3 * hd)], links.y)
        shrink.rest()
        for k in range(4):
            out_got[k].wait_recv()
            total = dot(ctxt[...], g[:, 2 * k * unit : (2 * k + 1) * unit])
            got_out[k, :, :] = (total + got_out[k, :, :].astype(FULL)).astype(LOW)
            local.start(got_out.at[k], red_out.at[k])
        expand.share_far()
        expand.share()
        expand.whole()
        load(0).start()
        lax.fori_loop(0, 4, forward, 0)
        shrink.relay()
        lax.fori_loop(4, 8, forward, 0)
        local.start(act, act_out)
        local.start(slope, slope_out)
        for k in range(4):
            shrink_block(2 * k + 1, send_shrink.at[k], None)
            shrink_got.append(links.send(send_shrink.at[k], got_shrink.at[k], links.core))
        pg_from_y.wait_recv()
        for k in range(4):
            rows = pl.ds((2 * k + 1) * unit, unit)
            send_heads[k, :, :] = dot(n1t[rows, :], pg[...]).astype(LOW)
            heads_got.append(links.send(send_heads.at[k], got_heads.at[k], links.core))
        shrink.share()
        for k in range(4):
            shrink_got[k].wait_recv()
            shrink_block(2 * k, got_shrink.at[k], got_shrink.at[k])
            local.start(got_shrink.at[k], red_shrink.at[k])

        up = n2
        for i in blocks:
            cols = slice(i * unit, (i + 1) * unit)
            grad = contract_last(pg[...], wh[cols, :])
            normal = (xr[:, cols].astype(FULL) - stat[:, 0:1]) * stat[:, 128:129]
            place = pl.ds(pl.multiple_of(links.block(i) * unit, unit), unit)
            sums[0:1, place] = jnp.sum(grad * normal, 0, keepdims=True)
            sums[1:2, place] = jnp.sum(grad, 0, keepdims=True)
            up[:, cols] = (grad * vecs[0:1, cols]).astype(LOW)
        local.start(up, up_out)
        sums[6:7, : pg.shape[1]] = jnp.sum(pg[...].astype(FULL), 0, keepdims=True)
        for k in range(4):
            heads_got[k].wait_recv()
            total = dot(n1t[2 * k * unit : (2 * k + 1) * unit, :], pg[...])
            got_heads[k, :, :] = (total + got_heads[k, :, :].astype(FULL)).astype(LOW)
            local.start(got_heads.at[k], red_heads.at[k])
        shrink.share_far()
        shrink.whole()
        links.end()
        local.end()

    pl.run_scoped(
        rest,
        pltpu.VMEM((2, width, unit), LOW),
        pltpu.VMEM(n2.shape, LOW),
        pltpu.VMEM((we.shape[1], tokens), LOW),
        pltpu.VMEM(got_heads.shape, LOW),
        pltpu.VMEM(got_out.shape, LOW),
        pltpu.VMEM(got_shrink.shape, LOW),
    )


def gather_call(x, g, heads_rows, output_rows, expand_weight, shrink_weight, raw, order):
    tokens, width = x.shape
    heads_wide, out_wide, units = heads_rows.shape[1], output_rows.shape[0], expand_weight.shape[1]
    hd = heads_wide // 6
    keys = 4 * tokens
    unit = width // 8
    low = lambda *shape: jax.ShapeDtypeStruct(shape, LOW)
    outs = [
        low(width, units),
        low(units, width),
        low(out_wide, width),
        low(tokens, units),
        low(tokens, units),
        low(width, tokens),
        low(tokens, width),
        low(out_wide, tokens),
        low(4, unit, heads_wide),
        low(4, out_wide, unit),
        low(4, units, unit),
        jax.ShapeDtypeStruct((8, width), FULL),
    ]
    vm = lambda *shape: pltpu.VMEM(shape, LOW)
    scratch = [
        pltpu.VMEM((4, width), FULL),
        *[pltpu.VMEM((2 * tokens, 128), FULL)] * 3,
        vm(width, heads_wide),
        vm(out_wide, width),
        vm(tokens, width),
        vm(tokens, width),
        vm(tokens, width),
        vm(tokens, width),
        vm(width, tokens),
        vm(width, tokens),
        pltpu.VMEM((tokens, 256), FULL),
        vm(3, tokens, hd),
        vm(3, keys, hd),
        vm(tokens, hd),
        vm(2 * tokens, hd),
        vm(out_wide, tokens),
        vm(hd, tokens),
        vm(tokens, heads_wide),
        vm(tokens, 3 * hd),
        pltpu.VMEM((2, 2 * tokens, hd), FULL),
        vm(2, 2 * tokens, hd),
        vm(2, 2 * tokens, hd),
        vm(4, unit, heads_wide),
        vm(4, out_wide, unit),
        vm(4, units, unit),
        pltpu.SemaphoreType.DMA((64,)),
        pltpu.SemaphoreType.DMA((2,)),
        pltpu.SemaphoreType.DMA((COPIES,)),
        pltpu.SemaphoreType.DMA((COPIES,)),
    ]
    return pl.pallas_call(
        functools.partial(gather_kernel, hd**-0.5),
        out_shape=outs,
        in_specs=[ANY] * 6 + [IN_VMEM, pl.BlockSpec(memory_space=pltpu.SMEM)],
        out_specs=[ANY] * 11 + [IN_VMEM],
        scratch_shapes=scratch,
        compiler_params=pltpu.CompilerParams(
            collective_id=0, has_side_effects=True, vmem_limit_bytes=VMEM_BYTES
        ),
    )(x, g, heads_rows, output_rows, expand_weight, shrink_weight, raw, order)


class Scattered:
    def __init__(self, links, local, block, cut, unit, via, got, stage, own, loaded):
        self.links, self.local, self.block, self.cut, self.unit = links, local, block, cut, unit
        self.via, self.got, self.stage, self.own = via, got, stage, own
        self.half = unit // 2
        if loaded:
            self.loads = [
                local.start(cut(block(1), self.half, self.half), stage.at[0]),
                local.start(cut(block(2), 0, self.half), stage.at[1]),
                local.start(block(0), own),
            ]

    def first(self):
        half, cut, far = self.half, self.cut, self.block(3)
        self.via_x = self.links.send(cut(far, 0, half), self.via.at[0], self.links.x)
        self.via_y = self.links.send(cut(far, half, half), self.via.at[1], self.links.y)

    def direct(self):
        half, cut = self.half, self.cut
        self.x_top = self.links.send(cut(self.block(1), 0, half), cut(self.got.at[0], 0, half), self.links.x)
        self.y_end = self.links.send(cut(self.block(2), half, half), cut(self.got.at[1], half, half), self.links.y)

    def second(self):
        half, cut = self.half, self.cut
        self.local.wait(*self.loads[:2])
        self.via_x.wait_recv()
        add_rows(self.stage.at[1], self.stage.at[1], self.via.at[0])
        self.y_top = self.links.send(self.stage.at[1], cut(self.got.at[1], 0, half), self.links.y)
        self.via_y.wait_recv()
        add_rows(self.stage.at[0], self.stage.at[0], self.via.at[1])
        self.x_end = self.links.send(self.stage.at[0], cut(self.got.at[0], half, half), self.links.x)

    def third(self, total, place):
        for copy in (self.x_top, self.x_end, self.y_top, self.y_end):
            copy.wait_recv()
        self.local.wait(self.loads[2])
        add_rows(total, self.own, self.got.at[0], self.got.at[1])
        self.kept = self.local.start(total, place)
        self.other = self.links.send(total, place, self.links.core)


def add_rows(target, *parts):
    rows, wide = target.shape
    step = min(rows, 32 if wide > 512 else 256)

    def one(c, carry):
        at = pl.ds(pl.multiple_of(c * step, step), step)
        total = parts[0][at, :].astype(FULL)
        for part in parts[1:]:
            total = total + part[at, :].astype(FULL)
        target[at, :] = total.astype(target.dtype)
        return carry

    lax.fori_loop(0, rows // step, one, 0)


class Line:
    def __init__(self, links, part, got, final, finish):
        self.links, self.part, self.got, self.final, self.finish = links, part, got, final, finish
        self.step = part.shape[0] // CHUNKS
        self.outer = jnp.logical_or(links.t == 0, links.t == links.line - 1)
        self.middle = jnp.logical_not(self.outer)
        self.inward = [self.make(c, part, final, links.pair) for c in range(CHUNKS)]
        self.across = [self.make(c, part, got, links.mirror) for c in range(CHUNKS)]
        self.outward = [self.make(c, final, final, links.pair) for c in range(CHUNKS)]

    def rows(self, c):
        return pl.ds(c * self.step, self.step)

    def make(self, c, source, target, peer):
        return self.links.prepare(source.at[self.rows(c), :], target.at[self.rows(c), :], peer)

    def start(self):
        @pl.when(self.outer)
        def _():
            for copy in self.inward:
                copy.start()

    def first(self, c):
        @pl.when(self.middle)
        def _():
            self.inward[c].wait_recv()
            rows = self.rows(c)
            add_rows(self.part.at[rows, :], self.part.at[rows, :], self.final.at[rows, :])
            self.across[c].start()

    def second(self, c):
        @pl.when(self.middle)
        def _():
            self.across[c].wait_recv()
            self.finish(self.rows(c))
            self.outward[c].start()

    def third(self, c):
        @pl.when(self.outer)
        def _():
            self.outward[c].wait_recv()

    def end(self):
        @pl.when(self.outer)
        def _():
            for copy in self.inward:
                copy.wait_send()

        @pl.when(self.middle)
        def _():
            for copy in self.across + self.outward:
                copy.wait_send()


CHUNKS = 8


def scatter_kernel(
    line_size,
    we_hbm, ws_hbm, wo_hbm, act_hbm, slope_hbm, n2t_hbm, up_hbm, ctxt_hbm, red_heads, red_out, red_shrink, x_hbm, g_hbm,
    raw, sums_in,
    layer_out, input_grad, heads_grad, output_grad, expand_grad, shrink_grad, got_expand, sums_out,
    ws, we, wo, act, slope, n2t, up, ctxt, g, part_branch, final_branch, final_up, got_branch, got_up,
    via_h, got_h, stage_h, own_h, via_o, got_o, stage_o, own_o, via_s, got_s, stage_s, own_s, via_e, got_e,
    total_rows, total_columns, total_out, grad_rows, vecs, sums, sums_got, local_sem, send_sem, recv_sem,
):
    links, local = Links(send_sem, recv_sem, line_size), Local(local_sem)
    tokens, width = g.shape
    unit = width // 8
    blocks = range(8)
    place = [pl.ds(pl.multiple_of(links.block(i) * unit, unit), unit) for i in blocks]

    def here(i):
        return pl.ds(i * unit, unit)

    first_loads = [local.start(ws_hbm, ws), local.start(act_hbm, act), local.start(ctxt_hbm, ctxt), local.start(wo_hbm, wo)]
    g_loads = [local.start(g_hbm.at[:, place[i]], g.at[:, here(i)]) for i in blocks]
    slope_load = local.start(slope_hbm, slope)
    we_load, up_load, n2t_load = local.start(we_hbm, we), local.start(up_hbm, up), local.start(n2t_hbm, n2t)
    links.meet()

    shrink = Scattered(links, local, lambda k: red_shrink.at[k], at_columns, unit, via_s, got_s, stage_s, own_s, True)
    heads = Scattered(links, local, lambda k: red_heads.at[k], at_rows, unit, via_h, got_h, stage_h, own_h, True)
    output = Scattered(links, local, lambda k: red_out.at[k], at_columns, unit, via_o, got_o, stage_o, own_o, True)
    shrink.first()
    heads.first()
    output.first()

    local.wait(*first_loads)
    context = ctxt[...].T
    for i in blocks:
        vecs[0:1, here(i)] = raw[2:3, place[i]]
        vecs[1:2, here(i)] = raw[6:7, place[i]]

    def branch_tile(j, carry):
        cols = tile_of(j, unit)
        part_branch[:, cols] = (dot(context, wo[:, cols]) + dot(act[...], ws[:, cols])).astype(LOW)
        return carry

    lax.fori_loop(0, 8, branch_tile, 0)
    x = act
    x_loads = [local.start(x_hbm.at[:, place[i]], x.at[:, here(i)]) for i in blocks]

    def finish_branch(rows):
        def one(c, carry):
            at = pl.ds(pl.multiple_of(rows.start + c * 16, 16), 16)
            total = part_branch[at, :].astype(FULL) + got_branch[at, :].astype(FULL)
            final_branch[at, :] = (x[at, :].astype(FULL) + total + vecs[1:2, :]).astype(LOW)
            return carry

        lax.fori_loop(0, rows.size // 16, one, 0)

    def finish_up(rows):
        add_rows(final_up.at[rows, :], up.at[rows, :], got_up.at[rows, :])

    line_branch = Line(links, part_branch, got_branch, final_branch, finish_branch)
    line_up = Line(links, up, got_up, final_up, finish_up)
    line_branch.start()

    local.wait(*g_loads, slope_load)
    sums[0, :, :] = sums_in[...]

    def hidden_tile(j, carry):
        cols = tile_of(j, unit)
        grad = (contract_last(g[...], ws[cols, :]) * slope[:, cols].astype(FULL)).astype(LOW)
        slope[:, cols] = grad
        sums[0, 5:6, cols] = jnp.sum(grad.astype(FULL), 0, keepdims=True)
        return carry

    lax.fori_loop(0, 8, hidden_tile, 0)
    local.wait(*x_loads, we_load, up_load, n2t_load)
    shrink.direct()
    heads.direct()
    output.direct()

    def up_block(i):
        cols = here(i)
        grad = contract_last(slope[...], we[i * unit : (i + 1) * unit, :])
        value = x[:, cols].astype(FULL)
        normal = (value - average) * inverse
        sums[0, 2:3, place[i]] = jnp.sum(grad * normal, 0, keepdims=True)
        sums[0, 3:4, place[i]] = jnp.sum(grad, 0, keepdims=True)
        up[:, cols] = (up[:, cols].astype(FULL) + grad * vecs[0:1, cols]).astype(LOW)

    total = jnp.zeros((tokens, 1), FULL)
    for i in blocks:
        total = total + jnp.sum(x[:, here(i)].astype(FULL), -1, keepdims=True)
    average = total * (1.0 / width)
    total = jnp.zeros((tokens, 1), FULL)
    for i in blocks:
        centred = x[:, here(i)].astype(FULL) - average
        total = total + jnp.sum(centred * centred, -1, keepdims=True)
    inverse = lax.rsqrt(total * (1.0 / width) + NORM_EPS)

    steps = [(line, c) for line in (line_branch, line_up) for c in range(CHUNKS)]
    out_copies = []
    rows_out = grad_rows.shape[1]

    def input_rows(c):
        slot = len(out_copies) % 2
        if len(out_copies) >= 2:
            local.wait(*out_copies[-2])
        rows = pl.ds(c * rows_out, rows_out)
        value = x[rows, :].astype(FULL)
        centred = value - jnp.mean(value, -1, keepdims=True)
        scale = lax.rsqrt(jnp.mean(centred * centred, -1, keepdims=True) + NORM_EPS)
        normal = centred * scale
        upstream = final_up[rows, :].astype(FULL)
        inner = upstream - jnp.mean(upstream, -1, keepdims=True)
        inner = inner - normal * jnp.mean(upstream * normal, -1, keepdims=True)
        grad_rows[slot, :, :] = g[rows, :].astype(FULL) + inner * scale
        out_copies.append(
            [local.start(grad_rows.at[slot, :, here(i)], input_grad.at[rows, place[i]]) for i in blocks]
        )

    def serve(count):
        for _ in range(count):
            at = serve.done
            if at < len(steps):
                steps[at][0].first(steps[at][1])
            if 2 <= at < len(steps) + 2:
                steps[at - 2][0].second(steps[at - 2][1])
            if at >= 4:
                line, c = steps[at - 4]
                line.third(c)
                if line is line_up:
                    for part in range(line.step // rows_out):
                        input_rows(c * (line.step // rows_out) + part)
            serve.done += 1

    serve.done = 0
    for i in range(4):
        up_block(i)
    serve(1)
    for i in range(4, 8):
        up_block(i)
    line_up.start()
    serve(1)

    def share(s, peers):
        return [links.send(sums.at[s], sums_got.at[4 * s + k], peer) for k, peer in enumerate(peers)]

    def shared(s, copies):
        for copy in copies:
            copy.wait_recv()
        total = sums[s, :, :] + sums_got[4 * s, :, :]
        if len(copies) > 1:
            total = total + (sums_got[4 * s + 1, :, :] + sums_got[4 * s + 2, :, :])
        sums[s + 1, :, :] = total

    first_share = share(0, [links.core])
    shrink.second()
    heads.second()
    output.second()
    serve(1)
    shared(0, first_share)
    second_share = share(1, [links.x, links.y, links.far])

    expand_got = []

    def expand_block(i, target):
        def one(c, carry):
            cols = tile_of(c, 512)
            part = dot(n2t[i * unit : (i + 1) * unit, :], slope[:, cols])
            if target is we:
                part = part + target[(i // 2) * unit : (i // 2 + 1) * unit, cols].astype(FULL)
            target[(i // 2) * unit : (i // 2 + 1) * unit, cols] = part.astype(LOW)
            return carry

        lax.fori_loop(0, slope.shape[1] // 512, one, 0)

    for k in (3, 1, 2, 0):
        expand_block(2 * k + 1, ws)
        rows = pl.ds(k * unit, unit)
        expand_got.append((k, links.send(ws.at[rows, :], got_expand.at[k], links.core)))
        if k in (1, 0):
            serve(1)
    expand = Scattered(
        links, local, lambda k: we.at[pl.ds(k * unit, unit), :], at_rows, unit, via_e, got_e, None, None, False
    )
    loads = []
    for k, copy in expand_got:
        copy.wait_recv()
        loads.append(local.start(got_expand.at[k], we.at[pl.ds(k * unit, unit), :]))
    for (k, copy), load in zip(expand_got, loads):
        local.wait(load)
        expand_block(2 * k, we)
        if k == 3:
            expand.first()
        if k == 1:
            serve(1)
    expand.direct()
    serve(4)
    shared(1, second_share)
    third_share = share(2, [links.pair, links.across, links.mirror])
    half_rows = pl.ds(pl.multiple_of(links.r * unit, unit), unit)
    output.third(total_out, output_grad.at[:, half_rows])
    heads.third(total_rows.at[:, pl.ds(0, own_h.shape[1])], heads_grad.at[half_rows, :])
    shrink.third(total_columns, shrink_grad.at[:, half_rows])
    serve(2)

    expand.via_x.wait_recv()
    top, end = pl.ds(2 * unit, unit // 2), pl.ds(unit + unit // 2, unit // 2)
    add_rows(we.at[top, :], we.at[top, :], via_e.at[0])
    expand.y_top = links.send(we.at[top, :], got_e.at[1, pl.ds(0, unit // 2), :], links.y)
    expand.via_y.wait_recv()
    add_rows(we.at[end, :], we.at[end, :], via_e.at[1])
    expand.x_end = links.send(we.at[end, :], got_e.at[0, pl.ds(unit // 2, unit // 2), :], links.x)
    serve(2)
    for i in blocks:
        local.start(final_branch.at[:, here(i)], layer_out.at[:, place[i]])
    serve(len(steps) + 4 - serve.done)
    shared(2, third_share)
    sums_out[0:4, :] = sums[3, 0:4, :]
    sums_out[4:8, :] = sums[2, 4:8, :]

    for copy in (expand.x_top, expand.x_end, expand.y_top, expand.y_end):
        copy.wait_recv()
    heads.other.wait_send()
    local.wait(heads.kept)
    add_rows(total_rows, we.at[pl.ds(0, unit), :], got_e.at[0], got_e.at[1])
    spot = expand_grad.at[pl.ds(pl.multiple_of(links.r * unit, unit), unit), :]
    local.start(total_rows, spot)
    last = links.send(total_rows, spot, links.core)
    for copy in (shrink.other, output.other, heads.other, last):
        copy.wait_recv()
    links.sent = [copy for copy in links.sent if copy is not heads.other]
    links.end()
    line_branch.end()
    line_up.end()
    local.end()


def scatter_call(line_size, arrays, x, g, raw, sums):
    tokens, width = x.shape
    expand_full, shrink_full, output_full, act, slope, n2t, up, ctxt, red_heads, red_out, red_shrink = arrays
    unit = width // 8
    units, heads_wide, out_wide = act.shape[1], red_heads.shape[2], ctxt.shape[0]
    low = lambda *shape: pltpu.VMEM(shape, LOW)
    full = lambda *shape: pltpu.VMEM(shape, FULL)
    half = unit // 2
    outs = [
        jax.ShapeDtypeStruct((tokens, width), LOW),
        jax.ShapeDtypeStruct((tokens, width), FULL),
        jax.ShapeDtypeStruct((2 * unit, heads_wide), FULL),
        jax.ShapeDtypeStruct((out_wide, 2 * unit), FULL),
        jax.ShapeDtypeStruct((2 * unit, units), FULL),
        jax.ShapeDtypeStruct((units, 2 * unit), FULL),
        jax.ShapeDtypeStruct((4, unit, units), LOW),
        jax.ShapeDtypeStruct((8, width), FULL),
    ]
    scratch = [
        low(units, width),
        low(width, units),
        low(out_wide, width),
        low(tokens, units),
        low(tokens, units),
        low(width, tokens),
        low(tokens, width),
        low(out_wide, tokens),
        low(tokens, width),
        low(tokens, width),
        low(tokens, width),
        low(tokens, width),
        low(tokens, width),
        low(tokens, width),
        low(2, half, heads_wide), low(2, unit, heads_wide), low(2, half, heads_wide), low(unit, heads_wide),
        low(2, out_wide, half), low(2, out_wide, unit), low(2, out_wide, half), low(out_wide, unit),
        low(2, units, half), low(2, units, unit), low(2, units, half), low(units, unit),
        low(2, half, units), low(2, unit, units),
        full(unit, units),
        full(units, unit),
        full(out_wide, unit),
        full(2, 32, width),
        full(2, width),
        full(4, 8, width),
        full(11, 8, width),
        pltpu.SemaphoreType.DMA((224,)),
        pltpu.SemaphoreType.DMA((COPIES,)),
        pltpu.SemaphoreType.DMA((COPIES,)),
    ]
    return pl.pallas_call(
        functools.partial(scatter_kernel, line_size),
        out_shape=outs,
        in_specs=[ANY] * 13 + [IN_VMEM] * 2,
        out_specs=[ANY] * 7 + [IN_VMEM],
        scratch_shapes=scratch,
        compiler_params=pltpu.CompilerParams(
            collective_id=1, has_side_effects=True, vmem_limit_bytes=VMEM_BYTES
        ),
    )(expand_full, shrink_full, output_full, act, slope, n2t, up, ctxt, red_heads, red_out, red_shrink, x, g, raw, sums)


def square_local(
    layer_input,
    block_order,
    first_gain,
    first_bias,
    second_gain,
    second_bias,
    heads_weight,
    heads_bias,
    output_weight,
    output_bias,
    expand_weight,
    expand_bias,
    shrink_weight,
    shrink_bias,
    cotangent,
):
    width = layer_input.shape[2]
    heads_rows = heads_weight.reshape(heads_weight.shape[0], -1)
    output_rows = output_weight.reshape(-1, output_weight.shape[2])
    wide = heads_rows.shape[1]
    raw = jnp.stack(
        [
            vec.astype(FULL)
            for vec in (
                first_gain,
                first_bias,
                second_gain,
                second_bias,
                expand_bias,
                jnp.pad(heads_bias.reshape(-1), (0, width - wide)),
                output_bias.astype(FULL) + shrink_bias.astype(FULL),
                jnp.zeros((width,), FULL),
            )
        ]
    )
    *gathered, sums = gather_call(
        layer_input[0], cotangent[0], heads_rows, output_rows, expand_weight, shrink_weight, raw, block_order
    )
    layer_output, input_grad, heads_grad, output_grad, expand_weight_grad, shrink_weight_grad, _, sums = scatter_call(
        lax.axis_size("tensor"),
        gathered,
        layer_input[0],
        cotangent[0],
        raw,
        sums,
    )
    return (
        layer_output[None],
        input_grad[None],
        sums[0],
        sums[1],
        sums[2],
        sums[3],
        heads_grad.reshape(heads_weight.shape),
        sums[6, :wide].reshape(heads_bias.shape),
        output_grad.reshape(output_weight.shape),
        sums[4],
        expand_weight_grad,
        sums[5],
        shrink_weight_grad,
        sums[4],
    )


def ring_local(
    layer_input,
    block_order,
    first_gain,
    first_bias,
    second_gain,
    second_bias,
    heads_weight,
    heads_bias,
    output_weight,
    output_bias,
    expand_weight,
    expand_bias,
    shrink_weight,
    shrink_bias,
    cotangent,
):
    tokens_here = layer_input.shape[1]
    fsdp_count = lax.axis_size("fsdp")
    head_dim = output_weight.shape[1]
    score_scale = head_dim ** (-0.5)
    order_row = block_order[0]
    device_slot = lax.axis_index("fsdp")
    own_block = jnp.sum(
        jnp.where(jnp.arange(fsdp_count, dtype=jnp.int32) == device_slot, order_row, 0)
    )
    offsets = jnp.arange(tokens_here, dtype=jnp.int32)
    query_pos = own_block * tokens_here + offsets
    key_pos = jnp.repeat(order_row, tokens_here) * tokens_here + jnp.tile(offsets, fsdp_count)
    allowed = key_pos[None, :] <= query_pos[:, None]
    cosine, sine_part = rotary_tables(query_pos, ROT)
    hidden_in = layer_input[0].astype(jnp.float32)
    gain_one = first_gain.astype(jnp.float32)
    shift_one = first_bias.astype(jnp.float32)
    gain_two = second_gain.astype(jnp.float32)
    shift_two = second_bias.astype(jnp.float32)
    norm_one_low = layer_norm(hidden_in, gain_one, shift_one).astype(jnp.bfloat16)
    norm_two_low = layer_norm(hidden_in, gain_two, shift_two).astype(jnp.bfloat16)
    heads_full, output_full, expand_full, shrink_full = (
        lax.all_gather(heads_weight, "fsdp", axis=0, tiled=True),
        lax.all_gather(output_weight, "fsdp", axis=2, tiled=True),
        lax.all_gather(expand_weight, "fsdp", axis=0, tiled=True),
        lax.all_gather(shrink_weight, "fsdp", axis=1, tiled=True),
    )
    projected = jnp.einsum(
        "td,dhe->hte", norm_one_low, heads_full, preferred_element_type=jnp.float32
    )
    projected = projected + heads_bias.astype(jnp.float32)[:, None, :]
    query_pre = projected[..., :head_dim]
    key_pre = projected[..., head_dim : 2 * head_dim]
    query_low = rotate(query_pre, cosine, sine_part).astype(jnp.bfloat16)
    key_low = rotate(key_pre, cosine, sine_part).astype(jnp.bfloat16)
    value_low = projected[..., 2 * head_dim :].astype(jnp.bfloat16)
    key_all, value_all = (
        lax.all_gather(key_low, "fsdp", axis=1, tiled=True),
        lax.all_gather(value_low, "fsdp", axis=1, tiled=True),
    )

    def attend_head(operands):
        query_head, key_head, value_head = operands
        probability = softmax_rows(contract_last(query_head, key_head) * score_scale, allowed)
        return jnp.dot(
            probability.astype(jnp.bfloat16), value_head, preferred_element_type=jnp.float32
        )

    context = lax.map(attend_head, (query_low, key_all, value_all))
    context_low = context.astype(jnp.bfloat16)
    expand_in = jnp.dot(
        norm_two_low, expand_full, preferred_element_type=jnp.float32
    ) + expand_bias.astype(jnp.float32)
    activation_low = jax.nn.gelu(expand_in, approximate=False).astype(jnp.bfloat16)
    branch_part = jnp.einsum(
        "hte,hed->td", context_low, output_full, preferred_element_type=jnp.float32
    )
    branch_part = branch_part + jnp.dot(
        activation_low, shrink_full, preferred_element_type=jnp.float32
    )
    branch = lax.psum(branch_part, "tensor")
    layer_output = (
        hidden_in + branch + output_bias.astype(jnp.float32) + shrink_bias.astype(jnp.float32)
    ).astype(jnp.bfloat16)[None]
    heads_back, output_back, expand_back, shrink_back = (
        lax.all_gather(heads_weight, "fsdp", axis=0, tiled=True),
        lax.all_gather(output_weight, "fsdp", axis=2, tiled=True),
        lax.all_gather(expand_weight, "fsdp", axis=0, tiled=True),
        lax.all_gather(shrink_weight, "fsdp", axis=1, tiled=True),
    )
    key_back, value_back = (
        lax.all_gather(key_low, "fsdp", axis=1, tiled=True),
        lax.all_gather(value_low, "fsdp", axis=1, tiled=True),
    )
    grad_out = cotangent[0]
    grad_float = grad_out.astype(jnp.float32)
    output_weight_grad = jnp.einsum(
        "hte,td->hed", context_low, grad_out, preferred_element_type=jnp.float32
    )
    shrink_weight_grad = contract_first(activation_low, grad_out)
    bias_total = jnp.sum(grad_float, 0)
    context_grad = jnp.einsum(
        "td,hed->hte", grad_out, output_back, preferred_element_type=jnp.float32
    ).astype(jnp.bfloat16)
    activation_grad = contract_last(grad_out, shrink_back)
    _, gelu_back = jax.vjp(lambda inner_val: jax.nn.gelu(inner_val, approximate=False), expand_in)
    expand_grad = gelu_back(activation_grad)[0].astype(jnp.bfloat16)
    expand_weight_grad = contract_first(norm_two_low, expand_grad)
    expand_bias_grad = jnp.sum(expand_grad.astype(jnp.float32), 0)
    norm_two_grad = contract_last(expand_grad, expand_back)

    def attend_back(operands):
        query_head, key_head, value_head, context_head = operands
        probability = softmax_rows(contract_last(query_head, key_head) * score_scale, allowed)
        prob_low = probability.astype(jnp.bfloat16)
        weight_grad = contract_last(context_head, value_head)
        row_inner = jnp.sum(probability * weight_grad, -1, keepdims=True)
        score_grad = (probability * (weight_grad - row_inner)).astype(jnp.bfloat16)
        query_grad = jnp.dot(score_grad, key_head, preferred_element_type=jnp.float32) * score_scale
        key_grad = contract_first(score_grad, query_head) * score_scale
        value_grad = contract_first(prob_low, context_head)
        return (query_grad, key_grad, value_grad)

    query_grad, key_grad_all, value_grad_all = lax.map(
        attend_back, (query_low, key_back, value_back, context_grad)
    )
    key_grad, value_grad = (
        lax.psum_scatter(key_grad_all, "fsdp", scatter_dimension=1, tiled=True),
        lax.psum_scatter(value_grad_all, "fsdp", scatter_dimension=1, tiled=True),
    )
    _, rotate_back = jax.vjp(lambda inner_val: rotate(inner_val, cosine, sine_part), query_pre)
    projected_grad = jnp.concatenate(
        [rotate_back(query_grad)[0], rotate_back(key_grad)[0], value_grad], -1
    ).astype(jnp.bfloat16)
    heads_weight_grad = jnp.einsum(
        "td,hte->dhe", norm_one_low, projected_grad, preferred_element_type=jnp.float32
    )
    heads_bias_grad = jnp.sum(projected_grad.astype(jnp.float32), 1)
    norm_one_grad = jnp.einsum(
        "hte,dhe->td", projected_grad, heads_back, preferred_element_type=jnp.float32
    )
    norm_one_grad, norm_two_grad = lax.psum((norm_one_grad, norm_two_grad), "tensor")
    _, first_back = jax.vjp(layer_norm, hidden_in, gain_one, shift_one)
    input_first, first_gain_grad, first_bias_grad = first_back(norm_one_grad)
    _, second_back = jax.vjp(layer_norm, hidden_in, gain_two, shift_two)
    input_second, second_gain_grad, second_bias_grad = second_back(norm_two_grad)
    input_grad = (grad_float + input_first + input_second)[None]
    small_sums = lax.psum(
        (
            first_gain_grad,
            first_bias_grad,
            second_gain_grad,
            second_bias_grad,
            bias_total,
            expand_bias_grad,
            heads_bias_grad,
        ),
        ("replica", "fsdp"),
    )
    shard_parts = (
        lax.psum_scatter(heads_weight_grad, "fsdp", scatter_dimension=0, tiled=True),
        lax.psum_scatter(output_weight_grad, "fsdp", scatter_dimension=2, tiled=True),
        lax.psum_scatter(expand_weight_grad, "fsdp", scatter_dimension=0, tiled=True),
        lax.psum_scatter(shrink_weight_grad, "fsdp", scatter_dimension=1, tiled=True),
    )
    reduced = lax.psum((shard_parts[0], shard_parts[1], shard_parts[2], shard_parts[3]), "replica")
    return (
        layer_output,
        input_grad,
        small_sums[0],
        small_sums[1],
        small_sums[2],
        small_sums[3],
        reduced[0],
        small_sums[6],
        reduced[1],
        small_sums[4],
        reduced[2],
        small_sums[5],
        reduced[3],
        small_sums[4],
    )


def solution(mesh):
    placed = (
        P("replica", "fsdp", None),
        P("replica", None),
        P(),
        P(),
        P(),
        P(),
        P("fsdp", "tensor", None),
        P("tensor", None),
        P("tensor", None, "fsdp"),
        P(),
        P("fsdp", "tensor"),
        P("tensor"),
        P("tensor", "fsdp"),
        P(),
        P("replica", "fsdp", None),
    )
    local = square_local if mesh.shape["fsdp"] == 4 and mesh.shape["replica"] == 2 and mesh.shape["tensor"] == 4 else ring_local
    return jax.shard_map(
        local,
        mesh=mesh,
        in_specs=placed,
        out_specs=(
            P("replica", "fsdp", None),
            P("replica", "fsdp", None),
            P(),
            P(),
            P(),
            P(),
            P("fsdp", "tensor", None),
            P("tensor", None),
            P("tensor", None, "fsdp"),
            P(),
            P("fsdp", "tensor"),
            P("tensor"),
            P("tensor", "fsdp"),
            P(),
        ),
        check_vma=False,
    )
```

```python
import functools
import math

import jax
import jax.numpy as jnp
from jax import lax
from jax.experimental import pallas as pl
from jax.experimental.pallas import tpu as pltpu
from jax.sharding import PartitionSpec as P

ROT = 64


NORM_EPS = 1e-05
MASKED = -1e30


def layer_norm(values_in, gain_vec, shift_vec):
    average = jnp.mean(values_in, -1, keepdims=True)
    centred = values_in - average
    spread_sq = jnp.mean(centred * centred, -1, keepdims=True)
    return centred * lax.rsqrt(spread_sq + NORM_EPS) * gain_vec + shift_vec


def rotate(values_in, cosine, sine_part):
    rot_width = cosine.shape[-1]
    half_width = rot_width // 2
    turning = values_in[..., :rot_width]
    swapped = jnp.concatenate([-turning[..., half_width:], turning[..., :half_width]], -1)
    return jnp.concatenate([turning * cosine + swapped * sine_part, values_in[..., rot_width:]], -1)


def rotary_tables(positions, rot_width):
    frequency = jnp.power(10000.0, -jnp.arange(0, rot_width, 2, dtype=jnp.float32) / rot_width)
    angle_half = positions.astype(jnp.float32)[:, None] * frequency[None, :]
    angles = jnp.concatenate([angle_half, angle_half], -1)
    return (jnp.cos(angles), jnp.sin(angles))


def contract_last(left_op, right_op):
    return lax.dot_general(
        left_op, right_op, (((1,), (1,)), ((), ())), preferred_element_type=jnp.float32
    )


def contract_first(left_op, right_op):
    return lax.dot_general(
        left_op, right_op, (((0,), (0,)), ((), ())), preferred_element_type=jnp.float32
    )


def softmax_rows(scores, allowed):
    masked_scores = jnp.where(allowed, scores, MASKED)
    row_top = jnp.max(masked_scores, -1, keepdims=True)
    exponent = jnp.exp(masked_scores - row_top)
    return exponent / jnp.sum(exponent, -1, keepdims=True)


LOW = jnp.bfloat16
FULL = jnp.float32


MESH = pl.DeviceIdType.MESH
ANY = pl.BlockSpec(memory_space=pl.ANY)
IN_VMEM = pl.BlockSpec(memory_space=pltpu.VMEM)
VMEM_BYTES = 63 * 2**20
COPIES = 160


class Links:
    def __init__(self, send_sem, recv_sem, line=0):
        self.send_sem, self.recv_sem, self.sent, self.count = send_sem, recv_sem, [], 0
        self.r, self.f, self.t = (lax.axis_index(name) for name in ("replica", "fsdp", "tensor"))
        self.xb, self.yb = lax.rem(self.f, 2), lax.div(self.f, 2)
        self.x = (self.r, self.f + 1 - 2 * self.xb, self.t)
        self.y = (self.r, lax.rem(self.f + 2, 4), self.t)
        self.core = (1 - self.r, self.f, self.t)
        self.peers = [self.x, self.y, self.core]
        if line:
            self.line = line
            self.left, self.right, self.across = (
                (self.r, self.f, lax.rem(self.t + step, line)) for step in (line - 1, 1, 2)
            )
            self.pair = (self.r, self.f, self.t + 1 - 2 * lax.rem(self.t, 2))
            self.far = (self.r, 3 - self.f, self.t)
            self.mirror = (self.r, self.f, line - 1 - self.t)
            self.peers += [self.far, self.left, self.right, self.across]

    def meet(self):
        barrier = pltpu.get_barrier_semaphore()
        for peer in self.peers:
            pl.semaphore_signal(barrier, inc=1, device_id=peer, device_id_type=MESH)
        pl.semaphore_wait(barrier, len(self.peers))

    def prepare(self, source, target, peer):
        self.count += 1
        return self.copy_at(self.count - 1, source, target, peer)

    def send(self, source, target, peer):
        copy = self.prepare(source, target, peer)
        copy.start()
        self.sent.append(copy)
        return copy

    def series(self, count):
        k = self.count
        self.count += count
        return k

    def copy_at(self, k, source, target, peer):
        return pltpu.make_async_remote_copy(
            src_ref=source,
            dst_ref=target,
            send_sem=self.send_sem.at[k],
            recv_sem=self.recv_sem.at[k],
            device_id=peer,
            device_id_type=MESH,
        )

    def sent_out(self, copy):
        copy.wait_send()
        self.sent = [other for other in self.sent if other is not copy]

    def end(self):
        for copy in self.sent:
            copy.wait_send()

    def block(self, i):
        place = 0
        for size, bit in ((4, self.yb), (2, self.xb), (1, self.r)):
            mine = lax.rem(lax.div(i, size), 2) if isinstance(i, jax.Array) else i // size % 2
            place = place + size * (mine + bit - 2 * mine * bit)
        return place


class Local:
    def __init__(self, sem):
        self.sem, self.count, self.open = sem, 0, []

    def start(self, source, target):
        copy = pltpu.make_async_copy(source, target, self.sem.at[self.count])
        self.count += 1
        copy.start()
        self.open.append(copy)
        return copy

    def wait(self, *copies):
        for copy in copies:
            copy.wait()
            self.open = [other for other in self.open if other is not copy]

    def end(self):
        self.wait(*list(self.open))


def at_rows(ref, start, size):
    return ref.at[pl.ds(start, size), :]


def at_columns(ref, start, size):
    return ref.at[:, pl.ds(start, size)]


class Gathered:
    def __init__(self, links, local, shard, full, cut, unit, copied=True):
        self.links, self.local, self.full, self.cut = links, local, full, cut
        self.shard, self.unit, self.half = shard, unit, unit // 2
        self.copies = [local.start(self.here(i), self.at(i)) for i in range(2)] if copied else []
        self.from_x, self.from_y = {}, {}

    def here(self, i):
        start = self.links.r * self.unit if i == 0 else (1 - self.links.r) * self.unit
        return self.cut(self.shard, pl.multiple_of(start, self.unit), self.unit)

    def mine(self, start, size):
        return self.cut(self.shard, pl.multiple_of(self.links.r * self.unit + start, self.half), size)

    def at(self, block, start=0, size=None):
        return self.cut(self.full, block * self.unit + start, self.unit if size is None else size)

    def to_x(self, lower):
        start = self.half if lower else 0
        source, target = self.mine(start, self.half), self.at(2, start, self.half)
        self.from_x[lower] = self.links.send(source, target, self.links.x)

    def to_y(self, lower):
        start = self.half if lower else 0
        source, target = self.mine(start, self.half), self.at(4, start, self.half)
        self.from_y[lower] = self.links.send(source, target, self.links.y)

    def first(self):
        self.to_x(False)
        self.to_y(True)

    def rest(self):
        self.to_x(True)
        self.to_y(False)

    def relay(self):
        half = self.half
        self.from_x[False].wait_recv()
        self.far_top = self.links.send(self.at(2, 0, half), self.at(6, 0, half), self.links.y)
        self.from_y[True].wait_recv()
        self.far_end = self.links.send(self.at(4, half, half), self.at(6, half, half), self.links.x)

    def share(self):
        self.from_y[False].wait_recv()
        self.core_y = self.links.send(self.at(4), self.at(5), self.links.core)
        self.from_x[True].wait_recv()
        self.core_x = self.links.send(self.at(2), self.at(3), self.links.core)

    def share_far(self):
        self.far_top.wait_recv()
        self.far_end.wait_recv()
        self.core_far = self.links.send(self.at(6), self.at(7), self.links.core)

    def whole(self):
        self.local.wait(*self.copies)
        for copy in (self.core_x, self.core_y, self.core_far):
            copy.wait_recv()


def tile_of(j, size):
    return pl.ds(pl.multiple_of(j * size, size), size)


def dot(left, right):
    return jnp.dot(left, right, preferred_element_type=FULL)


def spin(values_in, cosine, sine_one, sine_two):
    head = values_in[:, :128]
    turned_head = (
        head * cosine + pltpu.roll(head, 96, 1) * sine_one + pltpu.roll(head, 32, 1) * sine_two
    )
    return jnp.concatenate([turned_head, values_in[:, 128:]], -1)


def attend_kernel(
    score_scale,
    x_hbm, g_hbm, wh_hbm, wo_hbm, we_hbm, raw, order,
    we, wo_out, wh_out, n2_out, n1t_out, n2t_out, ctx_out, pg_out, sums,
    vecs, cosine, sine_one, sine_two, wh, wo, xr, g, n1, n2, n1t, n2t, qkv_away, qkv, dctx_away, dctx, ctxt, ctxt_all,
    pg, pgq, pg_away, kvg, kvg_away, kvg_got, local_sem, send_sem, recv_sem,
):
    links, local = Links(send_sem, recv_sem), Local(local_sem)
    tokens, width = xr.shape
    hd = dctx.shape[1]
    unit = width // 8
    blocks = range(8)
    x_in, g_in = [], []
    for i in blocks:
        cols = pl.ds(pl.multiple_of(links.block(i) * unit, unit), unit)
        x_in.append(local.start(x_hbm.at[:, cols], xr.at[:, pl.ds(i * unit, unit)]))
        g_in.append(local.start(g_hbm.at[:, cols], g.at[:, pl.ds(i * unit, unit)]))
    links.meet()
    heads = Gathered(links, local, wh_hbm, wh, at_rows, unit)
    output = Gathered(links, local, wo_hbm, wo, at_columns, unit)
    expand = Gathered(links, local, we_hbm, we, at_rows, unit)
    heads.first()
    heads.rest()

    for i in blocks:
        cols = pl.ds(pl.multiple_of(links.block(i) * unit, unit), unit)
        vecs[0:4, i * unit : (i + 1) * unit] = raw[0:4, cols]
    local.wait(*x_in)

    def norm_rows(c, carry):
        rows = tile_of(c, 64)
        value = xr[rows, :].astype(FULL)
        average = jnp.mean(value, -1, keepdims=True)
        centred = value - average
        inverse = lax.rsqrt(jnp.mean(centred * centred, -1, keepdims=True) + NORM_EPS)
        normal = centred * inverse
        n1[rows, :] = (normal * vecs[0:1, :] + vecs[1:2, :]).astype(LOW)
        n2[rows, :] = (normal * vecs[2:3, :] + vecs[3:4, :]).astype(LOW)
        return carry

    lax.fori_loop(0, tokens // 64, norm_rows, 0)
    bases = [
        order[0, (links.yb if step < 2 else 1 - links.yb) * 2 + (links.xb if step % 2 == 0 else 1 - links.xb)]
        * tokens
        for step in (0, 2, 1, 3)
    ]

    def table_rows(c, carry):
        rows = tile_of(c, 64)
        lane = lax.broadcasted_iota(jnp.int32, (64, 128), 1)
        row = lax.broadcasted_iota(jnp.int32, (64, 128), 0) + c * 64
        spot = row + jnp.where(row < tokens, bases[0], bases[1] - tokens)
        pace = jnp.exp(lax.rem(lane, ROT // 2).astype(FULL) * (-2.0 / ROT * math.log(10000.0)))
        angle = spot.astype(FULL) * pace
        sine = jnp.sin(angle)
        cosine[rows, :] = jnp.where(lane < ROT, jnp.cos(angle), 1.0)
        sine_one[rows, :] = jnp.where(lane < ROT // 2, -sine, 0.0)
        sine_two[rows, :] = jnp.where(jnp.logical_and(lane >= ROT // 2, lane < ROT), sine, 0.0)
        return carry

    lax.fori_loop(0, 2 * tokens // 64, table_rows, 0)
    heads.relay()
    output.first()
    output.rest()

    def turn_tiles(j, carry):
        cols = tile_of(j, unit)
        n1t[cols, :] = n1[:, cols].T
        n2t[cols, :] = n2[:, cols].T
        return carry

    lax.fori_loop(0, 8, turn_tiles, 0)
    local.start(n2, n2_out)
    local.start(n1t, n1t_out)
    local.start(n2t, n2t_out)
    sums[...] = jnp.zeros_like(sums)
    local.wait(*g_in)
    for i in blocks:
        cols = pl.ds(pl.multiple_of(links.block(i) * unit, unit), unit)
        sums[4:5, cols] = jnp.sum(g[:, i * unit : (i + 1) * unit].astype(FULL), 0, keepdims=True)
    heads.share()
    heads.share_far()
    heads.whole()
    local.start(wh, wh_out)
    output.relay()

    own, away = links.yb * 3 * hd, (1 - links.yb) * 3 * hd

    def project(c, start, target):
        cols = pl.ds(pl.multiple_of(start + c * hd, hd), hd)
        value = dot(n1[...], wh[:, cols]) + raw[5:6, cols]
        if c < 2:
            value = spin(value, cosine[:tokens, :], sine_one[:tokens, :], sine_two[:tokens, :])
        target[c, :tokens, :] = value.astype(LOW)

    def place_of(c, part):
        return qkv.at[c, pl.ds(part * tokens, tokens), :]

    from_y, from_x, from_far = {}, {}, {}
    for c in (1, 2, 0):
        project(c, away, qkv_away)
        from_y[c] = links.send(qkv_away.at[c], place_of(c, 1), links.y)
    for c in (1, 2):
        project(c, own, qkv)
        from_x[c] = links.send(place_of(c, 0), place_of(c, 2), links.x)
    from_y[1].wait_recv()
    from_far[1] = links.send(place_of(1, 1), place_of(1, 3), links.x)
    project(0, own, qkv)
    output.share()
    output.share_far()
    from_y[2].wait_recv()
    from_far[2] = links.send(place_of(2, 1), place_of(2, 3), links.x)
    output.whole()
    local.start(wo, wo_out)
    rows_own = pl.ds(pl.multiple_of(links.yb * hd, hd), hd)
    rows_away = pl.ds(pl.multiple_of((1 - links.yb) * hd, hd), hd)
    dctx_away[...] = contract_last(g[...], wo[rows_away, :]).astype(LOW)
    dctx_from_y = links.send(dctx_away, dctx.at[pl.ds(tokens, tokens), :], links.y)
    dctx[:tokens, :] = contract_last(g[...], wo[rows_own, :]).astype(LOW)
    expand.first()
    expand.to_y(False)
    for copy in (from_y[0], dctx_from_y, *from_x.values(), *from_far.values()):
        copy.wait_recv()

    def attention(kt, vt, dk, dv, prob, wgt, prob_low, grad_low):
        keys = qkv.shape[1]
        step = tokens
        lag = lax.broadcasted_iota(jnp.int32, (step, hd), 0) - lax.broadcasted_iota(jnp.int32, (step, hd), 1)
        parts = [pl.ds(i * step, step) for i in range(keys // step)]
        for part in parts:
            kt[:, part] = qkv[1, part, :].T
            vt[:, part] = qkv[2, part, :].T
        dk[...] = jnp.zeros_like(dk)
        dv[...] = jnp.zeros_like(dv)

        def one(b, carry):
            rows = tile_of(b, hd)
            query, grad = qkv[0, rows, :], dctx[rows, :]
            ahead = jnp.where(b < tokens // hd, bases[0], bases[1] - tokens) + b * hd
            top = jnp.full((1, hd), MASKED, FULL)
            for i, part in enumerate(parts):
                scores = contract_last(qkv[1, part, :], query) * score_scale
                scores = jnp.where(lag <= ahead - bases[i], scores, MASKED)
                prob[part, :] = scores
                top = jnp.maximum(top, jnp.max(scores, 0, keepdims=True))
            total = jnp.zeros((1, hd), FULL)
            for part in parts:
                exponent = jnp.exp(prob[part, :] - top)
                prob[part, :] = exponent
                total = total + jnp.sum(exponent, 0, keepdims=True)
            share = 1.0 / total
            inner = jnp.zeros((1, hd), FULL)
            for part in parts:
                weight = contract_last(qkv[2, part, :], grad)
                chance = prob[part, :] * share
                prob[part, :] = chance
                prob_low[part, :] = chance.astype(LOW)
                wgt[part, :] = weight
                inner = inner + jnp.sum(chance * weight, 0, keepdims=True)
            for part in parts:
                grad_low[part, :] = (prob[part, :] * (wgt[part, :] - inner)).astype(LOW)
            ctxt_all[:, rows] = dot(vt[...], prob_low[...]).astype(LOW)
            query_grad = dot(kt[...], grad_low[...]) * score_scale
            for part in parts:
                dv[part, :] += dot(prob_low[part, :], grad)
                dk[part, :] += dot(grad_low[part, :], query)
            turned_grad = spin(query_grad.T, cosine[rows, :], -sine_one[rows, :], -sine_two[rows, :])
            pgq[rows, :] = turned_grad.astype(LOW)
            return carry

        lax.fori_loop(0, 2 * tokens // hd, one, 0)
        ctxt[rows_own, :] = ctxt_all[:, :tokens]
        pg[:, pl.ds(pl.multiple_of(own, hd), hd)] = pgq[:tokens, :]
        for i, total in enumerate((dk, dv)):
            kvg_away[i, :, :] = total[2 * tokens :, :].astype(LOW)
            kvg[i, :, :] = total[: 2 * tokens, :]

    keys = qkv.shape[1]
    pl.run_scoped(
        attention,
        pltpu.VMEM((hd, keys), LOW),
        pltpu.VMEM((hd, keys), LOW),
        pltpu.VMEM((keys, hd), FULL),
        pltpu.VMEM((keys, hd), FULL),
        pltpu.VMEM((keys, hd), FULL),
        pltpu.VMEM((keys, hd), FULL),
        pltpu.VMEM((keys, hd), LOW),
        pltpu.VMEM((keys, hd), LOW),
    )
    def head_columns(ref, start, i):
        return ref.at[:, pl.ds(pl.multiple_of(start + i * hd, hd), hd)]

    def send_grad(i):
        source = pgq.at[pl.ds(tokens, tokens), :] if i == 0 else head_columns(pg_away, 0, i - 1)
        return links.send(source, head_columns(pg, own, i), links.y)

    kvg_from_x = {i: links.send(kvg_away.at[i], kvg_got.at[i], links.x) for i in (1, 0)}
    pg_from_y = [send_grad(0)]
    ctx_from_y = links.send(ctxt_all.at[:, pl.ds(tokens, tokens)], ctxt.at[rows_own, :], links.y)
    expand.relay()
    expand.to_x(True)

    for i in (1, 0):
        kvg_from_x[i].wait_recv()
        for away_rows, target in ((True, pg_away), (False, pg)):
            rows = pl.ds(tokens if away_rows else 0, tokens)
            total = kvg[i, rows, :] + kvg_got[i, rows, :].astype(FULL)
            if i == 0:
                total = spin(total * score_scale, cosine[rows, :], -sine_one[rows, :], -sine_two[rows, :])
            head_columns(target, 0 if away_rows else own, i if away_rows else 1 + i)[...] = total.astype(LOW)
            if away_rows:
                pg_from_y.append(send_grad(1 + i))
    ctx_from_y.wait_recv()
    local.start(ctxt, ctx_out)
    expand.share()
    expand.share_far()
    for copy in pg_from_y:
        copy.wait_recv()
    local.start(pg, pg_out)
    expand.whole()
    links.end()
    local.end()


def attend_call(x, g, heads_rows, output_rows, expand_weight, raw, order):
    tokens, width = x.shape
    heads_wide, out_wide, units = heads_rows.shape[1], output_rows.shape[0], expand_weight.shape[1]
    hd = heads_wide // 6
    keys = 4 * tokens
    low = lambda *shape: jax.ShapeDtypeStruct(shape, LOW)
    outs = [
        low(width, units),
        low(out_wide, width),
        low(width, heads_wide),
        low(tokens, width),
        low(width, tokens),
        low(width, tokens),
        low(out_wide, tokens),
        low(tokens, heads_wide),
        jax.ShapeDtypeStruct((8, width), FULL),
    ]
    vm = lambda *shape: pltpu.VMEM(shape, LOW)
    scratch = [
        pltpu.VMEM((4, width), FULL),
        *[pltpu.VMEM((2 * tokens, 128), FULL)] * 3,
        vm(width, heads_wide),
        vm(out_wide, width),
        vm(tokens, width),
        vm(tokens, width),
        vm(tokens, width),
        vm(tokens, width),
        vm(width, tokens),
        vm(width, tokens),
        vm(3, tokens, hd),
        vm(3, keys, hd),
        vm(tokens, hd),
        vm(2 * tokens, hd),
        vm(out_wide, tokens),
        vm(hd, 2 * tokens),
        vm(tokens, heads_wide),
        vm(2 * tokens, hd),
        vm(tokens, 2 * hd),
        pltpu.VMEM((2, 2 * tokens, hd), FULL),
        vm(2, 2 * tokens, hd),
        vm(2, 2 * tokens, hd),
        pltpu.SemaphoreType.DMA((64,)),
        pltpu.SemaphoreType.DMA((COPIES,)),
        pltpu.SemaphoreType.DMA((COPIES,)),
    ]
    return pl.pallas_call(
        functools.partial(attend_kernel, hd**-0.5),
        out_shape=outs,
        in_specs=[ANY] * 5 + [IN_VMEM, pl.BlockSpec(memory_space=pltpu.SMEM)],
        out_specs=[ANY] * 8 + [IN_VMEM],
        scratch_shapes=scratch,
        compiler_params=pltpu.CompilerParams(
            collective_id=0, has_side_effects=True, vmem_limit_bytes=VMEM_BYTES
        ),
    )(x, g, heads_rows, output_rows, expand_weight, raw, order)


class Scattered:
    def __init__(self, links, local, block, cut, unit, via, got, stage=None, own=None):
        self.links, self.local, self.block, self.cut, self.unit = links, local, block, cut, unit
        self.via, self.got, self.stage, self.own = via, got, stage, own
        self.half = unit // 2

    def load(self):
        self.loads = [
            self.local.start(self.cut(self.block(1), self.half, self.half), self.stage[0]),
            self.local.start(self.cut(self.block(2), 0, self.half), self.stage[1]),
            self.local.start(self.block(0), self.own),
        ]

    def first(self):
        half, cut, far = self.half, self.cut, self.block(3)
        self.via_x = self.links.send(cut(far, 0, half), self.via.at[0], self.links.x)
        self.via_y = self.links.send(cut(far, half, half), self.via.at[1], self.links.y)

    def direct(self):
        half, cut = self.half, self.cut
        self.x_top = self.links.send(cut(self.block(1), 0, half), cut(self.got.at[0], 0, half), self.links.x)
        self.y_end = self.links.send(cut(self.block(2), half, half), cut(self.got.at[1], half, half), self.links.y)

    def second(self):
        half, cut = self.half, self.cut
        self.local.wait(*self.loads[:2])
        self.via_x.wait_recv()
        add_rows(self.stage[1], self.stage[1], self.via.at[0])
        self.y_top = self.links.send(self.stage[1], cut(self.got.at[1], 0, half), self.links.y)
        self.via_y.wait_recv()
        add_rows(self.stage[0], self.stage[0], self.via.at[1])
        self.x_end = self.links.send(self.stage[0], cut(self.got.at[0], half, half), self.links.x)

    def third(self, slots, place, step):
        for copy in (self.x_top, self.x_end, self.y_top, self.y_end):
            copy.wait_recv()
        self.local.wait(self.loads[2])
        self.other = []
        for start in range(0, self.own.shape[0], step):
            rows = pl.ds(start, step)
            at, total = slots.take()
            add_rows(total, self.own.at[rows, :], self.got.at[0, rows, :], self.got.at[1, rows, :])
            kept = self.local.start(total, place.at[rows, :])
            other = self.links.send(total, place.at[rows, :], self.links.core)
            self.other.append(other)

            def done(kept=kept, other=other):
                self.local.wait(kept)
                self.links.sent_out(other)

            slots.busy[at] = done


def add_rows(target, *parts):
    rows, wide = target.shape
    step = min(rows, 32 if wide > 512 else 256)

    def one(c, carry):
        at = pl.ds(pl.multiple_of(c * step, step), step)
        total = parts[0][at, :].astype(FULL)
        for part in parts[1:]:
            total = total + part[at, :].astype(FULL)
        target[at, :] = total.astype(target.dtype)
        return carry

    lax.fori_loop(0, rows // step, one, 0)


class Line:
    def __init__(self, links, part, got, final, chunks, cut, finish):
        self.links, self.part, self.got, self.final, self.cut, self.finish = links, part, got, final, cut, finish
        self.chunks = chunks
        self.outer = jnp.logical_or(links.t == 0, links.t == links.line - 1)
        self.middle = jnp.logical_not(self.outer)
        self.inward = [self.make(c, part, final, links.pair) for c in range(chunks)]
        self.across = [self.make(c, part, got, links.mirror) for c in range(chunks)]
        self.outward = [self.make(c, final, final, links.pair) for c in range(chunks)]

    def make(self, c, source, target, peer):
        return self.links.prepare(self.cut(source, c), self.cut(target, c), peer)

    def start(self, *chunks):
        @pl.when(self.outer)
        def _():
            for c in chunks:
                self.inward[c].start()

    def first(self, c):
        @pl.when(self.middle)
        def _():
            self.inward[c].wait_recv()
            part = self.cut(self.part, c)
            add_rows(part, part, self.cut(self.final, c))
            self.across[c].start()

    def second(self, c):
        @pl.when(self.middle)
        def _():
            self.across[c].wait_recv()
            self.finish(c)
            self.outward[c].start()

    def third(self, c):
        @pl.when(self.outer)
        def _():
            self.outward[c].wait_recv()

    def end(self):
        @pl.when(self.outer)
        def _():
            for copy in self.inward:
                copy.wait_send()

        @pl.when(self.middle)
        def _():
            for copy in self.across + self.outward:
                copy.wait_send()


class Slots:
    def __init__(self, *refs):
        self.refs, self.busy, self.count = refs, {}, 0

    def take(self):
        at = self.count % len(self.refs)
        self.count += 1
        if at in self.busy:
            self.busy.pop(at)()
        return at, self.refs[at]

    def end(self):
        for wait in self.busy.values():
            wait()
        self.busy = {}


def update_kernel(
    line_size,
    we_hbm, wo_hbm, wh_hbm, n2_hbm, n1t_hbm, n2t_hbm, ctxt_hbm, pg_hbm, x_hbm, g_hbm, we_own, ws_own, raw, sums_in,
    layer_out, input_grad, heads_grad, output_grad, expand_grad, shrink_grad, ws, got_core_s, got_core_o, got_core_h,
    got_core_e, red_s, red_o, red_h, sums_out,
    x, g, up, act, actt, slope, nt, pg, ctxt, ctx, wo, room_s, room_o, room_h,
    part_branch, got_branch, final_branch, got_up, final_up, via_h, got_h, stage_h, own_h, via_o, got_o, stage_o, own_o,
    via_s, got_s, via_e, got_e, room_e, total_rows, total_columns, grad_rows, vecs, sums, sums_got, gains, gains_got,
    loop_sem, block_sem, local_sem, send_sem, recv_sem,
):
    links, local = Links(send_sem, recv_sem, line_size), Local(local_sem)
    tokens, width = g.shape
    unit = width // 8
    blocks = range(8)
    place = [pl.ds(pl.multiple_of(links.block(i) * unit, unit), unit) for i in blocks]

    def here(i):
        return pl.ds(i * unit, unit)

    weight = Gathered(links, local, ws_own, ws, at_columns, unit, False)
    rest_rows = pl.ds(2 * unit, width - 2 * unit)

    def tile(j):
        return pl.ds(pl.multiple_of(j * unit, unit), unit)

    def placed(i):
        return pl.ds(pl.multiple_of(links.block(i) * unit, unit), unit)

    def stream(count, load, body):
        def copies(j):
            pairs = load(j, lax.rem(j, 2))
            return [pltpu.make_async_copy(*pair, loop_sem.at[n, lax.rem(j, 2)]) for n, pair in enumerate(pairs)]

        for copy in copies(0):
            copy.start()

        def one(j, carry):
            @pl.when(j + 1 < count)
            def _():
                for copy in copies(j + 1):
                    copy.start()

            for copy in copies(j):
                copy.wait()
            body(j, lax.rem(j, 2))
            return carry

        lax.fori_loop(0, count, one, 0)

    n2_load = local.start(n2_hbm, up)
    small_loads = [local.start(ctxt_hbm, ctxt), local.start(wo_hbm, wo)]
    g_loads = [local.start(g_hbm.at[:, place[i]], g.at[:, here(i)]) for i in blocks]
    links.meet()
    weight.first()
    weight.rest()
    late_loads = [local.start(pg_hbm, pg), local.start(n1t_hbm, nt)]
    late_loads += [local.start(x_hbm.at[:, place[i]], x.at[:, here(i)]) for i in blocks]
    for i in blocks:
        vecs[0:1, here(i)] = raw[2:3, place[i]]
        vecs[1:2, here(i)] = raw[6:7, place[i]] + raw[7:8, place[i]]
        vecs[2:3, here(i)] = raw[0:1, place[i]]

    local.wait(n2_load)

    def forward(j, slot):
        cols = tile(j)
        value = dot(up[...], room_s[slot]) + raw[4:5, cols]
        normal_share = 0.5 * (1.0 + lax.erf(value * (0.5**0.5)))
        low_act = (value * normal_share).astype(LOW)
        act[:, cols] = low_act
        actt[cols, :] = low_act.T
        density = jnp.exp(value * value * -0.5) * 0.3989422804014327
        slope[:, cols] = (normal_share + value * density).astype(LOW)

    stream(8, lambda j, slot: [(we_hbm.at[:, tile(j)], room_s.at[slot])], forward)
    weight.relay()
    local.wait(*small_loads)
    ctx[...] = ctxt[...].T

    rows_out = grad_rows.shape[1]

    def columns_cut(ref, c):
        return ref.at[:, here(c)]

    def rows_cut(ref, c):
        return ref.at[pl.ds(c * rows_out, rows_out), :]

    def finish_branch(c):
        cols = here(c)

        def one(part, carry):
            at = tile_of(part, 128)
            total = part_branch[at, cols].astype(FULL) + got_branch[at, cols].astype(FULL)
            final_branch[at, cols] = (x[at, cols].astype(FULL) + total + vecs[1:2, cols]).astype(LOW)
            return carry

        lax.fori_loop(0, tokens // 128, one, 0)

    def finish_up(c):
        add_rows(rows_cut(final_up, c), rows_cut(up, c), rows_cut(got_up, c))

    line_branch = Line(links, part_branch, got_branch, final_branch, 8, columns_cut, finish_branch)
    line_up = Line(links, up, got_up, final_up, tokens // rows_out, rows_cut, finish_up)

    def branch_blocks(chunks, block, source):
        def one(n, slot):
            cols = tile(block(n))
            part_branch[:, cols] = (dot(ctx[...], wo[:, cols]) + dot(act[...], room_s[slot])).astype(LOW)
            for at, chunk in enumerate(chunks):
                pl.when(n == at)(functools.partial(line_branch.start, chunk))

        stream(len(chunks), lambda n, slot: [(source(n), room_s.at[slot])], one)

    steps = [(line_branch, c) for c in (0, 1, 2, 4, 3, 5, 6, 7)] + [(line_up, c) for c in range(line_up.chunks)]
    out_copies = []

    def input_rows(c):
        slot = len(out_copies) % 2
        if len(out_copies) >= 2:
            local.wait(*out_copies[-2])
        rows = pl.ds(c * rows_out, rows_out)
        value = x[rows, :].astype(FULL)
        centred = value - jnp.mean(value, -1, keepdims=True)
        scale = lax.rsqrt(jnp.mean(centred * centred, -1, keepdims=True) + NORM_EPS)
        normal = centred * scale
        upstream = final_up[rows, :].astype(FULL)
        inner = upstream - jnp.mean(upstream, -1, keepdims=True)
        inner = inner - normal * jnp.mean(upstream * normal, -1, keepdims=True)
        grad_rows[slot, :, :] = g[rows, :].astype(FULL) + inner * scale
        out_copies.append(
            [local.start(grad_rows.at[slot, :, here(i)], input_grad.at[rows, place[i]]) for i in blocks]
        )

    def serve(count):
        for _ in range(count):
            at = serve.done
            if at < len(steps):
                steps[at][0].first(steps[at][1])
            if 2 <= at < len(steps) + 2:
                steps[at - 2][0].second(steps[at - 2][1])
            if at >= 4:
                line, c = steps[at - 4]
                line.third(c)
                if line is line_up:
                    input_rows(c)
                else:
                    local.start(final_branch.at[:, here(c)], layer_out.at[:, place[c]])
            serve.done += 1

    serve.done = 0
    branch_blocks((0, 1), lambda n: n, lambda n: at_columns(ws_own, pl.multiple_of((links.r + n - 2 * links.r * n) * unit, unit), unit))
    local.wait(*g_loads)

    order = (3, 1, 2, 0)

    def turn_of(n):
        return jnp.where(n == 0, 3, jnp.where(n == 3, 0, n))

    class Reduced:
        def __init__(self, room, got, block):
            self.room, self.got, self.block = room, got, block

        def to_core(self):
            first = links.series(4)

            def one(n, carry):
                k = turn_of(n)
                self.block(2 * k + 1, self.room.at[n], False)
                links.copy_at(first + n, self.room.at[n], self.got.at[k], links.core).start()
                return carry

            lax.fori_loop(0, 4, one, 0)
            self.copies = [
                links.copy_at(first + n, self.room.at[n], self.got.at[order[n]], links.core) for n in range(4)
            ]

        def fetch(self):
            for n in range(4):
                self.copies[n].wait_send()
                self.copies[n].wait_recv()
                pltpu.make_async_copy(self.got.at[order[n]], self.room.at[n], block_sem.at[n]).start()

        def add(self, red):
            def one(n, carry):
                k = turn_of(n)
                pltpu.make_async_copy(self.got.at[k], self.room.at[n], block_sem.at[n]).wait()
                self.block(2 * k, self.room.at[n], True)
                if red is not None:
                    pltpu.make_async_copy(self.room.at[n], red.at[k], block_sem.at[4 + n]).start()
                return carry

            lax.fori_loop(0, 4, one, 0)
            if red is not None:
                for n in range(4):
                    pltpu.make_async_copy(self.room.at[n], red.at[order[n]], block_sem.at[4 + n]).wait()

    def product(left, right, ref, add):
        part = dot(left, right)
        if add:
            part = part + ref[...].astype(FULL)
        ref[...] = part.astype(LOW)

    def shrink_block(i, ref, add):
        product(actt[...], g[:, tile(i)], ref, add)

    def output_block(i, ref, add):
        product(ctxt[...], g[:, tile(i)], ref, add)

    def heads_block(i, ref, add):
        product(nt[tile(i), :], pg[...], ref, add)

    def expand_block(i, ref, add):
        product(nt[tile(i), :], slope[...], ref, add)

    stage_s = (actt.at[:, pl.ds(unit, unit // 2)], actt.at[:, pl.ds(unit + unit // 2, unit // 2)])
    shrink = Scattered(
        links, local, lambda k: red_s.at[k], at_columns, unit, via_s, got_s, stage_s, actt.at[:, pl.ds(0, unit)]
    )
    heads = Scattered(
        links, local, lambda k: red_h.at[k], at_rows, unit, via_h, got_h, (stage_h.at[0], stage_h.at[1]), own_h
    )
    output = Scattered(
        links, local, lambda k: red_o.at[k], at_columns, unit, via_o, got_o, (stage_o.at[0], stage_o.at[1]), own_o
    )
    shrink_sum = Reduced(room_s, got_core_s, shrink_block)
    heads_sum = Reduced(room_h, got_core_h, heads_block)
    output_sum = Reduced(room_o, got_core_o, output_block)
    expand_sum = Reduced(room_e, got_core_e, expand_block)
    shrink_sum.to_core()
    weight.share()
    shrink_sum.fetch()
    shrink_sum.add(red_s)
    shrink.first()
    shrink.direct()
    shrink.load()
    serve(1)
    local.wait(*late_loads)
    heads_sum.to_core()
    weight.core_y.wait_recv()
    weight.core_x.wait_recv()
    ahead = lambda n: jnp.where(n < 2, 2 + 2 * n, 2 * n - 1)
    branch_blocks((2, 4, 3, 5), ahead, lambda n: ws.at[:, tile(ahead(n))])
    serve(1)
    heads_sum.fetch()
    heads_sum.add(red_h)
    heads.first()
    heads.direct()
    heads.load()
    sums[0, :, :] = sums_in[...]
    sums[0, 6:7, : pg.shape[1]] = jnp.sum(pg[...].astype(FULL), 0, keepdims=True)
    weight.share_far()

    total = jnp.zeros((tokens, 1), FULL)
    for i in blocks:
        total = total + jnp.sum(x[:, here(i)].astype(FULL), -1, keepdims=True)
    average = total * (1.0 / width)
    total = jnp.zeros((tokens, 1), FULL)
    for i in blocks:
        centred = x[:, here(i)].astype(FULL) - average
        total = total + jnp.sum(centred * centred, -1, keepdims=True)
    inverse = lax.rsqrt(total * (1.0 / width) + NORM_EPS)
    def up_part(i, grad, first):
        cols, spot = tile(i), placed(i)
        normal = (x[:, cols].astype(FULL) - average) * inverse
        row = 0 if first else 2
        sums[0, row : row + 1, spot] = jnp.sum(grad * normal, 0, keepdims=True)
        sums[0, row + 1 : row + 2, spot] = jnp.sum(grad, 0, keepdims=True)
        scaled = grad * (vecs[2:3, cols] if first else vecs[0:1, cols])
        up[:, cols] = (scaled if first else up[:, cols].astype(FULL) + scaled).astype(LOW)

    def first_block(i, slot):
        up_part(i, contract_last(pg[...], room_h[slot]), True)

    stream(8, lambda i, slot: [(wh_hbm.at[tile(i), :], room_h.at[slot])], first_block)
    n2t_load = local.start(n2t_hbm, nt)
    serve(1)
    weight.core_far.wait_recv()
    branch_blocks((6, 7), lambda n: n + 6, lambda n: ws.at[:, tile(n + 6)])
    serve(1)

    def hidden_tile(j, slot):
        cols = tile(j)
        grad = (contract_last(g[...], room_e[slot]) * slope[:, cols].astype(FULL)).astype(LOW)
        slope[:, cols] = grad
        sums[0, 5:6, cols] = jnp.sum(grad.astype(FULL), 0, keepdims=True)

    def shrink_rows(j, slot):
        rows = tile(j)
        pairs = [(weight.here(i).at[rows, :], room_e.at[slot, :, here(i)]) for i in range(2)]
        return pairs + [(ws.at[rows, rest_rows], room_e.at[slot, :, rest_rows])]

    stream(8, shrink_rows, hidden_tile)
    shrink.second()
    serve(2)

    def second_block(i, slot):
        up_part(i, contract_last(slope[...], room_e[slot]), False)

    stream(8, lambda i, slot: [(we_hbm.at[tile(i), :], room_e.at[slot])], second_block)
    line_up.start(*range(line_up.chunks))
    serve(2)

    def share(s, peers):
        return [links.send(sums.at[s], sums_got.at[4 * s + k], peer) for k, peer in enumerate(peers)]

    def shared(s, copies):
        for copy in copies:
            copy.wait_recv()
        total = sums[s, :, :] + sums_got[4 * s, :, :]
        if len(copies) > 1:
            total = total + (sums_got[4 * s + 1, :, :] + sums_got[4 * s + 2, :, :])
        sums[s + 1, :, :] = total

    def share_line(s, peer):
        return links.send(gains.at[s], gains_got.at[s], peer)

    def shared_line(s, copy):
        copy.wait_recv()
        gains[s + 1, :, :] = gains[s, :, :] + gains_got[s, :, :]

    first_share = share(0, [links.core])
    output_sum.to_core()
    heads.second()
    shared(0, first_share)
    second_share = share(1, [links.x, links.y, links.far])
    output_sum.fetch()
    output_sum.add(red_o)
    output.first()
    output.direct()
    output.load()
    serve(1)

    local.wait(n2t_load)
    expand_sum.to_core()
    serve(1)
    expand_sum.fetch()
    expand_sum.add(None)
    red = {k: room_e.at[order.index(k)] for k in range(4)}
    expand = Scattered(links, local, lambda k: red[k], at_rows, unit, via_e, got_e)
    expand.first()
    expand.direct()
    serve(3)
    output.second()
    shared(1, second_share)
    for row in range(4):
        for side in range(2):
            at = 2 * row + side
            gains[0, at : at + 1, :] = sums[2, row : row + 1, side * (width // 2) : (side + 1) * (width // 2)]
    pair_share = share_line(0, links.pair)
    serve(2)
    half_rows = pl.ds(pl.multiple_of(links.r * unit, unit), unit)
    column_slots = Slots(total_columns.at[0], total_columns.at[1])
    total_slots = Slots(total_rows.at[:, pl.ds(0, own_h.shape[1])])
    heads.third(total_slots, heads_grad.at[half_rows, :], unit)
    serve(1)
    shrink.third(column_slots, shrink_grad.at[:, half_rows], total_columns.shape[1])
    serve(1)

    expand.via_x.wait_recv()
    top, end = red[2].at[pl.ds(0, unit // 2), :], red[1].at[pl.ds(unit // 2, unit // 2), :]
    add_rows(top, top, via_e.at[0])
    expand.y_top = links.send(top, got_e.at[1, pl.ds(0, unit // 2), :], links.y)
    expand.via_y.wait_recv()
    add_rows(end, end, via_e.at[1])
    expand.x_end = links.send(end, got_e.at[0, pl.ds(unit // 2, unit // 2), :], links.x)
    serve(2)
    serve(len(steps) - 1 - serve.done)
    shared_line(0, pair_share)
    across_share = share_line(1, links.across)
    serve(len(steps) + 4 - serve.done)
    output.third(column_slots, output_grad.at[:, half_rows], total_columns.shape[1])
    shared_line(1, across_share)
    for row in range(4):
        for side in range(2):
            at = 2 * row + side
            sums_out[row : row + 1, side * (width // 2) : (side + 1) * (width // 2)] = gains[2, at : at + 1, :]
    sums_out[4:8, :] = sums[2, 4:8, :]

    for copy in (expand.x_top, expand.x_end, expand.y_top, expand.y_end):
        copy.wait_recv()
    total_slots.end()
    column_slots.end()
    add_rows(total_rows, red[0], got_e.at[0], got_e.at[1])
    spot = expand_grad.at[half_rows, :]
    local.start(total_rows, spot)
    last = links.send(total_rows, spot, links.core)
    for copy in (*shrink.other, *output.other, *heads.other, last):
        copy.wait_recv()
    links.end()
    line_branch.end()
    line_up.end()
    local.end()


def update_call(line_size, arrays, x, g, expand_weight, shrink_weight, raw, sums):
    tokens, width = x.shape
    expand_full, output_full, heads_full = arrays[:3]
    unit, half = width // 8, width // 16
    units, heads_wide, out_wide = shrink_weight.shape[0], heads_full.shape[1], output_full.shape[0]
    low = lambda *shape: pltpu.VMEM(shape, LOW)
    full = lambda *shape: pltpu.VMEM(shape, FULL)
    work = lambda *shape: jax.ShapeDtypeStruct(shape, LOW)
    outs = [
        work(tokens, width),
        jax.ShapeDtypeStruct((tokens, width), FULL),
        jax.ShapeDtypeStruct((2 * unit, heads_wide), FULL),
        jax.ShapeDtypeStruct((out_wide, 2 * unit), FULL),
        jax.ShapeDtypeStruct((2 * unit, units), FULL),
        jax.ShapeDtypeStruct((units, 2 * unit), FULL),
        work(units, width),
        work(4, units, unit),
        work(4, out_wide, unit),
        work(4, unit, heads_wide),
        work(4, unit, units),
        work(4, units, unit),
        work(4, out_wide, unit),
        work(4, unit, heads_wide),
        jax.ShapeDtypeStruct((8, width), FULL),
    ]
    scratch = [
        low(tokens, width), low(tokens, width), low(tokens, width), low(tokens, units),
        low(units, tokens), low(tokens, units), low(width, tokens), low(tokens, heads_wide),
        low(out_wide, tokens), low(tokens, out_wide), low(out_wide, width),
        low(4, units, unit), low(4, out_wide, unit), low(4, unit, heads_wide),
        *[low(tokens, width)] * 5,
        low(2, half, heads_wide), low(2, unit, heads_wide), low(2, half, heads_wide), low(unit, heads_wide),
        low(2, out_wide, half), low(2, out_wide, unit), low(2, out_wide, half), low(out_wide, unit),
        low(2, units, half), low(2, units, unit),
        low(2, half, units), low(2, unit, units), low(4, unit, units),
        full(unit, units), full(2, out_wide, unit),
        full(2, 32, width), full(4, width), full(3, 8, width), full(7, 8, width), full(3, 8, width // 2), full(2, 8, width // 2),
        pltpu.SemaphoreType.DMA((3, 2)),
        pltpu.SemaphoreType.DMA((8,)),
        pltpu.SemaphoreType.DMA((320,)),
        pltpu.SemaphoreType.DMA((COPIES,)),
        pltpu.SemaphoreType.DMA((COPIES,)),
    ]
    return pl.pallas_call(
        functools.partial(update_kernel, line_size),
        out_shape=outs,
        in_specs=[ANY] * 12 + [IN_VMEM] * 2,
        out_specs=[ANY] * 14 + [IN_VMEM],
        scratch_shapes=scratch,
        compiler_params=pltpu.CompilerParams(
            collective_id=1, has_side_effects=True, vmem_limit_bytes=VMEM_BYTES
        ),
    )(*arrays, x, g, expand_weight, shrink_weight, raw, sums)


def square_local(
    layer_input,
    block_order,
    first_gain,
    first_bias,
    second_gain,
    second_bias,
    heads_weight,
    heads_bias,
    output_weight,
    output_bias,
    expand_weight,
    expand_bias,
    shrink_weight,
    shrink_bias,
    cotangent,
):
    width = layer_input.shape[2]
    heads_rows = heads_weight.reshape(heads_weight.shape[0], -1)
    output_rows = output_weight.reshape(-1, output_weight.shape[2])
    wide = heads_rows.shape[1]
    pieces = [first_gain, first_bias, second_gain, second_bias, expand_bias, heads_bias.reshape(-1)]
    pieces += [jnp.zeros((width - wide,), LOW), output_bias, shrink_bias]
    raw = jnp.concatenate([piece.astype(FULL) for piece in pieces]).reshape(8, width)
    *kept, sums = attend_call(
        layer_input[0], cotangent[0], heads_rows, output_rows, expand_weight, raw, block_order
    )
    layer_output, input_grad, heads_grad, output_grad, expand_weight_grad, shrink_weight_grad, *_, sums = update_call(
        lax.axis_size("tensor"), kept, layer_input[0], cotangent[0], expand_weight, shrink_weight, raw, sums
    )
    return (
        layer_output[None],
        input_grad[None],
        sums[0],
        sums[1],
        sums[2],
        sums[3],
        heads_grad.reshape(heads_weight.shape),
        sums[6, :wide].reshape(heads_bias.shape),
        output_grad.reshape(output_weight.shape),
        sums[4],
        expand_weight_grad,
        sums[5],
        shrink_weight_grad,
        sums[4],
    )


def ring_local(
    layer_input,
    block_order,
    first_gain,
    first_bias,
    second_gain,
    second_bias,
    heads_weight,
    heads_bias,
    output_weight,
    output_bias,
    expand_weight,
    expand_bias,
    shrink_weight,
    shrink_bias,
    cotangent,
):
    tokens_here = layer_input.shape[1]
    fsdp_count = lax.axis_size("fsdp")
    head_dim = output_weight.shape[1]
    score_scale = head_dim ** (-0.5)
    order_row = block_order[0]
    device_slot = lax.axis_index("fsdp")
    own_block = jnp.sum(
        jnp.where(jnp.arange(fsdp_count, dtype=jnp.int32) == device_slot, order_row, 0)
    )
    offsets = jnp.arange(tokens_here, dtype=jnp.int32)
    query_pos = own_block * tokens_here + offsets
    key_pos = jnp.repeat(order_row, tokens_here) * tokens_here + jnp.tile(offsets, fsdp_count)
    allowed = key_pos[None, :] <= query_pos[:, None]
    cosine, sine_part = rotary_tables(query_pos, ROT)
    hidden_in = layer_input[0].astype(jnp.float32)
    gain_one = first_gain.astype(jnp.float32)
    shift_one = first_bias.astype(jnp.float32)
    gain_two = second_gain.astype(jnp.float32)
    shift_two = second_bias.astype(jnp.float32)
    norm_one_low = layer_norm(hidden_in, gain_one, shift_one).astype(jnp.bfloat16)
    norm_two_low = layer_norm(hidden_in, gain_two, shift_two).astype(jnp.bfloat16)
    heads_full, output_full, expand_full, shrink_full = (
        lax.all_gather(heads_weight, "fsdp", axis=0, tiled=True),
        lax.all_gather(output_weight, "fsdp", axis=2, tiled=True),
        lax.all_gather(expand_weight, "fsdp", axis=0, tiled=True),
        lax.all_gather(shrink_weight, "fsdp", axis=1, tiled=True),
    )
    projected = jnp.einsum(
        "td,dhe->hte", norm_one_low, heads_full, preferred_element_type=jnp.float32
    )
    projected = projected + heads_bias.astype(jnp.float32)[:, None, :]
    query_pre = projected[..., :head_dim]
    key_pre = projected[..., head_dim : 2 * head_dim]
    query_low = rotate(query_pre, cosine, sine_part).astype(jnp.bfloat16)
    key_low = rotate(key_pre, cosine, sine_part).astype(jnp.bfloat16)
    value_low = projected[..., 2 * head_dim :].astype(jnp.bfloat16)
    key_all, value_all = (
        lax.all_gather(key_low, "fsdp", axis=1, tiled=True),
        lax.all_gather(value_low, "fsdp", axis=1, tiled=True),
    )

    def attend_head(operands):
        query_head, key_head, value_head = operands
        probability = softmax_rows(contract_last(query_head, key_head) * score_scale, allowed)
        return jnp.dot(
            probability.astype(jnp.bfloat16), value_head, preferred_element_type=jnp.float32
        )

    context = lax.map(attend_head, (query_low, key_all, value_all))
    context_low = context.astype(jnp.bfloat16)
    expand_in = jnp.dot(
        norm_two_low, expand_full, preferred_element_type=jnp.float32
    ) + expand_bias.astype(jnp.float32)
    activation_low = jax.nn.gelu(expand_in, approximate=False).astype(jnp.bfloat16)
    branch_part = jnp.einsum(
        "hte,hed->td", context_low, output_full, preferred_element_type=jnp.float32
    )
    branch_part = branch_part + jnp.dot(
        activation_low, shrink_full, preferred_element_type=jnp.float32
    )
    branch = lax.psum(branch_part, "tensor")
    layer_output = (
        hidden_in + branch + output_bias.astype(jnp.float32) + shrink_bias.astype(jnp.float32)
    ).astype(jnp.bfloat16)[None]
    heads_back, output_back, expand_back, shrink_back = (
        lax.all_gather(heads_weight, "fsdp", axis=0, tiled=True),
        lax.all_gather(output_weight, "fsdp", axis=2, tiled=True),
        lax.all_gather(expand_weight, "fsdp", axis=0, tiled=True),
        lax.all_gather(shrink_weight, "fsdp", axis=1, tiled=True),
    )
    key_back, value_back = (
        lax.all_gather(key_low, "fsdp", axis=1, tiled=True),
        lax.all_gather(value_low, "fsdp", axis=1, tiled=True),
    )
    grad_out = cotangent[0]
    grad_float = grad_out.astype(jnp.float32)
    output_weight_grad = jnp.einsum(
        "hte,td->hed", context_low, grad_out, preferred_element_type=jnp.float32
    )
    shrink_weight_grad = contract_first(activation_low, grad_out)
    bias_total = jnp.sum(grad_float, 0)
    context_grad = jnp.einsum(
        "td,hed->hte", grad_out, output_back, preferred_element_type=jnp.float32
    ).astype(jnp.bfloat16)
    activation_grad = contract_last(grad_out, shrink_back)
    _, gelu_back = jax.vjp(lambda inner_val: jax.nn.gelu(inner_val, approximate=False), expand_in)
    expand_grad = gelu_back(activation_grad)[0].astype(jnp.bfloat16)
    expand_weight_grad = contract_first(norm_two_low, expand_grad)
    expand_bias_grad = jnp.sum(expand_grad.astype(jnp.float32), 0)
    norm_two_grad = contract_last(expand_grad, expand_back)

    def attend_back(operands):
        query_head, key_head, value_head, context_head = operands
        probability = softmax_rows(contract_last(query_head, key_head) * score_scale, allowed)
        prob_low = probability.astype(jnp.bfloat16)
        weight_grad = contract_last(context_head, value_head)
        row_inner = jnp.sum(probability * weight_grad, -1, keepdims=True)
        score_grad = (probability * (weight_grad - row_inner)).astype(jnp.bfloat16)
        query_grad = jnp.dot(score_grad, key_head, preferred_element_type=jnp.float32) * score_scale
        key_grad = contract_first(score_grad, query_head) * score_scale
        value_grad = contract_first(prob_low, context_head)
        return (query_grad, key_grad, value_grad)

    query_grad, key_grad_all, value_grad_all = lax.map(
        attend_back, (query_low, key_back, value_back, context_grad)
    )
    key_grad, value_grad = (
        lax.psum_scatter(key_grad_all, "fsdp", scatter_dimension=1, tiled=True),
        lax.psum_scatter(value_grad_all, "fsdp", scatter_dimension=1, tiled=True),
    )
    _, rotate_back = jax.vjp(lambda inner_val: rotate(inner_val, cosine, sine_part), query_pre)
    projected_grad = jnp.concatenate(
        [rotate_back(query_grad)[0], rotate_back(key_grad)[0], value_grad], -1
    ).astype(jnp.bfloat16)
    heads_weight_grad = jnp.einsum(
        "td,hte->dhe", norm_one_low, projected_grad, preferred_element_type=jnp.float32
    )
    heads_bias_grad = jnp.sum(projected_grad.astype(jnp.float32), 1)
    norm_one_grad = jnp.einsum(
        "hte,dhe->td", projected_grad, heads_back, preferred_element_type=jnp.float32
    )
    norm_one_grad, norm_two_grad = lax.psum((norm_one_grad, norm_two_grad), "tensor")
    _, first_back = jax.vjp(layer_norm, hidden_in, gain_one, shift_one)
    input_first, first_gain_grad, first_bias_grad = first_back(norm_one_grad)
    _, second_back = jax.vjp(layer_norm, hidden_in, gain_two, shift_two)
    input_second, second_gain_grad, second_bias_grad = second_back(norm_two_grad)
    input_grad = (grad_float + input_first + input_second)[None]
    small_sums = lax.psum(
        (
            first_gain_grad,
            first_bias_grad,
            second_gain_grad,
            second_bias_grad,
            bias_total,
            expand_bias_grad,
            heads_bias_grad,
        ),
        ("replica", "fsdp"),
    )
    shard_parts = (
        lax.psum_scatter(heads_weight_grad, "fsdp", scatter_dimension=0, tiled=True),
        lax.psum_scatter(output_weight_grad, "fsdp", scatter_dimension=2, tiled=True),
        lax.psum_scatter(expand_weight_grad, "fsdp", scatter_dimension=0, tiled=True),
        lax.psum_scatter(shrink_weight_grad, "fsdp", scatter_dimension=1, tiled=True),
    )
    reduced = lax.psum((shard_parts[0], shard_parts[1], shard_parts[2], shard_parts[3]), "replica")
    return (
        layer_output,
        input_grad,
        small_sums[0],
        small_sums[1],
        small_sums[2],
        small_sums[3],
        reduced[0],
        small_sums[6],
        reduced[1],
        small_sums[4],
        reduced[2],
        small_sums[5],
        reduced[3],
        small_sums[4],
    )


def solution(mesh):
    placed = (
        P("replica", "fsdp", None),
        P("replica", None),
        P(),
        P(),
        P(),
        P(),
        P("fsdp", "tensor", None),
        P("tensor", None),
        P("tensor", None, "fsdp"),
        P(),
        P("fsdp", "tensor"),
        P("tensor"),
        P("tensor", "fsdp"),
        P(),
        P("replica", "fsdp", None),
    )
    local = square_local if mesh.shape["fsdp"] == 4 and mesh.shape["replica"] == 2 and mesh.shape["tensor"] == 4 else ring_local
    return jax.shard_map(
        local,
        mesh=mesh,
        in_specs=placed,
        out_specs=(
            P("replica", "fsdp", None),
            P("replica", "fsdp", None),
            P(),
            P(),
            P(),
            P(),
            P("fsdp", "tensor", None),
            P("tensor", None),
            P("tensor", None, "fsdp"),
            P(),
            P("fsdp", "tensor"),
            P("tensor"),
            P("tensor", "fsdp"),
            P(),
        ),
        check_vma=False,
    )
```

```python
import functools
import math

import jax
import jax.numpy as jnp
from jax import lax
from jax.experimental import pallas as pl
from jax.experimental.pallas import tpu as pltpu
from jax.sharding import PartitionSpec as P

ROT = 64


NORM_EPS = 1e-05
MASKED = -1e30


def layer_norm(values_in, gain_vec, shift_vec):
    average = jnp.mean(values_in, -1, keepdims=True)
    centred = values_in - average
    spread_sq = jnp.mean(centred * centred, -1, keepdims=True)
    return centred * lax.rsqrt(spread_sq + NORM_EPS) * gain_vec + shift_vec


def rotate(values_in, cosine, sine_part):
    rot_width = cosine.shape[-1]
    half_width = rot_width // 2
    turning = values_in[..., :rot_width]
    swapped = jnp.concatenate([-turning[..., half_width:], turning[..., :half_width]], -1)
    return jnp.concatenate([turning * cosine + swapped * sine_part, values_in[..., rot_width:]], -1)


def rotary_tables(positions, rot_width):
    frequency = jnp.power(10000.0, -jnp.arange(0, rot_width, 2, dtype=jnp.float32) / rot_width)
    angle_half = positions.astype(jnp.float32)[:, None] * frequency[None, :]
    angles = jnp.concatenate([angle_half, angle_half], -1)
    return (jnp.cos(angles), jnp.sin(angles))


def contract_last(left_op, right_op):
    return lax.dot_general(
        left_op, right_op, (((1,), (1,)), ((), ())), preferred_element_type=jnp.float32
    )


def contract_first(left_op, right_op):
    return lax.dot_general(
        left_op, right_op, (((0,), (0,)), ((), ())), preferred_element_type=jnp.float32
    )


def softmax_rows(scores, allowed):
    masked_scores = jnp.where(allowed, scores, MASKED)
    row_top = jnp.max(masked_scores, -1, keepdims=True)
    exponent = jnp.exp(masked_scores - row_top)
    return exponent / jnp.sum(exponent, -1, keepdims=True)


LOW = jnp.bfloat16
FULL = jnp.float32


MESH = pl.DeviceIdType.MESH
ANY = pl.BlockSpec(memory_space=pl.ANY)
IN_VMEM = pl.BlockSpec(memory_space=pltpu.VMEM)
VMEM_BYTES = 63 * 2**20
COPIES = 224


class Sent:
    def __init__(self, links, k, source, target, peer):
        self.links, self.k, self.source, self.target, self.peer = links, k, source, target, peer

    def copy(self):
        return self.links.copy_at(self.k, self.source, self.target, self.peer)

    def start(self):
        self.copy().start()

    def wait_recv(self):
        self.copy().wait_recv()

    def wait_send(self):
        self.copy().wait_send()


class Links:
    def __init__(self, send_sem, recv_sem, line=0):
        self.send_sem, self.recv_sem, self.sent, self.count = send_sem, recv_sem, [], 0
        self.r, self.f, self.t = (lax.axis_index(name) for name in ("replica", "fsdp", "tensor"))
        self.xb, self.yb = lax.rem(self.f, 2), lax.div(self.f, 2)
        self.x = (self.r, self.f + 1 - 2 * self.xb, self.t)
        self.y = (self.r, lax.rem(self.f + 2, 4), self.t)
        self.core = (1 - self.r, self.f, self.t)
        self.peers = [self.x, self.y, self.core]
        if line:
            self.line = line
            self.left, self.right, self.across = (
                (self.r, self.f, lax.rem(self.t + step, line)) for step in (line - 1, 1, 2)
            )
            self.pair = (self.r, self.f, self.t + 1 - 2 * lax.rem(self.t, 2))
            self.far = (self.r, 3 - self.f, self.t)
            self.mirror = (self.r, self.f, line - 1 - self.t)
            self.peers += [self.far, self.left, self.right, self.across]

    def meet(self):
        barrier = pltpu.get_barrier_semaphore()
        for peer in self.peers:
            pl.semaphore_signal(barrier, inc=1, device_id=peer, device_id_type=MESH)
        pl.semaphore_wait(barrier, len(self.peers))

    def prepare(self, source, target, peer):
        self.count += 1
        return Sent(self, self.count - 1, source, target, peer)

    def send(self, source, target, peer):
        copy = self.prepare(source, target, peer)
        copy.start()
        self.sent.append(copy)
        return copy

    def series(self, count):
        k = self.count
        self.count += count
        return k

    def copy_at(self, k, source, target, peer):
        return pltpu.make_async_remote_copy(
            src_ref=source,
            dst_ref=target,
            send_sem=self.send_sem.at[k],
            recv_sem=self.recv_sem.at[k],
            device_id=peer,
            device_id_type=MESH,
        )

    def sent_out(self, copy):
        copy.wait_send()
        self.sent = [other for other in self.sent if other is not copy]

    def end(self):
        for copy in self.sent:
            copy.wait_send()

    def block(self, i):
        place = 0
        for size, bit in ((4, self.yb), (2, self.xb), (1, self.r)):
            mine = lax.rem(lax.div(i, size), 2) if isinstance(i, jax.Array) else i // size % 2
            place = place + size * (mine + bit - 2 * mine * bit)
        return place


class Local:
    def __init__(self, sem):
        self.sem, self.count, self.open = sem, 0, []

    def start(self, source, target):
        copy = pltpu.make_async_copy(source, target, self.sem.at[self.count])
        self.count += 1
        copy.start()
        self.open.append(copy)
        return copy

    def wait(self, *copies):
        for copy in copies:
            copy.wait()
            self.open = [other for other in self.open if other is not copy]

    def end(self):
        self.wait(*list(self.open))


def at_rows(ref, start, size):
    return ref.at[pl.ds(start, size), :]


def at_columns(ref, start, size):
    return ref.at[:, pl.ds(start, size)]


class Gathered:
    def __init__(self, links, local, shard, full, cut, unit, copied=True):
        self.links, self.local, self.full, self.cut = links, local, full, cut
        self.shard, self.unit, self.half = shard, unit, unit // 2
        self.starts = [pl.multiple_of(links.r * unit + start, self.half) for start in (0, self.half)]
        self.bases = [pl.multiple_of(base * unit, unit) for base in (links.r, 1 - links.r)]
        self.copies = [local.start(self.here(i), self.at(i)) for i in range(2)] if copied else []
        self.from_x, self.from_y = {}, {}

    def here(self, i):
        return self.cut(self.shard, self.bases[i], self.unit)

    def mine(self, lower):
        return self.cut(self.shard, self.starts[lower], self.half)

    def at(self, block, start=0, size=None):
        return self.cut(self.full, block * self.unit + start, self.unit if size is None else size)

    def to_x(self, lower):
        source, target = self.mine(lower), self.at(2, self.half * lower, self.half)
        self.from_x[lower] = self.links.send(source, target, self.links.x)

    def to_y(self, lower):
        source, target = self.mine(lower), self.at(4, self.half * lower, self.half)
        self.from_y[lower] = self.links.send(source, target, self.links.y)

    def first(self):
        self.to_x(False)
        self.to_y(True)

    def rest(self):
        self.to_x(True)
        self.to_y(False)

    def pass_y(self):
        half = self.half
        self.from_x[False].wait_recv()
        self.far_top = self.links.send(self.at(2, 0, half), self.at(6, 0, half), self.links.y)

    def pass_x(self):
        half = self.half
        self.from_y[True].wait_recv()
        self.far_end = self.links.send(self.at(4, half, half), self.at(6, half, half), self.links.x)

    def relay(self):
        self.pass_y()
        self.pass_x()

    def share(self):
        self.from_y[False].wait_recv()
        self.core_y = self.links.send(self.at(4), self.at(5), self.links.core)
        self.from_x[True].wait_recv()
        self.core_x = self.links.send(self.at(2), self.at(3), self.links.core)

    def share_far(self):
        self.far_top.wait_recv()
        self.far_end.wait_recv()
        self.core_far = self.links.send(self.at(6), self.at(7), self.links.core)

    def passed(self):
        for copy in (self.far_top, self.far_end, self.core_x, self.core_y, self.core_far):
            self.links.sent_out(copy)

    def whole(self):
        self.local.wait(*self.copies)
        for copy in (self.core_x, self.core_y, self.core_far):
            copy.wait_recv()


def odd(j):
    return j % 2 if isinstance(j, int) else lax.rem(j, 2)


def tile_of(j, size):
    return pl.ds(pl.multiple_of(j * size, size), size)


def dot(left, right):
    return jnp.dot(left, right, preferred_element_type=FULL)


def spin(values_in, cosine, sine):
    head = values_in[:, :128]
    lane = lax.broadcasted_iota(jnp.int32, head.shape, 1)
    swapped = jnp.where(lane < ROT // 2, pltpu.roll(head, 96, 1), pltpu.roll(head, 32, 1))
    return jnp.concatenate([head * cosine + swapped * sine, values_in[:, 128:]], -1)


class Scattered:
    def __init__(self, links, local, blocks, cut, unit, via, got, stage=None, own=None):
        self.links, self.local, self.blocks, self.cut, self.unit = links, local, blocks, cut, unit
        self.via, self.got = [via.at[n] for n in range(2)], [got.at[n] for n in range(2)]
        self.stage, self.own = stage, own
        self.half, self.loads = unit // 2, []

    def load(self):
        self.loads = [
            self.local.start(self.cut(self.blocks[1], self.half, self.half), self.stage[0]),
            self.local.start(self.cut(self.blocks[2], 0, self.half), self.stage[1]),
            self.local.start(self.blocks[0], self.own),
        ]

    def first(self):
        half, cut, far = self.half, self.cut, self.blocks[3]
        self.via_x = self.links.send(cut(far, 0, half), self.via[0], self.links.x)
        self.via_y = self.links.send(cut(far, half, half), self.via[1], self.links.y)

    def direct(self):
        half, cut = self.half, self.cut
        self.x_top = self.links.send(cut(self.blocks[1], 0, half), cut(self.got[0], 0, half), self.links.x)
        self.y_end = self.links.send(cut(self.blocks[2], half, half), cut(self.got[1], half, half), self.links.y)

    def second(self):
        half, cut = self.half, self.cut
        self.local.wait(*self.loads[:2])
        self.via_x.wait_recv()
        add_rows(self.stage[1], self.stage[1], self.via[0])
        self.y_top = self.links.send(self.stage[1], cut(self.got[1], 0, half), self.links.y)
        self.via_y.wait_recv()
        add_rows(self.stage[0], self.stage[0], self.via[1])
        self.x_end = self.links.send(self.stage[0], cut(self.got[0], half, half), self.links.x)

    def third(self, slots, place, step, between=lambda: None):
        for copy in (self.x_top, self.x_end, self.y_top, self.y_end):
            copy.wait_recv()
        if self.loads:
            self.local.wait(self.loads[2])
        self.other = []
        for start in range(0, self.own.shape[0], step):
            between()
            rows = pl.ds(start, step)
            at, total = slots.take()
            add_rows(total, self.own.at[rows, :], self.got[0].at[rows, :], self.got[1].at[rows, :])
            kept = self.local.start(total, place.at[rows, :])
            other = self.links.send(total, place.at[rows, :], self.links.core)
            self.other.append(other)

            def done(kept=kept, other=other):
                self.local.wait(kept)
                self.links.sent_out(other)

            slots.busy[at] = done


def add_rows(target, *parts):
    rows, wide = target.shape
    step = min(rows, 32 if wide > 512 else 256)

    def one(c, carry):
        at = pl.ds(pl.multiple_of(c * step, step), step)
        total = parts[0][at, :].astype(FULL)
        for part in parts[1:]:
            total = total + part[at, :].astype(FULL)
        target[at, :] = total.astype(target.dtype)
        return carry

    lax.fori_loop(0, rows // step, one, 0)


class Line:
    def __init__(self, links, part, got, final, chunks, cut, finish):
        self.links, self.part, self.got, self.final, self.cut, self.finish = links, part, got, final, cut, finish
        self.chunks = chunks
        self.outer = jnp.logical_or(links.t == 0, links.t == links.line - 1)
        self.middle = jnp.logical_not(self.outer)
        self.inward = [self.make(c, part, final, links.pair) for c in range(chunks)]
        self.across = [self.make(c, part, got, links.mirror) for c in range(chunks)]
        self.outward = [self.make(c, final, final, links.pair) for c in range(chunks)]

    def make(self, c, source, target, peer):
        return self.links.prepare(self.cut(source, c), self.cut(target, c), peer)

    def start(self, *chunks):
        @pl.when(self.outer)
        def _():
            for c in chunks:
                self.inward[c].start()

    def first(self, c):
        @pl.when(self.middle)
        def _():
            self.inward[c].wait_recv()
            part = self.cut(self.part, c)
            add_rows(part, part, self.cut(self.final, c))
            self.across[c].start()

    def second(self, c):
        @pl.when(self.middle)
        def _():
            self.across[c].wait_recv()
            self.finish(c)
            self.outward[c].start()

    def third(self, c):
        @pl.when(self.outer)
        def _():
            self.outward[c].wait_recv()

    def end(self):
        @pl.when(self.outer)
        def _():
            for copy in self.inward:
                copy.wait_send()

        @pl.when(self.middle)
        def _():
            for copy in self.across + self.outward:
                copy.wait_send()


class Slots:
    def __init__(self, *refs):
        self.refs, self.busy, self.count = refs, {}, 0

    def take(self):
        at = self.count % len(self.refs)
        self.count += 1
        if at in self.busy:
            self.busy.pop(at)()
        return at, self.refs[at]

    def end(self):
        for wait in self.busy.values():
            wait()
        self.busy = {}


def block_kernel(
    score_scale, line_size,
    x_hbm, g_hbm, wh_hbm, wo_hbm, we_own, ws_own, raw, order,
    layer_out, input_grad, heads_grad, output_grad, expand_grad, shrink_grad, we, ws, n2t_hbm, got_core_s, got_core_o,
    got_core_h, got_core_e, red_s, red_o, red_h, sums_out,
    x, g, up, n1, nt, stat, wh, wo, qkv, dctx, ctxt, pg, kvg_got, got_branch, final_branch, got_up, final_up,
    via_h, got_h, via_o, got_o, via_s, got_s, via_e, got_e, vecs, sums, sums_got, gains, gains_got,
    loop_sem, block_sem, local_sem, send_sem, recv_sem,
):
    links, local = Links(send_sem, recv_sem, line_size), Local(local_sem)
    tokens, width = x.shape
    units, heads_wide, out_wide = we.shape[1], wh.shape[1], wo.shape[0]
    hd = dctx.shape[1]
    unit = width // 8
    blocks = range(8)
    room_s = qkv
    place = [pl.ds(pl.multiple_of(links.block(i) * unit, unit), unit) for i in blocks]

    def here(i):
        return pl.ds(i * unit, unit)

    rest_rows = pl.ds(2 * unit, width - 2 * unit)

    def tile(j):
        return pl.ds(j * unit if isinstance(j, int) else pl.multiple_of(j * unit, unit), unit)

    def placed(i):
        return pl.ds(pl.multiple_of(links.block(i) * unit, unit), unit)

    def stream(start, end, load, body):
        def copies(j):
            pairs = load(j, odd(j))
            return [pltpu.make_async_copy(*pair, loop_sem.at[n, odd(j)]) for n, pair in enumerate(pairs)]

        for copy in copies(start):
            copy.start()

        def one(j, carry):
            @pl.when(j + 1 < end)
            def _():
                for copy in copies(j + 1):
                    copy.start()

            for copy in copies(j):
                copy.wait()
            body(j, odd(j))
            return carry

        lax.fori_loop(start, end, one, 0)

    x_in, g_in = [], []
    for i in blocks:
        cols = pl.ds(pl.multiple_of(links.block(i) * unit, unit), unit)
        x_in.append(local.start(x_hbm.at[:, cols], x.at[:, pl.ds(i * unit, unit)]))
        g_in.append(local.start(g_hbm.at[:, cols], g.at[:, pl.ds(i * unit, unit)]))
    links.meet()
    heads_in = Gathered(links, local, wh_hbm, wh, at_rows, unit)
    output_in = Gathered(links, local, wo_hbm, wo, at_columns, unit)
    expand = Gathered(links, local, we_own, we, at_rows, unit)
    weight = Gathered(links, local, ws_own, ws, at_columns, unit, False)
    heads_in.first()
    heads_in.rest()

    turns = (3, 1, 2, 0)

    def turn_of(n):
        return jnp.where(n == 0, 3, jnp.where(n == 3, 0, n))

    class Reduced:
        def __init__(self, room, got, block):
            self.room, self.got, self.block = room, got, block
            self.gots = [got.at[k] for k in range(4)]

        def to_core(self):
            first = links.series(4)

            def one(n, carry):
                k = turn_of(n)
                self.block(2 * k + 1, self.room(n), False)
                links.copy_at(first + n, self.room(n), self.got.at[k], links.core).start()
                return carry

            lax.fori_loop(0, 4, one, 0)
            self.copies = [Sent(links, first + n, self.room(n), self.gots[turns[n]], links.core) for n in range(4)]

        def fetch(self):
            for n in range(4):
                self.copies[n].wait_send()
                self.copies[n].wait_recv()
                pltpu.make_async_copy(self.got.at[turns[n]], self.room(n), block_sem.at[n]).start()

        def add(self, red):
            def one(n, carry):
                k = turn_of(n)
                pltpu.make_async_copy(self.got.at[k], self.room(n), block_sem.at[n]).wait()
                self.block(2 * k, self.room(n), True)
                if red is not None:
                    pltpu.make_async_copy(self.room(n), red.at[k], block_sem.at[4 + n]).start()
                return carry

            lax.fori_loop(0, 4, one, 0)
            if red is not None:
                for n in range(4):
                    pltpu.make_async_copy(self.room(n), red.at[turns[n]], block_sem.at[4 + n]).wait()

    def product(left, right, ref, add):
        part = dot(left, right)
        if add:
            part = part + ref[...].astype(FULL)
        ref[...] = part.astype(LOW)

    def heads_block(i, ref, add):
        product(nt[tile(i), :], pg[...], ref, add)

    heads_sum = Reduced(lambda n: wh.at[tile(n), :], got_core_h, heads_block)
    own_h = at_rows(wh, 4 * unit, unit)
    stage_h = (at_rows(wh, 5 * unit, unit // 2), at_rows(wh, 5 * unit + unit // 2, unit // 2))
    heads = Scattered(links, local, [red_h.at[k] for k in range(4)], at_rows, unit, via_h, got_h, stage_h, own_h)
    shrink = Scattered(links, local, [red_s.at[k] for k in range(4)], at_columns, unit, via_s, got_s)
    output = Scattered(links, local, [red_o.at[k] for k in range(4)], at_columns, unit, via_o, got_o)

    def up_part(i, grad, first):
        cols, spot = tile(i), placed(i)
        normal = (x[:, cols].astype(FULL) - stat[:, 0:1]) * stat[:, 128:129]
        row = 0 if first else 2
        sums[0, row : row + 1, spot] = jnp.sum(grad * normal, 0, keepdims=True)
        sums[0, row + 1 : row + 2, spot] = jnp.sum(grad, 0, keepdims=True)
        scaled = grad * (vecs[0:1, cols] if first else vecs[2:3, cols])
        n1[:, cols] = (scaled if first else n1[:, cols].astype(FULL) + scaled).astype(LOW)

    def attend(qkv_away, dctx_away, ctxt_all, pgq, pg_away, kvg_away, cosine, sines, dk, dv, stage):
        for i in blocks:
            cols = pl.ds(pl.multiple_of(links.block(i) * unit, unit), unit)
            vecs[0:4, i * unit : (i + 1) * unit] = raw[0:4, cols]
            vecs[4:5, i * unit : (i + 1) * unit] = raw[6:7, cols] + raw[7:8, cols]
        local.wait(*x_in)

        def norm_rows(c, carry):
            rows = tile_of(c, 64)
            value = x[rows, :].astype(FULL)
            average = jnp.mean(value, -1, keepdims=True)
            centred = value - average
            inverse = lax.rsqrt(jnp.mean(centred * centred, -1, keepdims=True) + NORM_EPS)
            normal = centred * inverse
            both = [jnp.broadcast_to(part, (64, 128)) for part in (average, inverse)]
            stat[rows, :] = jnp.concatenate(both, -1)
            n1[rows, :] = (normal * vecs[0:1, :] + vecs[1:2, :]).astype(LOW)
            up[rows, :] = (normal * vecs[2:3, :] + vecs[3:4, :]).astype(LOW)
            return carry

        lax.fori_loop(0, tokens // 64, norm_rows, 0)
        bases = [
            order[0, (links.yb if step < 2 else 1 - links.yb) * 2 + (links.xb if step % 2 == 0 else 1 - links.xb)]
            * tokens
            for step in (0, 2, 1, 3)
        ]

        def table_rows(c, carry):
            rows = tile_of(c, 64)
            lane = lax.broadcasted_iota(jnp.int32, (64, 128), 1)
            row = lax.broadcasted_iota(jnp.int32, (64, 128), 0) + c * 64
            spot = row + jnp.where(row < tokens, bases[0], bases[1] - tokens)
            pace = jnp.exp(lax.rem(lane, ROT // 2).astype(FULL) * (-2.0 / ROT * math.log(10000.0)))
            angle = spot.astype(FULL) * pace
            sine = jnp.sin(angle)
            cosine[rows, :] = jnp.where(lane < ROT, jnp.cos(angle), 1.0)
            sines[rows, :] = jnp.where(lane < ROT // 2, -sine, jnp.where(lane < ROT, sine, 0.0))
            return carry

        lax.fori_loop(0, 2 * tokens // 64, table_rows, 0)
        heads_in.relay()
        output_in.first()
        output_in.rest()

        def turned_copy(j):
            slot = odd(j)
            return pltpu.make_async_copy(stage.at[slot], n2t_hbm.at[tile_of(j, unit), :], loop_sem.at[0, slot])

        def turn_tiles(j, carry):
            cols = tile_of(j, unit)
            nt[cols, :] = n1[:, cols].T

            @pl.when(j >= 2)
            def _():
                turned_copy(j - 2).wait()

            stage[odd(j), :, :] = up[:, cols].T
            turned_copy(j).start()
            return carry

        lax.fori_loop(0, 8, turn_tiles, 0)
        for j in (6, 7):
            turned_copy(j).wait()
        sums[0, :, :] = jnp.zeros(sums.shape[1:], FULL)
        local.wait(*g_in)
        for i in blocks:
            cols = pl.ds(pl.multiple_of(links.block(i) * unit, unit), unit)
            sums[0, 4:5, cols] = jnp.sum(g[:, i * unit : (i + 1) * unit].astype(FULL), 0, keepdims=True)
        heads_in.share()
        heads_in.share_far()
        heads_in.whole()
        output_in.relay()

        own, away = links.yb * 3 * hd, (1 - links.yb) * 3 * hd

        def project(c, start, target):
            cols = pl.ds(pl.multiple_of(start + c * hd, hd), hd)
            value = dot(n1[...], wh[:, cols]) + raw[5:6, cols]
            if c < 2:
                value = spin(value, cosine[:tokens, :], sines[:tokens, :])
            target[c, :tokens, :] = value.astype(LOW)

        def place_of(c, part):
            return qkv.at[c, pl.ds(part * tokens, tokens), :]

        from_y, from_x, from_far = {}, {}, {}
        for c in (1, 2, 0):
            project(c, away, qkv_away)
            from_y[c] = links.send(qkv_away.at[c], place_of(c, 1), links.y)
        for c in (1, 2):
            project(c, own, qkv)
            from_x[c] = links.send(place_of(c, 0), place_of(c, 2), links.x)
        from_y[1].wait_recv()
        from_far[1] = links.send(place_of(1, 1), place_of(1, 3), links.x)
        project(0, own, qkv)
        output_in.share()
        output_in.share_far()
        from_y[2].wait_recv()
        from_far[2] = links.send(place_of(2, 1), place_of(2, 3), links.x)
        output_in.whole()
        rows_own = pl.ds(pl.multiple_of(links.yb * hd, hd), hd)
        rows_away = pl.ds(pl.multiple_of((1 - links.yb) * hd, hd), hd)
        dctx_away[...] = contract_last(g[...], wo[rows_away, :]).astype(LOW)
        dctx_from_y = links.send(dctx_away, dctx.at[pl.ds(tokens, tokens), :], links.y)
        dctx[:tokens, :] = contract_last(g[...], wo[rows_own, :]).astype(LOW)
        expand.first()
        expand.to_y(False)
        for copy in (from_y[0], dctx_from_y, *from_x.values(), *from_far.values()):
            copy.wait_recv()

        def attention(kt, vt, prob, wgt, prob_low, grad_low):
            keys = qkv.shape[1]
            step = tokens
            lag = lax.broadcasted_iota(jnp.int32, (step, hd), 0) - lax.broadcasted_iota(jnp.int32, (step, hd), 1)
            parts = [pl.ds(i * step, step) for i in range(keys // step)]
            for part in parts:
                kt[:, part] = qkv[1, part, :].T
                vt[:, part] = qkv[2, part, :].T
            dk[...] = jnp.zeros_like(dk)
            dv[...] = jnp.zeros_like(dv)

            def one(b, carry):
                rows = tile_of(b, hd)
                query, grad = qkv[0, rows, :], dctx[rows, :]
                ahead = jnp.where(b < tokens // hd, bases[0], bases[1] - tokens) + b * hd
                top = jnp.full((1, hd), MASKED, FULL)
                for i, part in enumerate(parts):
                    scores = contract_last(qkv[1, part, :], query) * score_scale
                    scores = jnp.where(lag <= ahead - bases[i], scores, MASKED)
                    prob[part, :] = scores
                    top = jnp.maximum(top, jnp.max(scores, 0, keepdims=True))
                total = jnp.zeros((1, hd), FULL)
                for part in parts:
                    exponent = jnp.exp(prob[part, :] - top)
                    prob[part, :] = exponent
                    total = total + jnp.sum(exponent, 0, keepdims=True)
                share = 1.0 / total
                inner = jnp.zeros((1, hd), FULL)
                for part in parts:
                    weight = contract_last(qkv[2, part, :], grad)
                    chance = prob[part, :] * share
                    prob[part, :] = chance
                    prob_low[part, :] = chance.astype(LOW)
                    wgt[part, :] = weight
                    inner = inner + jnp.sum(chance * weight, 0, keepdims=True)
                for part in parts:
                    grad_low[part, :] = (prob[part, :] * (wgt[part, :] - inner)).astype(LOW)
                ctxt_all[:, rows] = dot(vt[...], prob_low[...]).astype(LOW)
                query_grad = dot(kt[...], grad_low[...]) * score_scale
                for part in parts:
                    dv[part, :] += dot(prob_low[part, :], grad)
                    dk[part, :] += dot(grad_low[part, :], query)
                turned_grad = spin(query_grad.T, cosine[rows, :], -sines[rows, :])
                pgq[rows, :] = turned_grad.astype(LOW)
                return carry

            lax.fori_loop(0, 2 * tokens // hd, one, 0)
            ctxt[rows_own, :] = ctxt_all[:, :tokens]
            pg[:, pl.ds(pl.multiple_of(own, hd), hd)] = pgq[:tokens, :]
            for i, total in enumerate((dk, dv)):
                kvg_away[i, :, :] = total[2 * tokens :, :].astype(LOW)

        keys = qkv.shape[1]
        pl.run_scoped(
            attention,
            pltpu.VMEM((hd, keys), LOW),
            pltpu.VMEM((hd, keys), LOW),
            pltpu.VMEM((keys, hd), FULL),
            pltpu.VMEM((keys, hd), FULL),
            pltpu.VMEM((keys, hd), LOW),
            pltpu.VMEM((keys, hd), LOW),
        )

        def head_columns(ref, start, i):
            return ref.at[:, pl.ds(pl.multiple_of(start + i * hd, hd), hd)]

        def send_grad(i):
            source = pgq.at[pl.ds(tokens, tokens), :] if i == 0 else head_columns(pg_away, 0, i - 1)
            return links.send(source, head_columns(pg, own, i), links.y)

        kvg_from_x = {i: links.send(kvg_away.at[i], kvg_got.at[i], links.x) for i in (1, 0)}
        pg_from_y = [send_grad(0)]
        ctx_from_y = links.send(ctxt_all.at[:, pl.ds(tokens, tokens)], ctxt.at[rows_own, :], links.y)
        expand.pass_x()
        expand.to_x(True)

        for i in (1, 0):
            kvg_from_x[i].wait_recv()
            for away_rows, target in ((True, pg_away), (False, pg)):
                rows = pl.ds(tokens if away_rows else 0, tokens)
                total = (dk, dv)[i][rows, :] + kvg_got[i, rows, :].astype(FULL)
                if i == 0:
                    total = spin(total * score_scale, cosine[rows, :], -sines[rows, :])
                head_columns(target, 0 if away_rows else own, i if away_rows else 1 + i)[...] = total.astype(LOW)
                if away_rows:
                    pg_from_y.append(send_grad(1 + i))
        expand.pass_y()
        weight.first()
        weight.rest()
        ctx_from_y.wait_recv()
        for copy in pg_from_y:
            copy.wait_recv()

        def first_block(i, carry):
            up_part(i, contract_last(pg[...], wh[tile(i), :]), True)
            return carry

        lax.fori_loop(0, 8, first_block, 0)
        sums[0, 6:7, :heads_wide] = jnp.sum(pg[...].astype(FULL), 0, keepdims=True)
        heads_in.passed()
        heads_sum.to_core()
        expand.share()
        expand.share_far()
        expand.whole()
        for copy in (*from_y.values(), *from_x.values(), *from_far.values(), dctx_from_y, *kvg_from_x.values(), *pg_from_y, ctx_from_y):
            links.sent_out(copy)

    low, full = (functools.partial(lambda kind, *shape: pltpu.VMEM(shape, kind), kind) for kind in (LOW, FULL))
    pl.run_scoped(
        attend,
        low(3, tokens, hd),
        low(tokens, hd),
        low(hd, 2 * tokens),
        low(2 * tokens, hd),
        low(tokens, 2 * hd),
        low(2, 2 * tokens, hd),
        full(2 * tokens, 128),
        full(2 * tokens, 128),
        full(4 * tokens, hd),
        full(4 * tokens, hd),
        low(2, unit, tokens),
    )

    def update(act, actt, slope, ctx, room_o, stage_o, own_o, room_e, total_rows, total_columns, grad_rows):
        def forward(j, slot):
            cols = tile(j)
            value = dot(up[...], room_s[slot]) + raw[4:5, cols]
            normal_share = 0.5 * (1.0 + lax.erf(value * (0.5**0.5)))
            low_act = (value * normal_share).astype(LOW)
            act[:, cols] = low_act
            actt[cols, :] = low_act.T
            density = jnp.exp(value * value * -0.5) * 0.3989422804014327
            slope[:, cols] = (normal_share + value * density).astype(LOW)

        stream(0, 8, lambda j, slot: [(we.at[:, tile(j)], room_s.at[slot])], forward)
        weight.relay()
        ctx[...] = ctxt[...].T

        rows_out = grad_rows.shape[1]

        def columns_cut(ref, c):
            return ref.at[:, here(c)]

        def rows_cut(ref, c):
            return ref.at[pl.ds(c * rows_out, rows_out), :]

        def finish_branch(c):
            cols = here(c)

            def one(part, carry):
                at = tile_of(part, 128)
                total = up[at, cols].astype(FULL) + got_branch[at, cols].astype(FULL)
                final_branch[at, cols] = (x[at, cols].astype(FULL) + total + vecs[4:5, cols]).astype(LOW)
                return carry

            lax.fori_loop(0, tokens // 128, one, 0)

        def finish_up(c):
            add_rows(rows_cut(final_up, c), rows_cut(n1, c), rows_cut(got_up, c))

        line_branch = Line(links, up, got_branch, final_branch, 8, columns_cut, finish_branch)
        line_up = Line(links, n1, got_up, final_up, tokens // rows_out, rows_cut, finish_up)

        def branch_blocks(chunks, block, source):
            def one(n, slot):
                cols = tile(block(n))
                up[:, cols] = (dot(ctx[...], wo[:, cols]) + dot(act[...], room_s[slot])).astype(LOW)
                for at, chunk in enumerate(chunks):
                    pl.when(n == at)(functools.partial(line_branch.start, chunk))

            stream(0, len(chunks), lambda n, slot: [(source(n), room_s.at[slot])], one)

        steps = [(line_branch, c) for c in (0, 1, 2, 4, 3, 5, 6, 7)] + [(line_up, c) for c in range(line_up.chunks)]
        out_copies = []

        def input_rows(c):
            slot = len(out_copies) % 2
            if len(out_copies) >= 2:
                local.wait(*out_copies[-2])
            rows = pl.ds(c * rows_out, rows_out)
            value = x[rows, :].astype(FULL)
            centred = value - jnp.mean(value, -1, keepdims=True)
            scale = lax.rsqrt(jnp.mean(centred * centred, -1, keepdims=True) + NORM_EPS)
            normal = centred * scale
            upstream = final_up[rows, :].astype(FULL)
            inner = upstream - jnp.mean(upstream, -1, keepdims=True)
            inner = inner - normal * jnp.mean(upstream * normal, -1, keepdims=True)
            grad_rows[slot, :, :] = g[rows, :].astype(FULL) + inner * scale
            out_copies.append(
                [local.start(grad_rows.at[slot, :, here(i)], input_grad.at[rows, place[i]]) for i in blocks]
            )

        def serve(count):
            for _ in range(count):
                at = serve.done
                if at < len(steps):
                    steps[at][0].first(steps[at][1])
                if 2 <= at < len(steps) + 2:
                    steps[at - 2][0].second(steps[at - 2][1])
                if at >= 4:
                    line, c = steps[at - 4]
                    line.third(c)
                    if line is line_up:
                        input_rows(c)
                    else:
                        local.start(final_branch.at[:, here(c)], layer_out.at[:, place[c]])
                serve.done += 1

        serve.done = 0
        branch_blocks((0, 1), lambda n: n, lambda n: at_columns(ws_own, pl.multiple_of((links.r + n - 2 * links.r * n) * unit, unit), unit))

        def shrink_block(i, ref, add):
            product(actt[...], g[:, tile(i)], ref, add)

        def output_block(i, ref, add):
            product(ctxt[...], g[:, tile(i)], ref, add)

        def expand_block(i, ref, add):
            product(nt[tile(i), :], slope[...], ref, add)

        shrink.stage = (actt.at[:, pl.ds(unit, unit // 2)], actt.at[:, pl.ds(unit + unit // 2, unit // 2)])
        shrink.own = actt.at[:, pl.ds(0, unit)]
        output.stage, output.own = (stage_o.at[0], stage_o.at[1]), own_o
        shrink_sum = Reduced(lambda n: room_s.at[n], got_core_s, shrink_block)
        output_sum = Reduced(lambda n: room_o.at[n], got_core_o, output_block)
        expand_sum = Reduced(lambda n: room_e.at[n], got_core_e, expand_block)
        heads_sum.fetch()
        heads_sum.add(red_h)
        heads.first()
        heads.direct()
        heads.load()
        n2t_load = local.start(n2t_hbm, nt)
        weight.share()
        serve(1)
        weight.core_y.wait_recv()
        weight.core_x.wait_recv()
        ahead = lambda n: 2 * n + 2 - 3 * (n // 2 if isinstance(n, int) else lax.div(n, 2))
        branch_blocks((2, 4, 3, 5), ahead, lambda n: ws.at[:, tile(ahead(n))])
        serve(1)
        shrink_sum.to_core()
        weight.share_far()
        shrink_sum.fetch()
        shrink_sum.add(red_s)
        shrink.first()
        shrink.direct()
        shrink.load()
        serve(1)
        weight.core_far.wait_recv()
        branch_blocks((6, 7), lambda n: n + 6, lambda n: ws.at[:, tile(n + 6)])
        serve(1)

        def hidden_tile(j, slot):
            cols = tile(j)
            grad = (contract_last(g[...], room_e[slot]) * slope[:, cols].astype(FULL)).astype(LOW)
            slope[:, cols] = grad
            sums[0, 5:6, cols] = jnp.sum(grad.astype(FULL), 0, keepdims=True)

        def shrink_rows(j, slot):
            rows = tile(j)
            pairs = [(weight.here(i).at[rows, :], room_e.at[slot, :, here(i)]) for i in range(2)]
            return pairs + [(ws.at[rows, rest_rows], room_e.at[slot, :, rest_rows])]

        stream(0, 4, shrink_rows, hidden_tile)
        serve(1)
        stream(4, 8, shrink_rows, hidden_tile)
        serve(1)

        def second_block(i, slot):
            up_part(i, contract_last(slope[...], room_e[slot]), False)

        expand_rows = lambda i, slot: [(we.at[tile(i), :], room_e.at[slot])]
        stream(0, 4, expand_rows, second_block)
        serve(1)
        stream(4, 8, expand_rows, second_block)
        line_up.start(*range(line_up.chunks))
        serve(1)

        def share(s, peers):
            return [links.send(sums.at[s], sums_got.at[4 * s + k], peer) for k, peer in enumerate(peers)]

        def shared(s, copies):
            for copy in copies:
                copy.wait_recv()
            total = sums[s, :, :] + sums_got[4 * s, :, :]
            if len(copies) > 1:
                total = total + (sums_got[4 * s + 1, :, :] + sums_got[4 * s + 2, :, :])
            sums[s + 1, :, :] = total

        def share_line(s, peer):
            return links.send(gains.at[s], gains_got.at[s], peer)

        def shared_line(s, copy):
            copy.wait_recv()
            gains[s + 1, :, :] = gains[s, :, :] + gains_got[s, :, :]

        first_share = share(0, [links.core])
        output_sum.to_core()
        shared(0, first_share)
        second_share = share(1, [links.x, links.y, links.far])
        output_sum.fetch()
        output_sum.add(red_o)
        output.first()
        output.direct()
        output.load()

        local.wait(n2t_load)
        expand_sum.to_core()
        serve(1)
        shrink.second()
        serve(1)
        expand_sum.fetch()
        serve(1)
        expand_sum.add(None)
        red = {k: room_e.at[turns.index(k)] for k in range(4)}
        expand = Scattered(links, local, [red[k] for k in range(4)], at_rows, unit, via_e, got_e, None, red[0])
        expand.first()
        expand.direct()
        serve(2)
        half_rows = pl.ds(pl.multiple_of(links.r * unit, unit), unit)
        column_slots = Slots(total_columns.at[0], total_columns.at[1])
        serve(2)
        shrink.third(column_slots, shrink_grad.at[:, half_rows], total_columns.shape[1])
        serve(1)
        shared(1, second_share)
        for row in range(4):
            for side in range(2):
                at = 2 * row + side
                gains[0, at : at + 1, :] = sums[2, row : row + 1, side * (width // 2) : (side + 1) * (width // 2)]
        pair_share = share_line(0, links.pair)
        serve(3)

        expand.via_x.wait_recv()
        top, end = red[2].at[pl.ds(0, unit // 2), :], red[1].at[pl.ds(unit // 2, unit // 2), :]
        add_rows(top, top, via_e.at[0])
        expand.y_top = links.send(top, got_e.at[1, pl.ds(0, unit // 2), :], links.y)
        expand.via_y.wait_recv()
        add_rows(end, end, via_e.at[1])
        expand.x_end = links.send(end, got_e.at[0, pl.ds(unit // 2, unit // 2), :], links.x)
        heads.second()
        output.second()
        serve(len(steps) - 1 - serve.done)
        shared_line(0, pair_share)
        across_share = share_line(1, links.across)
        serve(2)
        expand_slots = Slots(total_rows.at[0], total_rows.at[1])
        expand.third(expand_slots, expand_grad.at[half_rows, :], total_rows.shape[1])
        serve(len(steps) + 4 - serve.done)
        expand_slots.end()
        total_slots = Slots(*[total_rows.at[n, :, pl.ds(0, heads_wide)] for n in range(2)])
        heads.third(total_slots, heads_grad.at[half_rows, :], total_rows.shape[1])
        output.third(column_slots, output_grad.at[:, half_rows], total_columns.shape[1])
        total_slots.end()
        column_slots.end()
        shared_line(1, across_share)
        for row in range(4):
            for side in range(2):
                at = 2 * row + side
                sums_out[row : row + 1, side * (width // 2) : (side + 1) * (width // 2)] = gains[2, at : at + 1, :]
        sums_out[4:8, :] = sums[2, 4:8, :]
        for copy in (*shrink.other, *output.other, *heads.other, *expand.other):
            copy.wait_recv()
        assert links.count <= COPIES
        links.end()
        line_branch.end()
        line_up.end()
        local.end()


    pl.run_scoped(
        update,
        low(tokens, units),
        low(units, tokens),
        low(tokens, units),
        low(tokens, out_wide),
        low(4, out_wide, unit),
        low(2, out_wide, unit // 2),
        low(out_wide, unit),
        low(4, unit, units),
        full(2, unit // 4, units),
        full(2, out_wide, unit),
        full(2, 32, width),
    )


def block_call(line_size, x, g, heads_rows, output_rows, expand_weight, shrink_weight, raw, order):
    tokens, width = x.shape
    heads_wide, out_wide, units = heads_rows.shape[1], output_rows.shape[0], expand_weight.shape[1]
    hd, unit, half = heads_wide // 6, width // 8, width // 16
    low = lambda *shape: pltpu.VMEM(shape, LOW)
    full = lambda *shape: pltpu.VMEM(shape, FULL)
    work = lambda *shape: jax.ShapeDtypeStruct(shape, LOW)
    outs = [
        work(tokens, width),
        jax.ShapeDtypeStruct((tokens, width), FULL),
        jax.ShapeDtypeStruct((2 * unit, heads_wide), FULL),
        jax.ShapeDtypeStruct((out_wide, 2 * unit), FULL),
        jax.ShapeDtypeStruct((2 * unit, units), FULL),
        jax.ShapeDtypeStruct((units, 2 * unit), FULL),
        work(width, units),
        work(units, width),
        work(width, tokens),
        work(4, units, unit),
        work(4, out_wide, unit),
        work(4, unit, heads_wide),
        work(4, unit, units),
        work(4, units, unit),
        work(4, out_wide, unit),
        work(4, unit, heads_wide),
        jax.ShapeDtypeStruct((8, width), FULL),
    ]
    scratch = [
        *[low(tokens, width)] * 4, low(width, tokens), full(tokens, 256),
        low(width, heads_wide), low(out_wide, width), low(4, 4 * tokens, hd), low(2 * tokens, hd),
        low(out_wide, tokens), low(tokens, heads_wide), low(2, 2 * tokens, hd),
        *[low(tokens, width)] * 4,
        low(2, half, heads_wide), low(2, unit, heads_wide),
        low(2, out_wide, half), low(2, out_wide, unit),
        low(2, units, half), low(2, units, unit),
        low(2, half, units), low(2, unit, units),
        full(8, width), full(3, 8, width), full(7, 8, width), full(3, 8, width // 2), full(2, 8, width // 2),
        pltpu.SemaphoreType.DMA((3, 2)),
        pltpu.SemaphoreType.DMA((8,)),
        pltpu.SemaphoreType.DMA((320,)),
        pltpu.SemaphoreType.DMA((COPIES,)),
        pltpu.SemaphoreType.DMA((COPIES,)),
    ]
    return pl.pallas_call(
        functools.partial(block_kernel, hd**-0.5, line_size),
        out_shape=outs,
        in_specs=[ANY] * 6 + [IN_VMEM, pl.BlockSpec(memory_space=pltpu.SMEM)],
        out_specs=[ANY] * 16 + [IN_VMEM],
        scratch_shapes=scratch,
        compiler_params=pltpu.CompilerParams(
            collective_id=0, has_side_effects=True, vmem_limit_bytes=VMEM_BYTES
        ),
    )(x, g, heads_rows, output_rows, expand_weight, shrink_weight, raw, order)


def square_local(
    layer_input,
    block_order,
    first_gain,
    first_bias,
    second_gain,
    second_bias,
    heads_weight,
    heads_bias,
    output_weight,
    output_bias,
    expand_weight,
    expand_bias,
    shrink_weight,
    shrink_bias,
    cotangent,
):
    width = layer_input.shape[2]
    heads_rows = heads_weight.reshape(heads_weight.shape[0], -1)
    output_rows = output_weight.reshape(-1, output_weight.shape[2])
    wide = heads_rows.shape[1]
    pieces = [first_gain, first_bias, second_gain, second_bias, expand_bias, heads_bias.reshape(-1)]
    pieces += [jnp.zeros((width - wide,), LOW), output_bias, shrink_bias]
    raw = jnp.concatenate([piece.astype(FULL) for piece in pieces]).reshape(8, width)
    layer_output, input_grad, heads_grad, output_grad, expand_weight_grad, shrink_weight_grad, *_, sums = block_call(
        lax.axis_size("tensor"),
        layer_input[0],
        cotangent[0],
        heads_rows,
        output_rows,
        expand_weight,
        shrink_weight,
        raw,
        block_order,
    )
    return (
        layer_output[None],
        input_grad[None],
        sums[0],
        sums[1],
        sums[2],
        sums[3],
        heads_grad.reshape(heads_weight.shape),
        sums[6, :wide].reshape(heads_bias.shape),
        output_grad.reshape(output_weight.shape),
        sums[4],
        expand_weight_grad,
        sums[5],
        shrink_weight_grad,
        sums[4],
    )


def ring_local(
    layer_input,
    block_order,
    first_gain,
    first_bias,
    second_gain,
    second_bias,
    heads_weight,
    heads_bias,
    output_weight,
    output_bias,
    expand_weight,
    expand_bias,
    shrink_weight,
    shrink_bias,
    cotangent,
):
    tokens_here = layer_input.shape[1]
    fsdp_count = lax.axis_size("fsdp")
    head_dim = output_weight.shape[1]
    score_scale = head_dim ** (-0.5)
    order_row = block_order[0]
    device_slot = lax.axis_index("fsdp")
    own_block = jnp.sum(
        jnp.where(jnp.arange(fsdp_count, dtype=jnp.int32) == device_slot, order_row, 0)
    )
    offsets = jnp.arange(tokens_here, dtype=jnp.int32)
    query_pos = own_block * tokens_here + offsets
    key_pos = jnp.repeat(order_row, tokens_here) * tokens_here + jnp.tile(offsets, fsdp_count)
    allowed = key_pos[None, :] <= query_pos[:, None]
    cosine, sine_part = rotary_tables(query_pos, ROT)
    hidden_in = layer_input[0].astype(jnp.float32)
    gain_one = first_gain.astype(jnp.float32)
    shift_one = first_bias.astype(jnp.float32)
    gain_two = second_gain.astype(jnp.float32)
    shift_two = second_bias.astype(jnp.float32)
    norm_one_low = layer_norm(hidden_in, gain_one, shift_one).astype(jnp.bfloat16)
    norm_two_low = layer_norm(hidden_in, gain_two, shift_two).astype(jnp.bfloat16)
    heads_full, output_full, expand_full, shrink_full = (
        lax.all_gather(heads_weight, "fsdp", axis=0, tiled=True),
        lax.all_gather(output_weight, "fsdp", axis=2, tiled=True),
        lax.all_gather(expand_weight, "fsdp", axis=0, tiled=True),
        lax.all_gather(shrink_weight, "fsdp", axis=1, tiled=True),
    )
    projected = jnp.einsum(
        "td,dhe->hte", norm_one_low, heads_full, preferred_element_type=jnp.float32
    )
    projected = projected + heads_bias.astype(jnp.float32)[:, None, :]
    query_pre = projected[..., :head_dim]
    key_pre = projected[..., head_dim : 2 * head_dim]
    query_low = rotate(query_pre, cosine, sine_part).astype(jnp.bfloat16)
    key_low = rotate(key_pre, cosine, sine_part).astype(jnp.bfloat16)
    value_low = projected[..., 2 * head_dim :].astype(jnp.bfloat16)
    key_all, value_all = (
        lax.all_gather(key_low, "fsdp", axis=1, tiled=True),
        lax.all_gather(value_low, "fsdp", axis=1, tiled=True),
    )

    def attend_head(operands):
        query_head, key_head, value_head = operands
        probability = softmax_rows(contract_last(query_head, key_head) * score_scale, allowed)
        return jnp.dot(
            probability.astype(jnp.bfloat16), value_head, preferred_element_type=jnp.float32
        )

    context = lax.map(attend_head, (query_low, key_all, value_all))
    context_low = context.astype(jnp.bfloat16)
    expand_in = jnp.dot(
        norm_two_low, expand_full, preferred_element_type=jnp.float32
    ) + expand_bias.astype(jnp.float32)
    activation_low = jax.nn.gelu(expand_in, approximate=False).astype(jnp.bfloat16)
    branch_part = jnp.einsum(
        "hte,hed->td", context_low, output_full, preferred_element_type=jnp.float32
    )
    branch_part = branch_part + jnp.dot(
        activation_low, shrink_full, preferred_element_type=jnp.float32
    )
    branch = lax.psum(branch_part, "tensor")
    layer_output = (
        hidden_in + branch + output_bias.astype(jnp.float32) + shrink_bias.astype(jnp.float32)
    ).astype(jnp.bfloat16)[None]
    heads_back, output_back, expand_back, shrink_back = (
        lax.all_gather(heads_weight, "fsdp", axis=0, tiled=True),
        lax.all_gather(output_weight, "fsdp", axis=2, tiled=True),
        lax.all_gather(expand_weight, "fsdp", axis=0, tiled=True),
        lax.all_gather(shrink_weight, "fsdp", axis=1, tiled=True),
    )
    key_back, value_back = (
        lax.all_gather(key_low, "fsdp", axis=1, tiled=True),
        lax.all_gather(value_low, "fsdp", axis=1, tiled=True),
    )
    grad_out = cotangent[0]
    grad_float = grad_out.astype(jnp.float32)
    output_weight_grad = jnp.einsum(
        "hte,td->hed", context_low, grad_out, preferred_element_type=jnp.float32
    )
    shrink_weight_grad = contract_first(activation_low, grad_out)
    bias_total = jnp.sum(grad_float, 0)
    context_grad = jnp.einsum(
        "td,hed->hte", grad_out, output_back, preferred_element_type=jnp.float32
    ).astype(jnp.bfloat16)
    activation_grad = contract_last(grad_out, shrink_back)
    _, gelu_back = jax.vjp(lambda inner_val: jax.nn.gelu(inner_val, approximate=False), expand_in)
    expand_grad = gelu_back(activation_grad)[0].astype(jnp.bfloat16)
    expand_weight_grad = contract_first(norm_two_low, expand_grad)
    expand_bias_grad = jnp.sum(expand_grad.astype(jnp.float32), 0)
    norm_two_grad = contract_last(expand_grad, expand_back)

    def attend_back(operands):
        query_head, key_head, value_head, context_head = operands
        probability = softmax_rows(contract_last(query_head, key_head) * score_scale, allowed)
        prob_low = probability.astype(jnp.bfloat16)
        weight_grad = contract_last(context_head, value_head)
        row_inner = jnp.sum(probability * weight_grad, -1, keepdims=True)
        score_grad = (probability * (weight_grad - row_inner)).astype(jnp.bfloat16)
        query_grad = jnp.dot(score_grad, key_head, preferred_element_type=jnp.float32) * score_scale
        key_grad = contract_first(score_grad, query_head) * score_scale
        value_grad = contract_first(prob_low, context_head)
        return (query_grad, key_grad, value_grad)

    query_grad, key_grad_all, value_grad_all = lax.map(
        attend_back, (query_low, key_back, value_back, context_grad)
    )
    key_grad, value_grad = (
        lax.psum_scatter(key_grad_all, "fsdp", scatter_dimension=1, tiled=True),
        lax.psum_scatter(value_grad_all, "fsdp", scatter_dimension=1, tiled=True),
    )
    _, rotate_back = jax.vjp(lambda inner_val: rotate(inner_val, cosine, sine_part), query_pre)
    projected_grad = jnp.concatenate(
        [rotate_back(query_grad)[0], rotate_back(key_grad)[0], value_grad], -1
    ).astype(jnp.bfloat16)
    heads_weight_grad = jnp.einsum(
        "td,hte->dhe", norm_one_low, projected_grad, preferred_element_type=jnp.float32
    )
    heads_bias_grad = jnp.sum(projected_grad.astype(jnp.float32), 1)
    norm_one_grad = jnp.einsum(
        "hte,dhe->td", projected_grad, heads_back, preferred_element_type=jnp.float32
    )
    norm_one_grad, norm_two_grad = lax.psum((norm_one_grad, norm_two_grad), "tensor")
    _, first_back = jax.vjp(layer_norm, hidden_in, gain_one, shift_one)
    input_first, first_gain_grad, first_bias_grad = first_back(norm_one_grad)
    _, second_back = jax.vjp(layer_norm, hidden_in, gain_two, shift_two)
    input_second, second_gain_grad, second_bias_grad = second_back(norm_two_grad)
    input_grad = (grad_float + input_first + input_second)[None]
    small_sums = lax.psum(
        (
            first_gain_grad,
            first_bias_grad,
            second_gain_grad,
            second_bias_grad,
            bias_total,
            expand_bias_grad,
            heads_bias_grad,
        ),
        ("replica", "fsdp"),
    )
    shard_parts = (
        lax.psum_scatter(heads_weight_grad, "fsdp", scatter_dimension=0, tiled=True),
        lax.psum_scatter(output_weight_grad, "fsdp", scatter_dimension=2, tiled=True),
        lax.psum_scatter(expand_weight_grad, "fsdp", scatter_dimension=0, tiled=True),
        lax.psum_scatter(shrink_weight_grad, "fsdp", scatter_dimension=1, tiled=True),
    )
    reduced = lax.psum((shard_parts[0], shard_parts[1], shard_parts[2], shard_parts[3]), "replica")
    return (
        layer_output,
        input_grad,
        small_sums[0],
        small_sums[1],
        small_sums[2],
        small_sums[3],
        reduced[0],
        small_sums[6],
        reduced[1],
        small_sums[4],
        reduced[2],
        small_sums[5],
        reduced[3],
        small_sums[4],
    )


def solution(mesh):
    placed = (
        P("replica", "fsdp", None),
        P("replica", None),
        P(),
        P(),
        P(),
        P(),
        P("fsdp", "tensor", None),
        P("tensor", None),
        P("tensor", None, "fsdp"),
        P(),
        P("fsdp", "tensor"),
        P("tensor"),
        P("tensor", "fsdp"),
        P(),
        P("replica", "fsdp", None),
    )
    local = square_local if mesh.shape["fsdp"] == 4 and mesh.shape["replica"] == 2 and mesh.shape["tensor"] == 4 else ring_local
    return jax.shard_map(
        local,
        mesh=mesh,
        in_specs=placed,
        out_specs=(
            P("replica", "fsdp", None),
            P("replica", "fsdp", None),
            P(),
            P(),
            P(),
            P(),
            P("fsdp", "tensor", None),
            P("tensor", None),
            P("tensor", None, "fsdp"),
            P(),
            P("fsdp", "tensor"),
            P("tensor"),
            P("tensor", "fsdp"),
            P(),
        ),
        check_vma=False,
    )
```

```python
import functools
import math

import jax
import jax.numpy as jnp
from jax import lax
from jax.experimental import pallas as pl
from jax.experimental.pallas import tpu as pltpu
from jax.sharding import PartitionSpec as P

ROT = 64


NORM_EPS = 1e-05
MASKED = -1e30


def layer_norm(values_in, gain_vec, shift_vec):
    average = jnp.mean(values_in, -1, keepdims=True)
    centred = values_in - average
    spread_sq = jnp.mean(centred * centred, -1, keepdims=True)
    return centred * lax.rsqrt(spread_sq + NORM_EPS) * gain_vec + shift_vec


def rotate(values_in, cosine, sine_part):
    rot_width = cosine.shape[-1]
    half_width = rot_width // 2
    turning = values_in[..., :rot_width]
    swapped = jnp.concatenate([-turning[..., half_width:], turning[..., :half_width]], -1)
    return jnp.concatenate([turning * cosine + swapped * sine_part, values_in[..., rot_width:]], -1)


def rotary_tables(positions, rot_width):
    frequency = jnp.power(10000.0, -jnp.arange(0, rot_width, 2, dtype=jnp.float32) / rot_width)
    angle_half = positions.astype(jnp.float32)[:, None] * frequency[None, :]
    angles = jnp.concatenate([angle_half, angle_half], -1)
    return (jnp.cos(angles), jnp.sin(angles))


def contract_last(left_op, right_op):
    return lax.dot_general(
        left_op, right_op, (((1,), (1,)), ((), ())), preferred_element_type=jnp.float32
    )


def contract_first(left_op, right_op):
    return lax.dot_general(
        left_op, right_op, (((0,), (0,)), ((), ())), preferred_element_type=jnp.float32
    )


def softmax_rows(scores, allowed):
    masked_scores = jnp.where(allowed, scores, MASKED)
    row_top = jnp.max(masked_scores, -1, keepdims=True)
    exponent = jnp.exp(masked_scores - row_top)
    return exponent / jnp.sum(exponent, -1, keepdims=True)


LOW = jnp.bfloat16
FULL = jnp.float32


MESH = pl.DeviceIdType.MESH
ANY = pl.BlockSpec(memory_space=pl.ANY)
IN_VMEM = pl.BlockSpec(memory_space=pltpu.VMEM)
VMEM_BYTES = 63 * 2**20
COPIES = 224


class Sent:
    def __init__(self, links, k, source, target, peer):
        self.links, self.k, self.source, self.target, self.peer = links, k, source, target, peer

    def copy(self):
        return self.links.copy_at(self.k, self.source, self.target, self.peer)

    def start(self):
        self.copy().start()

    def wait_recv(self):
        self.copy().wait_recv()

    def wait_send(self):
        self.copy().wait_send()


class Links:
    def __init__(self, send_sem, recv_sem, line=0):
        self.send_sem, self.recv_sem, self.sent, self.count = send_sem, recv_sem, [], 0
        self.r, self.f, self.t = (lax.axis_index(name) for name in ("replica", "fsdp", "tensor"))
        self.xb, self.yb = lax.rem(self.f, 2), lax.div(self.f, 2)
        self.x = (self.r, self.f + 1 - 2 * self.xb, self.t)
        self.y = (self.r, lax.rem(self.f + 2, 4), self.t)
        self.core = (1 - self.r, self.f, self.t)
        self.peers = [self.x, self.y, self.core]
        if line:
            self.line = line
            self.left, self.right, self.across = (
                (self.r, self.f, lax.rem(self.t + step, line)) for step in (line - 1, 1, 2)
            )
            self.pair = (self.r, self.f, self.t + 1 - 2 * lax.rem(self.t, 2))
            self.far = (self.r, 3 - self.f, self.t)
            self.mirror = (self.r, self.f, line - 1 - self.t)
            self.peers += [self.far, self.left, self.right, self.across]

    def meet(self):
        barrier = pltpu.get_barrier_semaphore()
        for peer in self.peers:
            pl.semaphore_signal(barrier, inc=1, device_id=peer, device_id_type=MESH)
        pl.semaphore_wait(barrier, len(self.peers))

    def prepare(self, source, target, peer):
        self.count += 1
        return Sent(self, self.count - 1, source, target, peer)

    def send(self, source, target, peer):
        copy = self.prepare(source, target, peer)
        copy.start()
        self.sent.append(copy)
        return copy

    def series(self, count):
        k = self.count
        self.count += count
        return k

    def copy_at(self, k, source, target, peer):
        return pltpu.make_async_remote_copy(
            src_ref=source,
            dst_ref=target,
            send_sem=self.send_sem.at[k],
            recv_sem=self.recv_sem.at[k],
            device_id=peer,
            device_id_type=MESH,
        )

    def sent_out(self, copy):
        copy.wait_send()
        self.sent = [other for other in self.sent if other is not copy]

    def end(self):
        for copy in self.sent:
            copy.wait_send()

    def block(self, i):
        place = 0
        for size, bit in ((4, self.yb), (2, self.xb), (1, self.r)):
            mine = lax.rem(lax.div(i, size), 2) if isinstance(i, jax.Array) else i // size % 2
            place = place + size * (mine + bit - 2 * mine * bit)
        return place


class Local:
    def __init__(self, sem):
        self.sem, self.count, self.open = sem, 0, []

    def start(self, source, target):
        copy = pltpu.make_async_copy(source, target, self.sem.at[self.count])
        self.count += 1
        copy.start()
        self.open.append(copy)
        return copy

    def wait(self, *copies):
        for copy in copies:
            copy.wait()
            self.open = [other for other in self.open if other is not copy]

    def end(self):
        self.wait(*list(self.open))


def at_rows(ref, start, size):
    return ref.at[pl.ds(start, size), :]


def at_columns(ref, start, size):
    return ref.at[:, pl.ds(start, size)]


class Gathered:
    def __init__(self, links, local, shard, full, cut, unit, copied=True):
        self.links, self.local, self.full, self.cut = links, local, full, cut
        self.shard, self.unit, self.half = shard, unit, unit // 2
        self.starts = [pl.multiple_of(links.r * unit + start, self.half) for start in (0, self.half)]
        self.bases = [pl.multiple_of(base * unit, unit) for base in (links.r, 1 - links.r)]
        self.copies = [local.start(self.here(i), self.at(i)) for i in range(2)] if copied else []
        self.from_x, self.from_y = {}, {}

    def here(self, i):
        return self.cut(self.shard, self.bases[i], self.unit)

    def mine(self, lower):
        return self.cut(self.shard, self.starts[lower], self.half)

    def at(self, block, start=0, size=None):
        return self.cut(self.full, block * self.unit + start, self.unit if size is None else size)

    def to_x(self, lower):
        source, target = self.mine(lower), self.at(2, self.half * lower, self.half)
        self.from_x[lower] = self.links.send(source, target, self.links.x)

    def to_y(self, lower):
        source, target = self.mine(lower), self.at(4, self.half * lower, self.half)
        self.from_y[lower] = self.links.send(source, target, self.links.y)

    def first(self):
        self.to_x(False)
        self.to_y(True)

    def rest(self):
        self.to_x(True)
        self.to_y(False)

    def pass_y(self):
        half = self.half
        self.from_x[False].wait_recv()
        self.far_top = self.links.send(self.at(2, 0, half), self.at(6, 0, half), self.links.y)

    def pass_x(self):
        half = self.half
        self.from_y[True].wait_recv()
        self.far_end = self.links.send(self.at(4, half, half), self.at(6, half, half), self.links.x)

    def relay(self):
        self.pass_y()
        self.pass_x()

    def share(self):
        self.from_y[False].wait_recv()
        self.core_y = self.links.send(self.at(4), self.at(5), self.links.core)
        self.from_x[True].wait_recv()
        self.core_x = self.links.send(self.at(2), self.at(3), self.links.core)

    def share_far(self):
        self.far_top.wait_recv()
        self.far_end.wait_recv()
        self.core_far = self.links.send(self.at(6), self.at(7), self.links.core)

    def passed(self):
        for copy in (self.far_top, self.far_end, self.core_x, self.core_y, self.core_far):
            self.links.sent_out(copy)

    def whole(self):
        self.local.wait(*self.copies)
        for copy in (self.core_x, self.core_y, self.core_far):
            copy.wait_recv()


def odd(j):
    return j % 2 if isinstance(j, int) else lax.rem(j, 2)


def tile_of(j, size):
    return pl.ds(pl.multiple_of(j * size, size), size)


def dot(left, right):
    return jnp.dot(left, right, preferred_element_type=FULL)


def spin(values_in, cosine, sine):
    head = values_in[:, :128]
    lane = lax.broadcasted_iota(jnp.int32, head.shape, 1)
    swapped = jnp.where(lane < ROT // 2, pltpu.roll(head, 96, 1), pltpu.roll(head, 32, 1))
    return jnp.concatenate([head * cosine + swapped * sine, values_in[:, 128:]], -1)


class Scattered:
    def __init__(self, links, local, blocks, cut, unit, via, got, stage=None, own=None):
        self.links, self.local, self.blocks, self.cut, self.unit = links, local, blocks, cut, unit
        self.via, self.got = [via.at[n] for n in range(2)], [got.at[n] for n in range(2)]
        self.stage, self.own = stage, own
        self.half, self.loads = unit // 2, []

    def load(self):
        self.loads = [
            self.local.start(self.cut(self.blocks[1], self.half, self.half), self.stage[0]),
            self.local.start(self.cut(self.blocks[2], 0, self.half), self.stage[1]),
            self.local.start(self.blocks[0], self.own),
        ]

    def first(self):
        half, cut, far = self.half, self.cut, self.blocks[3]
        self.via_x = self.links.send(cut(far, 0, half), self.via[0], self.links.x)
        self.via_y = self.links.send(cut(far, half, half), self.via[1], self.links.y)

    def direct(self):
        half, cut = self.half, self.cut
        self.x_top = self.links.send(cut(self.blocks[1], 0, half), cut(self.got[0], 0, half), self.links.x)
        self.y_end = self.links.send(cut(self.blocks[2], half, half), cut(self.got[1], half, half), self.links.y)

    def second(self):
        half, cut = self.half, self.cut
        self.local.wait(*self.loads[:2])
        self.via_x.wait_recv()
        add_rows(self.stage[1], self.stage[1], self.via[0])
        self.y_top = self.links.send(self.stage[1], cut(self.got[1], 0, half), self.links.y)
        self.via_y.wait_recv()
        add_rows(self.stage[0], self.stage[0], self.via[1])
        self.x_end = self.links.send(self.stage[0], cut(self.got[0], half, half), self.links.x)

    def third(self, slots, place, step, between=lambda: None):
        for copy in (self.x_top, self.x_end, self.y_top, self.y_end):
            copy.wait_recv()
        if self.loads:
            self.local.wait(self.loads[2])
        self.other = []
        for start in range(0, self.own.shape[0], step):
            between()
            rows = pl.ds(start, step)
            at, total = slots.take()
            add_rows(total, self.own.at[rows, :], self.got[0].at[rows, :], self.got[1].at[rows, :])
            kept = self.local.start(total, place.at[rows, :])
            other = self.links.send(total, place.at[rows, :], self.links.core)
            self.other.append(other)

            def done(kept=kept, other=other):
                self.local.wait(kept)
                self.links.sent_out(other)

            slots.busy[at] = done


def add_rows(target, *parts):
    rows, wide = target.shape
    step = min(rows, 32 if wide > 512 else 256)

    def one(c, carry):
        at = pl.ds(pl.multiple_of(c * step, step), step)
        total = parts[0][at, :].astype(FULL)
        for part in parts[1:]:
            total = total + part[at, :].astype(FULL)
        target[at, :] = total.astype(target.dtype)
        return carry

    lax.fori_loop(0, rows // step, one, 0)


class Line:
    def __init__(self, links, part, got, final, chunks, cut, finish):
        self.links, self.part, self.got, self.final, self.cut, self.finish = links, part, got, final, cut, finish
        self.chunks = chunks
        self.outer = jnp.logical_or(links.t == 0, links.t == links.line - 1)
        self.middle = jnp.logical_not(self.outer)
        self.inward = [self.make(c, part, final, links.pair) for c in range(chunks)]
        self.across = [self.make(c, part, got, links.mirror) for c in range(chunks)]
        self.outward = [self.make(c, final, final, links.pair) for c in range(chunks)]

    def make(self, c, source, target, peer):
        return self.links.prepare(self.cut(source, c), self.cut(target, c), peer)

    def start(self, *chunks):
        @pl.when(self.outer)
        def _():
            for c in chunks:
                self.inward[c].start()

    def first(self, c):
        @pl.when(self.middle)
        def _():
            self.inward[c].wait_recv()
            part = self.cut(self.part, c)
            add_rows(part, part, self.cut(self.final, c))
            self.across[c].start()

    def second(self, c):
        @pl.when(self.middle)
        def _():
            self.across[c].wait_recv()
            self.finish(c)
            self.outward[c].start()

    def third(self, c):
        @pl.when(self.outer)
        def _():
            self.outward[c].wait_recv()

    def end(self):
        @pl.when(self.outer)
        def _():
            for copy in self.inward:
                copy.wait_send()

        @pl.when(self.middle)
        def _():
            for copy in self.across + self.outward:
                copy.wait_send()


class Slots:
    def __init__(self, *refs):
        self.refs, self.busy, self.count = refs, {}, 0

    def take(self):
        at = self.count % len(self.refs)
        self.count += 1
        if at in self.busy:
            self.busy.pop(at)()
        return at, self.refs[at]

    def end(self):
        for wait in self.busy.values():
            wait()
        self.busy = {}


def block_kernel(
    score_scale, line_size,
    x_hbm, g_hbm, wh_hbm, wo_hbm, we_own, ws_own, gain_one, shift_one, gain_two, shift_two, units_bias, heads_bias,
    bias_one, bias_two, order,
    layer_out, input_grad, heads_grad, output_grad, expand_grad, shrink_grad, we, ws, n2t_hbm, got_core_s, got_core_o,
    got_core_h, got_core_e, red_s, red_o, red_h, sums_out,
    x, g, up, n1, nt, stat, wh, wo, qkv, dctx, ctxt, pg, kvg_got, got_branch, final_branch, got_up, final_up,
    via_h, got_h, via_o, got_o, via_s, got_s, via_e, got_e, raw, vecs, sums, sums_got, gains, gains_got,
    loop_sem, block_sem, local_sem, send_sem, recv_sem,
):
    links, local = Links(send_sem, recv_sem, line_size), Local(local_sem)
    tokens, width = x.shape
    units, heads_wide, out_wide = we.shape[1], wh.shape[1], wo.shape[0]
    hd = dctx.shape[1]
    unit = width // 8
    blocks = range(8)
    room_s = qkv
    place = [pl.ds(pl.multiple_of(links.block(i) * unit, unit), unit) for i in blocks]

    def here(i):
        return pl.ds(i * unit, unit)

    rest_rows = pl.ds(2 * unit, width - 2 * unit)

    def tile(j):
        return pl.ds(j * unit if isinstance(j, int) else pl.multiple_of(j * unit, unit), unit)

    def placed(i):
        return pl.ds(pl.multiple_of(links.block(i) * unit, unit), unit)

    def stream(start, end, load, body):
        def copies(j):
            pairs = load(j, odd(j))
            return [pltpu.make_async_copy(*pair, loop_sem.at[n, odd(j)]) for n, pair in enumerate(pairs)]

        for copy in copies(start):
            copy.start()

        def one(j, carry):
            @pl.when(j + 1 < end)
            def _():
                for copy in copies(j + 1):
                    copy.start()

            for copy in copies(j):
                copy.wait()
            body(j, odd(j))
            return carry

        lax.fori_loop(start, end, one, 0)

    x_in, g_in = [], []
    for i in blocks:
        cols = pl.ds(pl.multiple_of(links.block(i) * unit, unit), unit)
        x_in.append(local.start(x_hbm.at[:, cols], x.at[:, pl.ds(i * unit, unit)]))
        g_in.append(local.start(g_hbm.at[:, cols], g.at[:, pl.ds(i * unit, unit)]))
    links.meet()
    heads_in = Gathered(links, local, wh_hbm, wh, at_rows, unit)
    output_in = Gathered(links, local, wo_hbm, wo, at_columns, unit)
    expand = Gathered(links, local, we_own, we, at_rows, unit)
    weight = Gathered(links, local, ws_own, ws, at_columns, unit, False)
    heads_in.first()
    heads_in.rest()

    def row(ref):
        return ref[...].astype(FULL).reshape(1, -1)

    for i, vec in enumerate((gain_one, shift_one, gain_two, shift_two, units_bias)):
        raw[i : i + 1, :] = row(vec)
    raw[6:7, :] = row(bias_one) + row(bias_two)
    head_rows = heads_bias[...].astype(FULL)
    raw[5:6, : 3 * hd], raw[7:8, : 3 * hd] = head_rows[0:1, :], head_rows[1:2, :]

    turns = (3, 1, 2, 0)

    def turn_of(n):
        return jnp.where(n == 0, 3, jnp.where(n == 3, 0, n))

    class Reduced:
        def __init__(self, room, got, block):
            self.room, self.got, self.block = room, got, block
            self.gots = [got.at[k] for k in range(4)]

        def to_core(self):
            first = links.series(4)

            def one(n, carry):
                k = turn_of(n)
                self.block(2 * k + 1, self.room(n), False)
                links.copy_at(first + n, self.room(n), self.got.at[k], links.core).start()
                return carry

            lax.fori_loop(0, 4, one, 0)
            self.copies = [Sent(links, first + n, self.room(n), self.gots[turns[n]], links.core) for n in range(4)]

        def fetch(self):
            for n in range(4):
                self.copies[n].wait_send()
                self.copies[n].wait_recv()
                pltpu.make_async_copy(self.got.at[turns[n]], self.room(n), block_sem.at[n]).start()

        def add(self, red):
            def one(n, carry):
                k = turn_of(n)
                pltpu.make_async_copy(self.got.at[k], self.room(n), block_sem.at[n]).wait()
                self.block(2 * k, self.room(n), True)
                if red is not None:
                    pltpu.make_async_copy(self.room(n), red.at[k], block_sem.at[4 + n]).start()
                return carry

            lax.fori_loop(0, 4, one, 0)
            if red is not None:
                for n in range(4):
                    pltpu.make_async_copy(self.room(n), red.at[turns[n]], block_sem.at[4 + n]).wait()

    def product(left, right, ref, add):
        part = dot(left, right)
        if add:
            part = part + ref[...].astype(FULL)
        ref[...] = part.astype(LOW)

    def heads_block(i, ref, add):
        product(nt[tile(i), :], pg[...], ref, add)

    heads_sum = Reduced(lambda n: wh.at[tile(n), :], got_core_h, heads_block)
    own_h = at_rows(wh, 4 * unit, unit)
    stage_h = (at_rows(wh, 5 * unit, unit // 2), at_rows(wh, 5 * unit + unit // 2, unit // 2))
    heads = Scattered(links, local, [red_h.at[k] for k in range(4)], at_rows, unit, via_h, got_h, stage_h, own_h)
    shrink = Scattered(links, local, [red_s.at[k] for k in range(4)], at_columns, unit, via_s, got_s)
    output = Scattered(links, local, [red_o.at[k] for k in range(4)], at_columns, unit, via_o, got_o)

    def up_part(i, grad, first):
        cols, spot = tile(i), placed(i)
        normal = (x[:, cols].astype(FULL) - stat[:, 0:1]) * stat[:, 128:129]
        row = 0 if first else 2
        sums[0, row : row + 1, spot] = jnp.sum(grad * normal, 0, keepdims=True)
        sums[0, row + 1 : row + 2, spot] = jnp.sum(grad, 0, keepdims=True)
        scaled = grad * (vecs[0:1, cols] if first else vecs[2:3, cols])
        n1[:, cols] = (scaled if first else n1[:, cols].astype(FULL) + scaled).astype(LOW)

    def attend(qkv_away, dctx_away, ctxt_all, pgq, pg_away, kvg_away, cosine, sines, dk, dv, stage):
        for i in blocks:
            cols = pl.ds(pl.multiple_of(links.block(i) * unit, unit), unit)
            vecs[0:4, i * unit : (i + 1) * unit] = raw[0:4, cols]
            vecs[4:5, i * unit : (i + 1) * unit] = raw[6:7, cols]
        local.wait(*x_in)

        def norm_rows(c, carry):
            rows = tile_of(c, 64)
            value = x[rows, :].astype(FULL)
            average = jnp.mean(value, -1, keepdims=True)
            centred = value - average
            inverse = lax.rsqrt(jnp.mean(centred * centred, -1, keepdims=True) + NORM_EPS)
            normal = centred * inverse
            both = [jnp.broadcast_to(part, (64, 128)) for part in (average, inverse)]
            stat[rows, :] = jnp.concatenate(both, -1)
            n1[rows, :] = (normal * vecs[0:1, :] + vecs[1:2, :]).astype(LOW)
            up[rows, :] = (normal * vecs[2:3, :] + vecs[3:4, :]).astype(LOW)
            return carry

        lax.fori_loop(0, tokens // 64, norm_rows, 0)
        bases = [
            order[0, (links.yb if step < 2 else 1 - links.yb) * 2 + (links.xb if step % 2 == 0 else 1 - links.xb)]
            * tokens
            for step in (0, 2, 1, 3)
        ]

        def table_rows(c, carry):
            rows = tile_of(c, 64)
            lane = lax.broadcasted_iota(jnp.int32, (64, 128), 1)
            row = lax.broadcasted_iota(jnp.int32, (64, 128), 0) + c * 64
            spot = row + jnp.where(row < tokens, bases[0], bases[1] - tokens)
            pace = jnp.exp(lax.rem(lane, ROT // 2).astype(FULL) * (-2.0 / ROT * math.log(10000.0)))
            angle = spot.astype(FULL) * pace
            sine = jnp.sin(angle)
            cosine[rows, :] = jnp.where(lane < ROT, jnp.cos(angle), 1.0)
            sines[rows, :] = jnp.where(lane < ROT // 2, -sine, jnp.where(lane < ROT, sine, 0.0))
            return carry

        lax.fori_loop(0, 2 * tokens // 64, table_rows, 0)
        heads_in.relay()
        output_in.first()
        output_in.rest()

        def turned_copy(j):
            slot = odd(j)
            return pltpu.make_async_copy(stage.at[slot], n2t_hbm.at[tile_of(j, unit), :], loop_sem.at[0, slot])

        def turn_tiles(j, carry):
            cols = tile_of(j, unit)
            nt[cols, :] = n1[:, cols].T

            @pl.when(j >= 2)
            def _():
                turned_copy(j - 2).wait()

            stage[odd(j), :, :] = up[:, cols].T
            turned_copy(j).start()
            return carry

        lax.fori_loop(0, 8, turn_tiles, 0)
        for j in (6, 7):
            turned_copy(j).wait()
        sums[0, :, :] = jnp.zeros(sums.shape[1:], FULL)
        local.wait(*g_in)
        for i in blocks:
            cols = pl.ds(pl.multiple_of(links.block(i) * unit, unit), unit)
            sums[0, 4:5, cols] = jnp.sum(g[:, i * unit : (i + 1) * unit].astype(FULL), 0, keepdims=True)
        heads_in.share()
        heads_in.share_far()
        heads_in.whole()
        output_in.relay()

        own = links.yb * 3 * hd

        def project(c, head, target):
            cols = pl.ds(pl.multiple_of(head * 3 * hd + c * hd, hd), hd)
            bias = jnp.where(head == 0, raw[5:6, c * hd : (c + 1) * hd], raw[7:8, c * hd : (c + 1) * hd])
            value = dot(n1[...], wh[:, cols]) + bias
            if c < 2:
                value = spin(value, cosine[:tokens, :], sines[:tokens, :])
            target[c, :tokens, :] = value.astype(LOW)

        def place_of(c, part):
            return qkv.at[c, pl.ds(part * tokens, tokens), :]

        from_y, from_x, from_far = {}, {}, {}
        for c in (1, 2, 0):
            project(c, 1 - links.yb, qkv_away)
            from_y[c] = links.send(qkv_away.at[c], place_of(c, 1), links.y)
        for c in (1, 2):
            project(c, links.yb, qkv)
            from_x[c] = links.send(place_of(c, 0), place_of(c, 2), links.x)
        from_y[1].wait_recv()
        from_far[1] = links.send(place_of(1, 1), place_of(1, 3), links.x)
        project(0, links.yb, qkv)
        output_in.share()
        output_in.share_far()
        from_y[2].wait_recv()
        from_far[2] = links.send(place_of(2, 1), place_of(2, 3), links.x)
        output_in.whole()
        rows_own = pl.ds(pl.multiple_of(links.yb * hd, hd), hd)
        rows_away = pl.ds(pl.multiple_of((1 - links.yb) * hd, hd), hd)
        dctx_away[...] = contract_last(g[...], wo[rows_away, :]).astype(LOW)
        dctx_from_y = links.send(dctx_away, dctx.at[pl.ds(tokens, tokens), :], links.y)
        dctx[:tokens, :] = contract_last(g[...], wo[rows_own, :]).astype(LOW)
        expand.first()
        expand.to_y(False)
        for copy in (from_y[0], dctx_from_y, *from_x.values(), *from_far.values()):
            copy.wait_recv()

        def attention(kt, vt, prob, wgt, prob_low, grad_low):
            keys = qkv.shape[1]
            step = tokens
            lag = lax.broadcasted_iota(jnp.int32, (step, hd), 0) - lax.broadcasted_iota(jnp.int32, (step, hd), 1)
            parts = [pl.ds(i * step, step) for i in range(keys // step)]
            for part in parts:
                kt[:, part] = qkv[1, part, :].T
                vt[:, part] = qkv[2, part, :].T
            dk[...] = jnp.zeros_like(dk)
            dv[...] = jnp.zeros_like(dv)

            def one(b, carry):
                rows = tile_of(b, hd)
                query, grad = qkv[0, rows, :], dctx[rows, :]
                ahead = jnp.where(b < tokens // hd, bases[0], bases[1] - tokens) + b * hd
                top = jnp.full((1, hd), MASKED, FULL)
                for i, part in enumerate(parts):
                    scores = contract_last(qkv[1, part, :], query) * score_scale
                    scores = jnp.where(lag <= ahead - bases[i], scores, MASKED)
                    prob[part, :] = scores
                    top = jnp.maximum(top, jnp.max(scores, 0, keepdims=True))
                total = jnp.zeros((1, hd), FULL)
                for part in parts:
                    exponent = jnp.exp(prob[part, :] - top)
                    prob[part, :] = exponent
                    total = total + jnp.sum(exponent, 0, keepdims=True)
                share = 1.0 / total
                inner = jnp.zeros((1, hd), FULL)
                for part in parts:
                    weight = contract_last(qkv[2, part, :], grad)
                    chance = prob[part, :] * share
                    prob[part, :] = chance
                    prob_low[part, :] = chance.astype(LOW)
                    wgt[part, :] = weight
                    inner = inner + jnp.sum(chance * weight, 0, keepdims=True)
                for part in parts:
                    grad_low[part, :] = (prob[part, :] * (wgt[part, :] - inner)).astype(LOW)
                ctxt_all[:, rows] = dot(vt[...], prob_low[...]).astype(LOW)
                query_grad = dot(kt[...], grad_low[...]) * score_scale
                for part in parts:
                    dv[part, :] += dot(prob_low[part, :], grad)
                    dk[part, :] += dot(grad_low[part, :], query)
                turned_grad = spin(query_grad.T, cosine[rows, :], -sines[rows, :])
                pgq[rows, :] = turned_grad.astype(LOW)
                return carry

            lax.fori_loop(0, 2 * tokens // hd, one, 0)
            ctxt[rows_own, :] = ctxt_all[:, :tokens]
            pg[:, pl.ds(pl.multiple_of(own, hd), hd)] = pgq[:tokens, :]
            for i, total in enumerate((dk, dv)):
                kvg_away[i, :, :] = total[2 * tokens :, :].astype(LOW)

        keys = qkv.shape[1]
        pl.run_scoped(
            attention,
            pltpu.VMEM((hd, keys), LOW),
            pltpu.VMEM((hd, keys), LOW),
            pltpu.VMEM((keys, hd), FULL),
            pltpu.VMEM((keys, hd), FULL),
            pltpu.VMEM((keys, hd), LOW),
            pltpu.VMEM((keys, hd), LOW),
        )

        def head_columns(ref, start, i):
            return ref.at[:, pl.ds(pl.multiple_of(start + i * hd, hd), hd)]

        def send_grad(i):
            source = pgq.at[pl.ds(tokens, tokens), :] if i == 0 else head_columns(pg_away, 0, i - 1)
            return links.send(source, head_columns(pg, own, i), links.y)

        kvg_from_x = {i: links.send(kvg_away.at[i], kvg_got.at[i], links.x) for i in (1, 0)}
        pg_from_y = [send_grad(0)]
        ctx_from_y = links.send(ctxt_all.at[:, pl.ds(tokens, tokens)], ctxt.at[rows_own, :], links.y)
        expand.pass_x()
        expand.to_x(True)

        for i in (1, 0):
            kvg_from_x[i].wait_recv()
            for away_rows, target in ((True, pg_away), (False, pg)):
                rows = pl.ds(tokens if away_rows else 0, tokens)
                total = (dk, dv)[i][rows, :] + kvg_got[i, rows, :].astype(FULL)
                if i == 0:
                    total = spin(total * score_scale, cosine[rows, :], -sines[rows, :])
                head_columns(target, 0 if away_rows else own, i if away_rows else 1 + i)[...] = total.astype(LOW)
                if away_rows:
                    pg_from_y.append(send_grad(1 + i))
        expand.pass_y()
        weight.first()
        weight.rest()
        ctx_from_y.wait_recv()
        for copy in pg_from_y:
            copy.wait_recv()

        def first_block(i, carry):
            up_part(i, contract_last(pg[...], wh[tile(i), :]), True)
            return carry

        lax.fori_loop(0, 8, first_block, 0)
        sums[0, 6:7, :heads_wide] = jnp.sum(pg[...].astype(FULL), 0, keepdims=True)
        heads_in.passed()
        heads_sum.to_core()
        expand.share()
        expand.share_far()
        expand.whole()
        for copy in (*from_y.values(), *from_x.values(), *from_far.values(), dctx_from_y, *kvg_from_x.values(), *pg_from_y, ctx_from_y):
            links.sent_out(copy)

    low, full = (functools.partial(lambda kind, *shape: pltpu.VMEM(shape, kind), kind) for kind in (LOW, FULL))
    pl.run_scoped(
        attend,
        low(3, tokens, hd),
        low(tokens, hd),
        low(hd, 2 * tokens),
        low(2 * tokens, hd),
        low(tokens, 2 * hd),
        low(2, 2 * tokens, hd),
        full(2 * tokens, 128),
        full(2 * tokens, 128),
        full(4 * tokens, hd),
        full(4 * tokens, hd),
        low(2, unit, tokens),
    )

    def update(act, actt, slope, ctx, room_o, stage_o, own_o, room_e, total_rows, total_columns, grad_rows):
        def forward(j, slot):
            cols = tile(j)
            value = dot(up[...], room_s[slot]) + raw[4:5, cols]
            normal_share = 0.5 * (1.0 + lax.erf(value * (0.5**0.5)))
            low_act = (value * normal_share).astype(LOW)
            act[:, cols] = low_act
            actt[cols, :] = low_act.T
            density = jnp.exp(value * value * -0.5) * 0.3989422804014327
            slope[:, cols] = (normal_share + value * density).astype(LOW)

        stream(0, 8, lambda j, slot: [(we.at[:, tile(j)], room_s.at[slot])], forward)
        weight.relay()
        ctx[...] = ctxt[...].T

        rows_out = grad_rows.shape[1]

        def columns_cut(ref, c):
            return ref.at[:, here(c)]

        def rows_cut(ref, c):
            return ref.at[pl.ds(c * rows_out, rows_out), :]

        def finish_branch(c):
            cols = here(c)

            def one(part, carry):
                at = tile_of(part, 128)
                total = up[at, cols].astype(FULL) + got_branch[at, cols].astype(FULL)
                final_branch[at, cols] = (x[at, cols].astype(FULL) + total + vecs[4:5, cols]).astype(LOW)
                return carry

            lax.fori_loop(0, tokens // 128, one, 0)

        def finish_up(c):
            add_rows(rows_cut(final_up, c), rows_cut(n1, c), rows_cut(got_up, c))

        line_branch = Line(links, up, got_branch, final_branch, 8, columns_cut, finish_branch)
        line_up = Line(links, n1, got_up, final_up, tokens // rows_out, rows_cut, finish_up)

        def branch_blocks(chunks, block, source):
            def one(n, slot):
                cols = tile(block(n))
                up[:, cols] = (dot(ctx[...], wo[:, cols]) + dot(act[...], room_s[slot])).astype(LOW)
                for at, chunk in enumerate(chunks):
                    pl.when(n == at)(functools.partial(line_branch.start, chunk))

            stream(0, len(chunks), lambda n, slot: [(source(n), room_s.at[slot])], one)

        steps = [(line_branch, c) for c in (0, 1, 2, 4, 3, 5, 6, 7)] + [(line_up, c) for c in range(line_up.chunks)]
        out_copies = []

        def input_rows(c):
            slot = len(out_copies) % 2
            if len(out_copies) >= 2:
                local.wait(*out_copies[-2])
            rows = pl.ds(c * rows_out, rows_out)
            value = x[rows, :].astype(FULL)
            centred = value - jnp.mean(value, -1, keepdims=True)
            scale = lax.rsqrt(jnp.mean(centred * centred, -1, keepdims=True) + NORM_EPS)
            normal = centred * scale
            upstream = final_up[rows, :].astype(FULL)
            inner = upstream - jnp.mean(upstream, -1, keepdims=True)
            inner = inner - normal * jnp.mean(upstream * normal, -1, keepdims=True)
            grad_rows[slot, :, :] = g[rows, :].astype(FULL) + inner * scale
            out_copies.append(
                [local.start(grad_rows.at[slot, :, here(i)], input_grad.at[rows, place[i]]) for i in blocks]
            )

        def serve(count):
            for _ in range(count):
                at = serve.done
                if at < len(steps):
                    steps[at][0].first(steps[at][1])
                if 2 <= at < len(steps) + 2:
                    steps[at - 2][0].second(steps[at - 2][1])
                if at >= 4:
                    line, c = steps[at - 4]
                    line.third(c)
                    if line is line_up:
                        input_rows(c)
                    else:
                        local.start(final_branch.at[:, here(c)], layer_out.at[:, place[c]])
                serve.done += 1

        serve.done = 0
        branch_blocks((0, 1), lambda n: n, lambda n: at_columns(ws_own, pl.multiple_of((links.r + n - 2 * links.r * n) * unit, unit), unit))

        def shrink_block(i, ref, add):
            product(actt[...], g[:, tile(i)], ref, add)

        def output_block(i, ref, add):
            product(ctxt[...], g[:, tile(i)], ref, add)

        def expand_block(i, ref, add):
            product(nt[tile(i), :], slope[...], ref, add)

        shrink.stage = (actt.at[:, pl.ds(unit, unit // 2)], actt.at[:, pl.ds(unit + unit // 2, unit // 2)])
        shrink.own = actt.at[:, pl.ds(0, unit)]
        output.stage, output.own = (stage_o.at[0], stage_o.at[1]), own_o
        shrink_sum = Reduced(lambda n: room_s.at[n], got_core_s, shrink_block)
        output_sum = Reduced(lambda n: room_o.at[n], got_core_o, output_block)
        expand_sum = Reduced(lambda n: room_e.at[n], got_core_e, expand_block)
        heads_sum.fetch()
        heads_sum.add(red_h)
        heads.first()
        heads.direct()
        heads.load()
        n2t_load = local.start(n2t_hbm, nt)
        weight.share()
        serve(1)
        weight.core_y.wait_recv()
        weight.core_x.wait_recv()
        ahead = lambda n: 2 * n + 2 - 3 * (n // 2 if isinstance(n, int) else lax.div(n, 2))
        branch_blocks((2, 4, 3, 5), ahead, lambda n: ws.at[:, tile(ahead(n))])
        serve(1)
        shrink_sum.to_core()
        weight.share_far()
        shrink_sum.fetch()
        shrink_sum.add(red_s)
        shrink.first()
        shrink.direct()
        shrink.load()
        serve(1)
        weight.core_far.wait_recv()
        branch_blocks((6, 7), lambda n: n + 6, lambda n: ws.at[:, tile(n + 6)])
        serve(1)

        def hidden_tile(j, slot):
            cols = tile(j)
            grad = (contract_last(g[...], room_e[slot]) * slope[:, cols].astype(FULL)).astype(LOW)
            slope[:, cols] = grad
            sums[0, 5:6, cols] = jnp.sum(grad.astype(FULL), 0, keepdims=True)

        def shrink_rows(j, slot):
            rows = tile(j)
            pairs = [(weight.here(i).at[rows, :], room_e.at[slot, :, here(i)]) for i in range(2)]
            return pairs + [(ws.at[rows, rest_rows], room_e.at[slot, :, rest_rows])]

        stream(0, 4, shrink_rows, hidden_tile)
        serve(1)
        stream(4, 8, shrink_rows, hidden_tile)
        serve(1)

        def second_block(i, slot):
            up_part(i, contract_last(slope[...], room_e[slot]), False)

        expand_rows = lambda i, slot: [(we.at[tile(i), :], room_e.at[slot])]
        stream(0, 4, expand_rows, second_block)
        serve(1)
        stream(4, 8, expand_rows, second_block)
        line_up.start(*range(line_up.chunks))
        serve(1)

        def share(s, peers):
            return [links.send(sums.at[s], sums_got.at[4 * s + k], peer) for k, peer in enumerate(peers)]

        def shared(s, copies):
            for copy in copies:
                copy.wait_recv()
            total = sums[s, :, :] + sums_got[4 * s, :, :]
            if len(copies) > 1:
                total = total + (sums_got[4 * s + 1, :, :] + sums_got[4 * s + 2, :, :])
            sums[s + 1, :, :] = total

        def share_line(s, peer):
            return links.send(gains.at[s], gains_got.at[s], peer)

        def shared_line(s, copy):
            copy.wait_recv()
            gains[s + 1, :, :] = gains[s, :, :] + gains_got[s, :, :]

        first_share = share(0, [links.core])
        output_sum.to_core()
        shared(0, first_share)
        second_share = share(1, [links.x, links.y, links.far])
        output_sum.fetch()
        output_sum.add(red_o)
        output.first()
        output.direct()
        output.load()

        local.wait(n2t_load)
        expand_sum.to_core()
        serve(1)
        shrink.second()
        serve(1)
        expand_sum.fetch()
        serve(1)
        expand_sum.add(None)
        red = {k: room_e.at[turns.index(k)] for k in range(4)}
        expand = Scattered(links, local, [red[k] for k in range(4)], at_rows, unit, via_e, got_e, None, red[0])
        expand.first()
        expand.direct()
        serve(2)
        half_rows = pl.ds(pl.multiple_of(links.r * unit, unit), unit)
        column_slots = Slots(total_columns.at[0], total_columns.at[1])
        serve(2)
        shrink.third(column_slots, shrink_grad.at[:, half_rows], total_columns.shape[1])
        serve(1)
        shared(1, second_share)
        for row in range(4):
            for side in range(2):
                at = 2 * row + side
                gains[0, at : at + 1, :] = sums[2, row : row + 1, side * (width // 2) : (side + 1) * (width // 2)]
        pair_share = share_line(0, links.pair)
        serve(3)

        expand.via_x.wait_recv()
        top, end = red[2].at[pl.ds(0, unit // 2), :], red[1].at[pl.ds(unit // 2, unit // 2), :]
        add_rows(top, top, via_e.at[0])
        expand.y_top = links.send(top, got_e.at[1, pl.ds(0, unit // 2), :], links.y)
        expand.via_y.wait_recv()
        add_rows(end, end, via_e.at[1])
        expand.x_end = links.send(end, got_e.at[0, pl.ds(unit // 2, unit // 2), :], links.x)
        heads.second()
        output.second()
        serve(len(steps) - 1 - serve.done)
        shared_line(0, pair_share)
        across_share = share_line(1, links.across)
        serve(2)
        expand_slots = Slots(total_rows.at[0], total_rows.at[1])
        expand.third(expand_slots, expand_grad.at[half_rows, :], total_rows.shape[1])
        serve(len(steps) + 4 - serve.done)
        expand_slots.end()
        total_slots = Slots(*[total_rows.at[n, :, pl.ds(0, heads_wide)] for n in range(2)])
        heads.third(total_slots, heads_grad.at[half_rows, :], total_rows.shape[1])
        output.third(column_slots, output_grad.at[:, half_rows], total_columns.shape[1])
        total_slots.end()
        column_slots.end()
        shared_line(1, across_share)
        for row in range(4):
            for side in range(2):
                at = 2 * row + side
                sums_out[row : row + 1, side * (width // 2) : (side + 1) * (width // 2)] = gains[2, at : at + 1, :]
        sums_out[4:8, :] = sums[2, 4:8, :]
        for copy in (*shrink.other, *output.other, *heads.other, *expand.other):
            copy.wait_recv()
        assert links.count <= COPIES
        links.end()
        line_branch.end()
        line_up.end()
        local.end()


    pl.run_scoped(
        update,
        low(tokens, units),
        low(units, tokens),
        low(tokens, units),
        low(tokens, out_wide),
        low(4, out_wide, unit),
        low(2, out_wide, unit // 2),
        low(out_wide, unit),
        low(4, unit, units),
        full(2, unit // 4, units),
        full(2, out_wide, unit),
        full(2, 32, width),
    )


def block_call(line_size, x, g, heads_rows, output_rows, expand_weight, shrink_weight, vectors, order):
    tokens, width = x.shape
    heads_wide, out_wide, units = heads_rows.shape[1], output_rows.shape[0], expand_weight.shape[1]
    hd, unit, half = heads_wide // 6, width // 8, width // 16
    low = lambda *shape: pltpu.VMEM(shape, LOW)
    full = lambda *shape: pltpu.VMEM(shape, FULL)
    work = lambda *shape: jax.ShapeDtypeStruct(shape, LOW)
    outs = [
        work(tokens, width),
        jax.ShapeDtypeStruct((tokens, width), FULL),
        jax.ShapeDtypeStruct((2 * unit, heads_wide), FULL),
        jax.ShapeDtypeStruct((out_wide, 2 * unit), FULL),
        jax.ShapeDtypeStruct((2 * unit, units), FULL),
        jax.ShapeDtypeStruct((units, 2 * unit), FULL),
        work(width, units),
        work(units, width),
        work(width, tokens),
        work(4, units, unit),
        work(4, out_wide, unit),
        work(4, unit, heads_wide),
        work(4, unit, units),
        work(4, units, unit),
        work(4, out_wide, unit),
        work(4, unit, heads_wide),
        jax.ShapeDtypeStruct((8, width), FULL),
    ]
    scratch = [
        *[low(tokens, width)] * 4, low(width, tokens), full(tokens, 256),
        low(width, heads_wide), low(out_wide, width), low(4, 4 * tokens, hd), low(2 * tokens, hd),
        low(out_wide, tokens), low(tokens, heads_wide), low(2, 2 * tokens, hd),
        *[low(tokens, width)] * 4,
        low(2, half, heads_wide), low(2, unit, heads_wide),
        low(2, out_wide, half), low(2, out_wide, unit),
        low(2, units, half), low(2, units, unit),
        low(2, half, units), low(2, unit, units),
        full(8, width), full(8, width), full(3, 8, width), full(7, 8, width), full(3, 8, width // 2), full(2, 8, width // 2),
        pltpu.SemaphoreType.DMA((3, 2)),
        pltpu.SemaphoreType.DMA((8,)),
        pltpu.SemaphoreType.DMA((320,)),
        pltpu.SemaphoreType.DMA((COPIES,)),
        pltpu.SemaphoreType.DMA((COPIES,)),
    ]
    return pl.pallas_call(
        functools.partial(block_kernel, hd**-0.5, line_size),
        out_shape=outs,
        in_specs=[ANY] * 6 + [IN_VMEM] * 8 + [pl.BlockSpec(memory_space=pltpu.SMEM)],
        out_specs=[ANY] * 16 + [IN_VMEM],
        scratch_shapes=scratch,
        compiler_params=pltpu.CompilerParams(
            collective_id=0, has_side_effects=True, vmem_limit_bytes=VMEM_BYTES
        ),
    )(x, g, heads_rows, output_rows, expand_weight, shrink_weight, *vectors, order)


def square_local(
    layer_input,
    block_order,
    first_gain,
    first_bias,
    second_gain,
    second_bias,
    heads_weight,
    heads_bias,
    output_weight,
    output_bias,
    expand_weight,
    expand_bias,
    shrink_weight,
    shrink_bias,
    cotangent,
):
    heads_rows = heads_weight.reshape(heads_weight.shape[0], -1)
    output_rows = output_weight.reshape(-1, output_weight.shape[2])
    vectors = (first_gain, first_bias, second_gain, second_bias, expand_bias, heads_bias, output_bias, shrink_bias)
    *results, sums = block_call(
        lax.axis_size("tensor"),
        layer_input[0],
        cotangent[0],
        heads_rows,
        output_rows,
        expand_weight,
        shrink_weight,
        vectors,
        block_order,
    )
    results = store_call(results[:6], sums, heads_weight.shape)
    layer_output, input_grad, heads_grad, output_grad, expand_grad, shrink_grad = results[:6]
    first_gain_grad, first_bias_grad, second_gain_grad, second_bias_grad = (vec.reshape(-1) for vec in results[6:10])
    output_bias_grad, expand_bias_grad, shrink_bias_grad = (vec.reshape(-1) for vec in results[10:13])
    return (
        layer_output[None],
        input_grad[None],
        first_gain_grad,
        first_bias_grad,
        second_gain_grad,
        second_bias_grad,
        heads_grad,
        results[13],
        output_grad.reshape(output_weight.shape),
        output_bias_grad,
        expand_grad,
        expand_bias_grad,
        shrink_grad,
        shrink_bias_grad,
    )


def store_kernel(*refs):
    *full_in, sums = refs[:7]
    full_out, rows_out, heads_bias_out = refs[7:13], refs[13:20], refs[20]
    for source, target in zip(full_in, full_out):
        if len(target.shape) == len(source.shape):
            target[...] = source[...]
        else:
            wide = target.shape[2]
            for head in range(target.shape[1]):
                target[:, head, :] = source[:, head * wide : (head + 1) * wide]

    @pl.when(pl.program_id(0) == 0)
    def _():
        for row, target in zip((0, 1, 2, 3, 4, 5, 4), rows_out):
            target[...] = sums[row : row + 1, :]
        wide = heads_bias_out.shape[1]
        for head in range(heads_bias_out.shape[0]):
            heads_bias_out[head : head + 1, :] = sums[6:7, head * wide : (head + 1) * wide]


def store_call(results, sums, heads_shape):
    steps = 2
    width = sums.shape[1]

    def cut(shape):
        zeros = (0,) * (len(shape) - 1)
        return pl.BlockSpec((shape[0] // steps,) + tuple(shape[1:]), lambda i: (i, *zeros))

    def whole(shape):
        return pl.BlockSpec(tuple(shape), lambda i: (0,) * len(shape))

    kept = [result.shape for result in results]
    kept[2] = heads_shape
    rows, heads_bias = (1, width), heads_shape[1:]
    outs = [jax.ShapeDtypeStruct(shape, result.dtype) for shape, result in zip(kept, results)]
    outs += [jax.ShapeDtypeStruct(rows, FULL)] * 7 + [jax.ShapeDtypeStruct(heads_bias, FULL)]
    return pl.pallas_call(
        store_kernel,
        grid=(steps,),
        out_shape=outs,
        in_specs=[cut(result.shape) for result in results] + [whole(sums.shape)],
        out_specs=[cut(shape) for shape in kept] + [whole(rows)] * 7 + [whole(heads_bias)],
        compiler_params=pltpu.CompilerParams(vmem_limit_bytes=VMEM_BYTES),
    )(*results, sums)


def ring_local(
    layer_input,
    block_order,
    first_gain,
    first_bias,
    second_gain,
    second_bias,
    heads_weight,
    heads_bias,
    output_weight,
    output_bias,
    expand_weight,
    expand_bias,
    shrink_weight,
    shrink_bias,
    cotangent,
):
    tokens_here = layer_input.shape[1]
    fsdp_count = lax.axis_size("fsdp")
    head_dim = output_weight.shape[1]
    score_scale = head_dim ** (-0.5)
    order_row = block_order[0]
    device_slot = lax.axis_index("fsdp")
    own_block = jnp.sum(
        jnp.where(jnp.arange(fsdp_count, dtype=jnp.int32) == device_slot, order_row, 0)
    )
    offsets = jnp.arange(tokens_here, dtype=jnp.int32)
    query_pos = own_block * tokens_here + offsets
    key_pos = jnp.repeat(order_row, tokens_here) * tokens_here + jnp.tile(offsets, fsdp_count)
    allowed = key_pos[None, :] <= query_pos[:, None]
    cosine, sine_part = rotary_tables(query_pos, ROT)
    hidden_in = layer_input[0].astype(jnp.float32)
    gain_one = first_gain.astype(jnp.float32)
    shift_one = first_bias.astype(jnp.float32)
    gain_two = second_gain.astype(jnp.float32)
    shift_two = second_bias.astype(jnp.float32)
    norm_one_low = layer_norm(hidden_in, gain_one, shift_one).astype(jnp.bfloat16)
    norm_two_low = layer_norm(hidden_in, gain_two, shift_two).astype(jnp.bfloat16)
    heads_full, output_full, expand_full, shrink_full = (
        lax.all_gather(heads_weight, "fsdp", axis=0, tiled=True),
        lax.all_gather(output_weight, "fsdp", axis=2, tiled=True),
        lax.all_gather(expand_weight, "fsdp", axis=0, tiled=True),
        lax.all_gather(shrink_weight, "fsdp", axis=1, tiled=True),
    )
    projected = jnp.einsum(
        "td,dhe->hte", norm_one_low, heads_full, preferred_element_type=jnp.float32
    )
    projected = projected + heads_bias.astype(jnp.float32)[:, None, :]
    query_pre = projected[..., :head_dim]
    key_pre = projected[..., head_dim : 2 * head_dim]
    query_low = rotate(query_pre, cosine, sine_part).astype(jnp.bfloat16)
    key_low = rotate(key_pre, cosine, sine_part).astype(jnp.bfloat16)
    value_low = projected[..., 2 * head_dim :].astype(jnp.bfloat16)
    key_all, value_all = (
        lax.all_gather(key_low, "fsdp", axis=1, tiled=True),
        lax.all_gather(value_low, "fsdp", axis=1, tiled=True),
    )

    def attend_head(operands):
        query_head, key_head, value_head = operands
        probability = softmax_rows(contract_last(query_head, key_head) * score_scale, allowed)
        return jnp.dot(
            probability.astype(jnp.bfloat16), value_head, preferred_element_type=jnp.float32
        )

    context = lax.map(attend_head, (query_low, key_all, value_all))
    context_low = context.astype(jnp.bfloat16)
    expand_in = jnp.dot(
        norm_two_low, expand_full, preferred_element_type=jnp.float32
    ) + expand_bias.astype(jnp.float32)
    activation_low = jax.nn.gelu(expand_in, approximate=False).astype(jnp.bfloat16)
    branch_part = jnp.einsum(
        "hte,hed->td", context_low, output_full, preferred_element_type=jnp.float32
    )
    branch_part = branch_part + jnp.dot(
        activation_low, shrink_full, preferred_element_type=jnp.float32
    )
    branch = lax.psum(branch_part, "tensor")
    layer_output = (
        hidden_in + branch + output_bias.astype(jnp.float32) + shrink_bias.astype(jnp.float32)
    ).astype(jnp.bfloat16)[None]
    heads_back, output_back, expand_back, shrink_back = (
        lax.all_gather(heads_weight, "fsdp", axis=0, tiled=True),
        lax.all_gather(output_weight, "fsdp", axis=2, tiled=True),
        lax.all_gather(expand_weight, "fsdp", axis=0, tiled=True),
        lax.all_gather(shrink_weight, "fsdp", axis=1, tiled=True),
    )
    key_back, value_back = (
        lax.all_gather(key_low, "fsdp", axis=1, tiled=True),
        lax.all_gather(value_low, "fsdp", axis=1, tiled=True),
    )
    grad_out = cotangent[0]
    grad_float = grad_out.astype(jnp.float32)
    output_weight_grad = jnp.einsum(
        "hte,td->hed", context_low, grad_out, preferred_element_type=jnp.float32
    )
    shrink_weight_grad = contract_first(activation_low, grad_out)
    bias_total = jnp.sum(grad_float, 0)
    context_grad = jnp.einsum(
        "td,hed->hte", grad_out, output_back, preferred_element_type=jnp.float32
    ).astype(jnp.bfloat16)
    activation_grad = contract_last(grad_out, shrink_back)
    _, gelu_back = jax.vjp(lambda inner_val: jax.nn.gelu(inner_val, approximate=False), expand_in)
    expand_grad = gelu_back(activation_grad)[0].astype(jnp.bfloat16)
    expand_weight_grad = contract_first(norm_two_low, expand_grad)
    expand_bias_grad = jnp.sum(expand_grad.astype(jnp.float32), 0)
    norm_two_grad = contract_last(expand_grad, expand_back)

    def attend_back(operands):
        query_head, key_head, value_head, context_head = operands
        probability = softmax_rows(contract_last(query_head, key_head) * score_scale, allowed)
        prob_low = probability.astype(jnp.bfloat16)
        weight_grad = contract_last(context_head, value_head)
        row_inner = jnp.sum(probability * weight_grad, -1, keepdims=True)
        score_grad = (probability * (weight_grad - row_inner)).astype(jnp.bfloat16)
        query_grad = jnp.dot(score_grad, key_head, preferred_element_type=jnp.float32) * score_scale
        key_grad = contract_first(score_grad, query_head) * score_scale
        value_grad = contract_first(prob_low, context_head)
        return (query_grad, key_grad, value_grad)

    query_grad, key_grad_all, value_grad_all = lax.map(
        attend_back, (query_low, key_back, value_back, context_grad)
    )
    key_grad, value_grad = (
        lax.psum_scatter(key_grad_all, "fsdp", scatter_dimension=1, tiled=True),
        lax.psum_scatter(value_grad_all, "fsdp", scatter_dimension=1, tiled=True),
    )
    _, rotate_back = jax.vjp(lambda inner_val: rotate(inner_val, cosine, sine_part), query_pre)
    projected_grad = jnp.concatenate(
        [rotate_back(query_grad)[0], rotate_back(key_grad)[0], value_grad], -1
    ).astype(jnp.bfloat16)
    heads_weight_grad = jnp.einsum(
        "td,hte->dhe", norm_one_low, projected_grad, preferred_element_type=jnp.float32
    )
    heads_bias_grad = jnp.sum(projected_grad.astype(jnp.float32), 1)
    norm_one_grad = jnp.einsum(
        "hte,dhe->td", projected_grad, heads_back, preferred_element_type=jnp.float32
    )
    norm_one_grad, norm_two_grad = lax.psum((norm_one_grad, norm_two_grad), "tensor")
    _, first_back = jax.vjp(layer_norm, hidden_in, gain_one, shift_one)
    input_first, first_gain_grad, first_bias_grad = first_back(norm_one_grad)
    _, second_back = jax.vjp(layer_norm, hidden_in, gain_two, shift_two)
    input_second, second_gain_grad, second_bias_grad = second_back(norm_two_grad)
    input_grad = (grad_float + input_first + input_second)[None]
    small_sums = lax.psum(
        (
            first_gain_grad,
            first_bias_grad,
            second_gain_grad,
            second_bias_grad,
            bias_total,
            expand_bias_grad,
            heads_bias_grad,
        ),
        ("replica", "fsdp"),
    )
    shard_parts = (
        lax.psum_scatter(heads_weight_grad, "fsdp", scatter_dimension=0, tiled=True),
        lax.psum_scatter(output_weight_grad, "fsdp", scatter_dimension=2, tiled=True),
        lax.psum_scatter(expand_weight_grad, "fsdp", scatter_dimension=0, tiled=True),
        lax.psum_scatter(shrink_weight_grad, "fsdp", scatter_dimension=1, tiled=True),
    )
    reduced = lax.psum((shard_parts[0], shard_parts[1], shard_parts[2], shard_parts[3]), "replica")
    return (
        layer_output,
        input_grad,
        small_sums[0],
        small_sums[1],
        small_sums[2],
        small_sums[3],
        reduced[0],
        small_sums[6],
        reduced[1],
        small_sums[4],
        reduced[2],
        small_sums[5],
        reduced[3],
        small_sums[4],
    )


def solution(mesh):
    placed = (
        P("replica", "fsdp", None),
        P("replica", None),
        P(),
        P(),
        P(),
        P(),
        P("fsdp", "tensor", None),
        P("tensor", None),
        P("tensor", None, "fsdp"),
        P(),
        P("fsdp", "tensor"),
        P("tensor"),
        P("tensor", "fsdp"),
        P(),
        P("replica", "fsdp", None),
    )
    local = square_local if mesh.shape["fsdp"] == 4 and mesh.shape["replica"] == 2 and mesh.shape["tensor"] == 4 else ring_local
    return jax.shard_map(
        local,
        mesh=mesh,
        in_specs=placed,
        out_specs=(
            P("replica", "fsdp", None),
            P("replica", "fsdp", None),
            P(),
            P(),
            P(),
            P(),
            P("fsdp", "tensor", None),
            P("tensor", None),
            P("tensor", None, "fsdp"),
            P(),
            P("fsdp", "tensor"),
            P("tensor"),
            P("tensor", "fsdp"),
            P(),
        ),
        check_vma=False,
    )
```

```python
import functools
import math

import jax
import jax.numpy as jnp
from jax import lax
from jax.experimental import pallas as pl
from jax.experimental.pallas import tpu as pltpu
from jax.sharding import PartitionSpec as P

ROT = 64


NORM_EPS = 1e-05
MASKED = -1e30


def layer_norm(values_in, gain_vec, shift_vec):
    average = jnp.mean(values_in, -1, keepdims=True)
    centred = values_in - average
    spread_sq = jnp.mean(centred * centred, -1, keepdims=True)
    return centred * lax.rsqrt(spread_sq + NORM_EPS) * gain_vec + shift_vec


def rotate(values_in, cosine, sine_part):
    rot_width = cosine.shape[-1]
    half_width = rot_width // 2
    turning = values_in[..., :rot_width]
    swapped = jnp.concatenate([-turning[..., half_width:], turning[..., :half_width]], -1)
    return jnp.concatenate([turning * cosine + swapped * sine_part, values_in[..., rot_width:]], -1)


def rotary_tables(positions, rot_width):
    frequency = jnp.power(10000.0, -jnp.arange(0, rot_width, 2, dtype=jnp.float32) / rot_width)
    angle_half = positions.astype(jnp.float32)[:, None] * frequency[None, :]
    angles = jnp.concatenate([angle_half, angle_half], -1)
    return (jnp.cos(angles), jnp.sin(angles))


def contract_last(left_op, right_op):
    return lax.dot_general(
        left_op, right_op, (((1,), (1,)), ((), ())), preferred_element_type=jnp.float32
    )


def contract_first(left_op, right_op):
    return lax.dot_general(
        left_op, right_op, (((0,), (0,)), ((), ())), preferred_element_type=jnp.float32
    )


def softmax_rows(scores, allowed):
    masked_scores = jnp.where(allowed, scores, MASKED)
    row_top = jnp.max(masked_scores, -1, keepdims=True)
    exponent = jnp.exp(masked_scores - row_top)
    return exponent / jnp.sum(exponent, -1, keepdims=True)


LOW = jnp.bfloat16
FULL = jnp.float32


MESH = pl.DeviceIdType.MESH
ANY = pl.BlockSpec(memory_space=pl.ANY)
IN_VMEM = pl.BlockSpec(memory_space=pltpu.VMEM)
VMEM_BYTES = 63 * 2**20
COPIES = 157
LOCALS = 34


class Sent:
    def __init__(self, links, k, source, target, peer):
        self.links, self.k, self.source, self.target, self.peer = links, k, source, target, peer

    def copy(self):
        return self.links.copy_at(self.k, self.source, self.target, self.peer)

    def start(self):
        self.copy().start()

    def wait_recv(self):
        self.copy().wait_recv()

    def wait_send(self):
        self.copy().wait_send()


class Links:
    def __init__(self, send_sem, recv_sem, line=0):
        self.send_sem, self.recv_sem, self.sent, self.count = send_sem, recv_sem, [], 0
        self.r, self.f, self.t = (lax.axis_index(name) for name in ("replica", "fsdp", "tensor"))
        self.xb, self.yb = lax.rem(self.f, 2), lax.div(self.f, 2)
        self.x = (self.r, self.f + 1 - 2 * self.xb, self.t)
        self.y = (self.r, lax.rem(self.f + 2, 4), self.t)
        self.core = (1 - self.r, self.f, self.t)
        self.peers = [self.x, self.y, self.core]
        if line:
            self.line = line
            self.left, self.right, self.across = (
                (self.r, self.f, lax.rem(self.t + step, line)) for step in (line - 1, 1, 2)
            )
            self.pair = (self.r, self.f, self.t + 1 - 2 * lax.rem(self.t, 2))
            self.far = (self.r, 3 - self.f, self.t)
            self.mirror = (self.r, self.f, line - 1 - self.t)
            self.peers += [self.far, self.left, self.right, self.across]

    def meet(self):
        barrier = pltpu.get_barrier_semaphore()
        for peer in self.peers:
            pl.semaphore_signal(barrier, inc=1, device_id=peer, device_id_type=MESH)
        pl.semaphore_wait(barrier, len(self.peers))

    def prepare(self, source, target, peer):
        self.count += 1
        return Sent(self, self.count - 1, source, target, peer)

    def send(self, source, target, peer):
        copy = self.prepare(source, target, peer)
        copy.start()
        self.sent.append(copy)
        return copy

    def series(self, count):
        k = self.count
        self.count += count
        return k

    def copy_at(self, k, source, target, peer):
        return pltpu.make_async_remote_copy(
            src_ref=source,
            dst_ref=target,
            send_sem=self.send_sem.at[k],
            recv_sem=self.recv_sem.at[k],
            device_id=peer,
            device_id_type=MESH,
        )

    def sent_out(self, copy):
        copy.wait_send()
        self.sent = [other for other in self.sent if other is not copy]

    def end(self):
        for copy in self.sent:
            copy.wait_send()

    def block(self, i):
        place = 0
        for size, bit in ((4, self.yb), (2, self.xb), (1, self.r)):
            mine = lax.rem(lax.div(i, size), 2) if isinstance(i, jax.Array) else i // size % 2
            place = place + size * (mine + bit - 2 * mine * bit)
        return place


class Local:
    def __init__(self, sem):
        self.sem, self.count, self.open, self.free = sem, 0, [], []

    def start(self, source, target):
        if not self.free:
            self.free.append(self.count)
            self.count += 1
        k = self.free.pop(0)
        copy = pltpu.make_async_copy(source, target, self.sem.at[k])
        copy.start()
        self.open.append((copy, k))
        return copy

    def wait(self, *copies):
        for copy in copies:
            copy.wait()
            self.free += [k for other, k in self.open if other is copy]
            self.open = [pair for pair in self.open if pair[0] is not copy]

    def end(self):
        self.wait(*[copy for copy, _ in self.open])


def at_rows(ref, start, size):
    return ref.at[pl.ds(start, size), :]


def at_columns(ref, start, size):
    return ref.at[:, pl.ds(start, size)]


class Gathered:
    def __init__(self, links, local, shard, full, cut, unit, copied=True):
        self.links, self.local, self.full, self.cut = links, local, full, cut
        self.shard, self.unit, self.half = shard, unit, unit // 2
        self.starts = [pl.multiple_of(links.r * unit + start, self.half) for start in (0, self.half)]
        self.bases = [pl.multiple_of(base * unit, unit) for base in (links.r, 1 - links.r)]
        self.copies = [local.start(self.here(i), self.at(i)) for i in range(2)] if copied else []
        self.from_x, self.from_y = {}, {}

    def here(self, i):
        return self.cut(self.shard, self.bases[i], self.unit)

    def mine(self, lower):
        return self.cut(self.shard, self.starts[lower], self.half)

    def at(self, block, start=0, size=None):
        return self.cut(self.full, block * self.unit + start, self.unit if size is None else size)

    def to_x(self, lower):
        source, target = self.mine(lower), self.at(2, self.half * lower, self.half)
        self.from_x[lower] = self.links.send(source, target, self.links.x)

    def to_y(self, lower):
        source, target = self.mine(lower), self.at(4, self.half * lower, self.half)
        self.from_y[lower] = self.links.send(source, target, self.links.y)

    def first(self):
        self.to_x(False)
        self.to_y(True)

    def rest(self):
        self.to_x(True)
        self.to_y(False)

    def pass_y(self):
        half = self.half
        self.from_x[False].wait_recv()
        self.far_top = self.links.send(self.at(2, 0, half), self.at(6, 0, half), self.links.y)

    def pass_x(self):
        half = self.half
        self.from_y[True].wait_recv()
        self.far_end = self.links.send(self.at(4, half, half), self.at(6, half, half), self.links.x)

    def relay(self):
        self.pass_y()
        self.pass_x()

    def share(self):
        self.from_y[False].wait_recv()
        self.core_y = self.links.send(self.at(4), self.at(5), self.links.core)
        self.from_x[True].wait_recv()
        self.core_x = self.links.send(self.at(2), self.at(3), self.links.core)

    def share_far(self):
        self.far_top.wait_recv()
        self.far_end.wait_recv()
        self.core_far = self.links.send(self.at(6), self.at(7), self.links.core)

    def passed(self):
        for copy in (self.far_top, self.far_end, self.core_x, self.core_y, self.core_far):
            self.links.sent_out(copy)

    def whole(self):
        self.local.wait(*self.copies)
        for copy in (self.core_x, self.core_y, self.core_far):
            copy.wait_recv()


def odd(j):
    return j % 2 if isinstance(j, int) else lax.rem(j, 2)


def tile_of(j, size):
    return pl.ds(pl.multiple_of(j * size, size), size)


def dot(left, right):
    return jnp.dot(left, right, preferred_element_type=FULL)


def spin(values_in, cosine, sine):
    head = values_in[:, :128]
    lane = lax.broadcasted_iota(jnp.int32, head.shape, 1)
    swapped = jnp.where(lane < ROT // 2, pltpu.roll(head, 96, 1), pltpu.roll(head, 32, 1))
    return jnp.concatenate([head * cosine + swapped * sine, values_in[:, 128:]], -1)


class Scattered:
    def __init__(self, links, local, blocks, cut, unit, via, got, stage=None, own=None):
        self.links, self.local, self.blocks, self.cut, self.unit = links, local, blocks, cut, unit
        self.via, self.got = [via.at[n] for n in range(2)], [got.at[n] for n in range(2)]
        self.stage, self.own = stage, own
        self.half, self.loads = unit // 2, []

    def load(self):
        self.loads = [
            self.local.start(self.cut(self.blocks[1], self.half, self.half), self.stage[0]),
            self.local.start(self.cut(self.blocks[2], 0, self.half), self.stage[1]),
            self.local.start(self.blocks[0], self.own),
        ]

    def first(self):
        half, cut, far = self.half, self.cut, self.blocks[3]
        self.via_x = self.links.send(cut(far, 0, half), self.via[0], self.links.x)
        self.via_y = self.links.send(cut(far, half, half), self.via[1], self.links.y)

    def direct(self):
        half, cut = self.half, self.cut
        self.x_top = self.links.send(cut(self.blocks[1], 0, half), cut(self.got[0], 0, half), self.links.x)
        self.y_end = self.links.send(cut(self.blocks[2], half, half), cut(self.got[1], half, half), self.links.y)

    def second(self):
        half, cut = self.half, self.cut
        self.local.wait(*self.loads[:2])
        self.via_x.wait_recv()
        add_rows(self.stage[1], self.stage[1], self.via[0])
        self.y_top = self.links.send(self.stage[1], cut(self.got[1], 0, half), self.links.y)
        self.via_y.wait_recv()
        add_rows(self.stage[0], self.stage[0], self.via[1])
        self.x_end = self.links.send(self.stage[0], cut(self.got[0], half, half), self.links.x)

    def third(self, slots, place, step, between=lambda: None):
        for copy in (self.x_top, self.x_end, self.y_top, self.y_end):
            copy.wait_recv()
        if self.loads:
            self.local.wait(self.loads[2])
        self.other = []
        for start in range(0, self.own.shape[0], step):
            between()
            rows = pl.ds(start, step)
            at, total = slots.take()
            add_rows(total, self.own.at[rows, :], self.got[0].at[rows, :], self.got[1].at[rows, :])
            kept = self.local.start(total, place.at[rows, :])
            other = self.links.send(total, place.at[rows, :], self.links.core)
            self.other.append(other)

            def done(kept=kept, other=other):
                self.local.wait(kept)
                self.links.sent_out(other)

            slots.busy[at] = done


def add_rows(target, *parts):
    rows, wide = target.shape
    step = min(rows, 32 if wide > 512 else 256)

    def one(c, carry):
        at = pl.ds(pl.multiple_of(c * step, step), step)
        total = parts[0][at, :].astype(FULL)
        for part in parts[1:]:
            total = total + part[at, :].astype(FULL)
        target[at, :] = total.astype(target.dtype)
        return carry

    lax.fori_loop(0, rows // step, one, 0)


class Line:
    def __init__(self, links, part, got, final, chunks, cut, finish):
        self.links, self.part, self.got, self.final, self.cut, self.finish = links, part, got, final, cut, finish
        self.chunks = chunks
        self.outer = jnp.logical_or(links.t == 0, links.t == links.line - 1)
        self.middle = jnp.logical_not(self.outer)
        self.inward = [self.make(c, part, final, links.pair) for c in range(chunks)]
        self.across = [self.make(c, part, got, links.mirror) for c in range(chunks)]
        self.outward = [
            Sent(links, self.inward[c].k, cut(final, c), cut(final, c), links.pair) for c in range(chunks)
        ]

    def make(self, c, source, target, peer):
        return self.links.prepare(self.cut(source, c), self.cut(target, c), peer)

    def start(self, *chunks):
        @pl.when(self.outer)
        def _():
            for c in chunks:
                self.inward[c].start()

    def first(self, c):
        @pl.when(self.middle)
        def _():
            self.inward[c].wait_recv()
            part = self.cut(self.part, c)
            add_rows(part, part, self.cut(self.final, c))
            self.across[c].start()

    def second(self, c):
        @pl.when(self.middle)
        def _():
            self.across[c].wait_recv()
            self.finish(c)
            self.outward[c].start()

    def third(self, c):
        @pl.when(self.outer)
        def _():
            self.outward[c].wait_recv()

    def end(self):
        @pl.when(self.outer)
        def _():
            for copy in self.inward:
                copy.wait_send()

        @pl.when(self.middle)
        def _():
            for copy in self.across + self.outward:
                copy.wait_send()


class Slots:
    def __init__(self, *refs):
        self.refs, self.busy, self.count = refs, {}, 0

    def take(self):
        at = self.count % len(self.refs)
        self.count += 1
        if at in self.busy:
            self.busy.pop(at)()
        return at, self.refs[at]

    def end(self):
        for wait in self.busy.values():
            wait()
        self.busy = {}


def block_kernel(
    score_scale, line_size,
    x_hbm, g_hbm, wh_hbm, wo_hbm, we_own, ws_own, gain_one, shift_one, gain_two, shift_two, units_bias, heads_bias,
    bias_one, bias_two, order,
    layer_out, input_grad, heads_grad, output_grad, expand_grad, shrink_grad, we, ws, n2t_hbm, got_core_s, got_core_o,
    got_core_h, got_core_e, red_s, red_o, red_h, sums_out,
    x, g, up, n1, nt, stat, wh, wo, qkv, dctx, ctxt, pg, kvg_got, got_branch, final_branch, got_up, final_up,
    via_h, got_h, via_o, got_o, via_s, got_s, via_e, got_e, raw, vecs, sums, sums_got, gains, gains_got,
    loop_sem, block_sem, local_sem, send_sem, recv_sem,
):
    links, local = Links(send_sem, recv_sem, line_size), Local(local_sem)
    tokens, width = x.shape
    units, heads_wide, out_wide = we.shape[1], wh.shape[1], wo.shape[0]
    hd = dctx.shape[1]
    unit = width // 8
    blocks = range(8)
    room_s = qkv
    place = [pl.ds(pl.multiple_of(links.block(i) * unit, unit), unit) for i in blocks]

    def here(i):
        return pl.ds(i * unit, unit)

    rest_rows = pl.ds(2 * unit, width - 2 * unit)

    def tile(j):
        return pl.ds(j * unit if isinstance(j, int) else pl.multiple_of(j * unit, unit), unit)

    def placed(i):
        return pl.ds(pl.multiple_of(links.block(i) * unit, unit), unit)

    def stream(start, end, load, body):
        def copies(j):
            pairs = load(j, odd(j))
            return [pltpu.make_async_copy(*pair, loop_sem.at[n, odd(j)]) for n, pair in enumerate(pairs)]

        for copy in copies(start):
            copy.start()

        def one(j, carry):
            @pl.when(j + 1 < end)
            def _():
                for copy in copies(j + 1):
                    copy.start()

            for copy in copies(j):
                copy.wait()
            body(j, odd(j))
            return carry

        lax.fori_loop(start, end, one, 0)

    x_in, g_in = [], []
    for i in blocks:
        cols = pl.ds(pl.multiple_of(links.block(i) * unit, unit), unit)
        x_in.append(local.start(x_hbm.at[:, cols], x.at[:, pl.ds(i * unit, unit)]))
        g_in.append(local.start(g_hbm.at[:, cols], g.at[:, pl.ds(i * unit, unit)]))
    links.meet()
    heads_in = Gathered(links, local, wh_hbm, wh, at_rows, unit)
    output_in = Gathered(links, local, wo_hbm, wo, at_columns, unit)
    expand = Gathered(links, local, we_own, we, at_rows, unit)
    weight = Gathered(links, local, ws_own, ws, at_columns, unit, False)
    heads_in.first()
    heads_in.rest()

    def row(ref):
        return ref[...].astype(FULL).reshape(1, -1)

    for i, vec in enumerate((gain_one, shift_one, gain_two, shift_two, units_bias)):
        raw[i : i + 1, :] = row(vec)
    raw[6:7, :] = row(bias_one) + row(bias_two)
    head_rows = heads_bias[...].astype(FULL)
    raw[5:6, : 3 * hd], raw[7:8, : 3 * hd] = head_rows[0:1, :], head_rows[1:2, :]

    turns = (3, 1, 2, 0)

    def turn_of(n):
        return jnp.where(n == 0, 3, jnp.where(n == 3, 0, n))

    class Reduced:
        def __init__(self, room, got, block):
            self.room, self.got, self.block = room, got, block
            self.gots = [got.at[k] for k in range(4)]

        def to_core(self):
            first = links.series(4)

            def one(n, carry):
                k = turn_of(n)
                self.block(2 * k + 1, self.room(n), False)
                links.copy_at(first + n, self.room(n), self.got.at[k], links.core).start()
                return carry

            lax.fori_loop(0, 4, one, 0)
            self.copies = [Sent(links, first + n, self.room(n), self.gots[turns[n]], links.core) for n in range(4)]

        def fetch(self):
            for n in range(4):
                self.copies[n].wait_send()
                self.copies[n].wait_recv()
                pltpu.make_async_copy(self.got.at[turns[n]], self.room(n), block_sem.at[n]).start()

        def add(self, red):
            def one(n, carry):
                k = turn_of(n)
                pltpu.make_async_copy(self.got.at[k], self.room(n), block_sem.at[n]).wait()
                self.block(2 * k, self.room(n), True)
                if red is not None:
                    pltpu.make_async_copy(self.room(n), red.at[k], block_sem.at[4 + n]).start()
                return carry

            lax.fori_loop(0, 4, one, 0)
            if red is not None:
                for n in range(4):
                    pltpu.make_async_copy(self.room(n), red.at[turns[n]], block_sem.at[4 + n]).wait()

    def product(left, right, ref, add):
        part = dot(left, right)
        if add:
            part = part + ref[...].astype(FULL)
        ref[...] = part.astype(LOW)

    def heads_block(i, ref, add):
        product(nt[tile(i), :], pg[...], ref, add)

    heads_sum = Reduced(lambda n: wh.at[tile(n), :], got_core_h, heads_block)
    own_h = at_rows(wh, 4 * unit, unit)
    stage_h = (at_rows(wh, 5 * unit, unit // 2), at_rows(wh, 5 * unit + unit // 2, unit // 2))
    heads = Scattered(links, local, [red_h.at[k] for k in range(4)], at_rows, unit, via_h, got_h, stage_h, own_h)
    shrink = Scattered(links, local, [red_s.at[k] for k in range(4)], at_columns, unit, via_s, got_s)
    output = Scattered(links, local, [red_o.at[k] for k in range(4)], at_columns, unit, via_o, got_o)

    def up_part(i, grad, first):
        cols, spot = tile(i), placed(i)
        normal = (x[:, cols].astype(FULL) - stat[:, 0:1]) * stat[:, 128:129]
        row = 0 if first else 2
        sums[0, row : row + 1, spot] = jnp.sum(grad * normal, 0, keepdims=True)
        sums[0, row + 1 : row + 2, spot] = jnp.sum(grad, 0, keepdims=True)
        scaled = grad * (vecs[0:1, cols] if first else vecs[2:3, cols])
        n1[:, cols] = (scaled if first else n1[:, cols].astype(FULL) + scaled).astype(LOW)

    def attend(qkv_away, dctx_away, ctxt_all, pgq, pg_away, kvg_away, cosine, sines, dk, dv, stage):
        for i in blocks:
            cols = pl.ds(pl.multiple_of(links.block(i) * unit, unit), unit)
            vecs[0:4, i * unit : (i + 1) * unit] = raw[0:4, cols]
            vecs[4:5, i * unit : (i + 1) * unit] = raw[6:7, cols]
        local.wait(*x_in)

        def norm_rows(c, carry):
            rows = tile_of(c, 64)
            value = x[rows, :].astype(FULL)
            average = jnp.mean(value, -1, keepdims=True)
            centred = value - average
            inverse = lax.rsqrt(jnp.mean(centred * centred, -1, keepdims=True) + NORM_EPS)
            normal = centred * inverse
            both = [jnp.broadcast_to(part, (64, 128)) for part in (average, inverse)]
            stat[rows, :] = jnp.concatenate(both, -1)
            n1[rows, :] = (normal * vecs[0:1, :] + vecs[1:2, :]).astype(LOW)
            up[rows, :] = (normal * vecs[2:3, :] + vecs[3:4, :]).astype(LOW)
            return carry

        lax.fori_loop(0, tokens // 64, norm_rows, 0)
        bases = [
            order[0, (links.yb if step < 2 else 1 - links.yb) * 2 + (links.xb if step % 2 == 0 else 1 - links.xb)]
            * tokens
            for step in (0, 2, 1, 3)
        ]

        def table_rows(c, carry):
            rows = tile_of(c, 64)
            lane = lax.broadcasted_iota(jnp.int32, (64, 128), 1)
            row = lax.broadcasted_iota(jnp.int32, (64, 128), 0) + c * 64
            spot = row + jnp.where(row < tokens, bases[0], bases[1] - tokens)
            pace = jnp.exp(lax.rem(lane, ROT // 2).astype(FULL) * (-2.0 / ROT * math.log(10000.0)))
            angle = spot.astype(FULL) * pace
            sine = jnp.sin(angle)
            cosine[rows, :] = jnp.where(lane < ROT, jnp.cos(angle), 1.0)
            sines[rows, :] = jnp.where(lane < ROT // 2, -sine, jnp.where(lane < ROT, sine, 0.0))
            return carry

        lax.fori_loop(0, 2 * tokens // 64, table_rows, 0)
        heads_in.relay()
        output_in.first()
        output_in.rest()

        def turned_copy(j):
            slot = odd(j)
            return pltpu.make_async_copy(stage.at[slot], n2t_hbm.at[tile_of(j, unit), :], loop_sem.at[0, slot])

        def turn_tiles(j, carry):
            cols = tile_of(j, unit)
            nt[cols, :] = n1[:, cols].T

            @pl.when(j >= 2)
            def _():
                turned_copy(j - 2).wait()

            stage[odd(j), :, :] = up[:, cols].T
            turned_copy(j).start()
            return carry

        lax.fori_loop(0, 8, turn_tiles, 0)
        for j in (6, 7):
            turned_copy(j).wait()
        sums[0, :, :] = jnp.zeros(sums.shape[1:], FULL)
        local.wait(*g_in)
        for i in blocks:
            cols = pl.ds(pl.multiple_of(links.block(i) * unit, unit), unit)
            sums[0, 4:5, cols] = jnp.sum(g[:, i * unit : (i + 1) * unit].astype(FULL), 0, keepdims=True)
        heads_in.share()
        heads_in.share_far()
        heads_in.whole()
        output_in.relay()

        own = links.yb * 3 * hd

        def project(c, head, target):
            cols = pl.ds(pl.multiple_of(head * 3 * hd + c * hd, hd), hd)
            bias = jnp.where(head == 0, raw[5:6, c * hd : (c + 1) * hd], raw[7:8, c * hd : (c + 1) * hd])
            value = dot(n1[...], wh[:, cols]) + bias
            if c < 2:
                value = spin(value, cosine[:tokens, :], sines[:tokens, :])
            target[c, :tokens, :] = value.astype(LOW)

        def place_of(c, part):
            return qkv.at[c, pl.ds(part * tokens, tokens), :]

        from_y, from_x, from_far = {}, {}, {}
        for c in (1, 2):
            project(c, links.yb, qkv)
            from_x[c] = links.send(place_of(c, 0), place_of(c, 2), links.x)
        for c in (1, 2, 0):
            project(c, 1 - links.yb, qkv_away)
            from_y[c] = links.send(qkv_away.at[c], place_of(c, 1), links.y)
        from_y[1].wait_recv()
        from_far[1] = links.send(place_of(1, 1), place_of(1, 3), links.x)
        project(0, links.yb, qkv)
        output_in.share()
        output_in.share_far()
        from_y[2].wait_recv()
        from_far[2] = links.send(place_of(2, 1), place_of(2, 3), links.x)
        output_in.whole()
        rows_own = pl.ds(pl.multiple_of(links.yb * hd, hd), hd)
        rows_away = pl.ds(pl.multiple_of((1 - links.yb) * hd, hd), hd)
        dctx_away[...] = contract_last(g[...], wo[rows_away, :]).astype(LOW)
        dctx_from_y = links.send(dctx_away, dctx.at[pl.ds(tokens, tokens), :], links.y)
        dctx[:tokens, :] = contract_last(g[...], wo[rows_own, :]).astype(LOW)
        expand.first()
        expand.to_y(False)
        for copy in (from_y[0], dctx_from_y, *from_x.values(), *from_far.values()):
            copy.wait_recv()

        def attention(kt, vt, prob, wgt, prob_low, grad_low):
            keys = qkv.shape[1]
            step = tokens
            lag = lax.broadcasted_iota(jnp.int32, (step, hd), 0) - lax.broadcasted_iota(jnp.int32, (step, hd), 1)
            parts = [pl.ds(i * step, step) for i in range(keys // step)]
            for part in parts:
                kt[:, part] = qkv[1, part, :].T
                vt[:, part] = qkv[2, part, :].T
            dk[...] = jnp.zeros_like(dk)
            dv[...] = jnp.zeros_like(dv)

            def one(b, carry):
                rows = tile_of(b, hd)
                query, grad = qkv[0, rows, :], dctx[rows, :]
                ahead = jnp.where(b < tokens // hd, bases[0], bases[1] - tokens) + b * hd
                top = jnp.full((1, hd), MASKED, FULL)
                for i, part in enumerate(parts):
                    scores = contract_last(qkv[1, part, :], query) * score_scale
                    scores = jnp.where(lag <= ahead - bases[i], scores, MASKED)
                    prob[part, :] = scores
                    top = jnp.maximum(top, jnp.max(scores, 0, keepdims=True))
                total = jnp.zeros((1, hd), FULL)
                for part in parts:
                    exponent = jnp.exp(prob[part, :] - top)
                    prob[part, :] = exponent
                    total = total + jnp.sum(exponent, 0, keepdims=True)
                share = 1.0 / total
                inner = jnp.zeros((1, hd), FULL)
                for part in parts:
                    weight = contract_last(qkv[2, part, :], grad)
                    chance = prob[part, :] * share
                    prob[part, :] = chance
                    prob_low[part, :] = chance.astype(LOW)
                    wgt[part, :] = weight
                    inner = inner + jnp.sum(chance * weight, 0, keepdims=True)
                for part in parts:
                    grad_low[part, :] = (prob[part, :] * (wgt[part, :] - inner)).astype(LOW)
                ctxt_all[:, rows] = dot(vt[...], prob_low[...]).astype(LOW)
                query_grad = dot(kt[...], grad_low[...]) * score_scale
                for part in parts:
                    dv[part, :] += dot(prob_low[part, :], grad)
                    dk[part, :] += dot(grad_low[part, :], query)
                turned_grad = spin(query_grad.T, cosine[rows, :], -sines[rows, :])
                pgq[rows, :] = turned_grad.astype(LOW)
                return carry

            lax.fori_loop(0, 2 * tokens // hd, one, 0)
            ctxt[rows_own, :] = ctxt_all[:, :tokens]
            pg[:, pl.ds(pl.multiple_of(own, hd), hd)] = pgq[:tokens, :]
            for i, total in enumerate((dk, dv)):
                kvg_away[i, :, :] = total[2 * tokens :, :].astype(LOW)

        keys = qkv.shape[1]
        pl.run_scoped(
            attention,
            pltpu.VMEM((hd, keys), LOW),
            pltpu.VMEM((hd, keys), LOW),
            pltpu.VMEM((keys, hd), FULL),
            pltpu.VMEM((keys, hd), FULL),
            pltpu.VMEM((keys, hd), LOW),
            pltpu.VMEM((keys, hd), LOW),
        )

        def head_columns(ref, start, i):
            return ref.at[:, pl.ds(pl.multiple_of(start + i * hd, hd), hd)]

        def send_grad(i):
            source = pgq.at[pl.ds(tokens, tokens), :] if i == 0 else head_columns(pg_away, 0, i - 1)
            return links.send(source, head_columns(pg, own, i), links.y)

        kvg_from_x = {i: links.send(kvg_away.at[i], kvg_got.at[i], links.x) for i in (1, 0)}
        pg_from_y = [send_grad(0)]
        ctx_from_y = links.send(ctxt_all.at[:, pl.ds(tokens, tokens)], ctxt.at[rows_own, :], links.y)
        expand.pass_x()
        expand.to_x(True)

        for i in (1, 0):
            kvg_from_x[i].wait_recv()
            for away_rows, target in ((True, pg_away), (False, pg)):
                rows = pl.ds(tokens if away_rows else 0, tokens)
                total = (dk, dv)[i][rows, :] + kvg_got[i, rows, :].astype(FULL)
                if i == 0:
                    total = spin(total * score_scale, cosine[rows, :], -sines[rows, :])
                head_columns(target, 0 if away_rows else own, i if away_rows else 1 + i)[...] = total.astype(LOW)
                if away_rows:
                    pg_from_y.append(send_grad(1 + i))
        expand.pass_y()
        weight.first()
        weight.rest()
        ctx_from_y.wait_recv()
        for copy in pg_from_y:
            copy.wait_recv()

        def first_block(i, carry):
            up_part(i, contract_last(pg[...], wh[tile(i), :]), True)
            return carry

        lax.fori_loop(0, 8, first_block, 0)
        sums[0, 6:7, :heads_wide] = jnp.sum(pg[...].astype(FULL), 0, keepdims=True)
        heads_in.passed()
        heads_sum.to_core()
        expand.share()
        expand.share_far()
        expand.whole()
        for copy in (*from_y.values(), *from_x.values(), *from_far.values(), dctx_from_y, *kvg_from_x.values(), *pg_from_y, ctx_from_y):
            links.sent_out(copy)

    low, full = (functools.partial(lambda kind, *shape: pltpu.VMEM(shape, kind), kind) for kind in (LOW, FULL))
    pl.run_scoped(
        attend,
        low(3, tokens, hd),
        low(tokens, hd),
        low(hd, 2 * tokens),
        low(2 * tokens, hd),
        low(tokens, 2 * hd),
        low(2, 2 * tokens, hd),
        full(2 * tokens, 128),
        full(2 * tokens, 128),
        full(4 * tokens, hd),
        full(4 * tokens, hd),
        low(2, unit, tokens),
    )

    def update(act, actt, slope, ctx, room_o, stage_o, own_o, room_e, total_rows, total_columns, grad_rows):
        def forward(j, slot):
            cols = tile(j)
            value = dot(up[...], room_s[slot]) + raw[4:5, cols]
            normal_share = 0.5 * (1.0 + lax.erf(value * (0.5**0.5)))
            low_act = (value * normal_share).astype(LOW)
            act[:, cols] = low_act
            actt[cols, :] = low_act.T
            density = jnp.exp(value * value * -0.5) * 0.3989422804014327
            slope[:, cols] = (normal_share + value * density).astype(LOW)

        stream(0, 8, lambda j, slot: [(we.at[:, tile(j)], room_s.at[slot])], forward)
        weight.relay()
        ctx[...] = ctxt[...].T

        rows_out = grad_rows.shape[1]

        def columns_cut(ref, c):
            return ref.at[:, here(c)]

        def rows_cut(ref, c):
            return ref.at[pl.ds(c * rows_out, rows_out), :]

        def finish_branch(c):
            cols = here(c)

            def one(part, carry):
                at = tile_of(part, 128)
                total = up[at, cols].astype(FULL) + got_branch[at, cols].astype(FULL)
                final_branch[at, cols] = (x[at, cols].astype(FULL) + total + vecs[4:5, cols]).astype(LOW)
                return carry

            lax.fori_loop(0, tokens // 128, one, 0)

        def finish_up(c):
            add_rows(rows_cut(final_up, c), rows_cut(n1, c), rows_cut(got_up, c))

        line_branch = Line(links, up, got_branch, final_branch, 8, columns_cut, finish_branch)
        line_up = Line(links, n1, got_up, final_up, tokens // rows_out, rows_cut, finish_up)

        def branch_blocks(chunks, block, source):
            def one(n, slot):
                cols = tile(block(n))
                up[:, cols] = (dot(ctx[...], wo[:, cols]) + dot(act[...], room_s[slot])).astype(LOW)
                for at, chunk in enumerate(chunks):
                    pl.when(n == at)(functools.partial(line_branch.start, chunk))

            stream(0, len(chunks), lambda n, slot: [(source(n), room_s.at[slot])], one)

        steps = [(line_branch, c) for c in (0, 1, 2, 4, 3, 5, 6, 7)] + [(line_up, c) for c in range(line_up.chunks)]
        out_copies = []

        def input_rows(c):
            slot = len(out_copies) % 2
            if len(out_copies) >= 2:
                local.wait(*out_copies[-2])
            rows = pl.ds(c * rows_out, rows_out)
            value = x[rows, :].astype(FULL)
            centred = value - jnp.mean(value, -1, keepdims=True)
            scale = lax.rsqrt(jnp.mean(centred * centred, -1, keepdims=True) + NORM_EPS)
            normal = centred * scale
            upstream = final_up[rows, :].astype(FULL)
            inner = upstream - jnp.mean(upstream, -1, keepdims=True)
            inner = inner - normal * jnp.mean(upstream * normal, -1, keepdims=True)
            grad_rows[slot, :, :] = (g[rows, :].astype(FULL) + inner * scale).astype(LOW)
            out_copies.append(
                [local.start(grad_rows.at[slot, :, here(i)], input_grad.at[rows, place[i]]) for i in blocks]
            )

        def serve(count):
            for _ in range(count):
                at = serve.done
                if at < len(steps):
                    steps[at][0].first(steps[at][1])
                if 2 <= at < len(steps) + 2:
                    steps[at - 2][0].second(steps[at - 2][1])
                if at >= 4:
                    line, c = steps[at - 4]
                    line.third(c)
                    if line is line_up:
                        input_rows(c)
                    else:
                        local.start(final_branch.at[:, here(c)], layer_out.at[:, place[c]])
                serve.done += 1

        serve.done = 0
        branch_blocks((0, 1), lambda n: n, lambda n: at_columns(ws_own, pl.multiple_of((links.r + n - 2 * links.r * n) * unit, unit), unit))

        def shrink_block(i, ref, add):
            product(actt[...], g[:, tile(i)], ref, add)

        def output_block(i, ref, add):
            product(ctxt[...], g[:, tile(i)], ref, add)

        def expand_block(i, ref, add):
            product(nt[tile(i), :], slope[...], ref, add)

        shrink.stage = (actt.at[:, pl.ds(unit, unit // 2)], actt.at[:, pl.ds(unit + unit // 2, unit // 2)])
        shrink.own = actt.at[:, pl.ds(0, unit)]
        output.stage, output.own = (stage_o.at[0], stage_o.at[1]), own_o
        shrink_sum = Reduced(lambda n: room_s.at[n], got_core_s, shrink_block)
        output_sum = Reduced(lambda n: room_o.at[n], got_core_o, output_block)
        expand_sum = Reduced(lambda n: room_e.at[n], got_core_e, expand_block)
        heads_sum.fetch()
        heads_sum.add(red_h)
        heads.first()
        heads.direct()
        heads.load()
        n2t_load = local.start(n2t_hbm, nt)
        weight.share()
        serve(1)
        weight.core_y.wait_recv()
        weight.core_x.wait_recv()
        ahead = lambda n: 2 * n + 2 - 3 * (n // 2 if isinstance(n, int) else lax.div(n, 2))
        branch_blocks((2, 4, 3, 5), ahead, lambda n: ws.at[:, tile(ahead(n))])
        serve(1)
        shrink_sum.to_core()
        weight.share_far()
        shrink_sum.fetch()
        shrink_sum.add(red_s)
        shrink.first()
        shrink.direct()
        shrink.load()
        serve(1)
        weight.core_far.wait_recv()
        branch_blocks((6, 7), lambda n: n + 6, lambda n: ws.at[:, tile(n + 6)])
        serve(1)

        def hidden_tile(j, slot):
            cols = tile(j)
            grad = (contract_last(g[...], room_e[slot]) * slope[:, cols].astype(FULL)).astype(LOW)
            slope[:, cols] = grad
            sums[0, 5:6, cols] = jnp.sum(grad.astype(FULL), 0, keepdims=True)

        def shrink_rows(j, slot):
            rows = tile(j)
            pairs = [(weight.here(i).at[rows, :], room_e.at[slot, :, here(i)]) for i in range(2)]
            return pairs + [(ws.at[rows, rest_rows], room_e.at[slot, :, rest_rows])]

        stream(0, 4, shrink_rows, hidden_tile)
        serve(1)
        stream(4, 8, shrink_rows, hidden_tile)
        serve(1)

        def second_block(i, slot):
            up_part(i, contract_last(slope[...], room_e[slot]), False)

        expand_rows = lambda i, slot: [(we.at[tile(i), :], room_e.at[slot])]
        stream(0, 4, expand_rows, second_block)
        serve(1)
        stream(4, 8, expand_rows, second_block)
        line_up.start(*range(line_up.chunks))
        serve(1)

        def share(s, peers):
            return [links.send(sums.at[s], sums_got.at[4 * s + k], peer) for k, peer in enumerate(peers)]

        def shared(s, copies):
            for copy in copies:
                copy.wait_recv()
            total = sums[s, :, :] + sums_got[4 * s, :, :]
            if len(copies) > 1:
                total = total + (sums_got[4 * s + 1, :, :] + sums_got[4 * s + 2, :, :])
            sums[s + 1, :, :] = total

        def share_line(s, peer):
            return links.send(gains.at[s], gains_got.at[s], peer)

        def shared_line(s, copy):
            copy.wait_recv()
            gains[s + 1, :, :] = gains[s, :, :] + gains_got[s, :, :]

        first_share = share(0, [links.core])
        output_sum.to_core()
        shared(0, first_share)
        second_share = share(1, [links.x, links.y, links.far])
        output_sum.fetch()
        output_sum.add(red_o)
        output.first()
        output.direct()
        output.load()

        local.wait(n2t_load)
        expand_sum.to_core()
        serve(1)
        shrink.second()
        serve(1)
        expand_sum.fetch()
        serve(1)
        expand_sum.add(None)
        red = {k: room_e.at[turns.index(k)] for k in range(4)}
        expand = Scattered(links, local, [red[k] for k in range(4)], at_rows, unit, via_e, got_e, None, red[0])
        expand.first()
        expand.direct()
        serve(2)
        half_rows = pl.ds(pl.multiple_of(links.r * unit, unit), unit)
        column_slots = Slots(*[total_columns.at[n] for n in range(4)])
        serve(2)
        shrink.third(column_slots, shrink_grad.at[:, half_rows], total_columns.shape[1])
        serve(1)
        shared(1, second_share)
        for row in range(4):
            for side in range(2):
                at = 2 * row + side
                gains[0, at : at + 1, :] = sums[2, row : row + 1, side * (width // 2) : (side + 1) * (width // 2)]
        pair_share = share_line(0, links.pair)
        serve(3)

        expand.via_x.wait_recv()
        top, end = red[2].at[pl.ds(0, unit // 2), :], red[1].at[pl.ds(unit // 2, unit // 2), :]
        add_rows(top, top, via_e.at[0])
        expand.y_top = links.send(top, got_e.at[1, pl.ds(0, unit // 2), :], links.y)
        expand.via_y.wait_recv()
        add_rows(end, end, via_e.at[1])
        expand.x_end = links.send(end, got_e.at[0, pl.ds(unit // 2, unit // 2), :], links.x)
        heads.second()
        output.second()
        serve(len(steps) - 1 - serve.done)
        shared_line(0, pair_share)
        across_share = share_line(1, links.across)
        serve(2)
        expand_slots = Slots(*[total_rows.at[n] for n in range(4)])
        expand.third(expand_slots, expand_grad.at[half_rows, :], total_rows.shape[1])
        serve(len(steps) + 4 - serve.done)
        expand_slots.end()
        total_slots = Slots(*[total_rows.at[n, :, pl.ds(0, heads_wide)] for n in range(4)])
        heads.third(total_slots, heads_grad.at[half_rows, :], total_rows.shape[1])
        output.third(column_slots, output_grad.at[:, half_rows], total_columns.shape[1])
        total_slots.end()
        column_slots.end()
        shared_line(1, across_share)
        for row in range(4):
            for side in range(2):
                at = 2 * row + side
                sums_out[row : row + 1, side * (width // 2) : (side + 1) * (width // 2)] = gains[2, at : at + 1, :]
        sums_out[4:8, :] = sums[2, 4:8, :]
        for copy in (*shrink.other, *output.other, *heads.other, *expand.other):
            copy.wait_recv()
        assert links.count <= COPIES and local.count <= LOCALS
        links.end()
        line_branch.end()
        line_up.end()
        local.end()


    pl.run_scoped(
        update,
        low(tokens, units),
        low(units, tokens),
        low(tokens, units),
        low(tokens, out_wide),
        low(4, out_wide, unit),
        low(2, out_wide, unit // 2),
        low(out_wide, unit),
        low(4, unit, units),
        low(4, unit // 4, units),
        low(4, out_wide, unit),
        low(2, 32, width),
    )


def block_call(line_size, x, g, heads_rows, output_rows, expand_weight, shrink_weight, vectors, order):
    tokens, width = x.shape
    heads_wide, out_wide, units = heads_rows.shape[1], output_rows.shape[0], expand_weight.shape[1]
    hd, unit, half = heads_wide // 6, width // 8, width // 16
    low = lambda *shape: pltpu.VMEM(shape, LOW)
    full = lambda *shape: pltpu.VMEM(shape, FULL)
    work = lambda *shape: jax.ShapeDtypeStruct(shape, LOW)
    outs = [
        work(tokens, width),
        work(tokens, width),
        work(2 * unit, heads_wide),
        work(out_wide, 2 * unit),
        work(2 * unit, units),
        work(units, 2 * unit),
        work(width, units),
        work(units, width),
        work(width, tokens),
        work(4, units, unit),
        work(4, out_wide, unit),
        work(4, unit, heads_wide),
        work(4, unit, units),
        work(4, units, unit),
        work(4, out_wide, unit),
        work(4, unit, heads_wide),
        jax.ShapeDtypeStruct((8, width), FULL),
    ]
    scratch = [
        *[low(tokens, width)] * 4, low(width, tokens), full(tokens, 256),
        low(width, heads_wide), low(out_wide, width), low(4, 4 * tokens, hd), low(2 * tokens, hd),
        low(out_wide, tokens), low(tokens, heads_wide), low(2, 2 * tokens, hd),
        *[low(tokens, width)] * 4,
        low(2, half, heads_wide), low(2, unit, heads_wide),
        low(2, out_wide, half), low(2, out_wide, unit),
        low(2, units, half), low(2, units, unit),
        low(2, half, units), low(2, unit, units),
        full(8, width), full(8, width), full(3, 8, width), full(7, 8, width), full(3, 8, width // 2), full(2, 8, width // 2),
        pltpu.SemaphoreType.DMA((3, 2)),
        pltpu.SemaphoreType.DMA((8,)),
        pltpu.SemaphoreType.DMA((LOCALS,)),
        pltpu.SemaphoreType.DMA((COPIES,)),
        pltpu.SemaphoreType.DMA((COPIES,)),
    ]
    return pl.pallas_call(
        functools.partial(block_kernel, hd**-0.5, line_size),
        out_shape=outs,
        in_specs=[ANY] * 6 + [IN_VMEM] * 8 + [pl.BlockSpec(memory_space=pltpu.SMEM)],
        out_specs=[ANY] * 16 + [IN_VMEM],
        scratch_shapes=scratch,
        compiler_params=pltpu.CompilerParams(
            collective_id=0, has_side_effects=True, vmem_limit_bytes=VMEM_BYTES
        ),
    )(x, g, heads_rows, output_rows, expand_weight, shrink_weight, *vectors, order)


def square_local(
    layer_input,
    block_order,
    first_gain,
    first_bias,
    second_gain,
    second_bias,
    heads_weight,
    heads_bias,
    output_weight,
    output_bias,
    expand_weight,
    expand_bias,
    shrink_weight,
    shrink_bias,
    cotangent,
):
    heads_rows = heads_weight.reshape(heads_weight.shape[0], -1)
    output_rows = output_weight.reshape(-1, output_weight.shape[2])
    vectors = (first_gain, first_bias, second_gain, second_bias, expand_bias, heads_bias, output_bias, shrink_bias)
    *results, sums = block_call(
        lax.axis_size("tensor"),
        layer_input[0],
        cotangent[0],
        heads_rows,
        output_rows,
        expand_weight,
        shrink_weight,
        vectors,
        block_order,
    )
    results = store_call(results[:6], sums, heads_weight.shape)
    layer_output, input_grad, heads_grad, output_grad, expand_grad, shrink_grad = results[:6]
    first_gain_grad, first_bias_grad, second_gain_grad, second_bias_grad = (vec.reshape(-1) for vec in results[6:10])
    output_bias_grad, expand_bias_grad, shrink_bias_grad = (vec.reshape(-1) for vec in results[10:13])
    return (
        layer_output[None],
        input_grad[None],
        first_gain_grad,
        first_bias_grad,
        second_gain_grad,
        second_bias_grad,
        heads_grad,
        results[13],
        output_grad.reshape(output_weight.shape),
        output_bias_grad,
        expand_grad,
        expand_bias_grad,
        shrink_grad,
        shrink_bias_grad,
    )


def store_kernel(*refs):
    *full_in, sums = refs[:7]
    full_out, rows_out, heads_bias_out = refs[7:13], refs[13:20], refs[20]
    for source, target in zip(full_in, full_out):
        if len(target.shape) == len(source.shape):
            target[...] = source[...].astype(target.dtype)
        else:
            wide = target.shape[2]
            for head in range(target.shape[1]):
                target[:, head, :] = source[:, head * wide : (head + 1) * wide].astype(target.dtype)

    @pl.when(pl.program_id(0) == 0)
    def _():
        for row, target in zip((0, 1, 2, 3, 4, 5, 4), rows_out):
            target[...] = sums[row : row + 1, :]
        wide = heads_bias_out.shape[1]
        for head in range(heads_bias_out.shape[0]):
            heads_bias_out[head : head + 1, :] = sums[6:7, head * wide : (head + 1) * wide]


def store_call(results, sums, heads_shape):
    steps = 2
    width = sums.shape[1]

    def cut(shape):
        zeros = (0,) * (len(shape) - 1)
        return pl.BlockSpec((shape[0] // steps,) + tuple(shape[1:]), lambda i: (i, *zeros))

    def whole(shape):
        return pl.BlockSpec(tuple(shape), lambda i: (0,) * len(shape))

    kept = [result.shape for result in results]
    kept[2] = heads_shape
    rows, heads_bias = (1, width), heads_shape[1:]
    outs = [jax.ShapeDtypeStruct(shape, FULL if i else LOW) for i, shape in enumerate(kept)]
    outs += [jax.ShapeDtypeStruct(rows, FULL)] * 7 + [jax.ShapeDtypeStruct(heads_bias, FULL)]
    return pl.pallas_call(
        store_kernel,
        grid=(steps,),
        out_shape=outs,
        in_specs=[cut(result.shape) for result in results] + [whole(sums.shape)],
        out_specs=[cut(shape) for shape in kept] + [whole(rows)] * 7 + [whole(heads_bias)],
        compiler_params=pltpu.CompilerParams(vmem_limit_bytes=VMEM_BYTES),
    )(*results, sums)


def ring_local(
    layer_input,
    block_order,
    first_gain,
    first_bias,
    second_gain,
    second_bias,
    heads_weight,
    heads_bias,
    output_weight,
    output_bias,
    expand_weight,
    expand_bias,
    shrink_weight,
    shrink_bias,
    cotangent,
):
    tokens_here = layer_input.shape[1]
    fsdp_count = lax.axis_size("fsdp")
    head_dim = output_weight.shape[1]
    score_scale = head_dim ** (-0.5)
    order_row = block_order[0]
    device_slot = lax.axis_index("fsdp")
    own_block = jnp.sum(
        jnp.where(jnp.arange(fsdp_count, dtype=jnp.int32) == device_slot, order_row, 0)
    )
    offsets = jnp.arange(tokens_here, dtype=jnp.int32)
    query_pos = own_block * tokens_here + offsets
    key_pos = jnp.repeat(order_row, tokens_here) * tokens_here + jnp.tile(offsets, fsdp_count)
    allowed = key_pos[None, :] <= query_pos[:, None]
    cosine, sine_part = rotary_tables(query_pos, ROT)
    hidden_in = layer_input[0].astype(jnp.float32)
    gain_one = first_gain.astype(jnp.float32)
    shift_one = first_bias.astype(jnp.float32)
    gain_two = second_gain.astype(jnp.float32)
    shift_two = second_bias.astype(jnp.float32)
    norm_one_low = layer_norm(hidden_in, gain_one, shift_one).astype(jnp.bfloat16)
    norm_two_low = layer_norm(hidden_in, gain_two, shift_two).astype(jnp.bfloat16)
    heads_full, output_full, expand_full, shrink_full = (
        lax.all_gather(heads_weight, "fsdp", axis=0, tiled=True),
        lax.all_gather(output_weight, "fsdp", axis=2, tiled=True),
        lax.all_gather(expand_weight, "fsdp", axis=0, tiled=True),
        lax.all_gather(shrink_weight, "fsdp", axis=1, tiled=True),
    )
    projected = jnp.einsum(
        "td,dhe->hte", norm_one_low, heads_full, preferred_element_type=jnp.float32
    )
    projected = projected + heads_bias.astype(jnp.float32)[:, None, :]
    query_pre = projected[..., :head_dim]
    key_pre = projected[..., head_dim : 2 * head_dim]
    query_low = rotate(query_pre, cosine, sine_part).astype(jnp.bfloat16)
    key_low = rotate(key_pre, cosine, sine_part).astype(jnp.bfloat16)
    value_low = projected[..., 2 * head_dim :].astype(jnp.bfloat16)
    key_all, value_all = (
        lax.all_gather(key_low, "fsdp", axis=1, tiled=True),
        lax.all_gather(value_low, "fsdp", axis=1, tiled=True),
    )

    def attend_head(operands):
        query_head, key_head, value_head = operands
        probability = softmax_rows(contract_last(query_head, key_head) * score_scale, allowed)
        return jnp.dot(
            probability.astype(jnp.bfloat16), value_head, preferred_element_type=jnp.float32
        )

    context = lax.map(attend_head, (query_low, key_all, value_all))
    context_low = context.astype(jnp.bfloat16)
    expand_in = jnp.dot(
        norm_two_low, expand_full, preferred_element_type=jnp.float32
    ) + expand_bias.astype(jnp.float32)
    activation_low = jax.nn.gelu(expand_in, approximate=False).astype(jnp.bfloat16)
    branch_part = jnp.einsum(
        "hte,hed->td", context_low, output_full, preferred_element_type=jnp.float32
    )
    branch_part = branch_part + jnp.dot(
        activation_low, shrink_full, preferred_element_type=jnp.float32
    )
    branch = lax.psum(branch_part, "tensor")
    layer_output = (
        hidden_in + branch + output_bias.astype(jnp.float32) + shrink_bias.astype(jnp.float32)
    ).astype(jnp.bfloat16)[None]
    heads_back, output_back, expand_back, shrink_back = (
        lax.all_gather(heads_weight, "fsdp", axis=0, tiled=True),
        lax.all_gather(output_weight, "fsdp", axis=2, tiled=True),
        lax.all_gather(expand_weight, "fsdp", axis=0, tiled=True),
        lax.all_gather(shrink_weight, "fsdp", axis=1, tiled=True),
    )
    key_back, value_back = (
        lax.all_gather(key_low, "fsdp", axis=1, tiled=True),
        lax.all_gather(value_low, "fsdp", axis=1, tiled=True),
    )
    grad_out = cotangent[0]
    grad_float = grad_out.astype(jnp.float32)
    output_weight_grad = jnp.einsum(
        "hte,td->hed", context_low, grad_out, preferred_element_type=jnp.float32
    )
    shrink_weight_grad = contract_first(activation_low, grad_out)
    bias_total = jnp.sum(grad_float, 0)
    context_grad = jnp.einsum(
        "td,hed->hte", grad_out, output_back, preferred_element_type=jnp.float32
    ).astype(jnp.bfloat16)
    activation_grad = contract_last(grad_out, shrink_back)
    _, gelu_back = jax.vjp(lambda inner_val: jax.nn.gelu(inner_val, approximate=False), expand_in)
    expand_grad = gelu_back(activation_grad)[0].astype(jnp.bfloat16)
    expand_weight_grad = contract_first(norm_two_low, expand_grad)
    expand_bias_grad = jnp.sum(expand_grad.astype(jnp.float32), 0)
    norm_two_grad = contract_last(expand_grad, expand_back)

    def attend_back(operands):
        query_head, key_head, value_head, context_head = operands
        probability = softmax_rows(contract_last(query_head, key_head) * score_scale, allowed)
        prob_low = probability.astype(jnp.bfloat16)
        weight_grad = contract_last(context_head, value_head)
        row_inner = jnp.sum(probability * weight_grad, -1, keepdims=True)
        score_grad = (probability * (weight_grad - row_inner)).astype(jnp.bfloat16)
        query_grad = jnp.dot(score_grad, key_head, preferred_element_type=jnp.float32) * score_scale
        key_grad = contract_first(score_grad, query_head) * score_scale
        value_grad = contract_first(prob_low, context_head)
        return (query_grad, key_grad, value_grad)

    query_grad, key_grad_all, value_grad_all = lax.map(
        attend_back, (query_low, key_back, value_back, context_grad)
    )
    key_grad, value_grad = (
        lax.psum_scatter(key_grad_all, "fsdp", scatter_dimension=1, tiled=True),
        lax.psum_scatter(value_grad_all, "fsdp", scatter_dimension=1, tiled=True),
    )
    _, rotate_back = jax.vjp(lambda inner_val: rotate(inner_val, cosine, sine_part), query_pre)
    projected_grad = jnp.concatenate(
        [rotate_back(query_grad)[0], rotate_back(key_grad)[0], value_grad], -1
    ).astype(jnp.bfloat16)
    heads_weight_grad = jnp.einsum(
        "td,hte->dhe", norm_one_low, projected_grad, preferred_element_type=jnp.float32
    )
    heads_bias_grad = jnp.sum(projected_grad.astype(jnp.float32), 1)
    norm_one_grad = jnp.einsum(
        "hte,dhe->td", projected_grad, heads_back, preferred_element_type=jnp.float32
    )
    norm_one_grad, norm_two_grad = lax.psum((norm_one_grad, norm_two_grad), "tensor")
    _, first_back = jax.vjp(layer_norm, hidden_in, gain_one, shift_one)
    input_first, first_gain_grad, first_bias_grad = first_back(norm_one_grad)
    _, second_back = jax.vjp(layer_norm, hidden_in, gain_two, shift_two)
    input_second, second_gain_grad, second_bias_grad = second_back(norm_two_grad)
    input_grad = (grad_float + input_first + input_second)[None]
    small_sums = lax.psum(
        (
            first_gain_grad,
            first_bias_grad,
            second_gain_grad,
            second_bias_grad,
            bias_total,
            expand_bias_grad,
            heads_bias_grad,
        ),
        ("replica", "fsdp"),
    )
    shard_parts = (
        lax.psum_scatter(heads_weight_grad, "fsdp", scatter_dimension=0, tiled=True),
        lax.psum_scatter(output_weight_grad, "fsdp", scatter_dimension=2, tiled=True),
        lax.psum_scatter(expand_weight_grad, "fsdp", scatter_dimension=0, tiled=True),
        lax.psum_scatter(shrink_weight_grad, "fsdp", scatter_dimension=1, tiled=True),
    )
    reduced = lax.psum((shard_parts[0], shard_parts[1], shard_parts[2], shard_parts[3]), "replica")
    return (
        layer_output,
        input_grad,
        small_sums[0],
        small_sums[1],
        small_sums[2],
        small_sums[3],
        reduced[0],
        small_sums[6],
        reduced[1],
        small_sums[4],
        reduced[2],
        small_sums[5],
        reduced[3],
        small_sums[4],
    )


def solution(mesh):
    placed = (
        P("replica", "fsdp", None),
        P("replica", None),
        P(),
        P(),
        P(),
        P(),
        P("fsdp", "tensor", None),
        P("tensor", None),
        P("tensor", None, "fsdp"),
        P(),
        P("fsdp", "tensor"),
        P("tensor"),
        P("tensor", "fsdp"),
        P(),
        P("replica", "fsdp", None),
    )
    local = square_local if mesh.shape["fsdp"] == 4 and mesh.shape["replica"] == 2 and mesh.shape["tensor"] == 4 else ring_local
    return jax.shard_map(
        local,
        mesh=mesh,
        in_specs=placed,
        out_specs=(
            P("replica", "fsdp", None),
            P("replica", "fsdp", None),
            P(),
            P(),
            P(),
            P(),
            P("fsdp", "tensor", None),
            P("tensor", None),
            P("tensor", None, "fsdp"),
            P(),
            P("fsdp", "tensor"),
            P("tensor"),
            P("tensor", "fsdp"),
            P(),
        ),
        check_vma=False,
    )
```

```python
import functools
import math

import jax
import jax.numpy as jnp
from jax import lax
from jax.experimental import pallas as pl
from jax.experimental.pallas import tpu as pltpu
from jax.sharding import PartitionSpec as P

ROT = 64


NORM_EPS = 1e-05
MASKED = -1e30


def layer_norm(values_in, gain_vec, shift_vec):
    average = jnp.mean(values_in, -1, keepdims=True)
    centred = values_in - average
    spread_sq = jnp.mean(centred * centred, -1, keepdims=True)
    return centred * lax.rsqrt(spread_sq + NORM_EPS) * gain_vec + shift_vec


def rotate(values_in, cosine, sine_part):
    rot_width = cosine.shape[-1]
    half_width = rot_width // 2
    turning = values_in[..., :rot_width]
    swapped = jnp.concatenate([-turning[..., half_width:], turning[..., :half_width]], -1)
    return jnp.concatenate([turning * cosine + swapped * sine_part, values_in[..., rot_width:]], -1)


def rotary_tables(positions, rot_width):
    frequency = jnp.power(10000.0, -jnp.arange(0, rot_width, 2, dtype=jnp.float32) / rot_width)
    angle_half = positions.astype(jnp.float32)[:, None] * frequency[None, :]
    angles = jnp.concatenate([angle_half, angle_half], -1)
    return (jnp.cos(angles), jnp.sin(angles))


def contract_last(left_op, right_op):
    return lax.dot_general(
        left_op, right_op, (((1,), (1,)), ((), ())), preferred_element_type=jnp.float32
    )


def contract_first(left_op, right_op):
    return lax.dot_general(
        left_op, right_op, (((0,), (0,)), ((), ())), preferred_element_type=jnp.float32
    )


def softmax_rows(scores, allowed):
    masked_scores = jnp.where(allowed, scores, MASKED)
    row_top = jnp.max(masked_scores, -1, keepdims=True)
    exponent = jnp.exp(masked_scores - row_top)
    return exponent / jnp.sum(exponent, -1, keepdims=True)


LOW = jnp.bfloat16
FULL = jnp.float32


MESH = pl.DeviceIdType.MESH
ANY = pl.BlockSpec(memory_space=pl.ANY)
IN_VMEM = pl.BlockSpec(memory_space=pltpu.VMEM)
VMEM_BYTES = 63 * 2**20
COPIES = 157
LOCALS = 34


class Sent:
    def __init__(self, links, k, source, target, peer):
        self.links, self.k, self.source, self.target, self.peer = links, k, source, target, peer

    def copy(self):
        return self.links.copy_at(self.k, self.source, self.target, self.peer)

    def start(self):
        self.copy().start()

    def wait_recv(self):
        self.copy().wait_recv()

    def wait_send(self):
        self.copy().wait_send()


class Links:
    def __init__(self, send_sem, recv_sem, line=0):
        self.send_sem, self.recv_sem, self.sent, self.count = send_sem, recv_sem, [], 0
        self.r, self.f, self.t = (lax.axis_index(name) for name in ("replica", "fsdp", "tensor"))
        self.xb, self.yb = lax.rem(self.f, 2), lax.div(self.f, 2)
        self.x = (self.r, self.f + 1 - 2 * self.xb, self.t)
        self.y = (self.r, lax.rem(self.f + 2, 4), self.t)
        self.core = (1 - self.r, self.f, self.t)
        self.peers = [self.x, self.y, self.core]
        if line:
            self.line = line
            self.left, self.right, self.across = (
                (self.r, self.f, lax.rem(self.t + step, line)) for step in (line - 1, 1, 2)
            )
            self.pair = (self.r, self.f, self.t + 1 - 2 * lax.rem(self.t, 2))
            self.far = (self.r, 3 - self.f, self.t)
            self.mirror = (self.r, self.f, line - 1 - self.t)
            self.peers += [self.far, self.left, self.right, self.across]

    def meet(self):
        barrier = pltpu.get_barrier_semaphore()
        for peer in self.peers:
            pl.semaphore_signal(barrier, inc=1, device_id=peer, device_id_type=MESH)
        pl.semaphore_wait(barrier, len(self.peers))

    def prepare(self, source, target, peer):
        self.count += 1
        return Sent(self, self.count - 1, source, target, peer)

    def send(self, source, target, peer):
        copy = self.prepare(source, target, peer)
        copy.start()
        self.sent.append(copy)
        return copy

    def series(self, count):
        k = self.count
        self.count += count
        return k

    def copy_at(self, k, source, target, peer):
        return pltpu.make_async_remote_copy(
            src_ref=source,
            dst_ref=target,
            send_sem=self.send_sem.at[k],
            recv_sem=self.recv_sem.at[k],
            device_id=peer,
            device_id_type=MESH,
        )

    def sent_out(self, copy):
        copy.wait_send()
        self.sent = [other for other in self.sent if other is not copy]

    def end(self):
        for copy in self.sent:
            copy.wait_send()

    def block(self, i):
        place = 0
        for size, bit in ((4, self.yb), (2, self.xb), (1, self.r)):
            mine = lax.rem(lax.div(i, size), 2) if isinstance(i, jax.Array) else i // size % 2
            place = place + size * (mine + bit - 2 * mine * bit)
        return place


class Local:
    def __init__(self, sem):
        self.sem, self.count, self.open, self.free = sem, 0, [], []

    def start(self, source, target):
        if not self.free:
            self.free.append(self.count)
            self.count += 1
        k = self.free.pop(0)
        copy = pltpu.make_async_copy(source, target, self.sem.at[k])
        copy.start()
        self.open.append((copy, k))
        return copy

    def wait(self, *copies):
        for copy in copies:
            copy.wait()
            self.free += [k for other, k in self.open if other is copy]
            self.open = [pair for pair in self.open if pair[0] is not copy]

    def end(self):
        self.wait(*[copy for copy, _ in self.open])


def at_rows(ref, start, size):
    return ref.at[pl.ds(start, size), :]


def at_columns(ref, start, size):
    return ref.at[:, pl.ds(start, size)]


class Gathered:
    def __init__(self, links, local, shard, full, cut, unit, copied=True):
        self.links, self.local, self.full, self.cut = links, local, full, cut
        self.shard, self.unit, self.half = shard, unit, unit // 2
        self.starts = [pl.multiple_of(links.r * unit + start, self.half) for start in (0, self.half)]
        self.bases = [pl.multiple_of(base * unit, unit) for base in (links.r, 1 - links.r)]
        self.copies = [local.start(self.here(i), self.at(i)) for i in range(2)] if copied else []
        self.from_x, self.from_y = {}, {}

    def here(self, i):
        return self.cut(self.shard, self.bases[i], self.unit)

    def mine(self, lower):
        return self.cut(self.shard, self.starts[lower], self.half)

    def at(self, block, start=0, size=None):
        return self.cut(self.full, block * self.unit + start, self.unit if size is None else size)

    def to_x(self, lower):
        source, target = self.mine(lower), self.at(2, self.half * lower, self.half)
        self.from_x[lower] = self.links.send(source, target, self.links.x)

    def to_y(self, lower):
        source, target = self.mine(lower), self.at(4, self.half * lower, self.half)
        self.from_y[lower] = self.links.send(source, target, self.links.y)

    def first(self):
        self.to_x(False)
        self.to_y(True)

    def rest(self):
        self.to_x(True)
        self.to_y(False)

    def pass_y(self):
        half = self.half
        self.from_x[False].wait_recv()
        self.far_top = self.links.send(self.at(2, 0, half), self.at(6, 0, half), self.links.y)

    def pass_x(self):
        half = self.half
        self.from_y[True].wait_recv()
        self.far_end = self.links.send(self.at(4, half, half), self.at(6, half, half), self.links.x)

    def relay(self):
        self.pass_y()
        self.pass_x()

    def share(self):
        self.from_y[False].wait_recv()
        self.core_y = self.links.send(self.at(4), self.at(5), self.links.core)
        self.from_x[True].wait_recv()
        self.core_x = self.links.send(self.at(2), self.at(3), self.links.core)

    def share_far(self):
        self.far_top.wait_recv()
        self.far_end.wait_recv()
        self.core_far = self.links.send(self.at(6), self.at(7), self.links.core)

    def passed(self):
        for copy in (self.far_top, self.far_end, self.core_x, self.core_y, self.core_far):
            self.links.sent_out(copy)

    def whole(self):
        self.local.wait(*self.copies)
        for copy in (self.core_x, self.core_y, self.core_far):
            copy.wait_recv()


def odd(j):
    return j % 2 if isinstance(j, int) else lax.rem(j, 2)


def tile_of(j, size):
    return pl.ds(pl.multiple_of(j * size, size), size)


def dot(left, right):
    return jnp.dot(left, right, preferred_element_type=FULL)


def spin(values_in, cosine, sine):
    head = values_in[:, :128]
    lane = lax.broadcasted_iota(jnp.int32, head.shape, 1)
    swapped = jnp.where(lane < ROT // 2, pltpu.roll(head, 96, 1), pltpu.roll(head, 32, 1))
    return jnp.concatenate([head * cosine + swapped * sine, values_in[:, 128:]], -1)


class Scattered:
    def __init__(self, links, local, blocks, cut, unit, via, got, stage=None, own=None):
        self.links, self.local, self.blocks, self.cut, self.unit = links, local, blocks, cut, unit
        self.via, self.got = [via.at[n] for n in range(2)], [got.at[n] for n in range(2)]
        self.stage, self.own = stage, own
        self.half, self.loads = unit // 2, []

    def load(self):
        self.loads = [
            self.local.start(self.cut(self.blocks[1], self.half, self.half), self.stage[0]),
            self.local.start(self.cut(self.blocks[2], 0, self.half), self.stage[1]),
            self.local.start(self.blocks[0], self.own),
        ]

    def first(self):
        half, cut, far = self.half, self.cut, self.blocks[3]
        self.via_x = self.links.send(cut(far, 0, half), self.via[0], self.links.x)
        self.via_y = self.links.send(cut(far, half, half), self.via[1], self.links.y)

    def direct(self):
        half, cut = self.half, self.cut
        self.x_top = self.links.send(cut(self.blocks[1], 0, half), cut(self.got[0], 0, half), self.links.x)
        self.y_end = self.links.send(cut(self.blocks[2], half, half), cut(self.got[1], half, half), self.links.y)

    def second(self):
        half, cut = self.half, self.cut
        self.local.wait(*self.loads[:2])
        self.via_x.wait_recv()
        add_rows(self.stage[1], self.stage[1], self.via[0])
        self.y_top = self.links.send(self.stage[1], cut(self.got[1], 0, half), self.links.y)
        self.via_y.wait_recv()
        add_rows(self.stage[0], self.stage[0], self.via[1])
        self.x_end = self.links.send(self.stage[0], cut(self.got[0], half, half), self.links.x)

    def third(self, slots, place, step, between=lambda: None):
        for copy in (self.x_top, self.x_end, self.y_top, self.y_end):
            copy.wait_recv()
        if self.loads:
            self.local.wait(self.loads[2])
        self.other = []
        for start in range(0, self.own.shape[0], step):
            between()
            rows = pl.ds(start, step)
            at, total = slots.take()
            add_rows(total, self.own.at[rows, :], self.got[0].at[rows, :], self.got[1].at[rows, :])
            kept = self.local.start(total, place.at[rows, :])
            other = self.links.send(total, place.at[rows, :], self.links.core)
            self.other.append(other)

            def done(kept=kept, other=other):
                self.local.wait(kept)
                self.links.sent_out(other)

            slots.busy[at] = done


def add_rows(target, *parts):
    rows, wide = target.shape
    step = min(rows, 32 if wide > 512 else 256)

    def one(c, carry):
        at = pl.ds(pl.multiple_of(c * step, step), step)
        total = parts[0][at, :].astype(FULL)
        for part in parts[1:]:
            total = total + part[at, :].astype(FULL)
        target[at, :] = total.astype(target.dtype)
        return carry

    lax.fori_loop(0, rows // step, one, 0)


class Line:
    def __init__(self, links, part, got, final, chunks, cut, finish):
        self.links, self.part, self.got, self.final, self.cut, self.finish = links, part, got, final, cut, finish
        self.chunks = chunks
        self.outer = jnp.logical_or(links.t == 0, links.t == links.line - 1)
        self.middle = jnp.logical_not(self.outer)
        self.inward = [self.make(c, part, final, links.pair) for c in range(chunks)]
        self.across = [self.make(c, part, got, links.mirror) for c in range(chunks)]
        self.outward = [
            Sent(links, self.inward[c].k, cut(final, c), cut(final, c), links.pair) for c in range(chunks)
        ]

    def make(self, c, source, target, peer):
        return self.links.prepare(self.cut(source, c), self.cut(target, c), peer)

    def start(self, *chunks):
        @pl.when(self.outer)
        def _():
            for c in chunks:
                self.inward[c].start()

    def first(self, c):
        @pl.when(self.middle)
        def _():
            self.inward[c].wait_recv()
            part = self.cut(self.part, c)
            add_rows(part, part, self.cut(self.final, c))
            self.across[c].start()

    def second(self, c):
        @pl.when(self.middle)
        def _():
            self.across[c].wait_recv()
            self.finish(c)
            self.outward[c].start()

    def third(self, c):
        @pl.when(self.outer)
        def _():
            self.outward[c].wait_recv()

    def end(self):
        @pl.when(self.outer)
        def _():
            for copy in self.inward:
                copy.wait_send()

        @pl.when(self.middle)
        def _():
            for copy in self.across + self.outward:
                copy.wait_send()


class Slots:
    def __init__(self, *refs):
        self.refs, self.busy, self.count = refs, {}, 0

    def take(self):
        at = self.count % len(self.refs)
        self.count += 1
        if at in self.busy:
            self.busy.pop(at)()
        return at, self.refs[at]

    def end(self):
        for wait in self.busy.values():
            wait()
        self.busy = {}


def block_kernel(
    score_scale, line_size,
    x_hbm, g_hbm, wh_hbm, wo_hbm, we_own, ws_own, gain_one, shift_one, gain_two, shift_two, units_bias, heads_bias,
    bias_one, bias_two, order,
    layer_out, input_grad, heads_grad, output_grad, expand_grad, shrink_grad, we, ws, n2t_hbm, got_core_s, got_core_o,
    got_core_h, got_core_e, red_s, red_o, red_h, sums_out,
    x, g, up, n1, nt, stat, wh, wo, qkv, dctx, ctxt, pg, kvg_got, got_branch, final_branch, got_up, final_up,
    via_h, got_h, via_o, got_o, via_s, got_s, via_e, got_e, raw, vecs, sums, sums_got, gains, gains_got,
    loop_sem, block_sem, local_sem, send_sem, recv_sem,
):
    links, local = Links(send_sem, recv_sem, line_size), Local(local_sem)
    tokens, width = x.shape
    units, heads_wide, out_wide = we.shape[1], wh.shape[1], wo.shape[0]
    hd = dctx.shape[1]
    unit = width // 8
    blocks = range(8)
    room_s = qkv
    place = [pl.ds(pl.multiple_of(links.block(i) * unit, unit), unit) for i in blocks]

    def here(i):
        return pl.ds(i * unit, unit)

    rest_rows = pl.ds(2 * unit, width - 2 * unit)

    def tile(j):
        return pl.ds(j * unit if isinstance(j, int) else pl.multiple_of(j * unit, unit), unit)

    def placed(i):
        return pl.ds(pl.multiple_of(links.block(i) * unit, unit), unit)

    def stream(start, end, load, body):
        def copies(j):
            pairs = load(j, odd(j))
            return [pltpu.make_async_copy(*pair, loop_sem.at[n, odd(j)]) for n, pair in enumerate(pairs)]

        for copy in copies(start):
            copy.start()

        def one(j, carry):
            @pl.when(j + 1 < end)
            def _():
                for copy in copies(j + 1):
                    copy.start()

            for copy in copies(j):
                copy.wait()
            body(j, odd(j))
            return carry

        lax.fori_loop(start, end, one, 0)

    links.meet()
    heads_in = Gathered(links, local, wh_hbm, wh, at_rows, unit)
    heads_in.first()
    heads_in.rest()
    x_in, g_in = [], []
    for i in blocks:
        cols = pl.ds(pl.multiple_of(links.block(i) * unit, unit), unit)
        x_in.append(local.start(x_hbm.at[:, cols], x.at[:, pl.ds(i * unit, unit)]))
        g_in.append(local.start(g_hbm.at[:, cols], g.at[:, pl.ds(i * unit, unit)]))
    output_in = Gathered(links, local, wo_hbm, wo, at_columns, unit)
    expand = Gathered(links, local, we_own, we, at_rows, unit)
    weight = Gathered(links, local, ws_own, ws, at_columns, unit, False)

    def row(ref):
        return ref[...].astype(FULL).reshape(1, -1)

    for i, vec in enumerate((gain_one, shift_one, gain_two, shift_two, units_bias)):
        raw[i : i + 1, :] = row(vec)
    raw[6:7, :] = row(bias_one) + row(bias_two)
    head_rows = heads_bias[...].astype(FULL)
    raw[5:6, : 3 * hd], raw[7:8, : 3 * hd] = head_rows[0:1, :], head_rows[1:2, :]

    turns = (3, 1, 2, 0)

    def turn_of(n):
        return jnp.where(n == 0, 3, jnp.where(n == 3, 0, n))

    class Reduced:
        def __init__(self, room, got, block):
            self.room, self.got, self.block = room, got, block
            self.gots = [got.at[k] for k in range(4)]

        def to_core(self):
            first = links.series(4)

            def one(n, carry):
                k = turn_of(n)
                self.block(2 * k + 1, self.room(n), False)
                links.copy_at(first + n, self.room(n), self.got.at[k], links.core).start()
                return carry

            lax.fori_loop(0, 4, one, 0)
            self.copies = [Sent(links, first + n, self.room(n), self.gots[turns[n]], links.core) for n in range(4)]

        def fetch(self):
            for n in range(4):
                self.copies[n].wait_send()
                self.copies[n].wait_recv()
                pltpu.make_async_copy(self.got.at[turns[n]], self.room(n), block_sem.at[n]).start()

        def add(self, red):
            def one(n, carry):
                k = turn_of(n)
                pltpu.make_async_copy(self.got.at[k], self.room(n), block_sem.at[n]).wait()
                self.block(2 * k, self.room(n), True)
                if red is not None:
                    pltpu.make_async_copy(self.room(n), red.at[k], block_sem.at[4 + n]).start()
                return carry

            lax.fori_loop(0, 4, one, 0)
            if red is not None:
                for n in range(4):
                    pltpu.make_async_copy(self.room(n), red.at[turns[n]], block_sem.at[4 + n]).wait()

    def product(left, right, ref, add):
        part = dot(left, right)
        if add:
            part = part + ref[...].astype(FULL)
        ref[...] = part.astype(LOW)

    def heads_block(i, ref, add):
        product(nt[tile(i), :], pg[...], ref, add)

    heads_sum = Reduced(lambda n: wh.at[tile(n), :], got_core_h, heads_block)
    own_h = at_rows(wh, 4 * unit, unit)
    stage_h = (at_rows(wh, 5 * unit, unit // 2), at_rows(wh, 5 * unit + unit // 2, unit // 2))
    heads = Scattered(links, local, [red_h.at[k] for k in range(4)], at_rows, unit, via_h, got_h, stage_h, own_h)
    shrink = Scattered(links, local, [red_s.at[k] for k in range(4)], at_columns, unit, via_s, got_s)
    output = Scattered(links, local, [red_o.at[k] for k in range(4)], at_columns, unit, via_o, got_o)

    def up_part(i, grad, first):
        cols, spot = tile(i), placed(i)
        normal = (x[:, cols].astype(FULL) - stat[:, 0:1]) * stat[:, 128:129]
        row = 0 if first else 2
        sums[0, row : row + 1, spot] = jnp.sum(grad * normal, 0, keepdims=True)
        sums[0, row + 1 : row + 2, spot] = jnp.sum(grad, 0, keepdims=True)
        scaled = grad * (vecs[0:1, cols] if first else vecs[2:3, cols])
        n1[:, cols] = (scaled if first else n1[:, cols].astype(FULL) + scaled).astype(LOW)

    def attend(qkv_away, dctx_away, ctxt_all, pgq, pg_away, kvg_away, cosine, sines, dk, dv, stage):
        for i in blocks:
            cols = pl.ds(pl.multiple_of(links.block(i) * unit, unit), unit)
            vecs[0:4, i * unit : (i + 1) * unit] = raw[0:4, cols]
            vecs[4:5, i * unit : (i + 1) * unit] = raw[6:7, cols]
        local.wait(*x_in)

        def norm_rows(c, carry):
            rows = tile_of(c, 64)
            value = x[rows, :].astype(FULL)
            average = jnp.mean(value, -1, keepdims=True)
            centred = value - average
            inverse = lax.rsqrt(jnp.mean(centred * centred, -1, keepdims=True) + NORM_EPS)
            normal = centred * inverse
            both = [jnp.broadcast_to(part, (64, 128)) for part in (average, inverse)]
            stat[rows, :] = jnp.concatenate(both, -1)
            n1[rows, :] = (normal * vecs[0:1, :] + vecs[1:2, :]).astype(LOW)
            up[rows, :] = (normal * vecs[2:3, :] + vecs[3:4, :]).astype(LOW)
            return carry

        lax.fori_loop(0, tokens // 64, norm_rows, 0)
        bases = [
            order[0, (links.yb if step < 2 else 1 - links.yb) * 2 + (links.xb if step % 2 == 0 else 1 - links.xb)]
            * tokens
            for step in (0, 2, 1, 3)
        ]

        def table_rows(c, carry):
            rows = tile_of(c, 64)
            lane = lax.broadcasted_iota(jnp.int32, (64, 128), 1)
            row = lax.broadcasted_iota(jnp.int32, (64, 128), 0) + c * 64
            spot = row + jnp.where(row < tokens, bases[0], bases[1] - tokens)
            pace = jnp.exp(lax.rem(lane, ROT // 2).astype(FULL) * (-2.0 / ROT * math.log(10000.0)))
            angle = spot.astype(FULL) * pace
            sine = jnp.sin(angle)
            cosine[rows, :] = jnp.where(lane < ROT, jnp.cos(angle), 1.0)
            sines[rows, :] = jnp.where(lane < ROT // 2, -sine, jnp.where(lane < ROT, sine, 0.0))
            return carry

        lax.fori_loop(0, 2 * tokens // 64, table_rows, 0)
        heads_in.relay()
        output_in.first()
        output_in.rest()

        def turned_copy(j):
            slot = odd(j)
            return pltpu.make_async_copy(stage.at[slot], n2t_hbm.at[tile_of(j, unit), :], loop_sem.at[0, slot])

        def turn_tiles(j, carry):
            cols = tile_of(j, unit)
            nt[cols, :] = n1[:, cols].T

            @pl.when(j >= 2)
            def _():
                turned_copy(j - 2).wait()

            stage[odd(j), :, :] = up[:, cols].T
            turned_copy(j).start()
            return carry

        lax.fori_loop(0, 8, turn_tiles, 0)
        for j in (6, 7):
            turned_copy(j).wait()
        sums[0, :, :] = jnp.zeros(sums.shape[1:], FULL)
        local.wait(*g_in)
        for i in blocks:
            cols = pl.ds(pl.multiple_of(links.block(i) * unit, unit), unit)
            sums[0, 4:5, cols] = jnp.sum(g[:, i * unit : (i + 1) * unit].astype(FULL), 0, keepdims=True)
        heads_in.share()
        heads_in.share_far()
        heads_in.whole()
        output_in.relay()

        own = links.yb * 3 * hd

        def project(c, head, target):
            cols = pl.ds(pl.multiple_of(head * 3 * hd + c * hd, hd), hd)
            bias = jnp.where(head == 0, raw[5:6, c * hd : (c + 1) * hd], raw[7:8, c * hd : (c + 1) * hd])
            value = dot(n1[...], wh[:, cols]) + bias
            if c < 2:
                value = spin(value, cosine[:tokens, :], sines[:tokens, :])
            target[c, :tokens, :] = value.astype(LOW)

        def place_of(c, part):
            return qkv.at[c, pl.ds(part * tokens, tokens), :]

        from_y, from_x, from_far = {}, {}, {}
        for c in (1, 2):
            project(c, links.yb, qkv)
            from_x[c] = links.send(place_of(c, 0), place_of(c, 2), links.x)
        for c in (1, 2, 0):
            project(c, 1 - links.yb, qkv_away)
            from_y[c] = links.send(qkv_away.at[c], place_of(c, 1), links.y)
        from_y[1].wait_recv()
        from_far[1] = links.send(place_of(1, 1), place_of(1, 3), links.x)
        project(0, links.yb, qkv)
        output_in.share()
        output_in.share_far()
        from_y[2].wait_recv()
        from_far[2] = links.send(place_of(2, 1), place_of(2, 3), links.x)
        output_in.whole()
        rows_own = pl.ds(pl.multiple_of(links.yb * hd, hd), hd)
        rows_away = pl.ds(pl.multiple_of((1 - links.yb) * hd, hd), hd)
        dctx_away[...] = contract_last(g[...], wo[rows_away, :]).astype(LOW)
        dctx_from_y = links.send(dctx_away, dctx.at[pl.ds(tokens, tokens), :], links.y)
        dctx[:tokens, :] = contract_last(g[...], wo[rows_own, :]).astype(LOW)
        expand.first()
        expand.to_y(False)
        for copy in (from_y[0], dctx_from_y, *from_x.values(), *from_far.values()):
            copy.wait_recv()

        def attention(kt, vt, prob, wgt, prob_low, grad_low):
            keys = qkv.shape[1]
            step = tokens
            lag = lax.broadcasted_iota(jnp.int32, (step, hd), 0) - lax.broadcasted_iota(jnp.int32, (step, hd), 1)
            parts = [pl.ds(i * step, step) for i in range(keys // step)]
            for part in parts:
                kt[:, part] = qkv[1, part, :].T
                vt[:, part] = qkv[2, part, :].T
            dk[...] = jnp.zeros_like(dk)
            dv[...] = jnp.zeros_like(dv)

            def one(b, carry):
                rows = tile_of(b, hd)
                query, grad = qkv[0, rows, :], dctx[rows, :]
                ahead = jnp.where(b < tokens // hd, bases[0], bases[1] - tokens) + b * hd
                top = jnp.full((1, hd), MASKED, FULL)
                for i, part in enumerate(parts):
                    scores = contract_last(qkv[1, part, :], query) * score_scale
                    scores = jnp.where(lag <= ahead - bases[i], scores, MASKED)
                    prob[part, :] = scores
                    top = jnp.maximum(top, jnp.max(scores, 0, keepdims=True))
                total = jnp.zeros((1, hd), FULL)
                for part in parts:
                    exponent = jnp.exp(prob[part, :] - top)
                    prob[part, :] = exponent
                    total = total + jnp.sum(exponent, 0, keepdims=True)
                share = 1.0 / total
                inner = jnp.zeros((1, hd), FULL)
                for part in parts:
                    weight = contract_last(qkv[2, part, :], grad)
                    chance = prob[part, :] * share
                    prob[part, :] = chance
                    prob_low[part, :] = chance.astype(LOW)
                    wgt[part, :] = weight
                    inner = inner + jnp.sum(chance * weight, 0, keepdims=True)
                for part in parts:
                    grad_low[part, :] = (prob[part, :] * (wgt[part, :] - inner)).astype(LOW)
                ctxt_all[:, rows] = dot(vt[...], prob_low[...]).astype(LOW)
                query_grad = dot(kt[...], grad_low[...]) * score_scale
                for part in parts:
                    dv[part, :] += dot(prob_low[part, :], grad)
                    dk[part, :] += dot(grad_low[part, :], query)
                turned_grad = spin(query_grad.T, cosine[rows, :], -sines[rows, :])
                pgq[rows, :] = turned_grad.astype(LOW)
                return carry

            lax.fori_loop(0, 2 * tokens // hd, one, 0)
            ctxt[rows_own, :] = ctxt_all[:, :tokens]
            pg[:, pl.ds(pl.multiple_of(own, hd), hd)] = pgq[:tokens, :]
            for i, total in enumerate((dk, dv)):
                kvg_away[i, :, :] = total[2 * tokens :, :].astype(LOW)

        keys = qkv.shape[1]
        pl.run_scoped(
            attention,
            pltpu.VMEM((hd, keys), LOW),
            pltpu.VMEM((hd, keys), LOW),
            pltpu.VMEM((keys, hd), FULL),
            pltpu.VMEM((keys, hd), FULL),
            pltpu.VMEM((keys, hd), LOW),
            pltpu.VMEM((keys, hd), LOW),
        )

        def head_columns(ref, start, i):
            return ref.at[:, pl.ds(pl.multiple_of(start + i * hd, hd), hd)]

        def send_grad(i):
            source = pgq.at[pl.ds(tokens, tokens), :] if i == 0 else head_columns(pg_away, 0, i - 1)
            return links.send(source, head_columns(pg, own, i), links.y)

        kvg_from_x = {i: links.send(kvg_away.at[i], kvg_got.at[i], links.x) for i in (1, 0)}
        pg_from_y = [send_grad(0)]
        ctx_from_y = links.send(ctxt_all.at[:, pl.ds(tokens, tokens)], ctxt.at[rows_own, :], links.y)
        expand.pass_x()
        expand.to_x(True)

        for i in (1, 0):
            kvg_from_x[i].wait_recv()
            for away_rows, target in ((True, pg_away), (False, pg)):
                rows = pl.ds(tokens if away_rows else 0, tokens)
                total = (dk, dv)[i][rows, :] + kvg_got[i, rows, :].astype(FULL)
                if i == 0:
                    total = spin(total * score_scale, cosine[rows, :], -sines[rows, :])
                head_columns(target, 0 if away_rows else own, i if away_rows else 1 + i)[...] = total.astype(LOW)
                if away_rows:
                    pg_from_y.append(send_grad(1 + i))
        expand.pass_y()
        weight.first()
        weight.rest()
        ctx_from_y.wait_recv()
        for copy in pg_from_y:
            copy.wait_recv()

        def first_block(i, carry):
            up_part(i, contract_last(pg[...], wh[tile(i), :]), True)
            return carry

        lax.fori_loop(0, 8, first_block, 0)
        sums[0, 6:7, :heads_wide] = jnp.sum(pg[...].astype(FULL), 0, keepdims=True)
        heads_in.passed()
        heads_sum.to_core()
        expand.share()
        expand.share_far()
        expand.whole()
        for copy in (*from_y.values(), *from_x.values(), *from_far.values(), dctx_from_y, *kvg_from_x.values(), *pg_from_y, ctx_from_y):
            links.sent_out(copy)

    low, full = (functools.partial(lambda kind, *shape: pltpu.VMEM(shape, kind), kind) for kind in (LOW, FULL))
    pl.run_scoped(
        attend,
        low(3, tokens, hd),
        low(tokens, hd),
        low(hd, 2 * tokens),
        low(2 * tokens, hd),
        low(tokens, 2 * hd),
        low(2, 2 * tokens, hd),
        full(2 * tokens, 128),
        full(2 * tokens, 128),
        full(4 * tokens, hd),
        full(4 * tokens, hd),
        low(2, unit, tokens),
    )

    def update(act, actt, slope, ctx, room_o, stage_o, own_o, room_e, total_rows, total_columns, grad_rows):
        def forward(j, slot):
            cols = tile(j)
            value = dot(up[...], room_s[slot]) + raw[4:5, cols]
            normal_share = 0.5 * (1.0 + lax.erf(value * (0.5**0.5)))
            low_act = (value * normal_share).astype(LOW)
            act[:, cols] = low_act
            actt[cols, :] = low_act.T
            density = jnp.exp(value * value * -0.5) * 0.3989422804014327
            slope[:, cols] = (normal_share + value * density).astype(LOW)

        stream(0, 8, lambda j, slot: [(we.at[:, tile(j)], room_s.at[slot])], forward)
        weight.relay()
        ctx[...] = ctxt[...].T

        rows_out = grad_rows.shape[1]

        def columns_cut(ref, c):
            return ref.at[:, here(c)]

        def rows_cut(ref, c):
            return ref.at[pl.ds(c * rows_out, rows_out), :]

        def finish_branch(c):
            cols = here(c)

            def one(part, carry):
                at = tile_of(part, 128)
                total = up[at, cols].astype(FULL) + got_branch[at, cols].astype(FULL)
                final_branch[at, cols] = (x[at, cols].astype(FULL) + total + vecs[4:5, cols]).astype(LOW)
                return carry

            lax.fori_loop(0, tokens // 128, one, 0)

        def finish_up(c):
            add_rows(rows_cut(final_up, c), rows_cut(n1, c), rows_cut(got_up, c))

        line_branch = Line(links, up, got_branch, final_branch, 8, columns_cut, finish_branch)
        line_up = Line(links, n1, got_up, final_up, tokens // rows_out, rows_cut, finish_up)

        def branch_blocks(chunks, block, source):
            def one(n, slot):
                cols = tile(block(n))
                up[:, cols] = (dot(ctx[...], wo[:, cols]) + dot(act[...], room_s[slot])).astype(LOW)
                for at, chunk in enumerate(chunks):
                    pl.when(n == at)(functools.partial(line_branch.start, chunk))

            stream(0, len(chunks), lambda n, slot: [(source(n), room_s.at[slot])], one)

        steps = [(line_branch, c) for c in (0, 1, 2, 4, 3, 5, 6, 7)] + [(line_up, c) for c in range(line_up.chunks)]
        out_copies = []

        def input_rows(c):
            slot = len(out_copies) % 2
            if len(out_copies) >= 2:
                local.wait(*out_copies[-2])
            rows = pl.ds(c * rows_out, rows_out)
            value = x[rows, :].astype(FULL)
            centred = value - jnp.mean(value, -1, keepdims=True)
            scale = lax.rsqrt(jnp.mean(centred * centred, -1, keepdims=True) + NORM_EPS)
            normal = centred * scale
            upstream = final_up[rows, :].astype(FULL)
            inner = upstream - jnp.mean(upstream, -1, keepdims=True)
            inner = inner - normal * jnp.mean(upstream * normal, -1, keepdims=True)
            grad_rows[slot, :, :] = (g[rows, :].astype(FULL) + inner * scale).astype(LOW)
            out_copies.append(
                [local.start(grad_rows.at[slot, :, here(i)], input_grad.at[rows, place[i]]) for i in blocks]
            )

        def serve(count):
            for _ in range(count):
                at = serve.done
                if at < len(steps):
                    steps[at][0].first(steps[at][1])
                if 2 <= at < len(steps) + 2:
                    steps[at - 2][0].second(steps[at - 2][1])
                if at >= 4:
                    line, c = steps[at - 4]
                    line.third(c)
                    if line is line_up:
                        input_rows(c)
                    else:
                        local.start(final_branch.at[:, here(c)], layer_out.at[:, place[c]])
                serve.done += 1

        serve.done = 0
        branch_blocks((0, 1), lambda n: n, lambda n: at_columns(ws_own, pl.multiple_of((links.r + n - 2 * links.r * n) * unit, unit), unit))

        def shrink_block(i, ref, add):
            product(actt[...], g[:, tile(i)], ref, add)

        def output_block(i, ref, add):
            product(ctxt[...], g[:, tile(i)], ref, add)

        def expand_block(i, ref, add):
            product(nt[tile(i), :], slope[...], ref, add)

        shrink.stage = (actt.at[:, pl.ds(unit, unit // 2)], actt.at[:, pl.ds(unit + unit // 2, unit // 2)])
        shrink.own = actt.at[:, pl.ds(0, unit)]
        output.stage, output.own = (stage_o.at[0], stage_o.at[1]), own_o
        shrink_sum = Reduced(lambda n: room_s.at[n], got_core_s, shrink_block)
        output_sum = Reduced(lambda n: room_o.at[n], got_core_o, output_block)
        expand_sum = Reduced(lambda n: room_e.at[n], got_core_e, expand_block)
        heads_sum.fetch()
        heads_sum.add(red_h)
        heads.first()
        heads.direct()
        heads.load()
        n2t_load = local.start(n2t_hbm, nt)
        weight.share()
        serve(1)
        weight.core_y.wait_recv()
        weight.core_x.wait_recv()
        ahead = lambda n: 2 * n + 2 - 3 * (n // 2 if isinstance(n, int) else lax.div(n, 2))
        branch_blocks((2, 4, 3, 5), ahead, lambda n: ws.at[:, tile(ahead(n))])
        serve(1)
        shrink_sum.to_core()
        weight.share_far()
        serve(1)
        shrink_sum.fetch()
        shrink_sum.add(red_s)
        shrink.first()
        shrink.direct()
        shrink.load()
        serve(1)
        weight.core_far.wait_recv()
        branch_blocks((6, 7), lambda n: n + 6, lambda n: ws.at[:, tile(n + 6)])
        serve(1)

        def hidden_tile(j, slot):
            cols = tile(j)
            grad = (contract_last(g[...], room_e[slot]) * slope[:, cols].astype(FULL)).astype(LOW)
            slope[:, cols] = grad
            sums[0, 5:6, cols] = jnp.sum(grad.astype(FULL), 0, keepdims=True)

        def shrink_rows(j, slot):
            rows = tile(j)
            pairs = [(weight.here(i).at[rows, :], room_e.at[slot, :, here(i)]) for i in range(2)]
            return pairs + [(ws.at[rows, rest_rows], room_e.at[slot, :, rest_rows])]

        stream(0, 4, shrink_rows, hidden_tile)
        serve(1)
        stream(4, 8, shrink_rows, hidden_tile)
        serve(1)

        def second_block(i, slot):
            up_part(i, contract_last(slope[...], room_e[slot]), False)

        expand_rows = lambda i, slot: [(we.at[tile(i), :], room_e.at[slot])]
        stream(0, 4, expand_rows, second_block)
        serve(1)
        stream(4, 8, expand_rows, second_block)
        line_up.start(*range(line_up.chunks))

        def share(s, peers):
            return [links.send(sums.at[s], sums_got.at[4 * s + k], peer) for k, peer in enumerate(peers)]

        def shared(s, copies):
            for copy in copies:
                copy.wait_recv()
            total = sums[s, :, :] + sums_got[4 * s, :, :]
            if len(copies) > 1:
                total = total + (sums_got[4 * s + 1, :, :] + sums_got[4 * s + 2, :, :])
            sums[s + 1, :, :] = total

        def share_line(s, peer):
            return links.send(gains.at[s], gains_got.at[s], peer)

        def shared_line(s, copy):
            copy.wait_recv()
            gains[s + 1, :, :] = gains[s, :, :] + gains_got[s, :, :]

        first_share = share(0, [links.core])
        output_sum.to_core()
        shared(0, first_share)
        second_share = share(1, [links.x, links.y, links.far])
        output_sum.fetch()
        output_sum.add(red_o)
        output.first()
        output.direct()
        output.load()

        local.wait(n2t_load)
        expand_sum.to_core()
        serve(1)
        shrink.second()
        serve(1)
        expand_sum.fetch()
        serve(1)
        expand_sum.add(None)
        red = {k: room_e.at[turns.index(k)] for k in range(4)}
        expand = Scattered(links, local, [red[k] for k in range(4)], at_rows, unit, via_e, got_e, None, red[0])
        expand.first()
        expand.direct()
        serve(2)
        half_rows = pl.ds(pl.multiple_of(links.r * unit, unit), unit)
        column_slots = Slots(*[total_columns.at[n] for n in range(4)])
        serve(2)
        shrink.third(column_slots, shrink_grad.at[:, half_rows], total_columns.shape[1])
        serve(1)
        shared(1, second_share)
        for row in range(4):
            for side in range(2):
                at = 2 * row + side
                gains[0, at : at + 1, :] = sums[2, row : row + 1, side * (width // 2) : (side + 1) * (width // 2)]
        pair_share = share_line(0, links.pair)
        serve(3)

        expand.via_x.wait_recv()
        top, end = red[2].at[pl.ds(0, unit // 2), :], red[1].at[pl.ds(unit // 2, unit // 2), :]
        add_rows(top, top, via_e.at[0])
        expand.y_top = links.send(top, got_e.at[1, pl.ds(0, unit // 2), :], links.y)
        expand.via_y.wait_recv()
        add_rows(end, end, via_e.at[1])
        expand.x_end = links.send(end, got_e.at[0, pl.ds(unit // 2, unit // 2), :], links.x)
        heads.second()
        output.second()
        serve(len(steps) - 1 - serve.done)
        shared_line(0, pair_share)
        across_share = share_line(1, links.across)
        serve(2)
        expand_slots = Slots(*[total_rows.at[n] for n in range(4)])
        expand.third(expand_slots, expand_grad.at[half_rows, :], total_rows.shape[1])
        serve(len(steps) + 4 - serve.done)
        expand_slots.end()
        total_slots = Slots(*[total_rows.at[n, :, pl.ds(0, heads_wide)] for n in range(4)])
        heads.third(total_slots, heads_grad.at[half_rows, :], total_rows.shape[1])
        output.third(column_slots, output_grad.at[:, half_rows], total_columns.shape[1])
        total_slots.end()
        column_slots.end()
        shared_line(1, across_share)
        for row in range(4):
            for side in range(2):
                at = 2 * row + side
                sums_out[row : row + 1, side * (width // 2) : (side + 1) * (width // 2)] = gains[2, at : at + 1, :]
        sums_out[4:8, :] = sums[2, 4:8, :]
        for copy in (*shrink.other, *output.other, *heads.other, *expand.other):
            copy.wait_recv()
        assert links.count <= COPIES and local.count <= LOCALS
        links.end()
        line_branch.end()
        line_up.end()
        local.end()


    pl.run_scoped(
        update,
        low(tokens, units),
        low(units, tokens),
        low(tokens, units),
        low(tokens, out_wide),
        low(4, out_wide, unit),
        low(2, out_wide, unit // 2),
        low(out_wide, unit),
        low(4, unit, units),
        low(4, unit // 4, units),
        low(4, out_wide, unit),
        low(2, 32, width),
    )


def block_call(line_size, x, g, heads_rows, output_rows, expand_weight, shrink_weight, vectors, order):
    tokens, width = x.shape
    heads_wide, out_wide, units = heads_rows.shape[1], output_rows.shape[0], expand_weight.shape[1]
    hd, unit, half = heads_wide // 6, width // 8, width // 16
    low = lambda *shape: pltpu.VMEM(shape, LOW)
    full = lambda *shape: pltpu.VMEM(shape, FULL)
    work = lambda *shape: jax.ShapeDtypeStruct(shape, LOW)
    outs = [
        work(tokens, width),
        work(tokens, width),
        work(2 * unit, heads_wide),
        work(out_wide, 2 * unit),
        work(2 * unit, units),
        work(units, 2 * unit),
        work(width, units),
        work(units, width),
        work(width, tokens),
        work(4, units, unit),
        work(4, out_wide, unit),
        work(4, unit, heads_wide),
        work(4, unit, units),
        work(4, units, unit),
        work(4, out_wide, unit),
        work(4, unit, heads_wide),
        jax.ShapeDtypeStruct((8, width), FULL),
    ]
    scratch = [
        *[low(tokens, width)] * 4, low(width, tokens), full(tokens, 256),
        low(width, heads_wide), low(out_wide, width), low(4, 4 * tokens, hd), low(2 * tokens, hd),
        low(out_wide, tokens), low(tokens, heads_wide), low(2, 2 * tokens, hd),
        *[low(tokens, width)] * 4,
        low(2, half, heads_wide), low(2, unit, heads_wide),
        low(2, out_wide, half), low(2, out_wide, unit),
        low(2, units, half), low(2, units, unit),
        low(2, half, units), low(2, unit, units),
        full(8, width), full(8, width), full(3, 8, width), full(7, 8, width), full(3, 8, width // 2), full(2, 8, width // 2),
        pltpu.SemaphoreType.DMA((3, 2)),
        pltpu.SemaphoreType.DMA((8,)),
        pltpu.SemaphoreType.DMA((LOCALS,)),
        pltpu.SemaphoreType.DMA((COPIES,)),
        pltpu.SemaphoreType.DMA((COPIES,)),
    ]
    return pl.pallas_call(
        functools.partial(block_kernel, hd**-0.5, line_size),
        out_shape=outs,
        in_specs=[ANY] * 6 + [IN_VMEM] * 8 + [pl.BlockSpec(memory_space=pltpu.SMEM)],
        out_specs=[ANY] * 16 + [IN_VMEM],
        scratch_shapes=scratch,
        compiler_params=pltpu.CompilerParams(
            collective_id=0, has_side_effects=True, vmem_limit_bytes=VMEM_BYTES
        ),
    )(x, g, heads_rows, output_rows, expand_weight, shrink_weight, *vectors, order)


def square_local(
    layer_input,
    block_order,
    first_gain,
    first_bias,
    second_gain,
    second_bias,
    heads_weight,
    heads_bias,
    output_weight,
    output_bias,
    expand_weight,
    expand_bias,
    shrink_weight,
    shrink_bias,
    cotangent,
):
    heads_rows = heads_weight.reshape(heads_weight.shape[0], -1)
    output_rows = output_weight.reshape(-1, output_weight.shape[2])
    vectors = (first_gain, first_bias, second_gain, second_bias, expand_bias, heads_bias, output_bias, shrink_bias)
    *results, sums = block_call(
        lax.axis_size("tensor"),
        layer_input[0],
        cotangent[0],
        heads_rows,
        output_rows,
        expand_weight,
        shrink_weight,
        vectors,
        block_order,
    )
    results = store_call(results[:6], sums, heads_weight.shape)
    layer_output, input_grad, heads_grad, output_grad, expand_grad, shrink_grad = results[:6]
    first_gain_grad, first_bias_grad, second_gain_grad, second_bias_grad = (vec.reshape(-1) for vec in results[6:10])
    output_bias_grad, expand_bias_grad, shrink_bias_grad = (vec.reshape(-1) for vec in results[10:13])
    return (
        layer_output[None],
        input_grad[None],
        first_gain_grad,
        first_bias_grad,
        second_gain_grad,
        second_bias_grad,
        heads_grad,
        results[13],
        output_grad.reshape(output_weight.shape),
        output_bias_grad,
        expand_grad,
        expand_bias_grad,
        shrink_grad,
        shrink_bias_grad,
    )


def store_kernel(*refs):
    *full_in, sums = refs[:7]
    full_out, rows_out, heads_bias_out = refs[7:13], refs[13:20], refs[20]
    for source, target in zip(full_in, full_out):
        if len(target.shape) == len(source.shape):
            target[...] = source[...].astype(target.dtype)
        else:
            wide = target.shape[2]
            for head in range(target.shape[1]):
                target[:, head, :] = source[:, head * wide : (head + 1) * wide].astype(target.dtype)

    @pl.when(pl.program_id(0) == 0)
    def _():
        for row, target in zip((0, 1, 2, 3, 4, 5, 4), rows_out):
            target[...] = sums[row : row + 1, :]
        wide = heads_bias_out.shape[1]
        for head in range(heads_bias_out.shape[0]):
            heads_bias_out[head : head + 1, :] = sums[6:7, head * wide : (head + 1) * wide]


def store_call(results, sums, heads_shape):
    steps = 2
    width = sums.shape[1]

    def cut(shape):
        zeros = (0,) * (len(shape) - 1)
        return pl.BlockSpec((shape[0] // steps,) + tuple(shape[1:]), lambda i: (i, *zeros))

    def whole(shape):
        return pl.BlockSpec(tuple(shape), lambda i: (0,) * len(shape))

    kept = [result.shape for result in results]
    kept[2] = heads_shape
    rows, heads_bias = (1, width), heads_shape[1:]
    outs = [jax.ShapeDtypeStruct(shape, FULL if i else LOW) for i, shape in enumerate(kept)]
    outs += [jax.ShapeDtypeStruct(rows, FULL)] * 7 + [jax.ShapeDtypeStruct(heads_bias, FULL)]
    return pl.pallas_call(
        store_kernel,
        grid=(steps,),
        out_shape=outs,
        in_specs=[cut(result.shape) for result in results] + [whole(sums.shape)],
        out_specs=[cut(shape) for shape in kept] + [whole(rows)] * 7 + [whole(heads_bias)],
        compiler_params=pltpu.CompilerParams(vmem_limit_bytes=VMEM_BYTES),
    )(*results, sums)


def ring_local(
    layer_input,
    block_order,
    first_gain,
    first_bias,
    second_gain,
    second_bias,
    heads_weight,
    heads_bias,
    output_weight,
    output_bias,
    expand_weight,
    expand_bias,
    shrink_weight,
    shrink_bias,
    cotangent,
):
    tokens_here = layer_input.shape[1]
    fsdp_count = lax.axis_size("fsdp")
    head_dim = output_weight.shape[1]
    score_scale = head_dim ** (-0.5)
    order_row = block_order[0]
    device_slot = lax.axis_index("fsdp")
    own_block = jnp.sum(
        jnp.where(jnp.arange(fsdp_count, dtype=jnp.int32) == device_slot, order_row, 0)
    )
    offsets = jnp.arange(tokens_here, dtype=jnp.int32)
    query_pos = own_block * tokens_here + offsets
    key_pos = jnp.repeat(order_row, tokens_here) * tokens_here + jnp.tile(offsets, fsdp_count)
    allowed = key_pos[None, :] <= query_pos[:, None]
    cosine, sine_part = rotary_tables(query_pos, ROT)
    hidden_in = layer_input[0].astype(jnp.float32)
    gain_one = first_gain.astype(jnp.float32)
    shift_one = first_bias.astype(jnp.float32)
    gain_two = second_gain.astype(jnp.float32)
    shift_two = second_bias.astype(jnp.float32)
    norm_one_low = layer_norm(hidden_in, gain_one, shift_one).astype(jnp.bfloat16)
    norm_two_low = layer_norm(hidden_in, gain_two, shift_two).astype(jnp.bfloat16)
    heads_full, output_full, expand_full, shrink_full = (
        lax.all_gather(heads_weight, "fsdp", axis=0, tiled=True),
        lax.all_gather(output_weight, "fsdp", axis=2, tiled=True),
        lax.all_gather(expand_weight, "fsdp", axis=0, tiled=True),
        lax.all_gather(shrink_weight, "fsdp", axis=1, tiled=True),
    )
    projected = jnp.einsum(
        "td,dhe->hte", norm_one_low, heads_full, preferred_element_type=jnp.float32
    )
    projected = projected + heads_bias.astype(jnp.float32)[:, None, :]
    query_pre = projected[..., :head_dim]
    key_pre = projected[..., head_dim : 2 * head_dim]
    query_low = rotate(query_pre, cosine, sine_part).astype(jnp.bfloat16)
    key_low = rotate(key_pre, cosine, sine_part).astype(jnp.bfloat16)
    value_low = projected[..., 2 * head_dim :].astype(jnp.bfloat16)
    key_all, value_all = (
        lax.all_gather(key_low, "fsdp", axis=1, tiled=True),
        lax.all_gather(value_low, "fsdp", axis=1, tiled=True),
    )

    def attend_head(operands):
        query_head, key_head, value_head = operands
        probability = softmax_rows(contract_last(query_head, key_head) * score_scale, allowed)
        return jnp.dot(
            probability.astype(jnp.bfloat16), value_head, preferred_element_type=jnp.float32
        )

    context = lax.map(attend_head, (query_low, key_all, value_all))
    context_low = context.astype(jnp.bfloat16)
    expand_in = jnp.dot(
        norm_two_low, expand_full, preferred_element_type=jnp.float32
    ) + expand_bias.astype(jnp.float32)
    activation_low = jax.nn.gelu(expand_in, approximate=False).astype(jnp.bfloat16)
    branch_part = jnp.einsum(
        "hte,hed->td", context_low, output_full, preferred_element_type=jnp.float32
    )
    branch_part = branch_part + jnp.dot(
        activation_low, shrink_full, preferred_element_type=jnp.float32
    )
    branch = lax.psum(branch_part, "tensor")
    layer_output = (
        hidden_in + branch + output_bias.astype(jnp.float32) + shrink_bias.astype(jnp.float32)
    ).astype(jnp.bfloat16)[None]
    heads_back, output_back, expand_back, shrink_back = (
        lax.all_gather(heads_weight, "fsdp", axis=0, tiled=True),
        lax.all_gather(output_weight, "fsdp", axis=2, tiled=True),
        lax.all_gather(expand_weight, "fsdp", axis=0, tiled=True),
        lax.all_gather(shrink_weight, "fsdp", axis=1, tiled=True),
    )
    key_back, value_back = (
        lax.all_gather(key_low, "fsdp", axis=1, tiled=True),
        lax.all_gather(value_low, "fsdp", axis=1, tiled=True),
    )
    grad_out = cotangent[0]
    grad_float = grad_out.astype(jnp.float32)
    output_weight_grad = jnp.einsum(
        "hte,td->hed", context_low, grad_out, preferred_element_type=jnp.float32
    )
    shrink_weight_grad = contract_first(activation_low, grad_out)
    bias_total = jnp.sum(grad_float, 0)
    context_grad = jnp.einsum(
        "td,hed->hte", grad_out, output_back, preferred_element_type=jnp.float32
    ).astype(jnp.bfloat16)
    activation_grad = contract_last(grad_out, shrink_back)
    _, gelu_back = jax.vjp(lambda inner_val: jax.nn.gelu(inner_val, approximate=False), expand_in)
    expand_grad = gelu_back(activation_grad)[0].astype(jnp.bfloat16)
    expand_weight_grad = contract_first(norm_two_low, expand_grad)
    expand_bias_grad = jnp.sum(expand_grad.astype(jnp.float32), 0)
    norm_two_grad = contract_last(expand_grad, expand_back)

    def attend_back(operands):
        query_head, key_head, value_head, context_head = operands
        probability = softmax_rows(contract_last(query_head, key_head) * score_scale, allowed)
        prob_low = probability.astype(jnp.bfloat16)
        weight_grad = contract_last(context_head, value_head)
        row_inner = jnp.sum(probability * weight_grad, -1, keepdims=True)
        score_grad = (probability * (weight_grad - row_inner)).astype(jnp.bfloat16)
        query_grad = jnp.dot(score_grad, key_head, preferred_element_type=jnp.float32) * score_scale
        key_grad = contract_first(score_grad, query_head) * score_scale
        value_grad = contract_first(prob_low, context_head)
        return (query_grad, key_grad, value_grad)

    query_grad, key_grad_all, value_grad_all = lax.map(
        attend_back, (query_low, key_back, value_back, context_grad)
    )
    key_grad, value_grad = (
        lax.psum_scatter(key_grad_all, "fsdp", scatter_dimension=1, tiled=True),
        lax.psum_scatter(value_grad_all, "fsdp", scatter_dimension=1, tiled=True),
    )
    _, rotate_back = jax.vjp(lambda inner_val: rotate(inner_val, cosine, sine_part), query_pre)
    projected_grad = jnp.concatenate(
        [rotate_back(query_grad)[0], rotate_back(key_grad)[0], value_grad], -1
    ).astype(jnp.bfloat16)
    heads_weight_grad = jnp.einsum(
        "td,hte->dhe", norm_one_low, projected_grad, preferred_element_type=jnp.float32
    )
    heads_bias_grad = jnp.sum(projected_grad.astype(jnp.float32), 1)
    norm_one_grad = jnp.einsum(
        "hte,dhe->td", projected_grad, heads_back, preferred_element_type=jnp.float32
    )
    norm_one_grad, norm_two_grad = lax.psum((norm_one_grad, norm_two_grad), "tensor")
    _, first_back = jax.vjp(layer_norm, hidden_in, gain_one, shift_one)
    input_first, first_gain_grad, first_bias_grad = first_back(norm_one_grad)
    _, second_back = jax.vjp(layer_norm, hidden_in, gain_two, shift_two)
    input_second, second_gain_grad, second_bias_grad = second_back(norm_two_grad)
    input_grad = (grad_float + input_first + input_second)[None]
    small_sums = lax.psum(
        (
            first_gain_grad,
            first_bias_grad,
            second_gain_grad,
            second_bias_grad,
            bias_total,
            expand_bias_grad,
            heads_bias_grad,
        ),
        ("replica", "fsdp"),
    )
    shard_parts = (
        lax.psum_scatter(heads_weight_grad, "fsdp", scatter_dimension=0, tiled=True),
        lax.psum_scatter(output_weight_grad, "fsdp", scatter_dimension=2, tiled=True),
        lax.psum_scatter(expand_weight_grad, "fsdp", scatter_dimension=0, tiled=True),
        lax.psum_scatter(shrink_weight_grad, "fsdp", scatter_dimension=1, tiled=True),
    )
    reduced = lax.psum((shard_parts[0], shard_parts[1], shard_parts[2], shard_parts[3]), "replica")
    return (
        layer_output,
        input_grad,
        small_sums[0],
        small_sums[1],
        small_sums[2],
        small_sums[3],
        reduced[0],
        small_sums[6],
        reduced[1],
        small_sums[4],
        reduced[2],
        small_sums[5],
        reduced[3],
        small_sums[4],
    )


def solution(mesh):
    placed = (
        P("replica", "fsdp", None),
        P("replica", None),
        P(),
        P(),
        P(),
        P(),
        P("fsdp", "tensor", None),
        P("tensor", None),
        P("tensor", None, "fsdp"),
        P(),
        P("fsdp", "tensor"),
        P("tensor"),
        P("tensor", "fsdp"),
        P(),
        P("replica", "fsdp", None),
    )
    local = square_local if mesh.shape["fsdp"] == 4 and mesh.shape["replica"] == 2 and mesh.shape["tensor"] == 4 else ring_local
    return jax.shard_map(
        local,
        mesh=mesh,
        in_specs=placed,
        out_specs=(
            P("replica", "fsdp", None),
            P("replica", "fsdp", None),
            P(),
            P(),
            P(),
            P(),
            P("fsdp", "tensor", None),
            P("tensor", None),
            P("tensor", None, "fsdp"),
            P(),
            P("fsdp", "tensor"),
            P("tensor"),
            P("tensor", "fsdp"),
            P(),
        ),
        check_vma=False,
    )
```

```python
import functools
import math

import jax
import jax.numpy as jnp
from jax import lax
from jax.experimental import pallas as pl
from jax.experimental.pallas import tpu as pltpu
from jax.sharding import PartitionSpec as P

ROT = 64


NORM_EPS = 1e-05
MASKED = -1e30


def layer_norm(values_in, gain_vec, shift_vec):
    average = jnp.mean(values_in, -1, keepdims=True)
    centred = values_in - average
    spread_sq = jnp.mean(centred * centred, -1, keepdims=True)
    return centred * lax.rsqrt(spread_sq + NORM_EPS) * gain_vec + shift_vec


def rotate(values_in, cosine, sine_part):
    rot_width = cosine.shape[-1]
    half_width = rot_width // 2
    turning = values_in[..., :rot_width]
    swapped = jnp.concatenate([-turning[..., half_width:], turning[..., :half_width]], -1)
    return jnp.concatenate([turning * cosine + swapped * sine_part, values_in[..., rot_width:]], -1)


def rotary_tables(positions, rot_width):
    frequency = jnp.power(10000.0, -jnp.arange(0, rot_width, 2, dtype=jnp.float32) / rot_width)
    angle_half = positions.astype(jnp.float32)[:, None] * frequency[None, :]
    angles = jnp.concatenate([angle_half, angle_half], -1)
    return (jnp.cos(angles), jnp.sin(angles))


def contract_last(left_op, right_op):
    return lax.dot_general(
        left_op, right_op, (((1,), (1,)), ((), ())), preferred_element_type=jnp.float32
    )


def contract_first(left_op, right_op):
    return lax.dot_general(
        left_op, right_op, (((0,), (0,)), ((), ())), preferred_element_type=jnp.float32
    )


def softmax_rows(scores, allowed):
    masked_scores = jnp.where(allowed, scores, MASKED)
    row_top = jnp.max(masked_scores, -1, keepdims=True)
    exponent = jnp.exp(masked_scores - row_top)
    return exponent / jnp.sum(exponent, -1, keepdims=True)


LOW = jnp.bfloat16
FULL = jnp.float32


MESH = pl.DeviceIdType.MESH
ANY = pl.BlockSpec(memory_space=pl.ANY)
IN_VMEM = pl.BlockSpec(memory_space=pltpu.VMEM)
VMEM_BYTES = 63 * 2**20
COPIES = 157
LOCALS = 34


class Sent:
    def __init__(self, links, k, source, target, peer):
        self.links, self.k, self.source, self.target, self.peer = links, k, source, target, peer

    def copy(self):
        return self.links.copy_at(self.k, self.source, self.target, self.peer)

    def start(self):
        self.copy().start()

    def wait_recv(self):
        self.copy().wait_recv()

    def wait_send(self):
        self.copy().wait_send()


class Links:
    def __init__(self, send_sem, recv_sem, line=0):
        self.send_sem, self.recv_sem, self.sent, self.count = send_sem, recv_sem, [], 0
        self.r, self.f, self.t = (lax.axis_index(name) for name in ("replica", "fsdp", "tensor"))
        self.xb, self.yb = lax.rem(self.f, 2), lax.div(self.f, 2)
        self.x = (self.r, self.f + 1 - 2 * self.xb, self.t)
        self.y = (self.r, lax.rem(self.f + 2, 4), self.t)
        self.core = (1 - self.r, self.f, self.t)
        self.peers = [self.x, self.y, self.core]
        if line:
            self.line = line
            self.left, self.right, self.across = (
                (self.r, self.f, lax.rem(self.t + step, line)) for step in (line - 1, 1, 2)
            )
            self.pair = (self.r, self.f, self.t + 1 - 2 * lax.rem(self.t, 2))
            self.far = (self.r, 3 - self.f, self.t)
            self.mirror = (self.r, self.f, line - 1 - self.t)
            self.peers += [self.far, self.left, self.right, self.across]

    def meet(self):
        barrier = pltpu.get_barrier_semaphore()
        for peer in self.peers:
            pl.semaphore_signal(barrier, inc=1, device_id=peer, device_id_type=MESH)
        pl.semaphore_wait(barrier, len(self.peers))

    def prepare(self, source, target, peer):
        self.count += 1
        return Sent(self, self.count - 1, source, target, peer)

    def send(self, source, target, peer):
        copy = self.prepare(source, target, peer)
        copy.start()
        self.sent.append(copy)
        return copy

    def series(self, count):
        k = self.count
        self.count += count
        return k

    def copy_at(self, k, source, target, peer):
        return pltpu.make_async_remote_copy(
            src_ref=source,
            dst_ref=target,
            send_sem=self.send_sem.at[k],
            recv_sem=self.recv_sem.at[k],
            device_id=peer,
            device_id_type=MESH,
        )

    def sent_out(self, copy):
        copy.wait_send()
        self.sent = [other for other in self.sent if other is not copy]

    def end(self):
        for copy in self.sent:
            copy.wait_send()

    def block(self, i):
        place = 0
        for size, bit in ((4, self.yb), (2, self.xb), (1, self.r)):
            mine = lax.rem(lax.div(i, size), 2) if isinstance(i, jax.Array) else i // size % 2
            place = place + size * (mine + bit - 2 * mine * bit)
        return place


class Local:
    def __init__(self, sem):
        self.sem, self.count, self.open, self.free = sem, 0, [], []

    def start(self, source, target):
        if not self.free:
            self.free.append(self.count)
            self.count += 1
        k = self.free.pop(0)
        copy = pltpu.make_async_copy(source, target, self.sem.at[k])
        copy.start()
        self.open.append((copy, k))
        return copy

    def wait(self, *copies):
        for copy in copies:
            copy.wait()
            self.free += [k for other, k in self.open if other is copy]
            self.open = [pair for pair in self.open if pair[0] is not copy]

    def end(self):
        self.wait(*[copy for copy, _ in self.open])


def at_rows(ref, start, size):
    return ref.at[pl.ds(start, size), :]


def at_columns(ref, start, size):
    return ref.at[:, pl.ds(start, size)]


class Gathered:
    def __init__(self, links, local, shard, full, cut, unit, copied=True):
        self.links, self.local, self.full, self.cut = links, local, full, cut
        self.shard, self.unit, self.half = shard, unit, unit // 2
        self.starts = [pl.multiple_of(links.r * unit + start, self.half) for start in (0, self.half)]
        self.bases = [pl.multiple_of(base * unit, unit) for base in (links.r, 1 - links.r)]
        self.copies = [local.start(self.here(i), self.at(i)) for i in range(2)] if copied else []
        self.from_x, self.from_y = {}, {}

    def here(self, i):
        return self.cut(self.shard, self.bases[i], self.unit)

    def mine(self, lower):
        return self.cut(self.shard, self.starts[lower], self.half)

    def at(self, block, start=0, size=None):
        return self.cut(self.full, block * self.unit + start, self.unit if size is None else size)

    def to_x(self, lower):
        source, target = self.mine(lower), self.at(2, self.half * lower, self.half)
        self.from_x[lower] = self.links.send(source, target, self.links.x)

    def to_y(self, lower):
        source, target = self.mine(lower), self.at(4, self.half * lower, self.half)
        self.from_y[lower] = self.links.send(source, target, self.links.y)

    def first(self):
        self.to_x(False)
        self.to_y(True)

    def rest(self):
        self.to_x(True)
        self.to_y(False)

    def pass_y(self):
        half = self.half
        self.from_x[False].wait_recv()
        self.far_top = self.links.send(self.at(2, 0, half), self.at(6, 0, half), self.links.y)

    def pass_x(self):
        half = self.half
        self.from_y[True].wait_recv()
        self.far_end = self.links.send(self.at(4, half, half), self.at(6, half, half), self.links.x)

    def relay(self):
        self.pass_y()
        self.pass_x()

    def share(self):
        self.from_y[False].wait_recv()
        self.core_y = self.links.send(self.at(4), self.at(5), self.links.core)
        self.from_x[True].wait_recv()
        self.core_x = self.links.send(self.at(2), self.at(3), self.links.core)

    def share_far(self):
        self.far_top.wait_recv()
        self.far_end.wait_recv()
        self.core_far = self.links.send(self.at(6), self.at(7), self.links.core)

    def passed(self):
        for copy in (self.far_top, self.far_end, self.core_x, self.core_y, self.core_far):
            self.links.sent_out(copy)

    def whole(self):
        self.local.wait(*self.copies)
        for copy in (self.core_x, self.core_y, self.core_far):
            copy.wait_recv()


def odd(j):
    return j % 2 if isinstance(j, int) else lax.rem(j, 2)


def tile_of(j, size):
    return pl.ds(pl.multiple_of(j * size, size), size)


def dot(left, right):
    return jnp.dot(left, right, preferred_element_type=FULL)


def spin(values_in, cosine, sine):
    head = values_in[:, :128]
    lane = lax.broadcasted_iota(jnp.int32, head.shape, 1)
    swapped = jnp.where(lane < ROT // 2, pltpu.roll(head, 96, 1), pltpu.roll(head, 32, 1))
    return jnp.concatenate([head * cosine + swapped * sine, values_in[:, 128:]], -1)


class Scattered:
    def __init__(self, links, local, blocks, cut, unit, via, got, stage=None, own=None):
        self.links, self.local, self.blocks, self.cut, self.unit = links, local, blocks, cut, unit
        self.via, self.got = [via.at[n] for n in range(2)], [got.at[n] for n in range(2)]
        self.stage, self.own = stage, own
        self.half, self.loads = unit // 2, []

    def load(self):
        self.loads = [
            self.local.start(self.cut(self.blocks[1], self.half, self.half), self.stage[0]),
            self.local.start(self.cut(self.blocks[2], 0, self.half), self.stage[1]),
            self.local.start(self.blocks[0], self.own),
        ]

    def first(self):
        half, cut, far = self.half, self.cut, self.blocks[3]
        self.via_x = self.links.send(cut(far, 0, half), self.via[0], self.links.x)
        self.via_y = self.links.send(cut(far, half, half), self.via[1], self.links.y)

    def direct(self):
        half, cut = self.half, self.cut
        self.x_top = self.links.send(cut(self.blocks[1], 0, half), cut(self.got[0], 0, half), self.links.x)
        self.y_end = self.links.send(cut(self.blocks[2], half, half), cut(self.got[1], half, half), self.links.y)

    def second(self):
        half, cut = self.half, self.cut
        self.local.wait(*self.loads[:2])
        self.via_x.wait_recv()
        add_rows(self.stage[1], self.stage[1], self.via[0])
        self.y_top = self.links.send(self.stage[1], cut(self.got[1], 0, half), self.links.y)
        self.via_y.wait_recv()
        add_rows(self.stage[0], self.stage[0], self.via[1])
        self.x_end = self.links.send(self.stage[0], cut(self.got[0], half, half), self.links.x)

    def third(self, slots, place, step, between=lambda: None):
        for copy in (self.x_top, self.x_end, self.y_top, self.y_end):
            copy.wait_recv()
        if self.loads:
            self.local.wait(self.loads[2])
        self.other = []
        for start in range(0, self.own.shape[0], step):
            between()
            rows = pl.ds(start, step)
            at, total = slots.take()
            add_rows(total, self.own.at[rows, :], self.got[0].at[rows, :], self.got[1].at[rows, :])
            kept = self.local.start(total, place.at[rows, :])
            other = self.links.send(total, place.at[rows, :], self.links.core)
            self.other.append(other)

            def done(kept=kept, other=other):
                self.local.wait(kept)
                self.links.sent_out(other)

            slots.busy[at] = done


def add_rows(target, *parts):
    rows, wide = target.shape
    step = min(rows, 32 if wide > 512 else 256)

    def one(c, carry):
        at = pl.ds(pl.multiple_of(c * step, step), step)
        total = parts[0][at, :].astype(FULL)
        for part in parts[1:]:
            total = total + part[at, :].astype(FULL)
        target[at, :] = total.astype(target.dtype)
        return carry

    lax.fori_loop(0, rows // step, one, 0)


class Line:
    def __init__(self, links, part, got, final, chunks, cut, finish):
        self.links, self.part, self.got, self.final, self.cut, self.finish = links, part, got, final, cut, finish
        self.chunks = chunks
        self.outer = jnp.logical_or(links.t == 0, links.t == links.line - 1)
        self.middle = jnp.logical_not(self.outer)
        self.inward = [self.make(c, part, final, links.pair) for c in range(chunks)]
        self.across = [self.make(c, part, got, links.mirror) for c in range(chunks)]
        self.outward = [
            Sent(links, self.inward[c].k, cut(final, c), cut(final, c), links.pair) for c in range(chunks)
        ]

    def make(self, c, source, target, peer):
        return self.links.prepare(self.cut(source, c), self.cut(target, c), peer)

    def start(self, *chunks):
        @pl.when(self.outer)
        def _():
            for c in chunks:
                self.inward[c].start()

    def first(self, c):
        @pl.when(self.middle)
        def _():
            self.inward[c].wait_recv()
            part = self.cut(self.part, c)
            add_rows(part, part, self.cut(self.final, c))
            self.across[c].start()

    def second(self, c):
        @pl.when(self.middle)
        def _():
            self.across[c].wait_recv()
            self.finish(c)
            self.outward[c].start()

    def third(self, c):
        @pl.when(self.outer)
        def _():
            self.outward[c].wait_recv()

    def end(self):
        @pl.when(self.outer)
        def _():
            for copy in self.inward:
                copy.wait_send()

        @pl.when(self.middle)
        def _():
            for copy in self.across + self.outward:
                copy.wait_send()


class Slots:
    def __init__(self, *refs):
        self.refs, self.busy, self.count = refs, {}, 0

    def take(self):
        at = self.count % len(self.refs)
        self.count += 1
        if at in self.busy:
            self.busy.pop(at)()
        return at, self.refs[at]

    def end(self):
        for wait in self.busy.values():
            wait()
        self.busy = {}


def block_kernel(
    score_scale, line_size,
    x_hbm, g_hbm, wh_hbm, wo_hbm, we_own, ws_own, gain_one, shift_one, gain_two, shift_two, units_bias, heads_bias,
    bias_one, bias_two, order,
    layer_out, input_grad, heads_grad, output_grad, expand_grad, shrink_grad, we, ws, n2t_hbm, got_core_s, got_core_o,
    got_core_h, got_core_e, red_s, red_o, red_h, sums_out,
    x, g, up, n1, nt, stat, wh, wo, qkv, dctx, ctxt, pg, kvg_got, got_branch, final_branch, got_up, final_up,
    via_h, got_h, via_o, got_o, via_s, got_s, via_e, got_e, raw, vecs, sums, sums_got, sums_low, gains, gains_got,
    loop_sem, block_sem, local_sem, send_sem, recv_sem,
):
    links, local = Links(send_sem, recv_sem, line_size), Local(local_sem)
    tokens, width = x.shape
    units, heads_wide, out_wide = we.shape[1], wh.shape[1], wo.shape[0]
    hd = dctx.shape[1]
    unit = width // 8
    blocks = range(8)
    room_s = qkv
    place = [pl.ds(pl.multiple_of(links.block(i) * unit, unit), unit) for i in blocks]

    def here(i):
        return pl.ds(i * unit, unit)

    rest_rows = pl.ds(2 * unit, width - 2 * unit)

    def tile(j):
        return pl.ds(j * unit if isinstance(j, int) else pl.multiple_of(j * unit, unit), unit)

    def placed(i):
        return pl.ds(pl.multiple_of(links.block(i) * unit, unit), unit)

    def stream(start, end, load, body):
        def copies(j):
            pairs = load(j, odd(j))
            return [pltpu.make_async_copy(*pair, loop_sem.at[n, odd(j)]) for n, pair in enumerate(pairs)]

        for copy in copies(start):
            copy.start()

        def one(j, carry):
            @pl.when(j + 1 < end)
            def _():
                for copy in copies(j + 1):
                    copy.start()

            for copy in copies(j):
                copy.wait()
            body(j, odd(j))
            return carry

        lax.fori_loop(start, end, one, 0)

    links.meet()
    heads_in = Gathered(links, local, wh_hbm, wh, at_rows, unit)
    heads_in.first()
    heads_in.rest()
    x_in, g_in = [], []
    for i in blocks:
        cols = pl.ds(pl.multiple_of(links.block(i) * unit, unit), unit)
        x_in.append(local.start(x_hbm.at[:, cols], x.at[:, pl.ds(i * unit, unit)]))
        g_in.append(local.start(g_hbm.at[:, cols], g.at[:, pl.ds(i * unit, unit)]))
    output_in = Gathered(links, local, wo_hbm, wo, at_columns, unit)
    expand = Gathered(links, local, we_own, we, at_rows, unit)
    weight = Gathered(links, local, ws_own, ws, at_columns, unit, False)

    def row(ref):
        return ref[...].astype(FULL).reshape(1, -1)

    for i, vec in enumerate((gain_one, shift_one, gain_two, shift_two, units_bias)):
        raw[i : i + 1, :] = row(vec)
    raw[6:7, :] = row(bias_one) + row(bias_two)
    head_rows = heads_bias[...].astype(FULL)
    raw[5:6, : 3 * hd], raw[7:8, : 3 * hd] = head_rows[0:1, :], head_rows[1:2, :]

    turns = (3, 1, 2, 0)

    def turn_of(n):
        return jnp.where(n == 0, 3, jnp.where(n == 3, 0, n))

    class Reduced:
        def __init__(self, room, got, block):
            self.room, self.got, self.block = room, got, block
            self.gots = [got.at[k] for k in range(4)]

        def to_core(self):
            first = links.series(4)

            def one(n, carry):
                k = turn_of(n)
                self.block(2 * k + 1, self.room(n), False)
                links.copy_at(first + n, self.room(n), self.got.at[k], links.core).start()
                return carry

            lax.fori_loop(0, 4, one, 0)
            self.copies = [Sent(links, first + n, self.room(n), self.gots[turns[n]], links.core) for n in range(4)]

        def fetch(self):
            for n in range(4):
                self.copies[n].wait_send()
                self.copies[n].wait_recv()
                pltpu.make_async_copy(self.got.at[turns[n]], self.room(n), block_sem.at[n]).start()

        def add(self, red):
            def one(n, carry):
                k = turn_of(n)
                pltpu.make_async_copy(self.got.at[k], self.room(n), block_sem.at[n]).wait()
                self.block(2 * k, self.room(n), True)
                if red is not None:
                    pltpu.make_async_copy(self.room(n), red.at[k], block_sem.at[4 + n]).start()
                return carry

            lax.fori_loop(0, 4, one, 0)
            if red is not None:
                for n in range(4):
                    pltpu.make_async_copy(self.room(n), red.at[turns[n]], block_sem.at[4 + n]).wait()

    def product(left, right, ref, add):
        part = dot(left, right)
        if add:
            part = part + ref[...].astype(FULL)
        ref[...] = part.astype(LOW)

    def heads_block(i, ref, add):
        product(nt[tile(i), :], pg[...], ref, add)

    heads_sum = Reduced(lambda n: wh.at[tile(n), :], got_core_h, heads_block)
    own_h = at_rows(wh, 4 * unit, unit)
    stage_h = (at_rows(wh, 5 * unit, unit // 2), at_rows(wh, 5 * unit + unit // 2, unit // 2))
    heads = Scattered(links, local, [red_h.at[k] for k in range(4)], at_rows, unit, via_h, got_h, stage_h, own_h)
    shrink = Scattered(links, local, [red_s.at[k] for k in range(4)], at_columns, unit, via_s, got_s)
    output = Scattered(links, local, [red_o.at[k] for k in range(4)], at_columns, unit, via_o, got_o)

    def up_part(i, grad, first):
        cols, spot = tile(i), placed(i)
        normal = (x[:, cols].astype(FULL) - stat[:, 0:1]) * stat[:, 128:129]
        row = 0 if first else 2
        sums[0, row : row + 1, spot] = jnp.sum(grad * normal, 0, keepdims=True)
        sums[0, row + 1 : row + 2, spot] = jnp.sum(grad, 0, keepdims=True)
        scaled = grad * (vecs[0:1, cols] if first else vecs[2:3, cols])
        n1[:, cols] = (scaled if first else n1[:, cols].astype(FULL) + scaled).astype(LOW)

    def attend(qkv_away, dctx_away, ctxt_all, pgq, pg_away, kvg_away, cosine, sines, dk, dv, stage):
        for i in blocks:
            cols = pl.ds(pl.multiple_of(links.block(i) * unit, unit), unit)
            vecs[0:4, i * unit : (i + 1) * unit] = raw[0:4, cols]
            vecs[4:5, i * unit : (i + 1) * unit] = raw[6:7, cols]
        local.wait(*x_in)

        def norm_rows(c, carry):
            rows = tile_of(c, 64)
            value = x[rows, :].astype(FULL)
            average = jnp.mean(value, -1, keepdims=True)
            centred = value - average
            inverse = lax.rsqrt(jnp.mean(centred * centred, -1, keepdims=True) + NORM_EPS)
            normal = centred * inverse
            both = [jnp.broadcast_to(part, (64, 128)) for part in (average, inverse)]
            stat[rows, :] = jnp.concatenate(both, -1)
            n1[rows, :] = (normal * vecs[0:1, :] + vecs[1:2, :]).astype(LOW)
            up[rows, :] = (normal * vecs[2:3, :] + vecs[3:4, :]).astype(LOW)
            return carry

        lax.fori_loop(0, tokens // 64, norm_rows, 0)
        bases = [
            order[0, (links.yb if step < 2 else 1 - links.yb) * 2 + (links.xb if step % 2 == 0 else 1 - links.xb)]
            * tokens
            for step in (0, 2, 1, 3)
        ]

        def table_rows(c, carry):
            rows = tile_of(c, 64)
            lane = lax.broadcasted_iota(jnp.int32, (64, 128), 1)
            row = lax.broadcasted_iota(jnp.int32, (64, 128), 0) + c * 64
            spot = row + jnp.where(row < tokens, bases[0], bases[1] - tokens)
            pace = jnp.exp(lax.rem(lane, ROT // 2).astype(FULL) * (-2.0 / ROT * math.log(10000.0)))
            angle = spot.astype(FULL) * pace
            sine = jnp.sin(angle)
            cosine[rows, :] = jnp.where(lane < ROT, jnp.cos(angle), 1.0)
            sines[rows, :] = jnp.where(lane < ROT // 2, -sine, jnp.where(lane < ROT, sine, 0.0))
            return carry

        lax.fori_loop(0, 2 * tokens // 64, table_rows, 0)
        heads_in.relay()
        output_in.first()
        output_in.rest()

        def turned_copy(j):
            slot = odd(j)
            return pltpu.make_async_copy(stage.at[slot], n2t_hbm.at[tile_of(j, unit), :], loop_sem.at[0, slot])

        def turn_tiles(j, carry):
            cols = tile_of(j, unit)
            nt[cols, :] = n1[:, cols].T

            @pl.when(j >= 2)
            def _():
                turned_copy(j - 2).wait()

            stage[odd(j), :, :] = up[:, cols].T
            turned_copy(j).start()
            return carry

        lax.fori_loop(0, 8, turn_tiles, 0)
        for j in (6, 7):
            turned_copy(j).wait()
        sums[0, :, :] = jnp.zeros(sums.shape[1:], FULL)
        local.wait(*g_in)
        for i in blocks:
            cols = pl.ds(pl.multiple_of(links.block(i) * unit, unit), unit)
            sums[0, 4:5, cols] = jnp.sum(g[:, i * unit : (i + 1) * unit].astype(FULL), 0, keepdims=True)
        heads_in.share()
        heads_in.share_far()
        heads_in.whole()
        output_in.relay()

        own = links.yb * 3 * hd

        def project(c, head, target):
            cols = pl.ds(pl.multiple_of(head * 3 * hd + c * hd, hd), hd)
            bias = jnp.where(head == 0, raw[5:6, c * hd : (c + 1) * hd], raw[7:8, c * hd : (c + 1) * hd])
            value = dot(n1[...], wh[:, cols]) + bias
            if c < 2:
                value = spin(value, cosine[:tokens, :], sines[:tokens, :])
            target[c, :tokens, :] = value.astype(LOW)

        def place_of(c, part):
            return qkv.at[c, pl.ds(part * tokens, tokens), :]

        from_y, from_x, from_far = {}, {}, {}
        for c in (1, 2):
            project(c, links.yb, qkv)
            from_x[c] = links.send(place_of(c, 0), place_of(c, 2), links.x)
        for c in (1, 2, 0):
            project(c, 1 - links.yb, qkv_away)
            from_y[c] = links.send(qkv_away.at[c], place_of(c, 1), links.y)
        from_y[1].wait_recv()
        from_far[1] = links.send(place_of(1, 1), place_of(1, 3), links.x)
        project(0, links.yb, qkv)
        output_in.share()
        output_in.share_far()
        from_y[2].wait_recv()
        from_far[2] = links.send(place_of(2, 1), place_of(2, 3), links.x)
        output_in.whole()
        rows_own = pl.ds(pl.multiple_of(links.yb * hd, hd), hd)
        rows_away = pl.ds(pl.multiple_of((1 - links.yb) * hd, hd), hd)
        dctx_away[...] = contract_last(g[...], wo[rows_away, :]).astype(LOW)
        dctx_from_y = links.send(dctx_away, dctx.at[pl.ds(tokens, tokens), :], links.y)
        dctx[:tokens, :] = contract_last(g[...], wo[rows_own, :]).astype(LOW)
        expand.first()
        expand.to_y(False)
        for copy in (from_y[0], dctx_from_y, *from_x.values(), *from_far.values()):
            copy.wait_recv()

        def attention(kt, vt, prob, wgt, prob_low, grad_low):
            keys = qkv.shape[1]
            step = tokens
            lag = lax.broadcasted_iota(jnp.int32, (step, hd), 0) - lax.broadcasted_iota(jnp.int32, (step, hd), 1)
            parts = [pl.ds(i * step, step) for i in range(keys // step)]
            for part in parts:
                kt[:, part] = qkv[1, part, :].T
                vt[:, part] = qkv[2, part, :].T
            dk[...] = jnp.zeros_like(dk)
            dv[...] = jnp.zeros_like(dv)

            def one(b, carry):
                rows = tile_of(b, hd)
                query, grad = qkv[0, rows, :], dctx[rows, :]
                ahead = jnp.where(b < tokens // hd, bases[0], bases[1] - tokens) + b * hd
                top = jnp.full((1, hd), MASKED, FULL)
                for i, part in enumerate(parts):
                    scores = contract_last(qkv[1, part, :], query) * score_scale
                    scores = jnp.where(lag <= ahead - bases[i], scores, MASKED)
                    prob[part, :] = scores
                    top = jnp.maximum(top, jnp.max(scores, 0, keepdims=True))
                total = jnp.zeros((1, hd), FULL)
                for part in parts:
                    exponent = jnp.exp(prob[part, :] - top)
                    prob[part, :] = exponent
                    total = total + jnp.sum(exponent, 0, keepdims=True)
                share = 1.0 / total
                inner = jnp.zeros((1, hd), FULL)
                for part in parts:
                    weight = contract_last(qkv[2, part, :], grad)
                    chance = prob[part, :] * share
                    prob[part, :] = chance
                    prob_low[part, :] = chance.astype(LOW)
                    wgt[part, :] = weight
                    inner = inner + jnp.sum(chance * weight, 0, keepdims=True)
                for part in parts:
                    grad_low[part, :] = (prob[part, :] * (wgt[part, :] - inner)).astype(LOW)
                ctxt_all[:, rows] = dot(vt[...], prob_low[...]).astype(LOW)
                query_grad = dot(kt[...], grad_low[...]) * score_scale
                for part in parts:
                    dv[part, :] += dot(prob_low[part, :], grad)
                    dk[part, :] += dot(grad_low[part, :], query)
                turned_grad = spin(query_grad.T, cosine[rows, :], -sines[rows, :])
                pgq[rows, :] = turned_grad.astype(LOW)
                return carry

            lax.fori_loop(0, 2 * tokens // hd, one, 0)
            ctxt[rows_own, :] = ctxt_all[:, :tokens]
            pg[:, pl.ds(pl.multiple_of(own, hd), hd)] = pgq[:tokens, :]
            for i, total in enumerate((dk, dv)):
                kvg_away[i, :, :] = total[2 * tokens :, :].astype(LOW)

        keys = qkv.shape[1]
        pl.run_scoped(
            attention,
            pltpu.VMEM((hd, keys), LOW),
            pltpu.VMEM((hd, keys), LOW),
            pltpu.VMEM((keys, hd), FULL),
            pltpu.VMEM((keys, hd), FULL),
            pltpu.VMEM((keys, hd), LOW),
            pltpu.VMEM((keys, hd), LOW),
        )

        def head_columns(ref, start, i):
            return ref.at[:, pl.ds(pl.multiple_of(start + i * hd, hd), hd)]

        def send_grad(i):
            source = pgq.at[pl.ds(tokens, tokens), :] if i == 0 else head_columns(pg_away, 0, i - 1)
            return links.send(source, head_columns(pg, own, i), links.y)

        kvg_from_x = {i: links.send(kvg_away.at[i], kvg_got.at[i], links.x) for i in (1, 0)}
        pg_from_y = [send_grad(0)]
        ctx_from_y = links.send(ctxt_all.at[:, pl.ds(tokens, tokens)], ctxt.at[rows_own, :], links.y)
        expand.pass_x()
        expand.to_x(True)

        for i in (1, 0):
            kvg_from_x[i].wait_recv()
            for away_rows, target in ((True, pg_away), (False, pg)):
                rows = pl.ds(tokens if away_rows else 0, tokens)
                total = (dk, dv)[i][rows, :] + kvg_got[i, rows, :].astype(FULL)
                if i == 0:
                    total = spin(total * score_scale, cosine[rows, :], -sines[rows, :])
                head_columns(target, 0 if away_rows else own, i if away_rows else 1 + i)[...] = total.astype(LOW)
                if away_rows:
                    pg_from_y.append(send_grad(1 + i))
        expand.pass_y()
        weight.first()
        weight.rest()
        ctx_from_y.wait_recv()
        for copy in pg_from_y:
            copy.wait_recv()

        def first_block(i, carry):
            up_part(i, contract_last(pg[...], wh[tile(i), :]), True)
            return carry

        lax.fori_loop(0, 8, first_block, 0)
        sums[0, 6:7, :heads_wide] = jnp.sum(pg[...].astype(FULL), 0, keepdims=True)
        heads_in.passed()
        heads_sum.to_core()
        expand.share()
        expand.share_far()
        expand.whole()
        for copy in (*from_y.values(), *from_x.values(), *from_far.values(), dctx_from_y, *kvg_from_x.values(), *pg_from_y, ctx_from_y):
            links.sent_out(copy)

    low, full = (functools.partial(lambda kind, *shape: pltpu.VMEM(shape, kind), kind) for kind in (LOW, FULL))
    pl.run_scoped(
        attend,
        low(3, tokens, hd),
        low(tokens, hd),
        low(hd, 2 * tokens),
        low(2 * tokens, hd),
        low(tokens, 2 * hd),
        low(2, 2 * tokens, hd),
        full(2 * tokens, 128),
        full(2 * tokens, 128),
        full(4 * tokens, hd),
        full(4 * tokens, hd),
        low(2, unit, tokens),
    )

    def update(act, actt, slope, ctx, room_o, stage_o, own_o, room_e, total_rows, total_columns, grad_rows):
        def forward(j, slot):
            cols = tile(j)
            value = dot(up[...], room_s[slot]) + raw[4:5, cols]
            normal_share = 0.5 * (1.0 + lax.erf(value * (0.5**0.5)))
            low_act = (value * normal_share).astype(LOW)
            act[:, cols] = low_act
            actt[cols, :] = low_act.T
            density = jnp.exp(value * value * -0.5) * 0.3989422804014327
            slope[:, cols] = (normal_share + value * density).astype(LOW)

        stream(0, 8, lambda j, slot: [(we.at[:, tile(j)], room_s.at[slot])], forward)
        weight.relay()
        ctx[...] = ctxt[...].T

        rows_out = grad_rows.shape[1]

        def columns_cut(ref, c):
            return ref.at[:, here(c)]

        def rows_cut(ref, c):
            return ref.at[pl.ds(c * rows_out, rows_out), :]

        def finish_branch(c):
            cols = here(c)

            def one(part, carry):
                at = tile_of(part, 128)
                total = up[at, cols].astype(FULL) + got_branch[at, cols].astype(FULL)
                final_branch[at, cols] = (x[at, cols].astype(FULL) + total + vecs[4:5, cols]).astype(LOW)
                return carry

            lax.fori_loop(0, tokens // 128, one, 0)

        def finish_up(c):
            add_rows(rows_cut(final_up, c), rows_cut(n1, c), rows_cut(got_up, c))

        line_branch = Line(links, up, got_branch, final_branch, 8, columns_cut, finish_branch)
        line_up = Line(links, n1, got_up, final_up, tokens // rows_out, rows_cut, finish_up)

        def branch_blocks(chunks, block, source):
            def one(n, slot):
                cols = tile(block(n))
                up[:, cols] = (dot(ctx[...], wo[:, cols]) + dot(act[...], room_s[slot])).astype(LOW)
                for at, chunk in enumerate(chunks):
                    pl.when(n == at)(functools.partial(line_branch.start, chunk))

            stream(0, len(chunks), lambda n, slot: [(source(n), room_s.at[slot])], one)

        steps = [(line_branch, c) for c in (0, 1, 2, 4, 3, 5, 6, 7)] + [(line_up, c) for c in range(line_up.chunks)]
        out_copies = []

        def input_rows(c):
            slot = len(out_copies) % 2
            if len(out_copies) >= 2:
                local.wait(*out_copies[-2])
            rows = pl.ds(c * rows_out, rows_out)
            value = x[rows, :].astype(FULL)
            centred = value - jnp.mean(value, -1, keepdims=True)
            scale = lax.rsqrt(jnp.mean(centred * centred, -1, keepdims=True) + NORM_EPS)
            normal = centred * scale
            upstream = final_up[rows, :].astype(FULL)
            inner = upstream - jnp.mean(upstream, -1, keepdims=True)
            inner = inner - normal * jnp.mean(upstream * normal, -1, keepdims=True)
            grad_rows[slot, :, :] = (g[rows, :].astype(FULL) + inner * scale).astype(LOW)
            out_copies.append(
                [local.start(grad_rows.at[slot, :, here(i)], input_grad.at[rows, place[i]]) for i in blocks]
            )

        def serve(count):
            for _ in range(count):
                at = serve.done
                if at < len(steps):
                    steps[at][0].first(steps[at][1])
                if 2 <= at < len(steps) + 2:
                    steps[at - 2][0].second(steps[at - 2][1])
                if at >= 4:
                    line, c = steps[at - 4]
                    line.third(c)
                    if line is line_up:
                        input_rows(c)
                    else:
                        local.start(final_branch.at[:, here(c)], layer_out.at[:, place[c]])
                serve.done += 1

        serve.done = 0
        branch_blocks((0, 1), lambda n: n, lambda n: at_columns(ws_own, pl.multiple_of((links.r + n - 2 * links.r * n) * unit, unit), unit))

        def shrink_block(i, ref, add):
            product(actt[...], g[:, tile(i)], ref, add)

        def output_block(i, ref, add):
            product(ctxt[...], g[:, tile(i)], ref, add)

        def expand_block(i, ref, add):
            product(nt[tile(i), :], slope[...], ref, add)

        shrink.stage = (actt.at[:, pl.ds(unit, unit // 2)], actt.at[:, pl.ds(unit + unit // 2, unit // 2)])
        shrink.own = actt.at[:, pl.ds(0, unit)]
        output.stage, output.own = (stage_o.at[0], stage_o.at[1]), own_o
        shrink_sum = Reduced(lambda n: room_s.at[n], got_core_s, shrink_block)
        output_sum = Reduced(lambda n: room_o.at[n], got_core_o, output_block)
        expand_sum = Reduced(lambda n: room_e.at[n], got_core_e, expand_block)
        heads_sum.fetch()
        heads_sum.add(red_h)
        heads.first()
        heads.direct()
        heads.load()
        n2t_load = local.start(n2t_hbm, nt)
        weight.share()
        serve(1)
        weight.core_y.wait_recv()
        weight.core_x.wait_recv()
        ahead = lambda n: 2 * n + 2 - 3 * (n // 2 if isinstance(n, int) else lax.div(n, 2))
        branch_blocks((2, 4, 3, 5), ahead, lambda n: ws.at[:, tile(ahead(n))])
        serve(1)
        shrink_sum.to_core()
        weight.share_far()
        serve(1)
        shrink_sum.fetch()
        shrink_sum.add(red_s)
        shrink.first()
        shrink.direct()
        shrink.load()
        serve(1)
        weight.core_far.wait_recv()
        branch_blocks((6, 7), lambda n: n + 6, lambda n: ws.at[:, tile(n + 6)])
        serve(1)

        def hidden_tile(j, slot):
            cols = tile(j)
            grad = (contract_last(g[...], room_e[slot]) * slope[:, cols].astype(FULL)).astype(LOW)
            slope[:, cols] = grad
            sums[0, 5:6, cols] = jnp.sum(grad.astype(FULL), 0, keepdims=True)

        def shrink_rows(j, slot):
            rows = tile(j)
            pairs = [(weight.here(i).at[rows, :], room_e.at[slot, :, here(i)]) for i in range(2)]
            return pairs + [(ws.at[rows, rest_rows], room_e.at[slot, :, rest_rows])]

        stream(0, 4, shrink_rows, hidden_tile)
        serve(1)
        stream(4, 8, shrink_rows, hidden_tile)
        serve(1)

        def second_block(i, slot):
            up_part(i, contract_last(slope[...], room_e[slot]), False)

        expand_rows = lambda i, slot: [(we.at[tile(i), :], room_e.at[slot])]
        stream(0, 4, expand_rows, second_block)
        serve(1)
        stream(4, 8, expand_rows, second_block)
        line_up.start(*range(line_up.chunks))

        def share(s, peers):
            return [links.send(sums.at[s], sums_got.at[4 * s + k], peer) for k, peer in enumerate(peers)]

        def shared(s, copies):
            for copy in copies:
                copy.wait_recv()
            total = sums[s, :, :] + sums_got[4 * s, :, :]
            if len(copies) > 1:
                total = total + (sums_got[4 * s + 1, :, :] + sums_got[4 * s + 2, :, :])
            sums[s + 1, :, :] = total

        def share_line(s, peer):
            return links.send(gains.at[s], gains_got.at[s], peer)

        def shared_line(s, copy):
            copy.wait_recv()
            gains[s + 1, :, :] = gains[s, :, :] + gains_got[s, :, :]

        first_share = share(0, [links.core])
        output_sum.to_core()
        shared(0, first_share)
        halves = [sums[1, :, side * (width // 2) : (side + 1) * (width // 2)] for side in range(2)]
        sums_low[0, :, :] = jnp.concatenate(halves, 0).astype(LOW)
        second_share = [
            links.send(sums_low.at[0], sums_low.at[1 + k], peer)
            for k, peer in enumerate((links.x, links.y, links.far))
        ]
        output_sum.fetch()
        output_sum.add(red_o)
        output.first()
        output.direct()
        output.load()

        local.wait(n2t_load)
        expand_sum.to_core()
        serve(1)
        shrink.second()
        serve(1)
        expand_sum.fetch()
        serve(1)
        expand_sum.add(None)
        red = {k: room_e.at[turns.index(k)] for k in range(4)}
        expand = Scattered(links, local, [red[k] for k in range(4)], at_rows, unit, via_e, got_e, None, red[0])
        expand.first()
        expand.direct()
        serve(2)
        half_rows = pl.ds(pl.multiple_of(links.r * unit, unit), unit)
        column_slots = Slots(*[total_columns.at[n] for n in range(4)])
        serve(2)
        shrink.third(column_slots, shrink_grad.at[:, half_rows], total_columns.shape[1])
        serve(1)
        for copy in second_share:
            copy.wait_recv()
        parts = [sums_low[k, :, :].astype(FULL) for k in range(4)]
        total = (parts[0] + parts[1]) + (parts[2] + parts[3])
        for side in range(2):
            sums[2, :, side * (width // 2) : (side + 1) * (width // 2)] = total[8 * side : 8 * side + 8, :]
        for row in range(4):
            for side in range(2):
                at = 2 * row + side
                gains[0, at : at + 1, :] = sums[2, row : row + 1, side * (width // 2) : (side + 1) * (width // 2)]
        pair_share = share_line(0, links.pair)
        serve(3)

        expand.via_x.wait_recv()
        top, end = red[2].at[pl.ds(0, unit // 2), :], red[1].at[pl.ds(unit // 2, unit // 2), :]
        add_rows(top, top, via_e.at[0])
        expand.y_top = links.send(top, got_e.at[1, pl.ds(0, unit // 2), :], links.y)
        expand.via_y.wait_recv()
        add_rows(end, end, via_e.at[1])
        expand.x_end = links.send(end, got_e.at[0, pl.ds(unit // 2, unit // 2), :], links.x)
        heads.second()
        output.second()
        serve(len(steps) - 1 - serve.done)
        shared_line(0, pair_share)
        across_share = share_line(1, links.across)
        serve(2)
        expand_slots = Slots(*[total_rows.at[n] for n in range(4)])
        expand.third(expand_slots, expand_grad.at[half_rows, :], total_rows.shape[1])
        serve(len(steps) + 4 - serve.done)
        expand_slots.end()
        total_slots = Slots(*[total_rows.at[n, :, pl.ds(0, heads_wide)] for n in range(4)])
        heads.third(total_slots, heads_grad.at[half_rows, :], total_rows.shape[1])
        output.third(column_slots, output_grad.at[:, half_rows], total_columns.shape[1])
        total_slots.end()
        column_slots.end()
        shared_line(1, across_share)
        for row in range(4):
            for side in range(2):
                at = 2 * row + side
                sums_out[row : row + 1, side * (width // 2) : (side + 1) * (width // 2)] = gains[2, at : at + 1, :]
        sums_out[4:8, :] = sums[2, 4:8, :]
        for copy in (*shrink.other, *output.other, *heads.other, *expand.other):
            copy.wait_recv()
        assert links.count <= COPIES and local.count <= LOCALS
        links.end()
        line_branch.end()
        line_up.end()
        local.end()


    pl.run_scoped(
        update,
        low(tokens, units),
        low(units, tokens),
        low(tokens, units),
        low(tokens, out_wide),
        low(4, out_wide, unit),
        low(2, out_wide, unit // 2),
        low(out_wide, unit),
        low(4, unit, units),
        low(4, unit // 4, units),
        low(4, out_wide, unit),
        low(2, 32, width),
    )


def block_call(line_size, x, g, heads_rows, output_rows, expand_weight, shrink_weight, vectors, order):
    tokens, width = x.shape
    heads_wide, out_wide, units = heads_rows.shape[1], output_rows.shape[0], expand_weight.shape[1]
    hd, unit, half = heads_wide // 6, width // 8, width // 16
    low = lambda *shape: pltpu.VMEM(shape, LOW)
    full = lambda *shape: pltpu.VMEM(shape, FULL)
    work = lambda *shape: jax.ShapeDtypeStruct(shape, LOW)
    outs = [
        work(tokens, width),
        work(tokens, width),
        work(2 * unit, heads_wide),
        work(out_wide, 2 * unit),
        work(2 * unit, units),
        work(units, 2 * unit),
        work(width, units),
        work(units, width),
        work(width, tokens),
        work(4, units, unit),
        work(4, out_wide, unit),
        work(4, unit, heads_wide),
        work(4, unit, units),
        work(4, units, unit),
        work(4, out_wide, unit),
        work(4, unit, heads_wide),
        jax.ShapeDtypeStruct((8, width), FULL),
    ]
    scratch = [
        *[low(tokens, width)] * 4, low(width, tokens), full(tokens, 256),
        low(width, heads_wide), low(out_wide, width), low(4, 4 * tokens, hd), low(2 * tokens, hd),
        low(out_wide, tokens), low(tokens, heads_wide), low(2, 2 * tokens, hd),
        *[low(tokens, width)] * 4,
        low(2, half, heads_wide), low(2, unit, heads_wide),
        low(2, out_wide, half), low(2, out_wide, unit),
        low(2, units, half), low(2, units, unit),
        low(2, half, units), low(2, unit, units),
        full(8, width), full(8, width), full(3, 8, width), full(1, 8, width), low(4, 16, width // 2), full(3, 8, width // 2), full(2, 8, width // 2),
        pltpu.SemaphoreType.DMA((3, 2)),
        pltpu.SemaphoreType.DMA((8,)),
        pltpu.SemaphoreType.DMA((LOCALS,)),
        pltpu.SemaphoreType.DMA((COPIES,)),
        pltpu.SemaphoreType.DMA((COPIES,)),
    ]
    return pl.pallas_call(
        functools.partial(block_kernel, hd**-0.5, line_size),
        out_shape=outs,
        in_specs=[ANY] * 6 + [IN_VMEM] * 8 + [pl.BlockSpec(memory_space=pltpu.SMEM)],
        out_specs=[ANY] * 16 + [IN_VMEM],
        scratch_shapes=scratch,
        compiler_params=pltpu.CompilerParams(
            collective_id=0, has_side_effects=True, vmem_limit_bytes=VMEM_BYTES
        ),
    )(x, g, heads_rows, output_rows, expand_weight, shrink_weight, *vectors, order)


def square_local(
    layer_input,
    block_order,
    first_gain,
    first_bias,
    second_gain,
    second_bias,
    heads_weight,
    heads_bias,
    output_weight,
    output_bias,
    expand_weight,
    expand_bias,
    shrink_weight,
    shrink_bias,
    cotangent,
):
    heads_rows = heads_weight.reshape(heads_weight.shape[0], -1)
    output_rows = output_weight.reshape(-1, output_weight.shape[2])
    vectors = (first_gain, first_bias, second_gain, second_bias, expand_bias, heads_bias, output_bias, shrink_bias)
    *results, sums = block_call(
        lax.axis_size("tensor"),
        layer_input[0],
        cotangent[0],
        heads_rows,
        output_rows,
        expand_weight,
        shrink_weight,
        vectors,
        block_order,
    )
    results = store_call(results[:6], sums, heads_weight.shape)
    layer_output, input_grad, heads_grad, output_grad, expand_grad, shrink_grad = results[:6]
    first_gain_grad, first_bias_grad, second_gain_grad, second_bias_grad = (vec.reshape(-1) for vec in results[6:10])
    output_bias_grad, expand_bias_grad, shrink_bias_grad = (vec.reshape(-1) for vec in results[10:13])
    return (
        layer_output[None],
        input_grad[None],
        first_gain_grad,
        first_bias_grad,
        second_gain_grad,
        second_bias_grad,
        heads_grad,
        results[13],
        output_grad.reshape(output_weight.shape),
        output_bias_grad,
        expand_grad,
        expand_bias_grad,
        shrink_grad,
        shrink_bias_grad,
    )


def store_kernel(*refs):
    *full_in, sums = refs[:7]
    full_out, rows_out, heads_bias_out = refs[7:13], refs[13:20], refs[20]
    for source, target in zip(full_in, full_out):
        if len(target.shape) == len(source.shape):
            target[...] = source[...].astype(target.dtype)
        else:
            wide = target.shape[2]
            for head in range(target.shape[1]):
                target[:, head, :] = source[:, head * wide : (head + 1) * wide].astype(target.dtype)

    @pl.when(pl.program_id(0) == 0)
    def _():
        for row, target in zip((0, 1, 2, 3, 4, 5, 4), rows_out):
            target[...] = sums[row : row + 1, :]
        wide = heads_bias_out.shape[1]
        for head in range(heads_bias_out.shape[0]):
            heads_bias_out[head : head + 1, :] = sums[6:7, head * wide : (head + 1) * wide]


def store_call(results, sums, heads_shape):
    steps = 2
    width = sums.shape[1]

    def cut(shape):
        zeros = (0,) * (len(shape) - 1)
        return pl.BlockSpec((shape[0] // steps,) + tuple(shape[1:]), lambda i: (i, *zeros))

    def whole(shape):
        return pl.BlockSpec(tuple(shape), lambda i: (0,) * len(shape))

    kept = [result.shape for result in results]
    kept[2] = heads_shape
    rows, heads_bias = (1, width), heads_shape[1:]
    outs = [jax.ShapeDtypeStruct(shape, FULL if i else LOW) for i, shape in enumerate(kept)]
    outs += [jax.ShapeDtypeStruct(rows, FULL)] * 7 + [jax.ShapeDtypeStruct(heads_bias, FULL)]
    return pl.pallas_call(
        store_kernel,
        grid=(steps,),
        out_shape=outs,
        in_specs=[cut(result.shape) for result in results] + [whole(sums.shape)],
        out_specs=[cut(shape) for shape in kept] + [whole(rows)] * 7 + [whole(heads_bias)],
        compiler_params=pltpu.CompilerParams(vmem_limit_bytes=VMEM_BYTES),
    )(*results, sums)


def ring_local(
    layer_input,
    block_order,
    first_gain,
    first_bias,
    second_gain,
    second_bias,
    heads_weight,
    heads_bias,
    output_weight,
    output_bias,
    expand_weight,
    expand_bias,
    shrink_weight,
    shrink_bias,
    cotangent,
):
    tokens_here = layer_input.shape[1]
    fsdp_count = lax.axis_size("fsdp")
    head_dim = output_weight.shape[1]
    score_scale = head_dim ** (-0.5)
    order_row = block_order[0]
    device_slot = lax.axis_index("fsdp")
    own_block = jnp.sum(
        jnp.where(jnp.arange(fsdp_count, dtype=jnp.int32) == device_slot, order_row, 0)
    )
    offsets = jnp.arange(tokens_here, dtype=jnp.int32)
    query_pos = own_block * tokens_here + offsets
    key_pos = jnp.repeat(order_row, tokens_here) * tokens_here + jnp.tile(offsets, fsdp_count)
    allowed = key_pos[None, :] <= query_pos[:, None]
    cosine, sine_part = rotary_tables(query_pos, ROT)
    hidden_in = layer_input[0].astype(jnp.float32)
    gain_one = first_gain.astype(jnp.float32)
    shift_one = first_bias.astype(jnp.float32)
    gain_two = second_gain.astype(jnp.float32)
    shift_two = second_bias.astype(jnp.float32)
    norm_one_low = layer_norm(hidden_in, gain_one, shift_one).astype(jnp.bfloat16)
    norm_two_low = layer_norm(hidden_in, gain_two, shift_two).astype(jnp.bfloat16)
    heads_full, output_full, expand_full, shrink_full = (
        lax.all_gather(heads_weight, "fsdp", axis=0, tiled=True),
        lax.all_gather(output_weight, "fsdp", axis=2, tiled=True),
        lax.all_gather(expand_weight, "fsdp", axis=0, tiled=True),
        lax.all_gather(shrink_weight, "fsdp", axis=1, tiled=True),
    )
    projected = jnp.einsum(
        "td,dhe->hte", norm_one_low, heads_full, preferred_element_type=jnp.float32
    )
    projected = projected + heads_bias.astype(jnp.float32)[:, None, :]
    query_pre = projected[..., :head_dim]
    key_pre = projected[..., head_dim : 2 * head_dim]
    query_low = rotate(query_pre, cosine, sine_part).astype(jnp.bfloat16)
    key_low = rotate(key_pre, cosine, sine_part).astype(jnp.bfloat16)
    value_low = projected[..., 2 * head_dim :].astype(jnp.bfloat16)
    key_all, value_all = (
        lax.all_gather(key_low, "fsdp", axis=1, tiled=True),
        lax.all_gather(value_low, "fsdp", axis=1, tiled=True),
    )

    def attend_head(operands):
        query_head, key_head, value_head = operands
        probability = softmax_rows(contract_last(query_head, key_head) * score_scale, allowed)
        return jnp.dot(
            probability.astype(jnp.bfloat16), value_head, preferred_element_type=jnp.float32
        )

    context = lax.map(attend_head, (query_low, key_all, value_all))
    context_low = context.astype(jnp.bfloat16)
    expand_in = jnp.dot(
        norm_two_low, expand_full, preferred_element_type=jnp.float32
    ) + expand_bias.astype(jnp.float32)
    activation_low = jax.nn.gelu(expand_in, approximate=False).astype(jnp.bfloat16)
    branch_part = jnp.einsum(
        "hte,hed->td", context_low, output_full, preferred_element_type=jnp.float32
    )
    branch_part = branch_part + jnp.dot(
        activation_low, shrink_full, preferred_element_type=jnp.float32
    )
    branch = lax.psum(branch_part, "tensor")
    layer_output = (
        hidden_in + branch + output_bias.astype(jnp.float32) + shrink_bias.astype(jnp.float32)
    ).astype(jnp.bfloat16)[None]
    heads_back, output_back, expand_back, shrink_back = (
        lax.all_gather(heads_weight, "fsdp", axis=0, tiled=True),
        lax.all_gather(output_weight, "fsdp", axis=2, tiled=True),
        lax.all_gather(expand_weight, "fsdp", axis=0, tiled=True),
        lax.all_gather(shrink_weight, "fsdp", axis=1, tiled=True),
    )
    key_back, value_back = (
        lax.all_gather(key_low, "fsdp", axis=1, tiled=True),
        lax.all_gather(value_low, "fsdp", axis=1, tiled=True),
    )
    grad_out = cotangent[0]
    grad_float = grad_out.astype(jnp.float32)
    output_weight_grad = jnp.einsum(
        "hte,td->hed", context_low, grad_out, preferred_element_type=jnp.float32
    )
    shrink_weight_grad = contract_first(activation_low, grad_out)
    bias_total = jnp.sum(grad_float, 0)
    context_grad = jnp.einsum(
        "td,hed->hte", grad_out, output_back, preferred_element_type=jnp.float32
    ).astype(jnp.bfloat16)
    activation_grad = contract_last(grad_out, shrink_back)
    _, gelu_back = jax.vjp(lambda inner_val: jax.nn.gelu(inner_val, approximate=False), expand_in)
    expand_grad = gelu_back(activation_grad)[0].astype(jnp.bfloat16)
    expand_weight_grad = contract_first(norm_two_low, expand_grad)
    expand_bias_grad = jnp.sum(expand_grad.astype(jnp.float32), 0)
    norm_two_grad = contract_last(expand_grad, expand_back)

    def attend_back(operands):
        query_head, key_head, value_head, context_head = operands
        probability = softmax_rows(contract_last(query_head, key_head) * score_scale, allowed)
        prob_low = probability.astype(jnp.bfloat16)
        weight_grad = contract_last(context_head, value_head)
        row_inner = jnp.sum(probability * weight_grad, -1, keepdims=True)
        score_grad = (probability * (weight_grad - row_inner)).astype(jnp.bfloat16)
        query_grad = jnp.dot(score_grad, key_head, preferred_element_type=jnp.float32) * score_scale
        key_grad = contract_first(score_grad, query_head) * score_scale
        value_grad = contract_first(prob_low, context_head)
        return (query_grad, key_grad, value_grad)

    query_grad, key_grad_all, value_grad_all = lax.map(
        attend_back, (query_low, key_back, value_back, context_grad)
    )
    key_grad, value_grad = (
        lax.psum_scatter(key_grad_all, "fsdp", scatter_dimension=1, tiled=True),
        lax.psum_scatter(value_grad_all, "fsdp", scatter_dimension=1, tiled=True),
    )
    _, rotate_back = jax.vjp(lambda inner_val: rotate(inner_val, cosine, sine_part), query_pre)
    projected_grad = jnp.concatenate(
        [rotate_back(query_grad)[0], rotate_back(key_grad)[0], value_grad], -1
    ).astype(jnp.bfloat16)
    heads_weight_grad = jnp.einsum(
        "td,hte->dhe", norm_one_low, projected_grad, preferred_element_type=jnp.float32
    )
    heads_bias_grad = jnp.sum(projected_grad.astype(jnp.float32), 1)
    norm_one_grad = jnp.einsum(
        "hte,dhe->td", projected_grad, heads_back, preferred_element_type=jnp.float32
    )
    norm_one_grad, norm_two_grad = lax.psum((norm_one_grad, norm_two_grad), "tensor")
    _, first_back = jax.vjp(layer_norm, hidden_in, gain_one, shift_one)
    input_first, first_gain_grad, first_bias_grad = first_back(norm_one_grad)
    _, second_back = jax.vjp(layer_norm, hidden_in, gain_two, shift_two)
    input_second, second_gain_grad, second_bias_grad = second_back(norm_two_grad)
    input_grad = (grad_float + input_first + input_second)[None]
    small_sums = lax.psum(
        (
            first_gain_grad,
            first_bias_grad,
            second_gain_grad,
            second_bias_grad,
            bias_total,
            expand_bias_grad,
            heads_bias_grad,
        ),
        ("replica", "fsdp"),
    )
    shard_parts = (
        lax.psum_scatter(heads_weight_grad, "fsdp", scatter_dimension=0, tiled=True),
        lax.psum_scatter(output_weight_grad, "fsdp", scatter_dimension=2, tiled=True),
        lax.psum_scatter(expand_weight_grad, "fsdp", scatter_dimension=0, tiled=True),
        lax.psum_scatter(shrink_weight_grad, "fsdp", scatter_dimension=1, tiled=True),
    )
    reduced = lax.psum((shard_parts[0], shard_parts[1], shard_parts[2], shard_parts[3]), "replica")
    return (
        layer_output,
        input_grad,
        small_sums[0],
        small_sums[1],
        small_sums[2],
        small_sums[3],
        reduced[0],
        small_sums[6],
        reduced[1],
        small_sums[4],
        reduced[2],
        small_sums[5],
        reduced[3],
        small_sums[4],
    )


def solution(mesh):
    placed = (
        P("replica", "fsdp", None),
        P("replica", None),
        P(),
        P(),
        P(),
        P(),
        P("fsdp", "tensor", None),
        P("tensor", None),
        P("tensor", None, "fsdp"),
        P(),
        P("fsdp", "tensor"),
        P("tensor"),
        P("tensor", "fsdp"),
        P(),
        P("replica", "fsdp", None),
    )
    local = square_local if mesh.shape["fsdp"] == 4 and mesh.shape["replica"] == 2 and mesh.shape["tensor"] == 4 else ring_local
    return jax.shard_map(
        local,
        mesh=mesh,
        in_specs=placed,
        out_specs=(
            P("replica", "fsdp", None),
            P("replica", "fsdp", None),
            P(),
            P(),
            P(),
            P(),
            P("fsdp", "tensor", None),
            P("tensor", None),
            P("tensor", None, "fsdp"),
            P(),
            P("fsdp", "tensor"),
            P("tensor"),
            P("tensor", "fsdp"),
            P(),
        ),
        check_vma=False,
    )
```
